32 devices in a mesh: dp: 8 (over z, y), seq: 4 (over x, core).
Axes of the slice: x: 2, y: 2, z: 4, core: 2. Of those that a mesh axis runs over, the one named last changes fastest.
Arguments:
- tokens: bfloat16 [8, 2048, 1024], P('dp', 'seq'), may hold values from -6 to 6
- doc_ids: int32 [8, 2048], P('dp'), may hold values from 0 to 2, as said below
- cotangent: bfloat16 [8, 2048, 1024], P('dp', 'seq'), may hold values from -6 to 6
- w_qkv: float32 [1024, 3072], P(('dp', 'seq')), may hold values from -0.1875 to 0.1875
- w_out: float32 [1024, 1024], P(('dp', 'seq')), may hold values from -0.1875 to 0.1875
- attn_vecs: float32 [7, 1024], P(None, ('dp', 'seq'))
- head_scale: float32 [16], replicated, may hold values from 0.1 to 1.9
- w_fc1: float32 [1024, 4096], P(('dp', 'seq')), may hold values from -0.1875 to 0.1875
- w_fc2: float32 [4096, 1024], P(('dp', 'seq')), may hold values from -0.09375 to 0.09375
- ffn_vecs: float32 [3, 1024], P(None, ('dp', 'seq'))
- ffn_wide: float32 [3, 4096], P(None, ('dp', 'seq'))
Outputs:
- outputs: bfloat16 [8, 2048, 1024], P('dp', 'seq')
- grad_tokens: bfloat16 [8, 2048, 1024], P('dp', 'seq')
- grad_w_qkv: float32 [1024, 3072], P(('dp', 'seq'))
- grad_w_out: float32 [1024, 1024], P(('dp', 'seq'))
- grad_attn_vecs: float32 [7, 1024], P(None, ('dp', 'seq'))
- grad_head_scale: float32 [16], replicated
- grad_w_fc1: float32 [1024, 4096], P(('dp', 'seq'))
- grad_w_fc2: float32 [4096, 1024], P(('dp', 'seq'))
- grad_ffn_vecs: float32 [3, 1024], P(None, ('dp', 'seq'))
- grad_ffn_wide: float32 [3, 4096], P(None, ('dp', 'seq'))
The draws below stay inside these ranges and needn't reach their ends.
Inputs may be any that keep to these rules, and one draw needn't show every extreme that they name: `doc_ids`: every row holds three documents numbered 0, 1, 2 in order of position, each of one or more positions; document 1 begins before position 512 and ends at or after position 1536.
All inputs are finite; a program needn't handle non-finite values.
Results may differ from the reference program's by a relative error of at most 0.011.
Values may be sent and summed in bfloat16 or wider, within the bound.
A program may use at most 256 MiB of HBM per device.

```python
import math
import jax
import jax.numpy as jnp
from jax import lax

D = 1024
H = 16
HD = 64
FF = 4096
LEN = 2048
ROWS = 8
SPAN = 512


def vector_rows(key, gain_flags, row_count, row_width, spread, bias_scale):
    gain_key, bias_key = jax.random.split(key)
    gain_part = 1.0 + spread * jax.random.uniform(gain_key, (row_count, row_width), jnp.float32, -1.0, 1.0)
    bias_part = bias_scale * jax.random.normal(bias_key, (row_count, row_width), jnp.float32)
    chosen = jnp.array(gain_flags)[:, None] > 0
    return jnp.where(chosen, gain_part, bias_part)


def draw_attn_vecs(key, part):
    key = jax.random.fold_in(key, 11)
    return vector_rows(key, (1, 0, 0, 0, 0, 1, 0), 7, D, 0.3, 0.3)


def draw_ffn_vecs(key, part):
    key = jax.random.fold_in(key, 13)
    return vector_rows(key, (1, 0, 0), 3, D, 0.3, 0.3)


def draw_ffn_wide(key, part):
    key = jax.random.fold_in(key, 17)
    return vector_rows(key, (0, 1, 0), 3, FF, 0.3, 0.3)


def draw_doc_ids(key, part):
    key = jax.random.fold_in(key, 5)
    start_key, stop_key = jax.random.split(key)
    long_start = jax.random.randint(start_key, (ROWS, 1), 1, SPAN)
    long_stop = jax.random.randint(stop_key, (ROWS, 1), LEN - SPAN + 1, LEN)
    position = jnp.arange(LEN)[None, :]
    return ((position >= long_start).astype(jnp.int32) + (position >= long_stop).astype(jnp.int32)).astype(jnp.int32)


def levels(key, shape, cuts, smallest, top_value):
    def one(dim, blocks):
        heights = jax.random.uniform(jax.random.fold_in(jax.random.fold_in(key, 6), dim), (blocks,), jnp.float32, smallest / len(cuts), top_value / len(cuts))
        return jnp.repeat(jnp.exp(heights), shape[dim] // blocks).reshape((-1,) + (1,) * (len(shape) - dim - 1))

    gain = one(*cuts[0])
    for cut in cuts[1:]:
        gain = gain * one(*cut)
    return gain


def normal_values(key, dims, deviation, reach, cuts=(), dtype=jnp.bfloat16):
    result = jax.random.normal(key, dims, jnp.float32) * deviation
    if len(cuts) > 0:
        result = levels(key, dims, cuts, -0.22, 0.18) * result
    return jnp.clip(result, min=-reach, max=reach).astype(dtype)


def setup_inputs(seed: int = 0) -> dict:
    keys = jax.random.split(jax.random.key(seed), 12)
    return {
        "tokens": normal_values(keys[0], (ROWS, LEN, D), 1.0, 6.0, ((0, 8), (1, 4))),
        "doc_ids": draw_doc_ids(jax.random.fold_in(keys[11], 71), 0),
        "cotangent": normal_values(keys[2], (ROWS, LEN, D), 1.0, 6.0, ((0, 8), (1, 4))),
        "w_qkv": normal_values(keys[3], (D, 3 * D), D ** -0.5, 0.1875, ((0, 32),), jnp.float32),
        "w_out": normal_values(keys[4], (D, D), D ** -0.5, 0.1875, ((0, 32),), jnp.float32),
        "attn_vecs": draw_attn_vecs(jax.random.fold_in(keys[11], 71), 0),
        "head_scale": jnp.clip(1.0 + 0.18 * jax.random.normal(keys[6], (H,), jnp.float32), 0.1, 1.9),
        "w_fc1": normal_values(keys[7], (D, FF), D ** -0.5, 0.1875, ((0, 32),), jnp.float32),
        "w_fc2": normal_values(keys[8], (FF, D), FF ** -0.5, 0.09375, ((0, 32),), jnp.float32),
        "ffn_vecs": draw_ffn_vecs(jax.random.fold_in(keys[11], 71), 0),
        "ffn_wide": draw_ffn_wide(jax.random.fold_in(keys[11], 71), 0),
    }


EPSILON = 1e-05
NEGATIVE = -1e+30

@jax.custom_vjp
def low(v):
    return lax.optimization_barrier(v.astype(jnp.bfloat16)).astype(jnp.float32)

@jax.custom_vjp
def low_back(v):
    return v

def low_keep(v):
    return (low(v), None)

def low_pass(kept, grad):
    return (grad,)

def back_keep(v):
    return (v, None)

def back_low(kept, grad):
    return (low(grad),)
low.defvjp(low_keep, low_pass)
low_back.defvjp(back_keep, back_low)

def normalize(values):
    centre = lax.optimization_barrier(jnp.mean(values, -1, keepdims=True))
    centred = values - centre
    return centred * lax.rsqrt(lax.optimization_barrier(jnp.mean(centred * centred, -1, keepdims=True)) + EPSILON)

def gelu_exact(values):
    return 0.5 * values * (1.0 + jax.scipy.special.erf(values * math.sqrt(0.5)))

def project(operand, matrix):
    return jnp.einsum('gtd,de->gte', operand, matrix, precision=lax.Precision.HIGHEST)

def block_layer(inputs, doc_rows, weights):
    w_qkv, w_out, attn_vecs, head_scale, w_fc1, w_fc2, ffn_vecs, ffn_wide = weights
    highest = lax.Precision.HIGHEST
    group_size = inputs.shape[0]
    act_one = low(normalize(inputs) * attn_vecs[0] + attn_vecs[1])
    projected = project(act_one, w_qkv)
    queries = low_back(low(projected[..., :D] + attn_vecs[2])).reshape(group_size, LEN, H, HD)
    keys_all = low_back(low(projected[..., D:2 * D])).reshape(group_size, LEN, H, HD)
    values_all = low_back(low(projected[..., 2 * D:] + attn_vecs[3])).reshape(group_size, LEN, H, HD)
    raw_scores = low_back(jnp.einsum('gqhe,gkhe->ghqk', queries, keys_all, precision=highest))
    position = jnp.arange(LEN)
    allowed = (position[None, :] <= position[:, None])[None] & (doc_rows[:, :, None] == doc_rows[:, None, :])
    scores = jnp.where(allowed[:, None], raw_scores * HD ** (-0.5), NEGATIVE)
    shifted = jnp.exp(scores - lax.optimization_barrier(jnp.max(scores, -1, keepdims=True)))
    probs = low(shifted / lax.optimization_barrier(jnp.sum(shifted, -1, keepdims=True)))
    attended = low_back(jnp.einsum('ghqk,gkhe->gqhe', probs, values_all, precision=highest))
    scaled = low((attended * head_scale[None, None, :, None]).reshape(group_size, LEN, D))
    branch = low_back(project(scaled, w_out) + attn_vecs[4])
    hidden = inputs + normalize(branch) * attn_vecs[5] + attn_vecs[6]
    act_two = low(normalize(hidden) * ffn_vecs[0] + ffn_vecs[1])
    inner_act = low_back(project(act_two, w_fc1) + ffn_wide[0])
    mixed_act = low(normalize(gelu_exact(inner_act)) * ffn_wide[1] + ffn_wide[2])
    return hidden + low_back(project(mixed_act, w_fc2) + ffn_vecs[2])

def reference(tokens, doc_ids, cotangent, w_qkv, w_out, attn_vecs, head_scale, w_fc1, w_fc2, ffn_vecs, ffn_wide):
    group_size = math.gcd(ROWS, max(1, 2048 // LEN))

    def forward(inputs, master_qkv, master_out, master_attn, master_scale, master_fc1, master_fc2, master_ffn, master_wide):
        weights = (low(master_qkv), low(master_out), low(master_attn), master_scale, low(master_fc1), low(master_fc2), low(master_ffn), low(master_wide))
        grouped = inputs.reshape(ROWS // group_size, group_size, LEN, D)
        doc_groups = doc_ids.reshape(ROWS // group_size, group_size, LEN)

        def one_group(paired):
            return block_layer(paired[0], paired[1], weights)
        results = lax.map(jax.checkpoint(one_group), (grouped, doc_groups))
        return results.reshape(ROWS, LEN, D)
    outputs, pullback = jax.vjp(forward, tokens.astype(jnp.float32), w_qkv, w_out, attn_vecs, head_scale, w_fc1, w_fc2, ffn_vecs, ffn_wide)
    grads = pullback(cotangent.astype(jnp.float32))
    return (outputs.astype(jnp.bfloat16), grads[0].astype(jnp.bfloat16), grads[1], grads[2], grads[3], grads[4], grads[5], grads[6], grads[7], grads[8])
```

```python
import functools
import math

import jax
import jax.numpy as jnp
from jax import lax
from jax.experimental import pallas as pl
from jax.experimental.pallas import tpu as pltpu
from jax.sharding import PartitionSpec as P

EPSILON = 1e-05
NEGATIVE = -1e30
MESH = pl.DeviceIdType.MESH
BF = jnp.bfloat16
F32 = jnp.float32
NZ, NY, NX, NC = 4, 2, 2, 2
HBM = pl.BlockSpec(memory_space=pl.ANY)
VM = pl.BlockSpec(memory_space=pltpu.VMEM)


def normalize(values):
    centre = jnp.mean(values, -1, keepdims=True)
    centred = values - centre
    scale_inv = lax.rsqrt(jnp.mean(centred * centred, -1, keepdims=True) + EPSILON)
    return (centred * scale_inv, scale_inv)


def norm_back(grad_normed, normed, scale_inv):
    return scale_inv * (
        grad_normed
        - jnp.mean(grad_normed, -1, keepdims=True)
        - normed * jnp.mean(grad_normed * normed, -1, keepdims=True)
    )


def gelu_exact(values):
    return 0.5 * values * (1.0 + jax.scipy.special.erf(values * math.sqrt(0.5)))


def left_grad(activations, gradients):
    return lax.dot_general(
        activations, gradients, (((0,), (0,)), ((), ())), preferred_element_type=jnp.float32
    )


def right_back(gradients, matrix):
    return lax.dot_general(
        gradients, matrix, (((1,), (1,)), ((), ())), preferred_element_type=jnp.float32
    )


def masked_scores(queries, keys_block, query_pos, key_pos, query_ids, key_ids):
    raw_scores = jnp.einsum(
        "rqhe,rkhe->rhqk", queries, keys_block, preferred_element_type=jnp.float32
    )
    allowed = (key_pos[None, None, :] <= query_pos[None, :, None]) & (
        key_ids[:, None, :] == query_ids[:, :, None]
    )
    return jnp.where(allowed[:, None], raw_scores * queries.shape[3] ** (-0.5), NEGATIVE)


def attend(queries, keys_all, values_all, query_pos, query_ids, doc_rows, block_len):
    block_count = keys_all.shape[1] // block_len
    stat_shape = (queries.shape[0], queries.shape[2], queries.shape[1])

    def slice_block(block_index):
        start = block_index * block_len
        keys_block = lax.dynamic_slice_in_dim(keys_all, start, block_len, 1)
        values_block = lax.dynamic_slice_in_dim(values_all, start, block_len, 1)
        key_ids = lax.dynamic_slice_in_dim(doc_rows, start, block_len, 1)
        key_pos = start + jnp.arange(block_len, dtype=jnp.int32)
        return (
            values_block,
            masked_scores(queries, keys_block, query_pos, key_pos, query_ids, key_ids),
        )

    def first_pass(carry, block_index):
        running_max, running_sum = carry
        _, scores = slice_block(block_index)
        new_max = jnp.maximum(running_max, jnp.max(scores, -1))
        running_sum = running_sum * jnp.exp(running_max - new_max) + jnp.sum(
            jnp.exp(scores - new_max[..., None]), -1
        )
        return ((new_max, running_sum), None)

    start_stats = (jnp.full(stat_shape, NEGATIVE, jnp.float32), jnp.zeros(stat_shape, jnp.float32))
    (row_max, row_sum), _ = lax.scan(
        first_pass, start_stats, jnp.arange(block_count, dtype=jnp.int32)
    )
    log_total = row_max + jnp.log(row_sum)

    def second_pass(total_out, block_index):
        values_block, scores = slice_block(block_index)
        probs = jnp.exp(scores - log_total[..., None]).astype(jnp.bfloat16)
        return (
            total_out
            + jnp.einsum(
                "rhqk,rkhe->rqhe", probs, values_block, preferred_element_type=jnp.float32
            ),
            None,
        )

    attended, _ = lax.scan(
        second_pass, jnp.zeros(queries.shape, jnp.float32), jnp.arange(block_count, dtype=jnp.int32)
    )
    return (attended, log_total)


def attend_back(
    queries,
    keys_all,
    values_all,
    grad_out,
    log_total,
    delta,
    query_pos,
    query_ids,
    doc_rows,
    block_len,
):
    block_count = keys_all.shape[1] // block_len
    scale = queries.shape[3] ** (-0.5)

    def step(grad_queries, block_index):
        start = block_index * block_len
        keys_block = lax.dynamic_slice_in_dim(keys_all, start, block_len, 1)
        values_block = lax.dynamic_slice_in_dim(values_all, start, block_len, 1)
        key_ids = lax.dynamic_slice_in_dim(doc_rows, start, block_len, 1)
        key_pos = start + jnp.arange(block_len, dtype=jnp.int32)
        scores = masked_scores(queries, keys_block, query_pos, key_pos, query_ids, key_ids)
        probs = jnp.exp(scores - log_total[..., None])
        grad_probs = jnp.einsum(
            "rqhe,rkhe->rhqk", grad_out, values_block, preferred_element_type=jnp.float32
        )
        grad_scores = (probs * (grad_probs - delta[..., None]) * scale).astype(jnp.bfloat16)
        grad_queries = grad_queries + jnp.einsum(
            "rhqk,rkhe->rqhe", grad_scores, keys_block, preferred_element_type=jnp.float32
        )
        grad_keys = jnp.einsum(
            "rhqk,rqhe->rkhe", grad_scores, queries, preferred_element_type=jnp.float32
        )
        grad_values = jnp.einsum(
            "rhqk,rqhe->rkhe",
            probs.astype(jnp.bfloat16),
            grad_out,
            preferred_element_type=jnp.float32,
        )
        return (grad_queries, (grad_keys, grad_values))

    return lax.scan(
        step, jnp.zeros(queries.shape, jnp.float32), jnp.arange(block_count, dtype=jnp.int32)
    )


def local(
    tokens,
    doc_ids,
    cotangent,
    w_qkv,
    w_out,
    attn_vecs,
    head_scale,
    w_fc1,
    w_fc2,
    ffn_vecs,
    ffn_wide,
):
    row_count, span_len, model_width = tokens.shape
    head_count = head_scale.shape[0]
    head_size = model_width // head_count
    token_count = row_count * span_len
    brain = jnp.bfloat16
    single = jnp.float32
    gathered_qkv, gathered_out, attn_rows = (
        lax.all_gather(w_qkv.astype(brain), ("dp", "seq"), axis=0, tiled=True),
        lax.all_gather(w_out.astype(brain), ("dp", "seq"), axis=0, tiled=True),
        lax.all_gather(attn_vecs.astype(brain), ("dp", "seq"), axis=1, tiled=True),
    )
    attn_rows = attn_rows.astype(single)
    inputs = tokens.astype(single).reshape(token_count, model_width)
    normed_one, inv_one = normalize(inputs)
    act_one = (normed_one * attn_rows[0] + attn_rows[1]).astype(brain)
    projected = jnp.dot(act_one, gathered_qkv, preferred_element_type=single)
    queries = (projected[:, :model_width] + attn_rows[2]).astype(brain)
    keys_own = projected[:, model_width : 2 * model_width].astype(brain)
    values_own = (projected[:, 2 * model_width :] + attn_rows[3]).astype(brain)
    keys_all, values_all = (
        lax.all_gather(
            keys_own.reshape(row_count, span_len, model_width), "seq", axis=1, tiled=True
        ),
        lax.all_gather(
            values_own.reshape(row_count, span_len, model_width), "seq", axis=1, tiled=True
        ),
    )
    offset = lax.axis_index("seq") * span_len
    query_pos = offset + jnp.arange(span_len, dtype=jnp.int32)
    query_ids = lax.dynamic_slice_in_dim(doc_ids, offset, span_len, 1)
    queries_four = queries.reshape(row_count, span_len, head_count, head_size)
    keys_four = keys_all.reshape(row_count, -1, head_count, head_size)
    values_four = values_all.reshape(row_count, -1, head_count, head_size)
    attended, log_total = attend(
        queries_four, keys_four, values_four, query_pos, query_ids, doc_ids, span_len
    )
    scaled = (
        (attended * head_scale[None, None, :, None]).reshape(token_count, model_width).astype(brain)
    )
    branch = jnp.dot(scaled, gathered_out, preferred_element_type=single) + attn_rows[4]
    normed_branch, inv_branch = normalize(branch)
    hidden = inputs + normed_branch * attn_rows[5] + attn_rows[6]
    gathered_fc1, gathered_fc2, ffn_rows, wide_rows = (
        lax.all_gather(w_fc1.astype(brain), ("dp", "seq"), axis=0, tiled=True),
        lax.all_gather(w_fc2.astype(brain), ("dp", "seq"), axis=0, tiled=True),
        lax.all_gather(ffn_vecs.astype(brain), ("dp", "seq"), axis=1, tiled=True),
        lax.all_gather(ffn_wide.astype(brain), ("dp", "seq"), axis=1, tiled=True),
    )
    ffn_rows = ffn_rows.astype(single)
    wide_rows = wide_rows.astype(single)
    normed_two, inv_two = normalize(hidden)
    act_two = (normed_two * ffn_rows[0] + ffn_rows[1]).astype(brain)
    inner_act = jnp.dot(act_two, gathered_fc1, preferred_element_type=single) + wide_rows[0]
    activated, gelu_pull = jax.vjp(gelu_exact, inner_act)
    normed_three, inv_three = normalize(activated)
    mixed_act = (normed_three * wide_rows[1] + wide_rows[2]).astype(brain)
    result = hidden + jnp.dot(mixed_act, gathered_fc2, preferred_element_type=single) + ffn_rows[2]
    outputs = result.astype(brain).reshape(row_count, span_len, model_width)
    back_set = (
        lax.all_gather(w_qkv.astype(brain), ("dp", "seq"), axis=0, tiled=True),
        lax.all_gather(w_out.astype(brain), ("dp", "seq"), axis=0, tiled=True),
        lax.all_gather(attn_vecs.astype(brain), ("dp", "seq"), axis=1, tiled=True),
        lax.all_gather(w_fc1.astype(brain), ("dp", "seq"), axis=0, tiled=True),
        lax.all_gather(w_fc2.astype(brain), ("dp", "seq"), axis=0, tiled=True),
        lax.all_gather(ffn_vecs.astype(brain), ("dp", "seq"), axis=1, tiled=True),
        lax.all_gather(ffn_wide.astype(brain), ("dp", "seq"), axis=1, tiled=True),
    )
    gathered_qkv, gathered_out, attn_back, gathered_fc1, gathered_fc2, ffn_back, wide_back = (
        back_set
    )
    attn_rows = attn_back.astype(single)
    ffn_rows = ffn_back.astype(single)
    wide_rows = wide_back.astype(single)
    grad_top = cotangent.astype(single).reshape(token_count, model_width)
    grad_branch_two = grad_top.astype(brain)
    grad_fc2 = left_grad(mixed_act, grad_branch_two)
    grad_bias_two = jnp.sum(grad_branch_two.astype(single), 0)
    grad_mixed = right_back(grad_branch_two, gathered_fc2)
    grad_inner_gain = jnp.sum(grad_mixed * normed_three, 0)
    grad_inner_bias = jnp.sum(grad_mixed, 0)
    grad_activated = norm_back(grad_mixed * wide_rows[1], normed_three, inv_three)
    grad_inner = gelu_pull(grad_activated)[0].astype(brain)
    grad_fc1 = left_grad(act_two, grad_inner)
    grad_bias_one = jnp.sum(grad_inner.astype(single), 0)
    grad_act_two = right_back(grad_inner, gathered_fc1)
    grad_gain_two = jnp.sum(grad_act_two * normed_two, 0)
    grad_shift_two = jnp.sum(grad_act_two, 0)
    grad_hidden = grad_top + norm_back(grad_act_two * ffn_rows[0], normed_two, inv_two)
    ffn_sums = (
        lax.psum_scatter(grad_fc1, ("dp", "seq"), scatter_dimension=0, tiled=True),
        lax.psum_scatter(grad_fc2, ("dp", "seq"), scatter_dimension=0, tiled=True),
        lax.psum_scatter(
            jnp.stack([grad_gain_two, grad_shift_two, grad_bias_two]),
            ("dp", "seq"),
            scatter_dimension=1,
            tiled=True,
        ),
        lax.psum_scatter(
            jnp.stack([grad_bias_one, grad_inner_gain, grad_inner_bias]),
            ("dp", "seq"),
            scatter_dimension=1,
            tiled=True,
        ),
    )
    grad_post_gain = jnp.sum(grad_hidden * normed_branch, 0)
    grad_post_shift = jnp.sum(grad_hidden, 0)
    grad_branch = norm_back(grad_hidden * attn_rows[5], normed_branch, inv_branch).astype(brain)
    grad_out_bias = jnp.sum(grad_branch.astype(single), 0)
    grad_out = left_grad(scaled, grad_branch)
    grad_scaled = right_back(grad_branch, gathered_out).reshape(
        row_count, span_len, head_count, head_size
    )
    grad_scale = jnp.sum(grad_scaled * attended, (0, 1, 3))
    grad_attended = (grad_scaled * head_scale[None, None, :, None]).astype(brain)
    delta = jnp.transpose(jnp.sum(grad_attended.astype(single) * attended, -1), (0, 2, 1))
    grad_queries, key_parts = attend_back(
        queries_four,
        keys_four,
        values_four,
        grad_attended,
        log_total,
        delta,
        query_pos,
        query_ids,
        doc_ids,
        span_len,
    )
    partial_keys = jnp.transpose(key_parts[0], (1, 0, 2, 3, 4)).reshape(row_count, -1, model_width)
    partial_values = jnp.transpose(key_parts[1], (1, 0, 2, 3, 4)).reshape(
        row_count, -1, model_width
    )
    grad_keys, grad_values = (
        lax.psum_scatter(
            partial_keys.astype(jnp.bfloat16), "seq", scatter_dimension=1, tiled=True
        ).astype(jnp.float32),
        lax.psum_scatter(
            partial_values.astype(jnp.bfloat16), "seq", scatter_dimension=1, tiled=True
        ).astype(jnp.float32),
    )
    grad_qkv = jnp.concatenate(
        [
            grad_queries.reshape(token_count, model_width).astype(brain),
            grad_keys.reshape(token_count, model_width).astype(brain),
            grad_values.reshape(token_count, model_width).astype(brain),
        ],
        1,
    )
    grad_w_qkv = left_grad(act_one, grad_qkv)
    grad_query_bias = jnp.sum(grad_qkv[:, :model_width].astype(single), 0)
    grad_value_bias = jnp.sum(grad_qkv[:, 2 * model_width :].astype(single), 0)
    grad_act_one = right_back(grad_qkv, gathered_qkv)
    grad_gain_one = jnp.sum(grad_act_one * normed_one, 0)
    grad_shift_one = jnp.sum(grad_act_one, 0)
    grad_tokens = (
        (grad_hidden + norm_back(grad_act_one * attn_rows[0], normed_one, inv_one))
        .astype(brain)
        .reshape(row_count, span_len, model_width)
    )
    attn_stack = jnp.stack(
        [
            grad_gain_one,
            grad_shift_one,
            grad_query_bias,
            grad_value_bias,
            grad_out_bias,
            grad_post_gain,
            grad_post_shift,
        ]
    )
    attn_sums = (
        lax.psum_scatter(grad_w_qkv, ("dp", "seq"), scatter_dimension=0, tiled=True),
        lax.psum_scatter(grad_out, ("dp", "seq"), scatter_dimension=0, tiled=True),
        lax.psum_scatter(attn_stack, ("dp", "seq"), scatter_dimension=1, tiled=True),
    )
    scale_total = lax.psum(grad_scale, ("dp", "seq"))
    return (
        outputs,
        grad_tokens,
        attn_sums[0],
        attn_sums[1],
        attn_sums[2],
        scale_total,
        ffn_sums[0],
        ffn_sums[1],
        ffn_sums[2],
        ffn_sums[3],
    )


class Place:
    def __init__(self):
        self.dp = lax.axis_index("dp")
        self.seq = lax.axis_index("seq")
        self.z, self.y = self.dp // NY, self.dp % NY
        self.x, self.c = self.seq // NC, self.seq % NC

    def at(self, z=None, y=None, x=None, c=None):
        z = self.z if z is None else z
        y = self.y if y is None else y
        x = self.x if x is None else x
        c = self.c if c is None else c
        return (z * NY + y, x * NC + c)

    def zup(self, k):
        return (self.z + k) % NZ

    def group(self):
        near = [self.at(c=1 - self.c), self.at(x=1 - self.x), self.at(x=1 - self.x, c=1 - self.c)]
        return near + [self.at(y=1 - self.y)] + [self.at(z=self.zup(k)) for k in range(1, NZ)]


class Wire:
    def __init__(self, place, send, recv):
        self.place, self.send, self.recv, self.used, self.open = place, send, recv, 0, []

    def copy(self, src, dst, dev):
        n = self.used
        self.used += 1
        desc = pltpu.make_async_remote_copy(
            src_ref=src,
            dst_ref=dst,
            send_sem=self.send.at[n],
            recv_sem=self.recv.at[n],
            device_id=dev,
            device_id_type=MESH,
        )
        desc.start()
        self.open.append(desc)
        return desc

    def drain(self):
        for desc in self.open:
            desc.wait_send()


def greet(place):
    barrier = pltpu.get_barrier_semaphore()
    group = place.group()
    for dev in group:
        pl.semaphore_signal(barrier, inc=1, device_id=dev, device_id_type=MESH)
    pl.semaphore_wait(barrier, len(group))


def spread_zxy(wire, place, ref, swap=False):
    z, y, x = place.z, place.y, place.x
    own = ref.at[z, y, x]
    along_z = [wire.copy(own, own, place.at(z=place.zup(k))) for k in range(1, NZ)]
    first = place.at(y=1 - y) if swap else place.at(x=1 - x)
    second = place.at(x=1 - x) if swap else place.at(y=1 - y)

    def one(zk):
        return ref.at[zk, y, x]

    def two(zk):
        return ref.at[zk, :, x] if swap else ref.at[zk, y]

    firsts = [wire.copy(own, own, first)]
    yield
    for k in range(1, NZ):
        along_z[k - 1].wait_recv()
        zk = (z - k + NZ) % NZ
        firsts.append(wire.copy(one(zk), one(zk), first))
        yield
    seconds = []
    for k in range(NZ):
        firsts[k].wait_recv()
        zk = (z - k + NZ) % NZ
        seconds.append(wire.copy(two(zk), two(zk), second))
        yield
    for desc in seconds:
        desc.wait_recv()


def spread_xzy(wire, place, ref, swap=False):
    z, y, x = place.z, place.y, place.x
    own = ref.at[z, y, x]
    first = place.at(y=1 - y) if swap else place.at(x=1 - x)
    second = place.at(x=1 - x) if swap else place.at(y=1 - y)

    def two(zk):
        return ref.at[zk, :, x] if swap else ref.at[zk, y]

    start = wire.copy(own, own, first)
    yield
    start.wait_recv()
    step = wire.copy(two(z), two(z), place.at(z=place.zup(1)))
    seconds = [wire.copy(two(z), two(z), second)]
    yield
    for k in range(1, NZ):
        step.wait_recv()
        zk = (z - k + NZ) % NZ
        if k < NZ - 1:
            step = wire.copy(two(zk), two(zk), place.at(z=place.zup(1)))
        seconds.append(wire.copy(two(zk), two(zk), second))
        yield
    for desc in seconds:
        desc.wait_recv()


def rounds(tasks):
    tasks = list(tasks)
    while tasks:
        alive = []
        for task in tasks:
            try:
                next(task)
                alive.append(task)
            except StopIteration:
                pass
        tasks = alive


def gather_kernel(tok, wq4, vec, wo, f1, f2, tok_all, wq, vecs, wo_all, f1_all, f2_all, send, recv, local):
    place = Place()
    z, y, x, c, s, dp = place.z, place.y, place.x, place.c, place.seq, place.dp
    wire = Wire(place, send, recv)
    greet(place)
    core = place.at(c=1 - c)
    other = place.at(x=1 - x)
    across = place.at(x=1 - x, c=1 - c)
    rows = f1.shape[1]
    here = [
        pltpu.make_async_copy(tok, tok_all.at[s], local.at[0]),
        pltpu.make_async_copy(wq4.at[s], wq.at[dp, s], local.at[1]),
        pltpu.make_async_copy(vec, vecs.at[dp, s], local.at[2]),
        pltpu.make_async_copy(wo, wo_all.at[z, y, x, c], local.at[3]),
        pltpu.make_async_copy(f1.at[c], f1_all.at[z, y, x, pl.ds(c * rows, rows)], local.at[4]),
        pltpu.make_async_copy(f2, f2_all.at[z, y, x], local.at[5]),
    ]
    for desc in here:
        desc.start()
    quarter = []
    for dev, peer in ((core, s ^ 1), (other, s ^ 2), (across, s ^ 3)):
        quarter.append(wire.copy(wq4.at[peer], wq.at[dp, s], dev))
        quarter.append(wire.copy(vec, vecs.at[dp, s], dev))
    tok_x = wire.copy(tok, tok_all.at[s], other)
    tok_c = wire.copy(tok, tok_all.at[s], core)
    f1_c = wire.copy(f1.at[1 - c], f1_all.at[z, y, x, pl.ds(c * rows, rows)], core)
    for desc in here:
        desc.wait()
    for desc in quarter:
        desc.wait_recv()

    def by_dp(ref):
        own = ref.at[dp]
        along_z = [wire.copy(own, own, place.at(z=place.zup(k))) for k in range(1, NZ)]
        ys = [wire.copy(own, own, place.at(y=1 - y))]
        yield
        for k in range(1, NZ):
            along_z[k - 1].wait_recv()
            blk = ref.at[((z - k + NZ) % NZ) * NY + y]
            ys.append(wire.copy(blk, blk, place.at(y=1 - y)))
        yield
        for desc in ys:
            desc.wait_recv()

    def tokens():
        tok_x.wait_recv()
        blk = tok_all.at[s ^ 2]
        last = wire.copy(blk, blk, core)
        yield
        tok_c.wait_recv()
        last.wait_recv()

    f1_c.wait_recv()
    half1 = f1_all.shape[4] // 2
    half2 = f2_all.shape[3] // 2
    plane = wo_all.at[:, :, :, c]

    def outer():
        yield from spread_zxy(wire, place, plane)
        last = wire.copy(wo_all.at[:, :, :, c], wo_all.at[:, :, :, c], core)
        yield
        last.wait_recv()

    rounds(
        [
            by_dp(wq),
            by_dp(vecs),
            tokens(),
            spread_zxy(wire, place, f1_all.at[:, :, :, :, pl.ds(0, half1)]),
            spread_xzy(wire, place, f1_all.at[:, :, :, :, pl.ds(half1, half1)], swap=True),
            outer(),
            spread_zxy(wire, place, f2_all.at[:, :, :, pl.ds(0, half2)], swap=True),
            spread_xzy(wire, place, f2_all.at[:, :, :, pl.ds(half2, half2)]),
        ]
    )
    wire.drain()


COPIES = 96


def gather_all(tok, wq4, vec, wo, f1, f2):
    span, width = tok.shape
    rows, part = wq4.shape[1:]
    dps = NZ * NY
    out = (
        jax.ShapeDtypeStruct((NX * NC, span, width), BF),
        jax.ShapeDtypeStruct((dps, NX * NC, rows, part), BF),
        jax.ShapeDtypeStruct((dps, NX * NC) + vec.shape, BF),
        jax.ShapeDtypeStruct((NZ, NY, NX, NC) + wo.shape, BF),
        jax.ShapeDtypeStruct((NZ, NY, NX, NC * f1.shape[1], f1.shape[2]), BF),
        jax.ShapeDtypeStruct((NZ, NY, NX) + f2.shape, BF),
    )
    return pl.pallas_call(
        gather_kernel,
        out_shape=out,
        in_specs=[HBM] * 6,
        out_specs=[HBM] * 6,
        scratch_shapes=[
            pltpu.SemaphoreType.DMA((COPIES,)),
            pltpu.SemaphoreType.DMA((COPIES,)),
            pltpu.SemaphoreType.DMA((6,)),
        ],
        compiler_params=pltpu.CompilerParams(collective_id=1, has_side_effects=True),
        name="gather_weights",
    )(tok, wq4, vec, wo, f1, f2)


def add_into(total, term):
    lead, rows = total.shape[:-2], total.shape[-2]
    step = 16 if total.dtype == BF else 8
    count = math.prod(lead)
    per = rows // step

    def body(n, _):
        block = n // per
        at = []
        for dim in reversed(lead):
            at.append(block % dim)
            block = block // dim
        idx = tuple(reversed(at)) + (pl.ds(pl.multiple_of((n % per) * step, step), step), slice(None))
        total[idx] = (total[idx].astype(F32) + term[idx].astype(F32)).astype(total.dtype)
        return 0

    lax.fori_loop(0, count * per, body, 0)


def reduce_plane(wire, place, grad, own, got, got2, got3, out, local, swap=False, ready=None):
    z, y, x = place.z, place.y, place.x
    first = place.at(x=1 - x) if swap else place.at(y=1 - y)
    second = place.at(y=1 - y) if swap else place.at(x=1 - x)

    def two(zk, mine):
        if swap:
            return grad.at[zk, :, x if mine else 1 - x]
        return grad.at[zk, y if mine else 1 - y]

    order = [(z + k) % NZ for k in (1, 2, 3, 0)]
    sends = [wire.copy(two(zk, False), got.at[k], first) for k, zk in enumerate(order)]
    loads = [pltpu.make_async_copy(two(zk, True), own.at[k], local.at[k]) for k, zk in enumerate(order)]
    for desc in loads:
        desc.start()
    yield
    seconds = []
    keep, give = (y, 1 - y) if swap else (x, 1 - x)
    for k in range(NZ):
        loads[k].wait()
        sends[k].wait_recv()
        add_into(own.at[k], got.at[k])
        seconds.append(wire.copy(own.at[k, give], got2.at[k], second))
        yield
    along = []
    for k in range(NZ):
        seconds[k].wait_recv()
        add_into(own.at[k, keep], got2.at[k])
        if k < NZ - 1:
            along.append(wire.copy(own.at[k, keep], got3.at[k], place.at(z=place.zup(k + 1))))
        yield
    for desc in along:
        desc.wait_recv()
    lead = out.shape[0]
    step = 16 if grad.dtype == BF else 8

    def body(n, _):
        idx = (pl.ds(pl.multiple_of(n * step, step), step), slice(None))
        total = own[(NZ - 1, keep) + idx].astype(F32)
        for k in range(NZ - 1):
            total = total + got3[(k,) + idx].astype(F32)
        out[idx] = total
        return 0

    lax.fori_loop(0, lead // step, body, 0)


def reduce_kernel(g1, g2, go, gq, gv, o1, o2, oo, oq, ov, *scratch):
    (own1, got1, got1b, got1c, own2, got2, got2b, got2c, owno, goto, gotob, gotoc, outp, outg) = scratch[:14]
    (ownq, gotq, gotqb, sumq, bufq, f1buf, f1got, vown, vgot, vsum, vgot2, vgot3, send, recv, local) = scratch[14:]
    place = Place()
    z, y, x, c, s, dp = place.z, place.y, place.x, place.c, place.seq, place.dp
    wire = Wire(place, send, recv)
    greet(place)
    core = place.at(c=1 - c)
    rows_o = go.shape[4]
    swap_o = wire.copy(go.at[:, :, :, 1 - c], outg, core)
    load_o = pltpu.make_async_copy(go.at[:, :, :, c], outp, local.at[0])
    load_o.start()
    swap_v = wire.copy(gv.at[:, :, :, 1 - c], vgot, core)
    load_v = pltpu.make_async_copy(gv.at[:, :, :, c], vown, local.at[1])
    load_v.start()

    def vectors():
        load_v.wait()
        swap_v.wait_recv()
        add_into(vown, vgot)
        yield
        along_y = wire.copy(vown.at[:, 1 - y], vsum, place.at(y=1 - y))
        yield
        along_y.wait_recv()
        mine = vown.at[:, y]
        add_into(mine, vsum)
        along_x = wire.copy(vown.at[:, y, 1 - x], vgot2, place.at(x=1 - x))
        yield
        along_x.wait_recv()
        mine = vown.at[:, y, x]
        add_into(mine, vgot2)
        vgot3[pl.ds(z, 1)] = vown[pl.ds(z, 1), y, x]
        along = [wire.copy(vown.at[place.zup(k), y, x], vgot3.at[z], place.at(z=place.zup(k))) for k in range(1, NZ)]
        yield
        for desc in along:
            desc.wait_recv()
        ov[...] = ((vgot3[0] + vgot3[1]) + vgot3[2]) + vgot3[3]

    def outer():
        load_o.wait()
        swap_o.wait_recv()
        add_into(outp, outg)
        yield
        yield from reduce_plane(wire, place, outp, owno, goto, gotob, gotoc, oo, local.at[pl.ds(2, NZ)])

    def quarter():
        order = [(z + k) % NZ for k in (1, 2, 3, 0)]
        sends = [wire.copy(gq.at[zk, 1 - y], gotq.at[k], place.at(y=1 - y)) for k, zk in enumerate(order)]
        loads = [pltpu.make_async_copy(gq.at[zk, y], ownq.at[k], local.at[6 + k]) for k, zk in enumerate(order)]
        for desc in loads:
            desc.start()
        yield
        along = []
        for k in range(NZ):
            loads[k].wait()
            sends[k].wait_recv()
            add_into(ownq.at[k], gotq.at[k])
            if k < NZ - 1:
                along.append(wire.copy(ownq.at[k], gotqb.at[k], place.at(z=place.zup(k + 1))))
        yield
        for desc in along:
            desc.wait_recv()
        count, rows = sumq.shape[:2]

        def body(n, _):
            at = pl.ds(pl.multiple_of(n * 16, 16), 16)
            per = rows // 16
            total = ownq[NZ - 1, n // per, pl.ds(pl.multiple_of((n % per) * 16, 16), 16), :].astype(F32)
            for k in range(NZ - 1):
                total = total + gotqb[k, n // per, pl.ds(pl.multiple_of((n % per) * 16, 16), 16), :].astype(F32)
            sumq[n // per, pl.ds(pl.multiple_of((n % per) * 16, 16), 16), :] = total.astype(BF)
            return 0

        lax.fori_loop(0, count * (rows // 16), body, 0)
        parts = []
        for dev, peer in ((core, s ^ 1), (place.at(x=1 - x), s ^ 2), (place.at(x=1 - x, c=1 - c), s ^ 3)):
            parts.append(wire.copy(sumq.at[peer], oq.at[s], dev))
        mine = pltpu.make_async_copy(sumq.at[s], oq.at[s], local.at[10])
        mine.start()
        yield
        mine.wait()
        for desc in parts:
            desc.wait_recv()

    def first():
        yield from reduce_plane(wire, place, g1, own1, got1, got1b, got1c, f1buf, local.at[pl.ds(11, NZ)])
        rows = f1got.shape[0]
        part = wire.copy(f1buf.at[pl.ds((1 - c) * rows, rows)], f1got, core)
        o1[c] = f1buf[pl.ds(c * rows, rows)]
        yield
        part.wait_recv()
        o1[1 - c] = f1got[...]

    def second():
        yield from reduce_plane(wire, place, g2, own2, got2, got2b, got2c, o2, local.at[pl.ds(15, NZ)], swap=True)

    rounds([first(), second(), outer(), vectors(), quarter()])
    wire.drain()


def reduce_all(g1, g2, go, gq, gv):
    def bufs(block, dtype=BF):
        return [
            pltpu.VMEM((NZ, 2) + block, dtype),
            pltpu.VMEM((NZ, 2) + block, dtype),
            pltpu.VMEM((NZ,) + block, dtype),
            pltpu.VMEM((NZ - 1,) + block, dtype),
        ]

    b1, b2, bo = g1.shape[3:], g2.shape[3:], go.shape[4:]
    bq = gq.shape[2:]
    bv = gv.shape[4:]
    out = (
        jax.ShapeDtypeStruct((NC, b1[0] // NC, b1[1]), F32),
        jax.ShapeDtypeStruct(b2, F32),
        jax.ShapeDtypeStruct(bo, F32),
        jax.ShapeDtypeStruct(bq, BF),
        jax.ShapeDtypeStruct(bv, F32),
    )
    scratch = bufs(b1) + bufs(b2) + bufs(bo)
    scratch += [pltpu.VMEM((NZ, NY, NX) + bo, BF)] * 2
    scratch += [
        pltpu.VMEM((NZ,) + bq, BF),
        pltpu.VMEM((NZ,) + bq, BF),
        pltpu.VMEM((NZ - 1,) + bq, BF),
        pltpu.VMEM(bq, BF),
        pltpu.VMEM(bq, BF),
        pltpu.VMEM(b1, F32),
        pltpu.VMEM((b1[0] // NC, b1[1]), F32),
        pltpu.VMEM((NZ, NY, NX) + bv, F32),
        pltpu.VMEM((NZ, NY, NX) + bv, F32),
        pltpu.VMEM((NZ, NX) + bv, F32),
        pltpu.VMEM((NZ,) + bv, F32),
        pltpu.VMEM((NZ,) + bv, F32),
        pltpu.SemaphoreType.DMA((COPIES,)),
        pltpu.SemaphoreType.DMA((COPIES,)),
        pltpu.SemaphoreType.DMA((20,)),
    ]
    return pl.pallas_call(
        reduce_kernel,
        out_shape=out,
        in_specs=[HBM] * 5,
        out_specs=[VM] * 5,
        scratch_shapes=scratch,
        compiler_params=pltpu.CompilerParams(
            collective_id=2, has_side_effects=True, vmem_limit_bytes=48 * 1024 * 1024
        ),
        name="reduce_grads",
    )(g1, g2, go, gq, gv)


def nt(a, b):
    return lax.dot_general(a, b, (((1,), (1,)), ((), ())), preferred_element_type=F32)


def nn(a, b):
    return lax.dot_general(a, b, (((1,), (0,)), ((), ())), preferred_element_type=F32)


def pair_bias(idr, idc, qb, kb, size):
    qs = pl.multiple_of(qb * size, size)
    ks = pl.multiple_of(kb * size, size)
    key_pos = ks + lax.broadcasted_iota(jnp.int32, (size, size), 0)
    query_pos = qs + lax.broadcasted_iota(jnp.int32, (size, size), 1)
    same = idc[pl.ds(ks, size), :] == idr[:, pl.ds(qs, size)]
    return jnp.where((key_pos <= query_pos) & same, 0.0, NEGATIVE)


def mask_heads(dst, src, heads, head):
    lane = lax.broadcasted_iota(jnp.int32, src.shape, 1) // head
    whole = src[...]
    for h in range(heads):
        dst[h] = jnp.where(lane == h, whole, jnp.zeros_like(whole))


def attend_kernel(heads, size, q, k, v, idr, idc, scale, att, scaled, lse, km, vt, bias, top, low, acc):
    length, part = q.shape
    head = part // heads
    blocks = length // size
    mask_heads(km, k, heads, head)
    vt[...] = v[...].T

    def queries(qb, _):
        qs = pl.ds(pl.multiple_of(qb * size, size), size)
        top[...] = jnp.full(top.shape, NEGATIVE, F32)
        low[...] = jnp.zeros(low.shape, F32)
        acc[...] = jnp.zeros(acc.shape, F32)

        def keys(step, _):
            kb = qb - step
            ks = pl.ds(pl.multiple_of(kb * size, size), size)
            bias[...] = pair_bias(idr, idc, qb, kb, size)
            for h in range(heads):
                scores = nt(km[h, ks, :], q[qs, :]) + bias[...]
                old = top[h : h + 1, :]
                new = jnp.maximum(old, jnp.max(scores, 0, keepdims=True))
                probs = jnp.exp(scores - new)
                shrink = jnp.exp(old - new)
                top[h : h + 1, :] = new
                low[h : h + 1, :] = low[h : h + 1, :] * shrink + jnp.sum(probs, 0, keepdims=True)
                hs = slice(h * head, (h + 1) * head)
                acc[hs, :] = acc[hs, :] * shrink + nn(vt[hs, ks], probs.astype(BF))
            return 0

        lax.fori_loop(0, qb + 1, keys, 0)
        for h in range(heads):
            hs = slice(h * head, (h + 1) * head)
            acc[hs, :] = acc[hs, :] * (1.0 / low[h : h + 1, :])
        att[:, qs] = acc[...]
        lse[:, qs] = top[...] + jnp.log(low[...])
        scaled[qs, :] = (acc[...].T * scale[...]).astype(BF)
        return 0

    lax.fori_loop(0, blocks, queries, 0)


def row_attend(q, k, v, ids, scale, heads, size):
    length, part = q.shape
    rows = 8
    return pl.pallas_call(
        functools.partial(attend_kernel, heads, size),
        out_shape=(
            jax.ShapeDtypeStruct((part, length), F32),
            jax.ShapeDtypeStruct((length, part), BF),
            jax.ShapeDtypeStruct((rows, length), F32),
        ),
        in_specs=[VM] * 6,
        out_specs=[VM] * 3,
        scratch_shapes=[
            pltpu.VMEM((heads, length, part), BF),
            pltpu.VMEM((part, length), BF),
            pltpu.VMEM((size, size), F32),
            pltpu.VMEM((rows, size), F32),
            pltpu.VMEM((rows, size), F32),
            pltpu.VMEM((part, size), F32),
        ],
        compiler_params=pltpu.CompilerParams(vmem_limit_bytes=48 * 1024 * 1024),
        name="attend",
    )(q, k, v, ids.reshape(1, length), ids.reshape(length, 1), scale)


def attend_back_kernel(heads, size, q, k, v, do, att, lse, idr, idc, dq, dk, dv, delta, km, vm, qm, dm, kt, bias, acck, accv, accq):
    length, part = q.shape
    head = part // heads
    blocks = length // size
    mask_heads(km, k, heads, head)
    mask_heads(vm, v, heads, head)
    mask_heads(qm, q, heads, head)
    mask_heads(dm, do, heads, head)
    kt[...] = k[...].T
    accq[...] = jnp.zeros(accq.shape, F32)
    weighted = do[...].T.astype(F32) * att[...]
    delta[...] = jnp.zeros(delta.shape, F32)
    for h in range(heads):
        delta[h : h + 1, :] = jnp.sum(weighted[h * head : (h + 1) * head, :], 0, keepdims=True)

    def keys(kb, _):
        ks = pl.ds(pl.multiple_of(kb * size, size), size)
        acck[...] = jnp.zeros(acck.shape, F32)
        accv[...] = jnp.zeros(accv.shape, F32)

        def queries(qb, _):
            qs = pl.ds(pl.multiple_of(qb * size, size), size)
            bias[...] = pair_bias(idr, idc, qb, kb, size)
            for h in range(heads):
                scores = nt(km[h, ks, :], q[qs, :]) + bias[...]
                probs = jnp.exp(scores - lse[h : h + 1, qs])
                grad = nt(vm[h, ks, :], do[qs, :])
                ds = (probs * (grad - delta[h : h + 1, qs])).astype(BF)
                accv[...] += nn(probs.astype(BF), dm[h, qs, :])
                acck[...] += nn(ds, qm[h, qs, :])
                hs = slice(h * head, (h + 1) * head)
                accq[hs, qs] += nn(kt[hs, ks], ds)
            return 0

        lax.fori_loop(kb, blocks, queries, 0)
        dk[ks, :] = acck[...].astype(BF)
        dv[ks, :] = accv[...].astype(BF)
        return 0

    lax.fori_loop(0, blocks, keys, 0)
    for b in range(blocks):
        at = slice(b * size, (b + 1) * size)
        dq[at, :] = (accq[:, at].T * (head**-0.5)).astype(BF)


def row_attend_back(q, k, v, do, att, lse, ids, heads, size):
    length, part = q.shape
    return pl.pallas_call(
        functools.partial(attend_back_kernel, heads, size),
        out_shape=(jax.ShapeDtypeStruct((length, part), BF),) * 3 + (jax.ShapeDtypeStruct((8, length), F32),),
        in_specs=[VM] * 8,
        out_specs=[VM] * 4,
        scratch_shapes=[pltpu.VMEM((heads, length, part), BF)] * 4
        + [
            pltpu.VMEM((part, length), BF),
            pltpu.VMEM((size, size), F32),
            pltpu.VMEM((size, part), F32),
            pltpu.VMEM((size, part), F32),
            pltpu.VMEM((part, length), F32),
        ],
        compiler_params=pltpu.CompilerParams(vmem_limit_bytes=56 * 1024 * 1024),
        name="attend_back",
    )(q, k, v, do, att, lse, ids.reshape(1, length), ids.reshape(length, 1))


def trade(v, mask, perm_seq):
    pairs = [(d * perm_seq + s, d * perm_seq + (s ^ mask)) for d in range(NZ * NY) for s in range(perm_seq)]
    return lax.ppermute(v, ("dp", "seq"), pairs)


def fast(tokens, doc_ids, cotangent, w_qkv, w_out, attn_vecs, head_scale, w_fc1, w_fc2, ffn_vecs, ffn_wide):
    _, span, width = tokens.shape
    group = NX * NC
    length = span * group
    head_count = head_scale.shape[0]
    head = width // head_count
    heads = head_count // group
    part = heads * head
    seq = lax.axis_index("seq")
    core = seq % NC
    chips = NZ * NY * NX
    owners = chips * NC
    block = w_fc2.shape[0]
    units = chips * block
    swap = functools.partial(trade, perm_seq=group)
    shift = part * seq

    rows = w_qkv.shape[0]
    wq4 = w_qkv.astype(BF).reshape(rows, 3, group, part).transpose(2, 0, 1, 3).reshape(group, rows, 3 * part)
    f1 = w_fc1.astype(BF).reshape(rows, chips, NC, block).transpose(2, 0, 1, 3).reshape(NC, rows, units)
    a_len, f_len, w_len = attn_vecs.size, ffn_vecs.size, ffn_wide.size
    vec = jnp.concatenate([attn_vecs.reshape(-1), ffn_vecs.reshape(-1), ffn_wide.reshape(-1)]).astype(BF)
    vec = jnp.pad(vec, (0, 16 * 128 - vec.size)).reshape(16, 128)
    tok = tokens.reshape(span, width)
    tok_all, wq, vecs, wo, fc1, fc2 = gather_all(tok, wq4, vec, w_out.astype(BF), f1, w_fc2.astype(BF))
    tok_all = tok_all.reshape(length, width)
    wq = wq.reshape(width, 3 * part)
    wo = wo.reshape(width, width)
    fc1 = fc1.reshape(width, units)
    fc2 = fc2.reshape(units, width)
    vecs = vecs.reshape(owners, -1).astype(F32)

    def rows_of(at, size, count):
        return vecs[:, at : at + size].reshape(owners, count, -1).transpose(1, 0, 2).reshape(count, -1)

    attn_rows = rows_of(0, a_len, 7)
    ffn_rows = rows_of(a_len, f_len, 3)
    wide = rows_of(a_len + f_len, w_len, 3).reshape(3, chips, NC, block)
    wide = lax.dynamic_index_in_dim(wide, core, 2, keepdims=False).reshape(3, units)

    dtop = cotangent.reshape(span, width)
    dtop_pair = jnp.concatenate([dtop, swap(dtop, 1)], 0)

    act_one = (normalize(tok_all.astype(F32))[0] * attn_rows[0] + attn_rows[1]).astype(BF)
    proj = jnp.dot(act_one, wq, preferred_element_type=F32)
    bias_q = lax.dynamic_slice_in_dim(attn_rows[2], shift, part)
    bias_v = lax.dynamic_slice_in_dim(attn_rows[3], shift, part)
    q = (proj[:, :part] + bias_q).astype(BF) * jnp.asarray(head**-0.5, BF)
    k = proj[:, part : 2 * part].astype(BF)
    v = (proj[:, 2 * part :] + bias_v).astype(BF)
    scale_own = lax.dynamic_slice_in_dim(head_scale, heads * seq, heads)
    scale_lanes = jnp.repeat(scale_own, head).reshape(1, part)
    ids = doc_ids.reshape(length)
    size = span
    att, scaled, lse = row_attend(q, k, v, ids, scale_lanes, heads, size)

    def to_owners(blocks):
        return [lax.dynamic_index_in_dim(blocks, seq, 0, keepdims=False)] + [
            swap(lax.dynamic_index_in_dim(blocks, seq ^ m, 0, keepdims=False), m) for m in (1, 2, 3)
        ]

    got = jnp.stack(to_owners(scaled.reshape(group, span, part)))
    scaled_own = jnp.concatenate(
        [lax.dynamic_index_in_dim(got, seq ^ j, 0, keepdims=False) for j in range(group)], 1
    )
    inputs = tok.astype(F32)
    branch = jnp.dot(scaled_own, wo, preferred_element_type=F32) + attn_rows[4]
    normed_branch, inv_branch = normalize(branch)
    hidden = inputs + normed_branch * attn_rows[5] + attn_rows[6]
    normed_two, inv_two = normalize(hidden)
    act_two = (normed_two * ffn_rows[0] + ffn_rows[1]).astype(BF)

    act_pair = jnp.concatenate([act_two, swap(act_two, 1)], 0)

    def flip(stats):
        return jnp.concatenate([stats[span:], stats[:span]], 0)

    def both(stats):
        return stats + swap(flip(stats), 1)

    inner = jnp.dot(act_pair, fc1, preferred_element_type=F32) + wide[0]
    activated = gelu_exact(inner)
    total_units = units * NC
    centre = both(jnp.sum(activated, -1, keepdims=True)) / total_units
    centred = activated - centre
    inv_three = lax.rsqrt(both(jnp.sum(centred * centred, -1, keepdims=True)) / total_units + EPSILON)
    normed_three = centred * inv_three
    mixed = (normed_three * wide[1] + wide[2]).astype(BF)
    out_pair = jnp.dot(mixed, fc2, preferred_element_type=F32)
    result = hidden + ffn_rows[2] + (out_pair[:span] + swap(out_pair[span:], 1))
    outputs = result.astype(BF).reshape(1, span, width)

    grad_fc2 = left_grad(mixed, dtop_pair).astype(BF)
    grad_mixed = right_back(dtop_pair, fc2)
    gain_inner = jnp.sum(grad_mixed * normed_three, 0)
    bias_inner = jnp.sum(grad_mixed, 0)
    grad_norm = grad_mixed * wide[1]
    means = both(
        jnp.concatenate(
            [
                jnp.sum(grad_norm, -1, keepdims=True),
                jnp.sum(grad_norm * normed_three, -1, keepdims=True),
            ],
            1,
        )
    ) / total_units
    grad_activated = inv_three * (grad_norm - means[:, :1] - normed_three * means[:, 1:])
    grad_inner = (grad_activated * gelu_slope(inner)).astype(BF)
    grad_fc1 = left_grad(act_pair, grad_inner).astype(BF)
    bias_one = jnp.sum(grad_inner.astype(F32), 0)
    back_pair = right_back(grad_inner, fc1)
    grad_act_two = back_pair[:span] + swap(back_pair[span:], 1)
    top = dtop.astype(F32)
    gain_two = jnp.sum(grad_act_two * normed_two, 0)
    shift_two = jnp.sum(grad_act_two, 0)
    grad_hidden = top + norm_back(grad_act_two * ffn_rows[0], normed_two, inv_two)
    post_gain = jnp.sum(grad_hidden * normed_branch, 0)
    post_shift = jnp.sum(grad_hidden, 0)
    grad_branch = norm_back(grad_hidden * attn_rows[5], normed_branch, inv_branch).astype(BF)
    out_bias = jnp.sum(grad_branch.astype(F32), 0)
    grad_out = left_grad(scaled_own, grad_branch).astype(BF)
    grad_attended = (right_back(grad_branch, wo) * jnp.repeat(head_scale, head)).astype(BF)

    got = to_owners(grad_attended.reshape(span, group, part).transpose(1, 0, 2))
    do = jnp.zeros((length, part), BF)
    for m, piece in enumerate(got):
        do = lax.dynamic_update_slice_in_dim(do, piece, (seq ^ m) * span, 0)
    dq, dk, dv, delta = row_attend_back(q, k, v, do, att, lse, ids, heads, size)
    scale_part = jnp.sum(delta[:heads], 1) / scale_own
    grad_qkv = jnp.concatenate([dq, dk, dv], 1)
    grad_wq = left_grad(act_one, grad_qkv).astype(BF)
    query_bias = jnp.sum(dq.astype(F32), 0)
    value_bias = jnp.sum(dv.astype(F32), 0)
    da_all = right_back(grad_qkv, wq).astype(BF).reshape(group, span, width)
    mine = jnp.stack([lax.dynamic_index_in_dim(da_all, seq ^ m, 0, keepdims=False) for m in (0, 2)])
    give = jnp.stack([lax.dynamic_index_in_dim(da_all, seq ^ m, 0, keepdims=False) for m in (1, 3)])
    mine = mine.astype(F32) + swap(give, 1).astype(F32)
    grad_act_one = mine[0] + swap(mine[1].astype(BF), 2).astype(F32)
    normed_one, inv_one = normalize(inputs)
    gain_one = jnp.sum(grad_act_one * normed_one, 0)
    shift_one = jnp.sum(grad_act_one, 0)
    grad_tokens = (grad_hidden + norm_back(grad_act_one * attn_rows[0], normed_one, inv_one)).astype(BF)

    def widen(v, size, at):
        return lax.dynamic_update_slice_in_dim(jnp.zeros((size,), F32), v, at, 0)

    attn_grads = jnp.stack(
        [
            gain_one,
            shift_one,
            widen(query_bias, width, shift),
            widen(value_bias, width, shift),
            out_bias,
            post_gain,
            post_shift,
        ]
    )
    wide_grads = jnp.stack([bias_one, gain_inner, bias_inner]).reshape(3, chips, 1, block)
    is_core = (jnp.arange(NC) == core).astype(F32).reshape(1, 1, NC, 1)
    wide_grads = (wide_grads * is_core).reshape(3, NC * units)
    ffn_grads = jnp.stack([gain_two, shift_two, jnp.sum(top, 0)])
    scales = jnp.broadcast_to(widen(scale_part, head_count, heads * seq), (owners, head_count))

    def by_owner(g):
        return g.reshape(g.shape[0], owners, -1).transpose(1, 0, 2).reshape(owners, -1)

    packed = jnp.concatenate([by_owner(attn_grads), by_owner(ffn_grads), by_owner(wide_grads), scales], 1)
    packed = jnp.pad(packed, ((0, 0), (0, 8 * 128 - packed.shape[1]))).reshape(NZ, NY, NX, NC, 8, 128)
    o1, o2, oo, oq, ov = reduce_all(
        grad_fc1.reshape(NZ, NY, NX, NC * rows, units),
        grad_fc2.reshape(NZ, NY, NX, block, width),
        grad_out.reshape(NZ, NY, NX, NC, rows, width),
        grad_wq.reshape(NZ, NY, group, rows, 3 * part),
        packed,
    )
    grad_w1 = o1.reshape(NC, rows, chips, block).transpose(1, 2, 0, 3).reshape(rows, NC * units)
    grad_wqkv = oq.astype(F32).reshape(group, rows, 3, part).transpose(1, 2, 0, 3).reshape(rows, 3 * width)
    flat = ov.reshape(-1)
    end = a_len + f_len + w_len
    return (
        outputs,
        grad_tokens.reshape(1, span, width),
        grad_wqkv,
        oo,
        flat[:a_len].reshape(attn_vecs.shape),
        flat[end : end + head_count],
        grad_w1,
        o2,
        flat[a_len : a_len + f_len].reshape(ffn_vecs.shape),
        flat[a_len + f_len : end].reshape(ffn_wide.shape),
    )


def gelu_slope(u):
    return 0.5 * (1.0 + jax.scipy.special.erf(u * math.sqrt(0.5))) + u * jnp.exp(-0.5 * u * u) * (
        1.0 / math.sqrt(2.0 * math.pi)
    )


def solution(mesh):
    placed = (
        P("dp", "seq", None),
        P("dp", None),
        P("dp", "seq", None),
        P(("dp", "seq"), None),
        P(("dp", "seq"), None),
        P(None, ("dp", "seq")),
        P(),
        P(("dp", "seq"), None),
        P(("dp", "seq"), None),
        P(None, ("dp", "seq")),
        P(None, ("dp", "seq")),
    )
    results = (
        P("dp", "seq", None),
        P("dp", "seq", None),
        P(("dp", "seq"), None),
        P(("dp", "seq"), None),
        P(None, ("dp", "seq")),
        P(),
        P(("dp", "seq"), None),
        P(("dp", "seq"), None),
        P(None, ("dp", "seq")),
        P(None, ("dp", "seq")),
    )
    suits = mesh.shape["dp"] == NZ * NY and mesh.shape["seq"] == NX * NC
    return jax.shard_map(
        fast if suits else local, mesh=mesh, in_specs=placed, out_specs=results, check_vma=False
    )
```

```python
import functools
import math

import jax
import jax.numpy as jnp
from jax import lax
from jax.experimental import pallas as pl
from jax.experimental.pallas import tpu as pltpu
from jax.sharding import PartitionSpec as P

EPSILON = 1e-05
NEGATIVE = -1e30
MESH = pl.DeviceIdType.MESH
BF = jnp.bfloat16
F32 = jnp.float32
NZ, NY, NX, NC = 4, 2, 2, 2
HBM = pl.BlockSpec(memory_space=pl.ANY)
VM = pl.BlockSpec(memory_space=pltpu.VMEM)


def normalize(values):
    centre = jnp.mean(values, -1, keepdims=True)
    centred = values - centre
    scale_inv = lax.rsqrt(jnp.mean(centred * centred, -1, keepdims=True) + EPSILON)
    return (centred * scale_inv, scale_inv)


def norm_back(grad_normed, normed, scale_inv):
    return scale_inv * (
        grad_normed
        - jnp.mean(grad_normed, -1, keepdims=True)
        - normed * jnp.mean(grad_normed * normed, -1, keepdims=True)
    )


def gelu_exact(values):
    return 0.5 * values * (1.0 + jax.scipy.special.erf(values * math.sqrt(0.5)))


def left_grad(activations, gradients):
    return lax.dot_general(
        activations, gradients, (((0,), (0,)), ((), ())), preferred_element_type=jnp.float32
    )


def right_back(gradients, matrix):
    return lax.dot_general(
        gradients, matrix, (((1,), (1,)), ((), ())), preferred_element_type=jnp.float32
    )


def masked_scores(queries, keys_block, query_pos, key_pos, query_ids, key_ids):
    raw_scores = jnp.einsum(
        "rqhe,rkhe->rhqk", queries, keys_block, preferred_element_type=jnp.float32
    )
    allowed = (key_pos[None, None, :] <= query_pos[None, :, None]) & (
        key_ids[:, None, :] == query_ids[:, :, None]
    )
    return jnp.where(allowed[:, None], raw_scores * queries.shape[3] ** (-0.5), NEGATIVE)


def attend(queries, keys_all, values_all, query_pos, query_ids, doc_rows, block_len):
    block_count = keys_all.shape[1] // block_len
    stat_shape = (queries.shape[0], queries.shape[2], queries.shape[1])

    def slice_block(block_index):
        start = block_index * block_len
        keys_block = lax.dynamic_slice_in_dim(keys_all, start, block_len, 1)
        values_block = lax.dynamic_slice_in_dim(values_all, start, block_len, 1)
        key_ids = lax.dynamic_slice_in_dim(doc_rows, start, block_len, 1)
        key_pos = start + jnp.arange(block_len, dtype=jnp.int32)
        return (
            values_block,
            masked_scores(queries, keys_block, query_pos, key_pos, query_ids, key_ids),
        )

    def first_pass(carry, block_index):
        running_max, running_sum = carry
        _, scores = slice_block(block_index)
        new_max = jnp.maximum(running_max, jnp.max(scores, -1))
        running_sum = running_sum * jnp.exp(running_max - new_max) + jnp.sum(
            jnp.exp(scores - new_max[..., None]), -1
        )
        return ((new_max, running_sum), None)

    start_stats = (jnp.full(stat_shape, NEGATIVE, jnp.float32), jnp.zeros(stat_shape, jnp.float32))
    (row_max, row_sum), _ = lax.scan(
        first_pass, start_stats, jnp.arange(block_count, dtype=jnp.int32)
    )
    log_total = row_max + jnp.log(row_sum)

    def second_pass(total_out, block_index):
        values_block, scores = slice_block(block_index)
        probs = jnp.exp(scores - log_total[..., None]).astype(jnp.bfloat16)
        return (
            total_out
            + jnp.einsum(
                "rhqk,rkhe->rqhe", probs, values_block, preferred_element_type=jnp.float32
            ),
            None,
        )

    attended, _ = lax.scan(
        second_pass, jnp.zeros(queries.shape, jnp.float32), jnp.arange(block_count, dtype=jnp.int32)
    )
    return (attended, log_total)


def attend_back(
    queries,
    keys_all,
    values_all,
    grad_out,
    log_total,
    delta,
    query_pos,
    query_ids,
    doc_rows,
    block_len,
):
    block_count = keys_all.shape[1] // block_len
    scale = queries.shape[3] ** (-0.5)

    def step(grad_queries, block_index):
        start = block_index * block_len
        keys_block = lax.dynamic_slice_in_dim(keys_all, start, block_len, 1)
        values_block = lax.dynamic_slice_in_dim(values_all, start, block_len, 1)
        key_ids = lax.dynamic_slice_in_dim(doc_rows, start, block_len, 1)
        key_pos = start + jnp.arange(block_len, dtype=jnp.int32)
        scores = masked_scores(queries, keys_block, query_pos, key_pos, query_ids, key_ids)
        probs = jnp.exp(scores - log_total[..., None])
        grad_probs = jnp.einsum(
            "rqhe,rkhe->rhqk", grad_out, values_block, preferred_element_type=jnp.float32
        )
        grad_scores = (probs * (grad_probs - delta[..., None]) * scale).astype(jnp.bfloat16)
        grad_queries = grad_queries + jnp.einsum(
            "rhqk,rkhe->rqhe", grad_scores, keys_block, preferred_element_type=jnp.float32
        )
        grad_keys = jnp.einsum(
            "rhqk,rqhe->rkhe", grad_scores, queries, preferred_element_type=jnp.float32
        )
        grad_values = jnp.einsum(
            "rhqk,rqhe->rkhe",
            probs.astype(jnp.bfloat16),
            grad_out,
            preferred_element_type=jnp.float32,
        )
        return (grad_queries, (grad_keys, grad_values))

    return lax.scan(
        step, jnp.zeros(queries.shape, jnp.float32), jnp.arange(block_count, dtype=jnp.int32)
    )


def local(
    tokens,
    doc_ids,
    cotangent,
    w_qkv,
    w_out,
    attn_vecs,
    head_scale,
    w_fc1,
    w_fc2,
    ffn_vecs,
    ffn_wide,
):
    row_count, span_len, model_width = tokens.shape
    head_count = head_scale.shape[0]
    head_size = model_width // head_count
    token_count = row_count * span_len
    brain = jnp.bfloat16
    single = jnp.float32
    gathered_qkv, gathered_out, attn_rows = (
        lax.all_gather(w_qkv.astype(brain), ("dp", "seq"), axis=0, tiled=True),
        lax.all_gather(w_out.astype(brain), ("dp", "seq"), axis=0, tiled=True),
        lax.all_gather(attn_vecs.astype(brain), ("dp", "seq"), axis=1, tiled=True),
    )
    attn_rows = attn_rows.astype(single)
    inputs = tokens.astype(single).reshape(token_count, model_width)
    normed_one, inv_one = normalize(inputs)
    act_one = (normed_one * attn_rows[0] + attn_rows[1]).astype(brain)
    projected = jnp.dot(act_one, gathered_qkv, preferred_element_type=single)
    queries = (projected[:, :model_width] + attn_rows[2]).astype(brain)
    keys_own = projected[:, model_width : 2 * model_width].astype(brain)
    values_own = (projected[:, 2 * model_width :] + attn_rows[3]).astype(brain)
    keys_all, values_all = (
        lax.all_gather(
            keys_own.reshape(row_count, span_len, model_width), "seq", axis=1, tiled=True
        ),
        lax.all_gather(
            values_own.reshape(row_count, span_len, model_width), "seq", axis=1, tiled=True
        ),
    )
    offset = lax.axis_index("seq") * span_len
    query_pos = offset + jnp.arange(span_len, dtype=jnp.int32)
    query_ids = lax.dynamic_slice_in_dim(doc_ids, offset, span_len, 1)
    queries_four = queries.reshape(row_count, span_len, head_count, head_size)
    keys_four = keys_all.reshape(row_count, -1, head_count, head_size)
    values_four = values_all.reshape(row_count, -1, head_count, head_size)
    attended, log_total = attend(
        queries_four, keys_four, values_four, query_pos, query_ids, doc_ids, span_len
    )
    scaled = (
        (attended * head_scale[None, None, :, None]).reshape(token_count, model_width).astype(brain)
    )
    branch = jnp.dot(scaled, gathered_out, preferred_element_type=single) + attn_rows[4]
    normed_branch, inv_branch = normalize(branch)
    hidden = inputs + normed_branch * attn_rows[5] + attn_rows[6]
    gathered_fc1, gathered_fc2, ffn_rows, wide_rows = (
        lax.all_gather(w_fc1.astype(brain), ("dp", "seq"), axis=0, tiled=True),
        lax.all_gather(w_fc2.astype(brain), ("dp", "seq"), axis=0, tiled=True),
        lax.all_gather(ffn_vecs.astype(brain), ("dp", "seq"), axis=1, tiled=True),
        lax.all_gather(ffn_wide.astype(brain), ("dp", "seq"), axis=1, tiled=True),
    )
    ffn_rows = ffn_rows.astype(single)
    wide_rows = wide_rows.astype(single)
    normed_two, inv_two = normalize(hidden)
    act_two = (normed_two * ffn_rows[0] + ffn_rows[1]).astype(brain)
    inner_act = jnp.dot(act_two, gathered_fc1, preferred_element_type=single) + wide_rows[0]
    activated, gelu_pull = jax.vjp(gelu_exact, inner_act)
    normed_three, inv_three = normalize(activated)
    mixed_act = (normed_three * wide_rows[1] + wide_rows[2]).astype(brain)
    result = hidden + jnp.dot(mixed_act, gathered_fc2, preferred_element_type=single) + ffn_rows[2]
    outputs = result.astype(brain).reshape(row_count, span_len, model_width)
    back_set = (
        lax.all_gather(w_qkv.astype(brain), ("dp", "seq"), axis=0, tiled=True),
        lax.all_gather(w_out.astype(brain), ("dp", "seq"), axis=0, tiled=True),
        lax.all_gather(attn_vecs.astype(brain), ("dp", "seq"), axis=1, tiled=True),
        lax.all_gather(w_fc1.astype(brain), ("dp", "seq"), axis=0, tiled=True),
        lax.all_gather(w_fc2.astype(brain), ("dp", "seq"), axis=0, tiled=True),
        lax.all_gather(ffn_vecs.astype(brain), ("dp", "seq"), axis=1, tiled=True),
        lax.all_gather(ffn_wide.astype(brain), ("dp", "seq"), axis=1, tiled=True),
    )
    gathered_qkv, gathered_out, attn_back, gathered_fc1, gathered_fc2, ffn_back, wide_back = (
        back_set
    )
    attn_rows = attn_back.astype(single)
    ffn_rows = ffn_back.astype(single)
    wide_rows = wide_back.astype(single)
    grad_top = cotangent.astype(single).reshape(token_count, model_width)
    grad_branch_two = grad_top.astype(brain)
    grad_fc2 = left_grad(mixed_act, grad_branch_two)
    grad_bias_two = jnp.sum(grad_branch_two.astype(single), 0)
    grad_mixed = right_back(grad_branch_two, gathered_fc2)
    grad_inner_gain = jnp.sum(grad_mixed * normed_three, 0)
    grad_inner_bias = jnp.sum(grad_mixed, 0)
    grad_activated = norm_back(grad_mixed * wide_rows[1], normed_three, inv_three)
    grad_inner = gelu_pull(grad_activated)[0].astype(brain)
    grad_fc1 = left_grad(act_two, grad_inner)
    grad_bias_one = jnp.sum(grad_inner.astype(single), 0)
    grad_act_two = right_back(grad_inner, gathered_fc1)
    grad_gain_two = jnp.sum(grad_act_two * normed_two, 0)
    grad_shift_two = jnp.sum(grad_act_two, 0)
    grad_hidden = grad_top + norm_back(grad_act_two * ffn_rows[0], normed_two, inv_two)
    ffn_sums = (
        lax.psum_scatter(grad_fc1, ("dp", "seq"), scatter_dimension=0, tiled=True),
        lax.psum_scatter(grad_fc2, ("dp", "seq"), scatter_dimension=0, tiled=True),
        lax.psum_scatter(
            jnp.stack([grad_gain_two, grad_shift_two, grad_bias_two]),
            ("dp", "seq"),
            scatter_dimension=1,
            tiled=True,
        ),
        lax.psum_scatter(
            jnp.stack([grad_bias_one, grad_inner_gain, grad_inner_bias]),
            ("dp", "seq"),
            scatter_dimension=1,
            tiled=True,
        ),
    )
    grad_post_gain = jnp.sum(grad_hidden * normed_branch, 0)
    grad_post_shift = jnp.sum(grad_hidden, 0)
    grad_branch = norm_back(grad_hidden * attn_rows[5], normed_branch, inv_branch).astype(brain)
    grad_out_bias = jnp.sum(grad_branch.astype(single), 0)
    grad_out = left_grad(scaled, grad_branch)
    grad_scaled = right_back(grad_branch, gathered_out).reshape(
        row_count, span_len, head_count, head_size
    )
    grad_scale = jnp.sum(grad_scaled * attended, (0, 1, 3))
    grad_attended = (grad_scaled * head_scale[None, None, :, None]).astype(brain)
    delta = jnp.transpose(jnp.sum(grad_attended.astype(single) * attended, -1), (0, 2, 1))
    grad_queries, key_parts = attend_back(
        queries_four,
        keys_four,
        values_four,
        grad_attended,
        log_total,
        delta,
        query_pos,
        query_ids,
        doc_ids,
        span_len,
    )
    partial_keys = jnp.transpose(key_parts[0], (1, 0, 2, 3, 4)).reshape(row_count, -1, model_width)
    partial_values = jnp.transpose(key_parts[1], (1, 0, 2, 3, 4)).reshape(
        row_count, -1, model_width
    )
    grad_keys, grad_values = (
        lax.psum_scatter(
            partial_keys.astype(jnp.bfloat16), "seq", scatter_dimension=1, tiled=True
        ).astype(jnp.float32),
        lax.psum_scatter(
            partial_values.astype(jnp.bfloat16), "seq", scatter_dimension=1, tiled=True
        ).astype(jnp.float32),
    )
    grad_qkv = jnp.concatenate(
        [
            grad_queries.reshape(token_count, model_width).astype(brain),
            grad_keys.reshape(token_count, model_width).astype(brain),
            grad_values.reshape(token_count, model_width).astype(brain),
        ],
        1,
    )
    grad_w_qkv = left_grad(act_one, grad_qkv)
    grad_query_bias = jnp.sum(grad_qkv[:, :model_width].astype(single), 0)
    grad_value_bias = jnp.sum(grad_qkv[:, 2 * model_width :].astype(single), 0)
    grad_act_one = right_back(grad_qkv, gathered_qkv)
    grad_gain_one = jnp.sum(grad_act_one * normed_one, 0)
    grad_shift_one = jnp.sum(grad_act_one, 0)
    grad_tokens = (
        (grad_hidden + norm_back(grad_act_one * attn_rows[0], normed_one, inv_one))
        .astype(brain)
        .reshape(row_count, span_len, model_width)
    )
    attn_stack = jnp.stack(
        [
            grad_gain_one,
            grad_shift_one,
            grad_query_bias,
            grad_value_bias,
            grad_out_bias,
            grad_post_gain,
            grad_post_shift,
        ]
    )
    attn_sums = (
        lax.psum_scatter(grad_w_qkv, ("dp", "seq"), scatter_dimension=0, tiled=True),
        lax.psum_scatter(grad_out, ("dp", "seq"), scatter_dimension=0, tiled=True),
        lax.psum_scatter(attn_stack, ("dp", "seq"), scatter_dimension=1, tiled=True),
    )
    scale_total = lax.psum(grad_scale, ("dp", "seq"))
    return (
        outputs,
        grad_tokens,
        attn_sums[0],
        attn_sums[1],
        attn_sums[2],
        scale_total,
        ffn_sums[0],
        ffn_sums[1],
        ffn_sums[2],
        ffn_sums[3],
    )


class Place:
    def __init__(self):
        self.dp = lax.axis_index("dp")
        self.seq = lax.axis_index("seq")
        self.z, self.y = self.dp // NY, self.dp % NY
        self.x, self.c = self.seq // NC, self.seq % NC

    def at(self, z=None, y=None, x=None, c=None):
        z = self.z if z is None else z
        y = self.y if y is None else y
        x = self.x if x is None else x
        c = self.c if c is None else c
        return (z * NY + y, x * NC + c)

    def zup(self, k):
        return (self.z + k) % NZ

    def group(self):
        near = [self.at(c=1 - self.c), self.at(x=1 - self.x), self.at(x=1 - self.x, c=1 - self.c)]
        return near + [self.at(y=1 - self.y)] + [self.at(z=self.zup(k)) for k in range(1, NZ)]


class Wire:
    def __init__(self, place, send, recv):
        self.place, self.send, self.recv, self.used, self.open = place, send, recv, 0, []

    def copy(self, src, dst, dev):
        n = self.used
        self.used += 1
        desc = pltpu.make_async_remote_copy(
            src_ref=src,
            dst_ref=dst,
            send_sem=self.send.at[n],
            recv_sem=self.recv.at[n],
            device_id=dev,
            device_id_type=MESH,
        )
        desc.start()
        self.open.append(desc)
        return desc

    def drain(self):
        for desc in self.open:
            desc.wait_send()


def greet(place):
    barrier = pltpu.get_barrier_semaphore()
    group = place.group()
    for dev in group:
        pl.semaphore_signal(barrier, inc=1, device_id=dev, device_id_type=MESH)
    pl.semaphore_wait(barrier, len(group))


def spread_zxy(wire, place, ref, swap=False):
    z, y, x = place.z, place.y, place.x
    own = ref.at[z, y, x]
    along_z = [wire.copy(own, own, place.at(z=place.zup(k))) for k in range(1, NZ)]
    first = place.at(y=1 - y) if swap else place.at(x=1 - x)
    second = place.at(x=1 - x) if swap else place.at(y=1 - y)

    def one(zk):
        return ref.at[zk, y, x]

    def two(zk):
        return ref.at[zk, :, x] if swap else ref.at[zk, y]

    firsts = [wire.copy(own, own, first)]
    yield
    for k in range(1, NZ):
        along_z[k - 1].wait_recv()
        zk = (z - k + NZ) % NZ
        firsts.append(wire.copy(one(zk), one(zk), first))
        yield
    seconds = []
    for k in range(NZ):
        firsts[k].wait_recv()
        zk = (z - k + NZ) % NZ
        seconds.append(wire.copy(two(zk), two(zk), second))
        yield
    for desc in seconds:
        desc.wait_recv()


def spread_xzy(wire, place, ref, swap=False):
    z, y, x = place.z, place.y, place.x
    own = ref.at[z, y, x]
    first = place.at(y=1 - y) if swap else place.at(x=1 - x)
    second = place.at(x=1 - x) if swap else place.at(y=1 - y)

    def two(zk):
        return ref.at[zk, :, x] if swap else ref.at[zk, y]

    start = wire.copy(own, own, first)
    yield
    start.wait_recv()
    step = wire.copy(two(z), two(z), place.at(z=place.zup(1)))
    seconds = [wire.copy(two(z), two(z), second)]
    yield
    for k in range(1, NZ):
        step.wait_recv()
        zk = (z - k + NZ) % NZ
        if k < NZ - 1:
            step = wire.copy(two(zk), two(zk), place.at(z=place.zup(1)))
        seconds.append(wire.copy(two(zk), two(zk), second))
        yield
    for desc in seconds:
        desc.wait_recv()


def rounds(tasks):
    tasks = list(tasks)
    while tasks:
        alive = []
        for task in tasks:
            try:
                next(task)
                alive.append(task)
            except StopIteration:
                pass
        tasks = alive


def gather_kernel(tok, wq4, vec, wo, f1, f2, tok_all, wq, vecs, wo_all, f1_all, f2_all, send, recv, local):
    place = Place()
    z, y, x, c, s, dp = place.z, place.y, place.x, place.c, place.seq, place.dp
    wire = Wire(place, send, recv)
    greet(place)
    core = place.at(c=1 - c)
    other = place.at(x=1 - x)
    across = place.at(x=1 - x, c=1 - c)
    rows = f1.shape[1]
    here = [
        pltpu.make_async_copy(tok, tok_all.at[s], local.at[0]),
        pltpu.make_async_copy(wq4.at[s], wq.at[dp, s], local.at[1]),
        pltpu.make_async_copy(vec, vecs.at[dp, s], local.at[2]),
        pltpu.make_async_copy(wo, wo_all.at[z, y, x, c], local.at[3]),
        pltpu.make_async_copy(f1.at[c], f1_all.at[z, y, x, pl.ds(c * rows, rows)], local.at[4]),
        pltpu.make_async_copy(f2, f2_all.at[z, y, x], local.at[5]),
    ]
    for desc in here:
        desc.start()
    quarter = []
    for dev, peer in ((core, s ^ 1), (other, s ^ 2), (across, s ^ 3)):
        quarter.append(wire.copy(wq4.at[peer], wq.at[dp, s], dev))
        quarter.append(wire.copy(vec, vecs.at[dp, s], dev))
    tok_x = wire.copy(tok, tok_all.at[s], other)
    tok_c = wire.copy(tok, tok_all.at[s], core)
    f1_c = wire.copy(f1.at[1 - c], f1_all.at[z, y, x, pl.ds(c * rows, rows)], core)
    for desc in here:
        desc.wait()
    for desc in quarter:
        desc.wait_recv()

    def by_dp(ref):
        own = ref.at[dp]
        along_z = [wire.copy(own, own, place.at(z=place.zup(k))) for k in range(1, NZ)]
        ys = [wire.copy(own, own, place.at(y=1 - y))]
        yield
        for k in range(1, NZ):
            along_z[k - 1].wait_recv()
            blk = ref.at[((z - k + NZ) % NZ) * NY + y]
            ys.append(wire.copy(blk, blk, place.at(y=1 - y)))
        yield
        for desc in ys:
            desc.wait_recv()

    def tokens():
        tok_x.wait_recv()
        blk = tok_all.at[s ^ 2]
        last = wire.copy(blk, blk, core)
        yield
        tok_c.wait_recv()
        last.wait_recv()

    f1_c.wait_recv()
    half1 = f1_all.shape[4] // 2
    half2 = f2_all.shape[3] // 2
    plane = wo_all.at[:, :, :, c]

    def outer():
        yield from spread_zxy(wire, place, plane)
        last = wire.copy(wo_all.at[:, :, :, c], wo_all.at[:, :, :, c], core)
        yield
        last.wait_recv()

    rounds(
        [
            by_dp(wq),
            by_dp(vecs),
            tokens(),
            spread_zxy(wire, place, f1_all.at[:, :, :, :, pl.ds(0, half1)]),
            spread_xzy(wire, place, f1_all.at[:, :, :, :, pl.ds(half1, half1)], swap=True),
            outer(),
            spread_zxy(wire, place, f2_all.at[:, :, :, pl.ds(0, half2)]),
            spread_xzy(wire, place, f2_all.at[:, :, :, pl.ds(half2, half2)]),
        ]
    )
    wire.drain()


COPIES = 96


def gather_all(tok, wq4, vec, wo, f1, f2):
    span, width = tok.shape
    rows, part = wq4.shape[1:]
    dps = NZ * NY
    out = (
        jax.ShapeDtypeStruct((NX * NC, span, width), BF),
        jax.ShapeDtypeStruct((dps, NX * NC, rows, part), BF),
        jax.ShapeDtypeStruct((dps, NX * NC) + vec.shape, BF),
        jax.ShapeDtypeStruct((NZ, NY, NX, NC) + wo.shape, BF),
        jax.ShapeDtypeStruct((NZ, NY, NX, NC * f1.shape[1], f1.shape[2]), BF),
        jax.ShapeDtypeStruct((NZ, NY, NX) + f2.shape, BF),
    )
    return pl.pallas_call(
        gather_kernel,
        out_shape=out,
        in_specs=[VM] * 6,
        out_specs=[HBM] * 6,
        scratch_shapes=[
            pltpu.SemaphoreType.DMA((COPIES,)),
            pltpu.SemaphoreType.DMA((COPIES,)),
            pltpu.SemaphoreType.DMA((6,)),
        ],
        compiler_params=pltpu.CompilerParams(collective_id=1, has_side_effects=True, vmem_limit_bytes=16 * 1024 * 1024),
        name="gather_weights",
    )(tok, wq4, vec, wo, f1, f2)


def add_into(total, term):
    lead, rows = total.shape[:-2], total.shape[-2]
    step = 16 if total.dtype == BF else 8
    count = math.prod(lead)
    per = rows // step

    def body(n, _):
        block = n // per
        at = []
        for dim in reversed(lead):
            at.append(block % dim)
            block = block // dim
        idx = tuple(reversed(at)) + (pl.ds(pl.multiple_of((n % per) * step, step), step), slice(None))
        total[idx] = (total[idx].astype(F32) + term[idx].astype(F32)).astype(total.dtype)
        return 0

    lax.fori_loop(0, count * per, body, 0)


def reduce_plane(wire, place, grad, own, got, got2, got3, out, local, swap=False, ready=None):
    z, y, x = place.z, place.y, place.x
    first = place.at(x=1 - x) if swap else place.at(y=1 - y)
    second = place.at(y=1 - y) if swap else place.at(x=1 - x)

    def two(zk, mine):
        if swap:
            return grad.at[zk, :, x if mine else 1 - x]
        return grad.at[zk, y if mine else 1 - y]

    order = [(z + k) % NZ for k in (1, 2, 3, 0)]
    sends = [wire.copy(two(zk, False), got.at[k], first) for k, zk in enumerate(order)]
    loads = [pltpu.make_async_copy(two(zk, True), own.at[k], local.at[k]) for k, zk in enumerate(order)]
    for desc in loads:
        desc.start()
    yield
    seconds = []
    keep, give = (y, 1 - y) if swap else (x, 1 - x)
    for k in range(NZ):
        loads[k].wait()
        sends[k].wait_recv()
        add_into(own.at[k], got.at[k])
        seconds.append(wire.copy(own.at[k, give], got2.at[k], second))
        yield
    along = []
    for k in range(NZ):
        seconds[k].wait_recv()
        add_into(own.at[k, keep], got2.at[k])
        if k < NZ - 1:
            along.append(wire.copy(own.at[k, keep], got3.at[k], place.at(z=place.zup(k + 1))))
        yield
    for desc in along:
        desc.wait_recv()
    lead = out.shape[0]
    step = 16 if grad.dtype == BF else 8

    def body(n, _):
        idx = (pl.ds(pl.multiple_of(n * step, step), step), slice(None))
        total = own[(NZ - 1, keep) + idx].astype(F32)
        for k in range(NZ - 1):
            total = total + got3[(k,) + idx].astype(F32)
        out[idx] = total
        return 0

    lax.fori_loop(0, lead // step, body, 0)


def reduce_kernel(g1, g2, go, gq, gv, o1, o2, oo, oq, ov, *scratch):
    (own1, got1, got1b, got1c, own2, got2, got2b, got2c, owno, goto, gotob, gotoc, outp, outg) = scratch[:14]
    (ownq, gotq, gotqb, sumq, bufq, f1buf, f1got, vown, vgot, vsum, vgot2, vgot3, send, recv, local) = scratch[14:]
    place = Place()
    z, y, x, c, s, dp = place.z, place.y, place.x, place.c, place.seq, place.dp
    wire = Wire(place, send, recv)
    greet(place)
    core = place.at(c=1 - c)
    rows_o = go.shape[4]
    swap_o = wire.copy(go.at[:, :, :, 1 - c], outg, core)
    load_o = pltpu.make_async_copy(go.at[:, :, :, c], outp, local.at[0])
    load_o.start()
    swap_v = wire.copy(gv.at[:, :, :, 1 - c], vgot, core)
    load_v = pltpu.make_async_copy(gv.at[:, :, :, c], vown, local.at[1])
    load_v.start()

    def vectors():
        load_v.wait()
        swap_v.wait_recv()
        add_into(vown, vgot)
        yield
        along_y = wire.copy(vown.at[:, 1 - y], vsum, place.at(y=1 - y))
        yield
        along_y.wait_recv()
        mine = vown.at[:, y]
        add_into(mine, vsum)
        along_x = wire.copy(vown.at[:, y, 1 - x], vgot2, place.at(x=1 - x))
        yield
        along_x.wait_recv()
        mine = vown.at[:, y, x]
        add_into(mine, vgot2)
        vgot3[pl.ds(z, 1)] = vown[pl.ds(z, 1), y, x]
        along = [wire.copy(vown.at[place.zup(k), y, x], vgot3.at[z], place.at(z=place.zup(k))) for k in range(1, NZ)]
        yield
        for desc in along:
            desc.wait_recv()
        ov[...] = ((vgot3[0] + vgot3[1]) + vgot3[2]) + vgot3[3]

    def outer():
        load_o.wait()
        swap_o.wait_recv()
        add_into(outp, outg)
        yield
        yield from reduce_plane(wire, place, outp, owno, goto, gotob, gotoc, oo, local.at[pl.ds(2, NZ)], swap=True)

    def quarter():
        order = [(z + k) % NZ for k in (1, 2, 3, 0)]
        sends = [wire.copy(gq.at[zk, 1 - y], gotq.at[k], place.at(y=1 - y)) for k, zk in enumerate(order)]
        loads = [pltpu.make_async_copy(gq.at[zk, y], ownq.at[k], local.at[6 + k]) for k, zk in enumerate(order)]
        for desc in loads:
            desc.start()
        yield
        along = []
        for k in range(NZ):
            loads[k].wait()
            sends[k].wait_recv()
            add_into(ownq.at[k], gotq.at[k])
            if k < NZ - 1:
                along.append(wire.copy(ownq.at[k], gotqb.at[k], place.at(z=place.zup(k + 1))))
        yield
        for desc in along:
            desc.wait_recv()
        count, rows = sumq.shape[:2]

        def body(n, _):
            at = pl.ds(pl.multiple_of(n * 16, 16), 16)
            per = rows // 16
            total = ownq[NZ - 1, n // per, pl.ds(pl.multiple_of((n % per) * 16, 16), 16), :].astype(F32)
            for k in range(NZ - 1):
                total = total + gotqb[k, n // per, pl.ds(pl.multiple_of((n % per) * 16, 16), 16), :].astype(F32)
            sumq[n // per, pl.ds(pl.multiple_of((n % per) * 16, 16), 16), :] = total.astype(BF)
            return 0

        lax.fori_loop(0, count * (rows // 16), body, 0)
        parts = []
        for dev, peer in ((core, s ^ 1), (place.at(x=1 - x), s ^ 2), (place.at(x=1 - x, c=1 - c), s ^ 3)):
            parts.append(wire.copy(sumq.at[peer], oq.at[s], dev))
        mine = pltpu.make_async_copy(sumq.at[s], oq.at[s], local.at[10])
        mine.start()
        yield
        mine.wait()
        for desc in parts:
            desc.wait_recv()

    def first():
        yield from reduce_plane(wire, place, g1, own1, got1, got1b, got1c, f1buf, local.at[pl.ds(11, NZ)])
        rows = f1got.shape[0]
        part = wire.copy(f1buf.at[pl.ds((1 - c) * rows, rows)], f1got, core)
        o1[c] = f1buf[pl.ds(c * rows, rows)]
        yield
        part.wait_recv()
        o1[1 - c] = f1got[...]

    def second():
        yield from reduce_plane(wire, place, g2, own2, got2, got2b, got2c, o2, local.at[pl.ds(15, NZ)], swap=True)

    rounds([first(), second(), outer(), vectors(), quarter()])
    wire.drain()


def reduce_all(g1, g2, go, gq, gv):
    def bufs(block, dtype=BF):
        return [
            pltpu.VMEM((NZ, 2) + block, dtype),
            pltpu.VMEM((NZ, 2) + block, dtype),
            pltpu.VMEM((NZ,) + block, dtype),
            pltpu.VMEM((NZ - 1,) + block, dtype),
        ]

    b1, b2, bo = g1.shape[3:], g2.shape[3:], go.shape[4:]
    bq = gq.shape[2:]
    bv = gv.shape[4:]
    out = (
        jax.ShapeDtypeStruct((NC, b1[0] // NC, b1[1]), F32),
        jax.ShapeDtypeStruct(b2, F32),
        jax.ShapeDtypeStruct(bo, F32),
        jax.ShapeDtypeStruct(bq, BF),
        jax.ShapeDtypeStruct(bv, F32),
    )
    scratch = bufs(b1) + bufs(b2) + bufs(bo)
    scratch += [pltpu.VMEM((NZ, NY, NX) + bo, BF)] * 2
    scratch += [
        pltpu.VMEM((NZ,) + bq, BF),
        pltpu.VMEM((NZ,) + bq, BF),
        pltpu.VMEM((NZ - 1,) + bq, BF),
        pltpu.VMEM(bq, BF),
        pltpu.VMEM(bq, BF),
        pltpu.VMEM(b1, F32),
        pltpu.VMEM((b1[0] // NC, b1[1]), F32),
        pltpu.VMEM((NZ, NY, NX) + bv, F32),
        pltpu.VMEM((NZ, NY, NX) + bv, F32),
        pltpu.VMEM((NZ, NX) + bv, F32),
        pltpu.VMEM((NZ,) + bv, F32),
        pltpu.VMEM((NZ,) + bv, F32),
        pltpu.SemaphoreType.DMA((COPIES,)),
        pltpu.SemaphoreType.DMA((COPIES,)),
        pltpu.SemaphoreType.DMA((20,)),
    ]
    return pl.pallas_call(
        reduce_kernel,
        out_shape=out,
        in_specs=[HBM] * 5,
        out_specs=[VM] * 5,
        scratch_shapes=scratch,
        compiler_params=pltpu.CompilerParams(
            collective_id=2, has_side_effects=True, vmem_limit_bytes=48 * 1024 * 1024
        ),
        name="reduce_grads",
    )(g1, g2, go, gq, gv)


def nt(a, b):
    return lax.dot_general(a, b, (((1,), (1,)), ((), ())), preferred_element_type=F32)


def nn(a, b):
    return lax.dot_general(a, b, (((1,), (0,)), ((), ())), preferred_element_type=F32)


def pair_bias(idr, idc, qb, kb, size):
    qs = pl.multiple_of(qb * size, size)
    ks = pl.multiple_of(kb * size, size)
    key_pos = ks + lax.broadcasted_iota(jnp.int32, (size, size), 0)
    query_pos = qs + lax.broadcasted_iota(jnp.int32, (size, size), 1)
    same = idc[pl.ds(ks, size), :] == idr[:, pl.ds(qs, size)]
    return jnp.where((key_pos <= query_pos) & same, 0.0, NEGATIVE)


def mask_heads(dst, src, heads, head):
    lane = lax.broadcasted_iota(jnp.int32, src.shape, 1) // head
    whole = src[...]
    for h in range(heads):
        dst[h] = jnp.where(lane == h, whole, jnp.zeros_like(whole))


def attend_kernel(heads, size, q, k, v, idr, idc, scale, att, scaled, lse, km, vt, bias, top, low, acc):
    length, part = q.shape
    head = part // heads
    blocks = length // size
    mask_heads(km, k, heads, head)
    vt[...] = v[...].T

    def queries(qb, _):
        qs = pl.ds(pl.multiple_of(qb * size, size), size)
        top[...] = jnp.full(top.shape, NEGATIVE, F32)
        low[...] = jnp.zeros(low.shape, F32)
        acc[...] = jnp.zeros(acc.shape, F32)

        def keys(step, _):
            kb = qb - step
            ks = pl.ds(pl.multiple_of(kb * size, size), size)
            bias[...] = pair_bias(idr, idc, qb, kb, size)
            for h in range(heads):
                scores = nt(km[h, ks, :], q[qs, :]) + bias[...]
                old = top[h : h + 1, :]
                new = jnp.maximum(old, jnp.max(scores, 0, keepdims=True))
                probs = jnp.exp(scores - new)
                shrink = jnp.exp(old - new)
                top[h : h + 1, :] = new
                low[h : h + 1, :] = low[h : h + 1, :] * shrink + jnp.sum(probs, 0, keepdims=True)
                hs = slice(h * head, (h + 1) * head)
                acc[hs, :] = acc[hs, :] * shrink + nn(vt[hs, ks], probs.astype(BF))
            return 0

        lax.fori_loop(0, qb + 1, keys, 0)
        for h in range(heads):
            hs = slice(h * head, (h + 1) * head)
            acc[hs, :] = acc[hs, :] * (1.0 / low[h : h + 1, :])
        att[:, qs] = acc[...]
        lse[:, qs] = top[...] + jnp.log(low[...])
        scaled[qs, :] = (acc[...].T * scale[...]).astype(BF)
        return 0

    lax.fori_loop(0, blocks, queries, 0)


def row_attend(q, k, v, ids, scale, heads, size):
    length, part = q.shape
    rows = 8
    return pl.pallas_call(
        functools.partial(attend_kernel, heads, size),
        out_shape=(
            jax.ShapeDtypeStruct((part, length), F32),
            jax.ShapeDtypeStruct((length, part), BF),
            jax.ShapeDtypeStruct((rows, length), F32),
        ),
        in_specs=[VM] * 6,
        out_specs=[VM] * 3,
        scratch_shapes=[
            pltpu.VMEM((heads, length, part), BF),
            pltpu.VMEM((part, length), BF),
            pltpu.VMEM((size, size), F32),
            pltpu.VMEM((rows, size), F32),
            pltpu.VMEM((rows, size), F32),
            pltpu.VMEM((part, size), F32),
        ],
        compiler_params=pltpu.CompilerParams(vmem_limit_bytes=48 * 1024 * 1024),
        name="attend",
    )(q, k, v, ids.reshape(1, length), ids.reshape(length, 1), scale)


def attend_back_kernel(heads, size, q, k, v, do, att, lse, idr, idc, dq, dk, dv, delta, km, vm, qm, dm, kt, bias, acck, accv, accq):
    length, part = q.shape
    head = part // heads
    blocks = length // size
    mask_heads(km, k, heads, head)
    mask_heads(vm, v, heads, head)
    mask_heads(qm, q, heads, head)
    mask_heads(dm, do, heads, head)
    kt[...] = k[...].T
    accq[...] = jnp.zeros(accq.shape, F32)
    weighted = do[...].T.astype(F32) * att[...]
    delta[...] = jnp.zeros(delta.shape, F32)
    for h in range(heads):
        delta[h : h + 1, :] = jnp.sum(weighted[h * head : (h + 1) * head, :], 0, keepdims=True)

    def keys(kb, _):
        ks = pl.ds(pl.multiple_of(kb * size, size), size)
        acck[...] = jnp.zeros(acck.shape, F32)
        accv[...] = jnp.zeros(accv.shape, F32)

        def queries(qb, _):
            qs = pl.ds(pl.multiple_of(qb * size, size), size)
            bias[...] = pair_bias(idr, idc, qb, kb, size)
            for h in range(heads):
                scores = nt(km[h, ks, :], q[qs, :]) + bias[...]
                probs = jnp.exp(scores - lse[h : h + 1, qs])
                grad = nt(vm[h, ks, :], do[qs, :])
                ds = (probs * (grad - delta[h : h + 1, qs])).astype(BF)
                accv[...] += nn(probs.astype(BF), dm[h, qs, :])
                acck[...] += nn(ds, qm[h, qs, :])
                hs = slice(h * head, (h + 1) * head)
                accq[hs, qs] += nn(kt[hs, ks], ds)
            return 0

        lax.fori_loop(kb, blocks, queries, 0)
        dk[ks, :] = acck[...].astype(BF)
        dv[ks, :] = accv[...].astype(BF)
        return 0

    lax.fori_loop(0, blocks, keys, 0)
    for b in range(blocks):
        at = slice(b * size, (b + 1) * size)
        dq[at, :] = (accq[:, at].T * (head**-0.5)).astype(BF)


def row_attend_back(q, k, v, do, att, lse, ids, heads, size):
    length, part = q.shape
    return pl.pallas_call(
        functools.partial(attend_back_kernel, heads, size),
        out_shape=(jax.ShapeDtypeStruct((length, part), BF),) * 3 + (jax.ShapeDtypeStruct((8, length), F32),),
        in_specs=[VM] * 8,
        out_specs=[VM] * 4,
        scratch_shapes=[pltpu.VMEM((heads, length, part), BF)] * 4
        + [
            pltpu.VMEM((part, length), BF),
            pltpu.VMEM((size, size), F32),
            pltpu.VMEM((size, part), F32),
            pltpu.VMEM((size, part), F32),
            pltpu.VMEM((part, length), F32),
        ],
        compiler_params=pltpu.CompilerParams(vmem_limit_bytes=56 * 1024 * 1024),
        name="attend_back",
    )(q, k, v, do, att, lse, ids.reshape(1, length), ids.reshape(length, 1))


def trade(v, mask, perm_seq):
    pairs = [(d * perm_seq + s, d * perm_seq + (s ^ mask)) for d in range(NZ * NY) for s in range(perm_seq)]
    return lax.ppermute(v, ("dp", "seq"), pairs)


def fast(tokens, doc_ids, cotangent, w_qkv, w_out, attn_vecs, head_scale, w_fc1, w_fc2, ffn_vecs, ffn_wide):
    _, span, width = tokens.shape
    group = NX * NC
    length = span * group
    head_count = head_scale.shape[0]
    head = width // head_count
    heads = head_count // group
    part = heads * head
    seq = lax.axis_index("seq")
    core = seq % NC
    chips = NZ * NY * NX
    owners = chips * NC
    block = w_fc2.shape[0]
    units = chips * block
    swap = functools.partial(trade, perm_seq=group)
    shift = part * seq

    rows = w_qkv.shape[0]
    wq4 = w_qkv.astype(BF).reshape(rows, 3, group, part).transpose(2, 0, 1, 3).reshape(group, rows, 3 * part)
    f1 = w_fc1.astype(BF).reshape(rows, chips, NC, block).transpose(2, 0, 1, 3).reshape(NC, rows, units)
    a_len, f_len, w_len = attn_vecs.size, ffn_vecs.size, ffn_wide.size
    vec = jnp.concatenate([attn_vecs.reshape(-1), ffn_vecs.reshape(-1), ffn_wide.reshape(-1)]).astype(BF)
    vec = jnp.pad(vec, (0, 16 * 128 - vec.size)).reshape(16, 128)
    tok = tokens.reshape(span, width)
    tok_all, wq, vecs, wo, fc1, fc2 = gather_all(tok, wq4, vec, w_out.astype(BF), f1, w_fc2.astype(BF))
    tok_all = tok_all.reshape(length, width)
    wq = wq.reshape(width, 3 * part)
    wo = wo.reshape(width, width)
    fc1 = fc1.reshape(width, units)
    fc2 = fc2.reshape(units, width)
    vecs = vecs.reshape(owners, -1).astype(F32)

    def rows_of(at, size, count):
        return vecs[:, at : at + size].reshape(owners, count, -1).transpose(1, 0, 2).reshape(count, -1)

    attn_rows = rows_of(0, a_len, 7)
    ffn_rows = rows_of(a_len, f_len, 3)
    wide = rows_of(a_len + f_len, w_len, 3).reshape(3, chips, NC, block)
    wide = lax.dynamic_index_in_dim(wide, core, 2, keepdims=False).reshape(3, units)

    dtop = cotangent.reshape(span, width)
    dtop_pair = jnp.concatenate([dtop, swap(dtop, 1)], 0)

    act_one = (normalize(tok_all.astype(F32))[0] * attn_rows[0] + attn_rows[1]).astype(BF)
    proj = jnp.dot(act_one, wq, preferred_element_type=F32)
    bias_q = lax.dynamic_slice_in_dim(attn_rows[2], shift, part)
    bias_v = lax.dynamic_slice_in_dim(attn_rows[3], shift, part)
    q = (proj[:, :part] + bias_q).astype(BF) * jnp.asarray(head**-0.5, BF)
    k = proj[:, part : 2 * part].astype(BF)
    v = (proj[:, 2 * part :] + bias_v).astype(BF)
    scale_own = lax.dynamic_slice_in_dim(head_scale, heads * seq, heads)
    scale_lanes = jnp.repeat(scale_own, head).reshape(1, part)
    ids = doc_ids.reshape(length)
    size = span
    att, scaled, lse = row_attend(q, k, v, ids, scale_lanes, heads, size)

    def to_owners(blocks):
        return [lax.dynamic_index_in_dim(blocks, seq, 0, keepdims=False)] + [
            swap(lax.dynamic_index_in_dim(blocks, seq ^ m, 0, keepdims=False), m) for m in (1, 2, 3)
        ]

    got = jnp.stack(to_owners(scaled.reshape(group, span, part)))
    scaled_own = jnp.concatenate(
        [lax.dynamic_index_in_dim(got, seq ^ j, 0, keepdims=False) for j in range(group)], 1
    )
    inputs = tok.astype(F32)
    branch = jnp.dot(scaled_own, wo, preferred_element_type=F32) + attn_rows[4]
    normed_branch, inv_branch = normalize(branch)
    hidden = inputs + normed_branch * attn_rows[5] + attn_rows[6]
    normed_two, inv_two = normalize(hidden)
    act_two = (normed_two * ffn_rows[0] + ffn_rows[1]).astype(BF)

    act_pair = jnp.concatenate([act_two, swap(act_two, 1)], 0)

    def flip(stats):
        return jnp.concatenate([stats[span:], stats[:span]], 0)

    def both(stats):
        return stats + swap(flip(stats), 1)

    inner = jnp.dot(act_pair, fc1, preferred_element_type=F32) + wide[0]
    activated = gelu_exact(inner)
    total_units = units * NC
    centre = both(jnp.sum(activated, -1, keepdims=True)) / total_units
    centred = activated - centre
    inv_three = lax.rsqrt(both(jnp.sum(centred * centred, -1, keepdims=True)) / total_units + EPSILON)
    normed_three = centred * inv_three
    mixed = (normed_three * wide[1] + wide[2]).astype(BF)
    out_pair = jnp.dot(mixed, fc2, preferred_element_type=F32)
    result = hidden + ffn_rows[2] + (out_pair[:span] + swap(out_pair[span:], 1))
    outputs = result.astype(BF).reshape(1, span, width)

    grad_fc2 = left_grad(mixed, dtop_pair).astype(BF)
    grad_mixed = right_back(dtop_pair, fc2)
    gain_inner = jnp.sum(grad_mixed * normed_three, 0)
    bias_inner = jnp.sum(grad_mixed, 0)
    grad_norm = grad_mixed * wide[1]
    means = both(
        jnp.concatenate(
            [
                jnp.sum(grad_norm, -1, keepdims=True),
                jnp.sum(grad_norm * normed_three, -1, keepdims=True),
            ],
            1,
        )
    ) / total_units
    grad_activated = inv_three * (grad_norm - means[:, :1] - normed_three * means[:, 1:])
    grad_inner = (grad_activated * gelu_slope(inner)).astype(BF)
    grad_fc1 = left_grad(act_pair, grad_inner).astype(BF)
    bias_one = jnp.sum(grad_inner.astype(F32), 0)
    back_pair = right_back(grad_inner, fc1)
    grad_act_two = back_pair[:span] + swap(back_pair[span:], 1)
    top = dtop.astype(F32)
    gain_two = jnp.sum(grad_act_two * normed_two, 0)
    shift_two = jnp.sum(grad_act_two, 0)
    grad_hidden = top + norm_back(grad_act_two * ffn_rows[0], normed_two, inv_two)
    post_gain = jnp.sum(grad_hidden * normed_branch, 0)
    post_shift = jnp.sum(grad_hidden, 0)
    grad_branch = norm_back(grad_hidden * attn_rows[5], normed_branch, inv_branch).astype(BF)
    out_bias = jnp.sum(grad_branch.astype(F32), 0)
    grad_out = left_grad(scaled_own, grad_branch).astype(BF)
    grad_attended = (right_back(grad_branch, wo) * jnp.repeat(head_scale, head)).astype(BF)

    got = to_owners(grad_attended.reshape(span, group, part).transpose(1, 0, 2))
    do = jnp.zeros((length, part), BF)
    for m, piece in enumerate(got):
        do = lax.dynamic_update_slice_in_dim(do, piece, (seq ^ m) * span, 0)
    dq, dk, dv, delta = row_attend_back(q, k, v, do, att, lse, ids, heads, size)
    scale_part = jnp.sum(delta[:heads], 1) / scale_own
    grad_qkv = jnp.concatenate([dq, dk, dv], 1)
    grad_wq = left_grad(act_one, grad_qkv).astype(BF)
    query_bias = jnp.sum(dq.astype(F32), 0)
    value_bias = jnp.sum(dv.astype(F32), 0)
    da_all = right_back(grad_qkv, wq).astype(BF).reshape(group, span, width)
    mine = jnp.stack([lax.dynamic_index_in_dim(da_all, seq ^ m, 0, keepdims=False) for m in (0, 2)])
    give = jnp.stack([lax.dynamic_index_in_dim(da_all, seq ^ m, 0, keepdims=False) for m in (1, 3)])
    mine = mine.astype(F32) + swap(give, 1).astype(F32)
    grad_act_one = mine[0] + swap(mine[1].astype(BF), 2).astype(F32)
    normed_one, inv_one = normalize(inputs)
    gain_one = jnp.sum(grad_act_one * normed_one, 0)
    shift_one = jnp.sum(grad_act_one, 0)
    grad_tokens = (grad_hidden + norm_back(grad_act_one * attn_rows[0], normed_one, inv_one)).astype(BF)

    def widen(v, size, at):
        return lax.dynamic_update_slice_in_dim(jnp.zeros((size,), F32), v, at, 0)

    attn_grads = jnp.stack(
        [
            gain_one,
            shift_one,
            widen(query_bias, width, shift),
            widen(value_bias, width, shift),
            out_bias,
            post_gain,
            post_shift,
        ]
    )
    wide_grads = jnp.stack([bias_one, gain_inner, bias_inner]).reshape(3, chips, 1, block)
    is_core = (jnp.arange(NC) == core).astype(F32).reshape(1, 1, NC, 1)
    wide_grads = (wide_grads * is_core).reshape(3, NC * units)
    ffn_grads = jnp.stack([gain_two, shift_two, jnp.sum(top, 0)])
    scales = jnp.broadcast_to(widen(scale_part, head_count, heads * seq), (owners, head_count))

    def by_owner(g):
        return g.reshape(g.shape[0], owners, -1).transpose(1, 0, 2).reshape(owners, -1)

    packed = jnp.concatenate([by_owner(attn_grads), by_owner(ffn_grads), by_owner(wide_grads), scales], 1)
    packed = jnp.pad(packed, ((0, 0), (0, 8 * 128 - packed.shape[1]))).reshape(NZ, NY, NX, NC, 8, 128)
    o1, o2, oo, oq, ov = reduce_all(
        grad_fc1.reshape(NZ, NY, NX, NC * rows, units),
        grad_fc2.reshape(NZ, NY, NX, block, width),
        grad_out.reshape(NZ, NY, NX, NC, rows, width),
        grad_wq.reshape(NZ, NY, group, rows, 3 * part),
        packed,
    )
    grad_w1 = o1.reshape(NC, rows, chips, block).transpose(1, 2, 0, 3).reshape(rows, NC * units)
    grad_wqkv = oq.astype(F32).reshape(group, rows, 3, part).transpose(1, 2, 0, 3).reshape(rows, 3 * width)
    flat = ov.reshape(-1)
    end = a_len + f_len + w_len
    return (
        outputs,
        grad_tokens.reshape(1, span, width),
        grad_wqkv,
        oo,
        flat[:a_len].reshape(attn_vecs.shape),
        flat[end : end + head_count],
        grad_w1,
        o2,
        flat[a_len : a_len + f_len].reshape(ffn_vecs.shape),
        flat[a_len + f_len : end].reshape(ffn_wide.shape),
    )


def gelu_slope(u):
    return 0.5 * (1.0 + jax.scipy.special.erf(u * math.sqrt(0.5))) + u * jnp.exp(-0.5 * u * u) * (
        1.0 / math.sqrt(2.0 * math.pi)
    )


def solution(mesh):
    placed = (
        P("dp", "seq", None),
        P("dp", None),
        P("dp", "seq", None),
        P(("dp", "seq"), None),
        P(("dp", "seq"), None),
        P(None, ("dp", "seq")),
        P(),
        P(("dp", "seq"), None),
        P(("dp", "seq"), None),
        P(None, ("dp", "seq")),
        P(None, ("dp", "seq")),
    )
    results = (
        P("dp", "seq", None),
        P("dp", "seq", None),
        P(("dp", "seq"), None),
        P(("dp", "seq"), None),
        P(None, ("dp", "seq")),
        P(),
        P(("dp", "seq"), None),
        P(("dp", "seq"), None),
        P(None, ("dp", "seq")),
        P(None, ("dp", "seq")),
    )
    suits = mesh.shape["dp"] == NZ * NY and mesh.shape["seq"] == NX * NC
    return jax.shard_map(
        fast if suits else local, mesh=mesh, in_specs=placed, out_specs=results, check_vma=False
    )
```

```python
import functools
import math

import jax
import jax.numpy as jnp
from jax import lax
from jax.experimental import pallas as pl
from jax.experimental.pallas import tpu as pltpu
from jax.sharding import PartitionSpec as P

EPSILON = 1e-05
NEGATIVE = -1e30
MESH = pl.DeviceIdType.MESH
BF = jnp.bfloat16
F32 = jnp.float32
NZ, NY, NX, NC = 4, 2, 2, 2
HBM = pl.BlockSpec(memory_space=pl.ANY)
VM = pl.BlockSpec(memory_space=pltpu.VMEM)


def normalize(values):
    centre = jnp.mean(values, -1, keepdims=True)
    centred = values - centre
    scale_inv = lax.rsqrt(jnp.mean(centred * centred, -1, keepdims=True) + EPSILON)
    return (centred * scale_inv, scale_inv)


def norm_back(grad_normed, normed, scale_inv):
    return scale_inv * (
        grad_normed
        - jnp.mean(grad_normed, -1, keepdims=True)
        - normed * jnp.mean(grad_normed * normed, -1, keepdims=True)
    )


def gelu_exact(values):
    return 0.5 * values * (1.0 + jax.scipy.special.erf(values * math.sqrt(0.5)))


def left_grad(activations, gradients):
    return lax.dot_general(
        activations, gradients, (((0,), (0,)), ((), ())), preferred_element_type=jnp.float32
    )


def right_back(gradients, matrix):
    return lax.dot_general(
        gradients, matrix, (((1,), (1,)), ((), ())), preferred_element_type=jnp.float32
    )


def masked_scores(queries, keys_block, query_pos, key_pos, query_ids, key_ids):
    raw_scores = jnp.einsum(
        "rqhe,rkhe->rhqk", queries, keys_block, preferred_element_type=jnp.float32
    )
    allowed = (key_pos[None, None, :] <= query_pos[None, :, None]) & (
        key_ids[:, None, :] == query_ids[:, :, None]
    )
    return jnp.where(allowed[:, None], raw_scores * queries.shape[3] ** (-0.5), NEGATIVE)


def attend(queries, keys_all, values_all, query_pos, query_ids, doc_rows, block_len):
    block_count = keys_all.shape[1] // block_len
    stat_shape = (queries.shape[0], queries.shape[2], queries.shape[1])

    def slice_block(block_index):
        start = block_index * block_len
        keys_block = lax.dynamic_slice_in_dim(keys_all, start, block_len, 1)
        values_block = lax.dynamic_slice_in_dim(values_all, start, block_len, 1)
        key_ids = lax.dynamic_slice_in_dim(doc_rows, start, block_len, 1)
        key_pos = start + jnp.arange(block_len, dtype=jnp.int32)
        return (
            values_block,
            masked_scores(queries, keys_block, query_pos, key_pos, query_ids, key_ids),
        )

    def first_pass(carry, block_index):
        running_max, running_sum = carry
        _, scores = slice_block(block_index)
        new_max = jnp.maximum(running_max, jnp.max(scores, -1))
        running_sum = running_sum * jnp.exp(running_max - new_max) + jnp.sum(
            jnp.exp(scores - new_max[..., None]), -1
        )
        return ((new_max, running_sum), None)

    start_stats = (jnp.full(stat_shape, NEGATIVE, jnp.float32), jnp.zeros(stat_shape, jnp.float32))
    (row_max, row_sum), _ = lax.scan(
        first_pass, start_stats, jnp.arange(block_count, dtype=jnp.int32)
    )
    log_total = row_max + jnp.log(row_sum)

    def second_pass(total_out, block_index):
        values_block, scores = slice_block(block_index)
        probs = jnp.exp(scores - log_total[..., None]).astype(jnp.bfloat16)
        return (
            total_out
            + jnp.einsum(
                "rhqk,rkhe->rqhe", probs, values_block, preferred_element_type=jnp.float32
            ),
            None,
        )

    attended, _ = lax.scan(
        second_pass, jnp.zeros(queries.shape, jnp.float32), jnp.arange(block_count, dtype=jnp.int32)
    )
    return (attended, log_total)


def attend_back(
    queries,
    keys_all,
    values_all,
    grad_out,
    log_total,
    delta,
    query_pos,
    query_ids,
    doc_rows,
    block_len,
):
    block_count = keys_all.shape[1] // block_len
    scale = queries.shape[3] ** (-0.5)

    def step(grad_queries, block_index):
        start = block_index * block_len
        keys_block = lax.dynamic_slice_in_dim(keys_all, start, block_len, 1)
        values_block = lax.dynamic_slice_in_dim(values_all, start, block_len, 1)
        key_ids = lax.dynamic_slice_in_dim(doc_rows, start, block_len, 1)
        key_pos = start + jnp.arange(block_len, dtype=jnp.int32)
        scores = masked_scores(queries, keys_block, query_pos, key_pos, query_ids, key_ids)
        probs = jnp.exp(scores - log_total[..., None])
        grad_probs = jnp.einsum(
            "rqhe,rkhe->rhqk", grad_out, values_block, preferred_element_type=jnp.float32
        )
        grad_scores = (probs * (grad_probs - delta[..., None]) * scale).astype(jnp.bfloat16)
        grad_queries = grad_queries + jnp.einsum(
            "rhqk,rkhe->rqhe", grad_scores, keys_block, preferred_element_type=jnp.float32
        )
        grad_keys = jnp.einsum(
            "rhqk,rqhe->rkhe", grad_scores, queries, preferred_element_type=jnp.float32
        )
        grad_values = jnp.einsum(
            "rhqk,rqhe->rkhe",
            probs.astype(jnp.bfloat16),
            grad_out,
            preferred_element_type=jnp.float32,
        )
        return (grad_queries, (grad_keys, grad_values))

    return lax.scan(
        step, jnp.zeros(queries.shape, jnp.float32), jnp.arange(block_count, dtype=jnp.int32)
    )


def local(
    tokens,
    doc_ids,
    cotangent,
    w_qkv,
    w_out,
    attn_vecs,
    head_scale,
    w_fc1,
    w_fc2,
    ffn_vecs,
    ffn_wide,
):
    row_count, span_len, model_width = tokens.shape
    head_count = head_scale.shape[0]
    head_size = model_width // head_count
    token_count = row_count * span_len
    brain = jnp.bfloat16
    single = jnp.float32
    gathered_qkv, gathered_out, attn_rows = (
        lax.all_gather(w_qkv.astype(brain), ("dp", "seq"), axis=0, tiled=True),
        lax.all_gather(w_out.astype(brain), ("dp", "seq"), axis=0, tiled=True),
        lax.all_gather(attn_vecs.astype(brain), ("dp", "seq"), axis=1, tiled=True),
    )
    attn_rows = attn_rows.astype(single)
    inputs = tokens.astype(single).reshape(token_count, model_width)
    normed_one, inv_one = normalize(inputs)
    act_one = (normed_one * attn_rows[0] + attn_rows[1]).astype(brain)
    projected = jnp.dot(act_one, gathered_qkv, preferred_element_type=single)
    queries = (projected[:, :model_width] + attn_rows[2]).astype(brain)
    keys_own = projected[:, model_width : 2 * model_width].astype(brain)
    values_own = (projected[:, 2 * model_width :] + attn_rows[3]).astype(brain)
    keys_all, values_all = (
        lax.all_gather(
            keys_own.reshape(row_count, span_len, model_width), "seq", axis=1, tiled=True
        ),
        lax.all_gather(
            values_own.reshape(row_count, span_len, model_width), "seq", axis=1, tiled=True
        ),
    )
    offset = lax.axis_index("seq") * span_len
    query_pos = offset + jnp.arange(span_len, dtype=jnp.int32)
    query_ids = lax.dynamic_slice_in_dim(doc_ids, offset, span_len, 1)
    queries_four = queries.reshape(row_count, span_len, head_count, head_size)
    keys_four = keys_all.reshape(row_count, -1, head_count, head_size)
    values_four = values_all.reshape(row_count, -1, head_count, head_size)
    attended, log_total = attend(
        queries_four, keys_four, values_four, query_pos, query_ids, doc_ids, span_len
    )
    scaled = (
        (attended * head_scale[None, None, :, None]).reshape(token_count, model_width).astype(brain)
    )
    branch = jnp.dot(scaled, gathered_out, preferred_element_type=single) + attn_rows[4]
    normed_branch, inv_branch = normalize(branch)
    hidden = inputs + normed_branch * attn_rows[5] + attn_rows[6]
    gathered_fc1, gathered_fc2, ffn_rows, wide_rows = (
        lax.all_gather(w_fc1.astype(brain), ("dp", "seq"), axis=0, tiled=True),
        lax.all_gather(w_fc2.astype(brain), ("dp", "seq"), axis=0, tiled=True),
        lax.all_gather(ffn_vecs.astype(brain), ("dp", "seq"), axis=1, tiled=True),
        lax.all_gather(ffn_wide.astype(brain), ("dp", "seq"), axis=1, tiled=True),
    )
    ffn_rows = ffn_rows.astype(single)
    wide_rows = wide_rows.astype(single)
    normed_two, inv_two = normalize(hidden)
    act_two = (normed_two * ffn_rows[0] + ffn_rows[1]).astype(brain)
    inner_act = jnp.dot(act_two, gathered_fc1, preferred_element_type=single) + wide_rows[0]
    activated, gelu_pull = jax.vjp(gelu_exact, inner_act)
    normed_three, inv_three = normalize(activated)
    mixed_act = (normed_three * wide_rows[1] + wide_rows[2]).astype(brain)
    result = hidden + jnp.dot(mixed_act, gathered_fc2, preferred_element_type=single) + ffn_rows[2]
    outputs = result.astype(brain).reshape(row_count, span_len, model_width)
    back_set = (
        lax.all_gather(w_qkv.astype(brain), ("dp", "seq"), axis=0, tiled=True),
        lax.all_gather(w_out.astype(brain), ("dp", "seq"), axis=0, tiled=True),
        lax.all_gather(attn_vecs.astype(brain), ("dp", "seq"), axis=1, tiled=True),
        lax.all_gather(w_fc1.astype(brain), ("dp", "seq"), axis=0, tiled=True),
        lax.all_gather(w_fc2.astype(brain), ("dp", "seq"), axis=0, tiled=True),
        lax.all_gather(ffn_vecs.astype(brain), ("dp", "seq"), axis=1, tiled=True),
        lax.all_gather(ffn_wide.astype(brain), ("dp", "seq"), axis=1, tiled=True),
    )
    gathered_qkv, gathered_out, attn_back, gathered_fc1, gathered_fc2, ffn_back, wide_back = (
        back_set
    )
    attn_rows = attn_back.astype(single)
    ffn_rows = ffn_back.astype(single)
    wide_rows = wide_back.astype(single)
    grad_top = cotangent.astype(single).reshape(token_count, model_width)
    grad_branch_two = grad_top.astype(brain)
    grad_fc2 = left_grad(mixed_act, grad_branch_two)
    grad_bias_two = jnp.sum(grad_branch_two.astype(single), 0)
    grad_mixed = right_back(grad_branch_two, gathered_fc2)
    grad_inner_gain = jnp.sum(grad_mixed * normed_three, 0)
    grad_inner_bias = jnp.sum(grad_mixed, 0)
    grad_activated = norm_back(grad_mixed * wide_rows[1], normed_three, inv_three)
    grad_inner = gelu_pull(grad_activated)[0].astype(brain)
    grad_fc1 = left_grad(act_two, grad_inner)
    grad_bias_one = jnp.sum(grad_inner.astype(single), 0)
    grad_act_two = right_back(grad_inner, gathered_fc1)
    grad_gain_two = jnp.sum(grad_act_two * normed_two, 0)
    grad_shift_two = jnp.sum(grad_act_two, 0)
    grad_hidden = grad_top + norm_back(grad_act_two * ffn_rows[0], normed_two, inv_two)
    ffn_sums = (
        lax.psum_scatter(grad_fc1, ("dp", "seq"), scatter_dimension=0, tiled=True),
        lax.psum_scatter(grad_fc2, ("dp", "seq"), scatter_dimension=0, tiled=True),
        lax.psum_scatter(
            jnp.stack([grad_gain_two, grad_shift_two, grad_bias_two]),
            ("dp", "seq"),
            scatter_dimension=1,
            tiled=True,
        ),
        lax.psum_scatter(
            jnp.stack([grad_bias_one, grad_inner_gain, grad_inner_bias]),
            ("dp", "seq"),
            scatter_dimension=1,
            tiled=True,
        ),
    )
    grad_post_gain = jnp.sum(grad_hidden * normed_branch, 0)
    grad_post_shift = jnp.sum(grad_hidden, 0)
    grad_branch = norm_back(grad_hidden * attn_rows[5], normed_branch, inv_branch).astype(brain)
    grad_out_bias = jnp.sum(grad_branch.astype(single), 0)
    grad_out = left_grad(scaled, grad_branch)
    grad_scaled = right_back(grad_branch, gathered_out).reshape(
        row_count, span_len, head_count, head_size
    )
    grad_scale = jnp.sum(grad_scaled * attended, (0, 1, 3))
    grad_attended = (grad_scaled * head_scale[None, None, :, None]).astype(brain)
    delta = jnp.transpose(jnp.sum(grad_attended.astype(single) * attended, -1), (0, 2, 1))
    grad_queries, key_parts = attend_back(
        queries_four,
        keys_four,
        values_four,
        grad_attended,
        log_total,
        delta,
        query_pos,
        query_ids,
        doc_ids,
        span_len,
    )
    partial_keys = jnp.transpose(key_parts[0], (1, 0, 2, 3, 4)).reshape(row_count, -1, model_width)
    partial_values = jnp.transpose(key_parts[1], (1, 0, 2, 3, 4)).reshape(
        row_count, -1, model_width
    )
    grad_keys, grad_values = (
        lax.psum_scatter(
            partial_keys.astype(jnp.bfloat16), "seq", scatter_dimension=1, tiled=True
        ).astype(jnp.float32),
        lax.psum_scatter(
            partial_values.astype(jnp.bfloat16), "seq", scatter_dimension=1, tiled=True
        ).astype(jnp.float32),
    )
    grad_qkv = jnp.concatenate(
        [
            grad_queries.reshape(token_count, model_width).astype(brain),
            grad_keys.reshape(token_count, model_width).astype(brain),
            grad_values.reshape(token_count, model_width).astype(brain),
        ],
        1,
    )
    grad_w_qkv = left_grad(act_one, grad_qkv)
    grad_query_bias = jnp.sum(grad_qkv[:, :model_width].astype(single), 0)
    grad_value_bias = jnp.sum(grad_qkv[:, 2 * model_width :].astype(single), 0)
    grad_act_one = right_back(grad_qkv, gathered_qkv)
    grad_gain_one = jnp.sum(grad_act_one * normed_one, 0)
    grad_shift_one = jnp.sum(grad_act_one, 0)
    grad_tokens = (
        (grad_hidden + norm_back(grad_act_one * attn_rows[0], normed_one, inv_one))
        .astype(brain)
        .reshape(row_count, span_len, model_width)
    )
    attn_stack = jnp.stack(
        [
            grad_gain_one,
            grad_shift_one,
            grad_query_bias,
            grad_value_bias,
            grad_out_bias,
            grad_post_gain,
            grad_post_shift,
        ]
    )
    attn_sums = (
        lax.psum_scatter(grad_w_qkv, ("dp", "seq"), scatter_dimension=0, tiled=True),
        lax.psum_scatter(grad_out, ("dp", "seq"), scatter_dimension=0, tiled=True),
        lax.psum_scatter(attn_stack, ("dp", "seq"), scatter_dimension=1, tiled=True),
    )
    scale_total = lax.psum(grad_scale, ("dp", "seq"))
    return (
        outputs,
        grad_tokens,
        attn_sums[0],
        attn_sums[1],
        attn_sums[2],
        scale_total,
        ffn_sums[0],
        ffn_sums[1],
        ffn_sums[2],
        ffn_sums[3],
    )


class Place:
    def __init__(self):
        self.dp = lax.axis_index("dp")
        self.seq = lax.axis_index("seq")
        self.z, self.y = self.dp // NY, self.dp % NY
        self.x, self.c = self.seq // NC, self.seq % NC

    def at(self, z=None, y=None, x=None, c=None):
        z = self.z if z is None else z
        y = self.y if y is None else y
        x = self.x if x is None else x
        c = self.c if c is None else c
        return (z * NY + y, x * NC + c)

    def zup(self, k):
        return (self.z + k) % NZ

    def group(self):
        near = [self.at(c=1 - self.c), self.at(x=1 - self.x), self.at(x=1 - self.x, c=1 - self.c)]
        return near + [self.at(y=1 - self.y)] + [self.at(z=self.zup(k)) for k in range(1, NZ)]


class Copy:
    def __init__(self, desc):
        self.desc = desc

    def go(self):
        self.desc.start()
        return self

    def wait_recv(self):
        self.desc.wait_recv()

    def wait_send(self):
        self.desc.wait_send()


class Wire:
    def __init__(self, place, send, recv):
        self.place, self.send, self.recv, self.used, self.open = place, send, recv, 0, []

    def copy(self, src, dst, dev):
        n = self.used
        self.used += 1
        copy = Copy(
            pltpu.make_async_remote_copy(
                src_ref=src,
                dst_ref=dst,
                send_sem=self.send.at[n],
                recv_sem=self.recv.at[n],
                device_id=dev,
                device_id_type=MESH,
            )
        )
        self.open.append(copy)
        return copy

    def drain(self):
        for copy in self.open:
            copy.wait_send()


def greet(place):
    barrier = pltpu.get_barrier_semaphore()
    group = place.group()
    for dev in group:
        pl.semaphore_signal(barrier, inc=1, device_id=dev, device_id_type=MESH)
    pl.semaphore_wait(barrier, len(group))


def spread_zxy(wire, place, ref, swap=False):
    z, y, x = place.z, place.y, place.x
    own = ref.at[z, y, x]
    first = place.at(y=1 - y) if swap else place.at(x=1 - x)
    second = place.at(x=1 - x) if swap else place.at(y=1 - y)
    order = [(z - k + NZ) % NZ for k in range(NZ)]
    along_z = [wire.copy(own, own, place.at(z=place.zup(k))) for k in range(1, NZ)]
    firsts = [wire.copy(ref.at[zk, y, x], ref.at[zk, y, x], first) for zk in order]
    twos = [ref.at[zk, :, x] if swap else ref.at[zk, y] for zk in order]
    seconds = [wire.copy(two, two, second) for two in twos]
    yield
    for copy in along_z + firsts[:1]:
        copy.go()
    yield
    for k in range(1, NZ):
        along_z[k - 1].wait_recv()
        firsts[k].go()
        yield
    for k in range(NZ):
        firsts[k].wait_recv()
        seconds[k].go()
        yield
    for copy in seconds:
        copy.wait_recv()


def spread_xzy(wire, place, ref, swap=False):
    z, y, x = place.z, place.y, place.x
    own = ref.at[z, y, x]
    first = place.at(y=1 - y) if swap else place.at(x=1 - x)
    second = place.at(x=1 - x) if swap else place.at(y=1 - y)
    order = [(z - k + NZ) % NZ for k in range(NZ)]
    twos = [ref.at[zk, :, x] if swap else ref.at[zk, y] for zk in order]
    start = wire.copy(own, own, first)
    steps = [wire.copy(two, two, place.at(z=place.zup(1))) for two in twos[:-1]]
    seconds = [wire.copy(two, two, second) for two in twos]
    yield
    start.go()
    yield
    start.wait_recv()
    steps[0].go()
    seconds[0].go()
    yield
    for k in range(1, NZ):
        steps[k - 1].wait_recv()
        if k < NZ - 1:
            steps[k].go()
        seconds[k].go()
        yield
    for copy in seconds:
        copy.wait_recv()


def rounds(tasks):
    tasks = list(tasks)
    while tasks:
        alive = []
        for task in tasks:
            try:
                next(task)
                alive.append(task)
            except StopIteration:
                pass
        tasks = alive


COPIES = 104


def add_into(total, term):
    lead, rows = total.shape[:-2], total.shape[-2]
    step = 16 if total.dtype == BF else 8
    count = math.prod(lead)
    per = rows // step

    def body(n, _):
        block = n // per
        at = []
        for dim in reversed(lead):
            at.append(block % dim)
            block = block // dim
        idx = tuple(reversed(at)) + (pl.ds(pl.multiple_of((n % per) * step, step), step), slice(None))
        total[idx] = (total[idx].astype(F32) + term[idx].astype(F32)).astype(total.dtype)
        return 0

    lax.fori_loop(0, count * per, body, 0)


def reduce_plane(wire, place, grad, own, got, got2, got3, out, local, swap=False, ready=None):
    z, y, x = place.z, place.y, place.x
    first = place.at(x=1 - x) if swap else place.at(y=1 - y)
    second = place.at(y=1 - y) if swap else place.at(x=1 - x)

    def two(zk, mine):
        if swap:
            return grad.at[zk, :, x if mine else 1 - x]
        return grad.at[zk, y if mine else 1 - y]

    order = [(z + k) % NZ for k in (1, 2, 3, 0)]
    sends = [wire.copy(two(zk, False), got.at[k], first).go() for k, zk in enumerate(order)]
    loads = [pltpu.make_async_copy(two(zk, True), own.at[k], local.at[k]) for k, zk in enumerate(order)]
    for desc in loads:
        desc.start()
    yield
    seconds = []
    keep, give = (y, 1 - y) if swap else (x, 1 - x)
    for k in range(NZ):
        loads[k].wait()
        sends[k].wait_recv()
        add_into(own.at[k], got.at[k])
        seconds.append(wire.copy(own.at[k, give], got2.at[k], second).go())
        yield
    along = []
    for k in range(NZ):
        seconds[k].wait_recv()
        add_into(own.at[k, keep], got2.at[k])
        if k < NZ - 1:
            along.append(wire.copy(own.at[k, keep], got3.at[k], place.at(z=place.zup(k + 1))).go())
        yield
    for desc in along:
        desc.wait_recv()
    lead = out.shape[0]
    step = 16 if grad.dtype == BF else 8

    def body(n, _):
        idx = (pl.ds(pl.multiple_of(n * step, step), step), slice(None))
        total = own[(NZ - 1, keep) + idx].astype(F32)
        for k in range(NZ - 1):
            total = total + got3[(k,) + idx].astype(F32)
        out[idx] = total
        return 0

    lax.fori_loop(0, lead // step, body, 0)


def reduce_kernel(g1, g2, go, gq, gv, o1, o2, oo, oq, ov, *scratch):
    (own1, got1, got1b, got1c, own2, got2, got2b, got2c, owno, goto, gotob, gotoc, outp, outg) = scratch[:14]
    (ownq, gotq, gotqb, sumq, bufq, f1buf, f1got, vown, vgot, vsum, vgot2, vgot3, send, recv, local) = scratch[14:]
    place = Place()
    z, y, x, c, s, dp = place.z, place.y, place.x, place.c, place.seq, place.dp
    wire = Wire(place, send, recv)
    greet(place)
    core = place.at(c=1 - c)
    rows_o = go.shape[4]
    swap_o = wire.copy(go.at[:, :, :, 1 - c], outg, core).go()
    load_o = pltpu.make_async_copy(go.at[:, :, :, c], outp, local.at[0])
    load_o.start()
    swap_v = wire.copy(gv.at[:, :, :, 1 - c], vgot, core).go()
    load_v = pltpu.make_async_copy(gv.at[:, :, :, c], vown, local.at[1])
    load_v.start()

    def vectors():
        load_v.wait()
        swap_v.wait_recv()
        add_into(vown, vgot)
        yield
        along_y = wire.copy(vown.at[:, 1 - y], vsum, place.at(y=1 - y)).go()
        yield
        along_y.wait_recv()
        mine = vown.at[:, y]
        add_into(mine, vsum)
        along_x = wire.copy(vown.at[:, y, 1 - x], vgot2, place.at(x=1 - x)).go()
        yield
        along_x.wait_recv()
        mine = vown.at[:, y, x]
        add_into(mine, vgot2)
        vgot3[pl.ds(z, 1)] = vown[pl.ds(z, 1), y, x]
        along = [wire.copy(vown.at[place.zup(k), y, x], vgot3.at[z], place.at(z=place.zup(k))).go() for k in range(1, NZ)]
        yield
        for desc in along:
            desc.wait_recv()
        ov[...] = ((vgot3[0] + vgot3[1]) + vgot3[2]) + vgot3[3]

    def outer():
        load_o.wait()
        swap_o.wait_recv()
        add_into(outp, outg)
        yield
        yield from reduce_plane(wire, place, outp, owno, goto, gotob, gotoc, oo, local.at[pl.ds(2, NZ)], swap=True)

    def quarter():
        order = [(z + k) % NZ for k in (1, 2, 3, 0)]
        sends = [wire.copy(gq.at[zk, 1 - y], gotq.at[k], place.at(y=1 - y)).go() for k, zk in enumerate(order)]
        loads = [pltpu.make_async_copy(gq.at[zk, y], ownq.at[k], local.at[6 + k]) for k, zk in enumerate(order)]
        for desc in loads:
            desc.start()
        yield
        along = []
        for k in range(NZ):
            loads[k].wait()
            sends[k].wait_recv()
            add_into(ownq.at[k], gotq.at[k])
            if k < NZ - 1:
                along.append(wire.copy(ownq.at[k], gotqb.at[k], place.at(z=place.zup(k + 1))).go())
        yield
        for desc in along:
            desc.wait_recv()
        count, rows = sumq.shape[:2]

        def body(n, _):
            at = pl.ds(pl.multiple_of(n * 16, 16), 16)
            per = rows // 16
            total = ownq[NZ - 1, n // per, pl.ds(pl.multiple_of((n % per) * 16, 16), 16), :].astype(F32)
            for k in range(NZ - 1):
                total = total + gotqb[k, n // per, pl.ds(pl.multiple_of((n % per) * 16, 16), 16), :].astype(F32)
            sumq[n // per, pl.ds(pl.multiple_of((n % per) * 16, 16), 16), :] = total.astype(BF)
            return 0

        lax.fori_loop(0, count * (rows // 16), body, 0)
        parts = []
        for dev, peer in ((core, s ^ 1), (place.at(x=1 - x), s ^ 2), (place.at(x=1 - x, c=1 - c), s ^ 3)):
            parts.append(wire.copy(sumq.at[peer], oq.at[s], dev).go())
        mine = pltpu.make_async_copy(sumq.at[s], oq.at[s], local.at[10])
        mine.start()
        yield
        mine.wait()
        for desc in parts:
            desc.wait_recv()

    def first():
        yield from reduce_plane(wire, place, g1, own1, got1, got1b, got1c, f1buf, local.at[pl.ds(11, NZ)])
        rows = f1got.shape[0]
        part = wire.copy(f1buf.at[pl.ds((1 - c) * rows, rows)], f1got, core).go()
        o1[c] = f1buf[pl.ds(c * rows, rows)]
        yield
        part.wait_recv()
        o1[1 - c] = f1got[...]

    def second():
        yield from reduce_plane(wire, place, g2, own2, got2, got2b, got2c, o2, local.at[pl.ds(15, NZ)], swap=True)

    rounds([first(), second(), outer(), vectors(), quarter()])
    wire.drain()


def reduce_all(g1, g2, go, gq, gv):
    def bufs(block, dtype=BF):
        return [
            pltpu.VMEM((NZ, 2) + block, dtype),
            pltpu.VMEM((NZ, 2) + block, dtype),
            pltpu.VMEM((NZ,) + block, dtype),
            pltpu.VMEM((NZ - 1,) + block, dtype),
        ]

    b1, b2, bo = g1.shape[3:], g2.shape[3:], go.shape[4:]
    bq = gq.shape[2:]
    bv = gv.shape[4:]
    out = (
        jax.ShapeDtypeStruct((NC, b1[0] // NC, b1[1]), F32),
        jax.ShapeDtypeStruct(b2, F32),
        jax.ShapeDtypeStruct(bo, F32),
        jax.ShapeDtypeStruct(bq, BF),
        jax.ShapeDtypeStruct(bv, F32),
    )
    scratch = bufs(b1) + bufs(b2) + bufs(bo)
    scratch += [pltpu.VMEM((NZ, NY, NX) + bo, BF)] * 2
    scratch += [
        pltpu.VMEM((NZ,) + bq, BF),
        pltpu.VMEM((NZ,) + bq, BF),
        pltpu.VMEM((NZ - 1,) + bq, BF),
        pltpu.VMEM(bq, BF),
        pltpu.VMEM(bq, BF),
        pltpu.VMEM(b1, F32),
        pltpu.VMEM((b1[0] // NC, b1[1]), F32),
        pltpu.VMEM((NZ, NY, NX) + bv, F32),
        pltpu.VMEM((NZ, NY, NX) + bv, F32),
        pltpu.VMEM((NZ, NX) + bv, F32),
        pltpu.VMEM((NZ,) + bv, F32),
        pltpu.VMEM((NZ,) + bv, F32),
        pltpu.SemaphoreType.DMA((COPIES,)),
        pltpu.SemaphoreType.DMA((COPIES,)),
        pltpu.SemaphoreType.DMA((20,)),
    ]
    return pl.pallas_call(
        reduce_kernel,
        out_shape=out,
        in_specs=[HBM] * 5,
        out_specs=[VM] * 5,
        scratch_shapes=scratch,
        compiler_params=pltpu.CompilerParams(
            collective_id=2, has_side_effects=True, vmem_limit_bytes=48 * 1024 * 1024
        ),
        name="reduce_grads",
    )(g1, g2, go, gq, gv)


def nt(a, b):
    return lax.dot_general(a, b, (((1,), (1,)), ((), ())), preferred_element_type=F32)


def nn(a, b):
    return lax.dot_general(a, b, (((1,), (0,)), ((), ())), preferred_element_type=F32)


def pair_bias(idr, idc, qb, kb, size):
    qs = pl.multiple_of(qb * size, size)
    ks = pl.multiple_of(kb * size, size)
    key_pos = ks + lax.broadcasted_iota(jnp.int32, (size, size), 0)
    query_pos = qs + lax.broadcasted_iota(jnp.int32, (size, size), 1)
    same = idc[pl.ds(ks, size), :] == idr[:, pl.ds(qs, size)]
    return jnp.where((key_pos <= query_pos) & same, 0.0, NEGATIVE)


def mask_heads(dst, src, heads, head):
    lane = lax.broadcasted_iota(jnp.int32, src.shape, 1) // head
    whole = src[...]
    for h in range(heads):
        dst[h] = jnp.where(lane == h, whole, jnp.zeros_like(whole))


def attend_kernel(heads, size, q, k, v, idr, idc, scale, att, scaled, lse, km, vt, bias, top, low, acc):
    length, part = q.shape
    head = part // heads
    blocks = length // size
    mask_heads(km, k, heads, head)
    vt[...] = v[...].T

    def queries(qb, _):
        qs = pl.ds(pl.multiple_of(qb * size, size), size)
        top[...] = jnp.full(top.shape, NEGATIVE, F32)
        low[...] = jnp.zeros(low.shape, F32)
        acc[...] = jnp.zeros(acc.shape, F32)

        def keys(step, _):
            kb = qb - step
            ks = pl.ds(pl.multiple_of(kb * size, size), size)
            bias[...] = pair_bias(idr, idc, qb, kb, size)
            for h in range(heads):
                scores = nt(km[h, ks, :], q[qs, :]) + bias[...]
                old = top[h : h + 1, :]
                new = jnp.maximum(old, jnp.max(scores, 0, keepdims=True))
                probs = jnp.exp(scores - new)
                shrink = jnp.exp(old - new)
                top[h : h + 1, :] = new
                low[h : h + 1, :] = low[h : h + 1, :] * shrink + jnp.sum(probs, 0, keepdims=True)
                hs = slice(h * head, (h + 1) * head)
                acc[hs, :] = acc[hs, :] * shrink + nn(vt[hs, ks], probs.astype(BF))
            return 0

        lax.fori_loop(0, qb + 1, keys, 0)
        for h in range(heads):
            hs = slice(h * head, (h + 1) * head)
            acc[hs, :] = acc[hs, :] * (1.0 / low[h : h + 1, :])
        att[:, qs] = acc[...]
        lse[:, qs] = top[...] + jnp.log(low[...])
        scaled[qs, :] = (acc[...].T * scale[...]).astype(BF)
        return 0

    lax.fori_loop(0, blocks, queries, 0)


def row_attend(q, k, v, ids, scale, heads, size):
    length, part = q.shape
    rows = 8
    return pl.pallas_call(
        functools.partial(attend_kernel, heads, size),
        out_shape=(
            jax.ShapeDtypeStruct((part, length), F32),
            jax.ShapeDtypeStruct((length, part), BF),
            jax.ShapeDtypeStruct((rows, length), F32),
        ),
        in_specs=[VM] * 6,
        out_specs=[VM] * 3,
        scratch_shapes=[
            pltpu.VMEM((heads, length, part), BF),
            pltpu.VMEM((part, length), BF),
            pltpu.VMEM((size, size), F32),
            pltpu.VMEM((rows, size), F32),
            pltpu.VMEM((rows, size), F32),
            pltpu.VMEM((part, size), F32),
        ],
        compiler_params=pltpu.CompilerParams(vmem_limit_bytes=48 * 1024 * 1024),
        name="attend",
    )(q, k, v, ids.reshape(1, length), ids.reshape(length, 1), scale)


def attend_back_kernel(heads, size, q, k, v, do, att, lse, idr, idc, dq, dk, dv, delta, km, vm, qm, dm, kt, bias, acck, accv, accq):
    length, part = q.shape
    head = part // heads
    blocks = length // size
    mask_heads(km, k, heads, head)
    mask_heads(vm, v, heads, head)
    mask_heads(qm, q, heads, head)
    mask_heads(dm, do, heads, head)
    kt[...] = k[...].T
    accq[...] = jnp.zeros(accq.shape, F32)
    weighted = do[...].T.astype(F32) * att[...]
    delta[...] = jnp.zeros(delta.shape, F32)
    for h in range(heads):
        delta[h : h + 1, :] = jnp.sum(weighted[h * head : (h + 1) * head, :], 0, keepdims=True)

    def keys(kb, _):
        ks = pl.ds(pl.multiple_of(kb * size, size), size)
        acck[...] = jnp.zeros(acck.shape, F32)
        accv[...] = jnp.zeros(accv.shape, F32)

        def queries(qb, _):
            qs = pl.ds(pl.multiple_of(qb * size, size), size)
            bias[...] = pair_bias(idr, idc, qb, kb, size)
            for h in range(heads):
                scores = nt(km[h, ks, :], q[qs, :]) + bias[...]
                probs = jnp.exp(scores - lse[h : h + 1, qs])
                grad = nt(vm[h, ks, :], do[qs, :])
                ds = (probs * (grad - delta[h : h + 1, qs])).astype(BF)
                accv[...] += nn(probs.astype(BF), dm[h, qs, :])
                acck[...] += nn(ds, qm[h, qs, :])
                hs = slice(h * head, (h + 1) * head)
                accq[hs, qs] += nn(kt[hs, ks], ds)
            return 0

        lax.fori_loop(kb, blocks, queries, 0)
        dk[ks, :] = acck[...].astype(BF)
        dv[ks, :] = accv[...].astype(BF)
        return 0

    lax.fori_loop(0, blocks, keys, 0)
    for b in range(blocks):
        at = slice(b * size, (b + 1) * size)
        dq[at, :] = (accq[:, at].T * (head**-0.5)).astype(BF)


def row_attend_back(q, k, v, do, att, lse, ids, heads, size):
    length, part = q.shape
    return pl.pallas_call(
        functools.partial(attend_back_kernel, heads, size),
        out_shape=(jax.ShapeDtypeStruct((length, part), BF),) * 3 + (jax.ShapeDtypeStruct((8, length), F32),),
        in_specs=[VM] * 8,
        out_specs=[VM] * 4,
        scratch_shapes=[pltpu.VMEM((heads, length, part), BF)] * 4
        + [
            pltpu.VMEM((part, length), BF),
            pltpu.VMEM((size, size), F32),
            pltpu.VMEM((size, part), F32),
            pltpu.VMEM((size, part), F32),
            pltpu.VMEM((part, length), F32),
        ],
        compiler_params=pltpu.CompilerParams(vmem_limit_bytes=56 * 1024 * 1024),
        name="attend_back",
    )(q, k, v, do, att, lse, ids.reshape(1, length), ids.reshape(length, 1))


class Later:
    def __init__(self, tasks):
        self.tasks = list(tasks)
        for task in self.tasks:
            next(task)

    def step(self, count=1):
        for _ in range(count):
            if not self.tasks:
                return
            task = self.tasks.pop(0)
            try:
                next(task)
                self.tasks.append(task)
            except StopIteration:
                pass

    def finish(self):
        while self.tasks:
            self.step()


def forward_kernel(heads, *refs):
    tok, wq4, vec, wo, f1, f2, idr, idc, lanes = refs[:9]
    act, q, k, v, att, lse, own, wq, rows_all, wide_all, wo_all, f1_all, f2_all = refs[9:22]
    tok_all, actv, vecs, km, vt, bias, top, low, acc, scb, send, recv, local = refs[22:]
    place = Place()
    z, y, x, c, s, dp = place.z, place.y, place.x, place.c, place.seq, place.dp
    group = NX * NC
    wire = Wire(place, send, recv)
    core, other, across = place.at(c=1 - c), place.at(x=1 - x), place.at(x=1 - x, c=1 - c)
    span, width = tok.shape
    rows = f1.shape[1]
    length, part = q.shape
    head = part // heads

    greet(place)
    quarter = []
    for dev, peer in ((core, s ^ 1), (other, s ^ 2), (across, s ^ 3)):
        quarter.append(wire.copy(wq4.at[peer], wq.at[dp, s], dev).go())
        quarter.append(wire.copy(vec, vecs.at[s], dev).go())
    tok_x = wire.copy(tok, tok_all.at[s], other).go()
    tok_c = wire.copy(tok, tok_all.at[s], core).go()
    f1_c = wire.copy(f1.at[1 - c], f1_all.at[z, y, x, pl.ds(c * rows, rows)], core).go()
    here = [
        pltpu.make_async_copy(wq4.at[s], wq.at[dp, s], local.at[0]),
        pltpu.make_async_copy(vec, vecs.at[s], local.at[1]),
        pltpu.make_async_copy(tok, tok_all.at[s], local.at[2]),
        pltpu.make_async_copy(wo, wo_all.at[z, y, x, c], local.at[3]),
        pltpu.make_async_copy(f1.at[c], f1_all.at[z, y, x, pl.ds(c * rows, rows)], local.at[4]),
        pltpu.make_async_copy(f2, f2_all.at[z, y, x], local.at[5]),
    ]
    for desc in here:
        desc.start()
    for desc in here:
        desc.wait()
    for desc in quarter:
        desc.wait_recv()

    lane = vec.shape[2]
    blk = pl.multiple_of(dp * lane, lane)
    wide_blk = pl.multiple_of(dp * lane * group, lane * group)
    rows_all[:, pl.ds(blk, lane)] = (vecs[0, 0] + vecs[1, 0]) + (vecs[2, 0] + vecs[3, 0])
    for j in range(group):
        wide_all[:, pl.ds(pl.multiple_of(wide_blk + j * lane, lane), lane)] = vecs[j, 1]

    def by_dp(view):
        mine = view(dp)
        along_z = [wire.copy(mine, mine, place.at(z=place.zup(n))) for n in range(1, NZ)]
        got = [view(((z - n + NZ) % NZ) * NY + y) for n in range(1, NZ)]
        ys = [wire.copy(blk, blk, place.at(y=1 - y)) for blk in [mine] + got]
        yield
        for desc in along_z + ys[:1]:
            desc.go()
        yield
        for n in range(1, NZ):
            along_z[n - 1].wait_recv()
            ys[n].go()
        yield
        for desc in ys:
            desc.wait_recv()

    first = Later(
        [
            by_dp(lambda d: wq.at[d]),
            by_dp(lambda d: rows_all.at[:, pl.ds(pl.multiple_of(d * lane, lane), lane)]),
            by_dp(lambda d: wide_all.at[:, pl.ds(pl.multiple_of(d * lane * group, lane * group), lane * group)]),
        ]
    )
    first.step(3)
    half1 = f1_all.shape[4] // 2
    half2 = f2_all.shape[3] // 2
    plane = wo_all.at[:, :, :, c]

    def outer():
        last = wire.copy(plane, plane, core)
        yield from spread_zxy(wire, place, plane)
        last.go()
        yield
        last.wait_recv()

    f1_c.wait_recv()
    later = Later(
        [
            spread_zxy(wire, place, f1_all.at[:, :, :, :, pl.ds(0, half1)]),
            spread_xzy(wire, place, f1_all.at[:, :, :, :, pl.ds(half1, half1)], swap=True),
            outer(),
            spread_zxy(wire, place, f2_all.at[:, :, :, pl.ds(0, half2)]),
            spread_xzy(wire, place, f2_all.at[:, :, :, pl.ds(half2, half2)]),
        ]
    )
    first.step(3)
    tok_c.wait_recv()
    tok_x.wait_recv()
    blk = tok_all.at[s ^ 2]
    tok_last = wire.copy(blk, blk, core).go()
    first.finish()
    later.step(5)

    shift = pl.multiple_of(s * part, part)
    bias_q = rows_all[2:3, pl.ds(shift, part)].astype(F32)
    bias_v = rows_all[3:4, pl.ds(shift, part)].astype(F32)
    gain, base = rows_all[0:1, :].astype(F32), rows_all[1:2, :].astype(F32)
    keep = []
    for m in range(group):
        j = s ^ m
        if m == 3:
            tok_last.wait_recv()
        if m >= 2:
            keep[m - 2].wait()
        slot = actv.at[m % 2]
        step = 64

        def norm_rows(n, _, slot=slot, j=j):
            at = pl.ds(pl.multiple_of(n * step, step), step)
            values = tok_all[j, at, :].astype(F32)
            slot[at, :] = (normalize(values)[0] * gain + base).astype(BF)
            return 0

        lax.fori_loop(0, span // step, norm_rows, 0)
        at = pl.ds(pl.multiple_of(j * span, span), span)
        desc = pltpu.make_async_copy(slot, act.at[at], local.at[6 + m])
        desc.start()
        keep.append(desc)
        for n, (dst, add) in enumerate(((q, bias_q), (k, None), (v, bias_v))):
            weights = wq[:, :, :, n * part : (n + 1) * part].reshape(width, part)
            proj = nn(slot[...], weights)
            if add is not None:
                proj = proj + add
            if n == 0:
                proj = proj * (head**-0.5)
            dst[at, :] = proj.astype(BF)
        later.step(2)

    mask_heads(km, k, heads, head)
    vt[...] = v[...].T
    blocks = length // span
    returns = []
    for qb in reversed(range(blocks)):
        qs = slice(qb * span, (qb + 1) * span)
        top[...] = jnp.full(top.shape, NEGATIVE, F32)
        low[...] = jnp.zeros(low.shape, F32)
        acc[...] = jnp.zeros(acc.shape, F32)

        def keys(step, _, qb=qb, qs=qs):
            kb = qb - step
            ks = pl.ds(pl.multiple_of(kb * span, span), span)
            bias[...] = pair_bias(idr, idc, qb, kb, span)
            for h in range(heads):
                scores = nt(km[h, ks, :], q[qs, :]) + bias[...]
                old = top[h : h + 1, :]
                new = jnp.maximum(old, jnp.max(scores, 0, keepdims=True))
                probs = jnp.exp(scores - new)
                shrink = jnp.exp(old - new)
                top[h : h + 1, :] = new
                low[h : h + 1, :] = low[h : h + 1, :] * shrink + jnp.sum(probs, 0, keepdims=True)
                hs = slice(h * head, (h + 1) * head)
                acc[hs, :] = acc[hs, :] * shrink + nn(vt[hs, ks], probs.astype(BF))
            for n in range(qb + 1):

                @pl.when(step == n)
                def _():
                    later.step(3)

            return 0

        lax.fori_loop(0, qb + 1, keys, 0)
        for h in range(heads):
            hs = slice(h * head, (h + 1) * head)
            acc[hs, :] = acc[hs, :] * (1.0 / low[h : h + 1, :])
        att[:, qs] = acc[...]
        lse[:, qs] = top[...] + jnp.log(low[...])
        scb[qb] = (acc[...].T * lanes[...]).astype(BF)
        view = own.at[:, pl.ds(shift, part)]
        back = pltpu.make_async_remote_copy(
            src_ref=scb.at[qb],
            dst_ref=view,
            send_sem=send.at[COPIES - 1 - qb],
            recv_sem=recv.at[COPIES - 4 + (s ^ qb)],
            device_id=(dp, qb),
            device_id_type=MESH,
        )
        mine = pltpu.make_async_copy(scb.at[qb], view, local.at[10])
        returns.append((qb, back, mine))

        @pl.when(s == qb)
        def _():
            mine.start()

        @pl.when(s != qb)
        def _():
            back.start()

    later.finish()
    for desc in keep[-2:]:
        desc.wait()
    for qb, back, mine in returns:

        @pl.when(s == qb)
        def _():
            mine.wait()

        @pl.when(s != qb)
        def _():
            back.wait_send()

    for m in range(1, group):
        view = own.at[:, pl.ds(pl.multiple_of((s ^ m) * part, part), part)]
        pltpu.make_async_remote_copy(
            src_ref=scb.at[0],
            dst_ref=view,
            send_sem=send.at[COPIES - 1],
            recv_sem=recv.at[COPIES - 4 + m],
            device_id=core,
            device_id_type=MESH,
        ).wait_recv()
    wire.drain()


def forward(tok, wq4, vec, wo, f1, f2, ids, lanes, heads):
    span, width = tok.shape
    group, rows, triple = wq4.shape
    part = triple // 3
    length = span * group
    dps = NZ * NY
    lane = vec.shape[2]
    out = (
        (HBM, (length, width), BF),
        (VM, (length, part), BF),
        (VM, (length, part), BF),
        (VM, (length, part), BF),
        (VM, (part, length), F32),
        (VM, (8, length), F32),
        (VM, (span, width), BF),
        (VM, (dps, group, rows, triple), BF),
        (VM, (16, dps * lane), BF),
        (VM, (16, dps * group * lane), BF),
        (HBM, (NZ, NY, NX, NC) + wo.shape, BF),
        (HBM, (NZ, NY, NX, NC * f1.shape[1], f1.shape[2]), BF),
        (HBM, (NZ, NY, NX) + f2.shape, BF),
    )
    return pl.pallas_call(
        functools.partial(forward_kernel, heads),
        out_shape=tuple(jax.ShapeDtypeStruct(shape, dtype) for _, shape, dtype in out),
        in_specs=[VM] * 9,
        out_specs=[spec for spec, _, _ in out],
        scratch_shapes=[
            pltpu.VMEM((group, span, width), BF),
            pltpu.VMEM((2, span, width), BF),
            pltpu.VMEM((group,) + vec.shape, BF),
            pltpu.VMEM((heads, length, part), BF),
            pltpu.VMEM((part, length), BF),
            pltpu.VMEM((span, span), F32),
            pltpu.VMEM((8, span), F32),
            pltpu.VMEM((8, span), F32),
            pltpu.VMEM((part, span), F32),
            pltpu.VMEM((group, span, part), BF),
            pltpu.SemaphoreType.DMA((COPIES,)),
            pltpu.SemaphoreType.DMA((COPIES,)),
            pltpu.SemaphoreType.DMA((12,)),
        ],
        compiler_params=pltpu.CompilerParams(
            collective_id=1, has_side_effects=True, vmem_limit_bytes=56 * 1024 * 1024
        ),
        name="forward_row",
    )(tok, wq4, vec, wo, f1, f2, ids.reshape(1, length), ids.reshape(length, 1), lanes)


def trade(v, mask, perm_seq):
    pairs = [(d * perm_seq + s, d * perm_seq + (s ^ mask)) for d in range(NZ * NY) for s in range(perm_seq)]
    return lax.ppermute(v, ("dp", "seq"), pairs)


def fast(tokens, doc_ids, cotangent, w_qkv, w_out, attn_vecs, head_scale, w_fc1, w_fc2, ffn_vecs, ffn_wide):
    _, span, width = tokens.shape
    group = NX * NC
    length = span * group
    head_count = head_scale.shape[0]
    head = width // head_count
    heads = head_count // group
    part = heads * head
    seq = lax.axis_index("seq")
    core = seq % NC
    chips = NZ * NY * NX
    owners = chips * NC
    block = w_fc2.shape[0]
    units = chips * block
    swap = functools.partial(trade, perm_seq=group)
    shift = part * seq

    rows = w_qkv.shape[0]
    wq4 = w_qkv.astype(BF).reshape(rows, 3, group, part).transpose(2, 0, 1, 3).reshape(group, rows, 3 * part)
    f1 = w_fc1.astype(BF).reshape(rows, chips, NC, block).transpose(2, 0, 1, 3).reshape(NC, rows, units)
    a_len, f_len, w_len = attn_vecs.size, ffn_vecs.size, ffn_wide.size
    narrow = jnp.concatenate([attn_vecs, ffn_vecs], 0).astype(BF)
    count, each = narrow.shape
    lane = each * group
    narrow = lax.dynamic_update_slice(jnp.zeros((16, lane), BF), narrow, (0, seq * each))
    vec = jnp.stack([narrow, jnp.pad(ffn_wide.astype(BF), ((0, 16 - ffn_wide.shape[0]), (0, 0)))])
    tok = tokens.reshape(span, width)
    scale_own = lax.dynamic_slice_in_dim(head_scale, heads * seq, heads)
    scale_lanes = jnp.repeat(scale_own, head).reshape(1, part)
    ids = doc_ids.reshape(length)
    size = span
    act_one, q, k, v, att, lse, scaled_own, wq, rows_all, wide_all, wo, fc1, fc2 = forward(
        tok, wq4, vec, w_out.astype(BF), f1, w_fc2.astype(BF), ids, scale_lanes, heads
    )
    wq = wq.reshape(width, 3 * part)
    wo = wo.reshape(width, width)
    fc1 = fc1.reshape(width, units)
    fc2 = fc2.reshape(units, width)
    attn_rows = rows_all[: attn_vecs.shape[0]].astype(F32)
    ffn_rows = rows_all[attn_vecs.shape[0] : count].astype(F32)
    wide = wide_all[: ffn_wide.shape[0]].astype(F32).reshape(3, chips, NC, block)
    wide = lax.dynamic_index_in_dim(wide, core, 2, keepdims=False).reshape(3, units)

    dtop = cotangent.reshape(span, width)
    dtop_pair = jnp.concatenate([dtop, swap(dtop, 1)], 0)

    def to_owners(blocks):
        return [lax.dynamic_index_in_dim(blocks, seq, 0, keepdims=False)] + [
            swap(lax.dynamic_index_in_dim(blocks, seq ^ m, 0, keepdims=False), m) for m in (1, 2, 3)
        ]

    inputs = tok.astype(F32)
    branch = jnp.dot(scaled_own, wo, preferred_element_type=F32) + attn_rows[4]
    normed_branch, inv_branch = normalize(branch)
    hidden = inputs + normed_branch * attn_rows[5] + attn_rows[6]
    normed_two, inv_two = normalize(hidden)
    act_two = (normed_two * ffn_rows[0] + ffn_rows[1]).astype(BF)

    act_pair = jnp.concatenate([act_two, swap(act_two, 1)], 0)

    def flip(stats):
        return jnp.concatenate([stats[span:], stats[:span]], 0)

    def both(stats):
        return stats + swap(flip(stats), 1)

    inner = jnp.dot(act_pair, fc1, preferred_element_type=F32) + wide[0]
    activated = gelu_exact(inner)
    total_units = units * NC
    centre = both(jnp.sum(activated, -1, keepdims=True)) / total_units
    centred = activated - centre
    inv_three = lax.rsqrt(both(jnp.sum(centred * centred, -1, keepdims=True)) / total_units + EPSILON)
    normed_three = centred * inv_three
    mixed = (normed_three * wide[1] + wide[2]).astype(BF)
    out_pair = jnp.dot(mixed, fc2, preferred_element_type=F32)
    result = hidden + ffn_rows[2] + (out_pair[:span] + swap(out_pair[span:], 1))
    outputs = result.astype(BF).reshape(1, span, width)

    grad_fc2 = left_grad(mixed, dtop_pair).astype(BF)
    grad_mixed = right_back(dtop_pair, fc2)
    gain_inner = jnp.sum(grad_mixed * normed_three, 0)
    bias_inner = jnp.sum(grad_mixed, 0)
    grad_norm = grad_mixed * wide[1]
    means = both(
        jnp.concatenate(
            [
                jnp.sum(grad_norm, -1, keepdims=True),
                jnp.sum(grad_norm * normed_three, -1, keepdims=True),
            ],
            1,
        )
    ) / total_units
    grad_activated = inv_three * (grad_norm - means[:, :1] - normed_three * means[:, 1:])
    grad_inner = (grad_activated * gelu_slope(inner)).astype(BF)
    grad_fc1 = left_grad(act_pair, grad_inner).astype(BF)
    bias_one = jnp.sum(grad_inner.astype(F32), 0)
    back_pair = right_back(grad_inner, fc1)
    grad_act_two = back_pair[:span] + swap(back_pair[span:], 1)
    top = dtop.astype(F32)
    gain_two = jnp.sum(grad_act_two * normed_two, 0)
    shift_two = jnp.sum(grad_act_two, 0)
    grad_hidden = top + norm_back(grad_act_two * ffn_rows[0], normed_two, inv_two)
    post_gain = jnp.sum(grad_hidden * normed_branch, 0)
    post_shift = jnp.sum(grad_hidden, 0)
    grad_branch = norm_back(grad_hidden * attn_rows[5], normed_branch, inv_branch).astype(BF)
    out_bias = jnp.sum(grad_branch.astype(F32), 0)
    grad_out = left_grad(scaled_own, grad_branch).astype(BF)
    grad_attended = (right_back(grad_branch, wo) * jnp.repeat(head_scale, head)).astype(BF)

    got = to_owners(grad_attended.reshape(span, group, part).transpose(1, 0, 2))
    do = jnp.zeros((length, part), BF)
    for m, piece in enumerate(got):
        do = lax.dynamic_update_slice_in_dim(do, piece, (seq ^ m) * span, 0)
    dq, dk, dv, delta = row_attend_back(q, k, v, do, att, lse, ids, heads, size)
    scale_part = jnp.sum(delta[:heads], 1) / scale_own
    grad_qkv = jnp.concatenate([dq, dk, dv], 1)
    grad_wq = left_grad(act_one, grad_qkv).astype(BF)
    query_bias = jnp.sum(dq.astype(F32), 0)
    value_bias = jnp.sum(dv.astype(F32), 0)
    da_all = right_back(grad_qkv, wq).astype(BF).reshape(group, span, width)
    mine = jnp.stack([lax.dynamic_index_in_dim(da_all, seq ^ m, 0, keepdims=False) for m in (0, 2)])
    give = jnp.stack([lax.dynamic_index_in_dim(da_all, seq ^ m, 0, keepdims=False) for m in (1, 3)])
    mine = mine.astype(F32) + swap(give, 1).astype(F32)
    grad_act_one = mine[0] + swap(mine[1].astype(BF), 2).astype(F32)
    normed_one, inv_one = normalize(inputs)
    gain_one = jnp.sum(grad_act_one * normed_one, 0)
    shift_one = jnp.sum(grad_act_one, 0)
    grad_tokens = (grad_hidden + norm_back(grad_act_one * attn_rows[0], normed_one, inv_one)).astype(BF)

    def widen(v, size, at):
        return lax.dynamic_update_slice_in_dim(jnp.zeros((size,), F32), v, at, 0)

    attn_grads = jnp.stack(
        [
            gain_one,
            shift_one,
            widen(query_bias, width, shift),
            widen(value_bias, width, shift),
            out_bias,
            post_gain,
            post_shift,
        ]
    )
    wide_grads = jnp.stack([bias_one, gain_inner, bias_inner]).reshape(3, chips, 1, block)
    is_core = (jnp.arange(NC) == core).astype(F32).reshape(1, 1, NC, 1)
    wide_grads = (wide_grads * is_core).reshape(3, NC * units)
    ffn_grads = jnp.stack([gain_two, shift_two, jnp.sum(top, 0)])
    scales = jnp.broadcast_to(widen(scale_part, head_count, heads * seq), (owners, head_count))

    def by_owner(g):
        return g.reshape(g.shape[0], owners, -1).transpose(1, 0, 2).reshape(owners, -1)

    packed = jnp.concatenate([by_owner(attn_grads), by_owner(ffn_grads), by_owner(wide_grads), scales], 1)
    packed = jnp.pad(packed, ((0, 0), (0, 8 * 128 - packed.shape[1]))).reshape(NZ, NY, NX, NC, 8, 128)
    o1, o2, oo, oq, ov = reduce_all(
        grad_fc1.reshape(NZ, NY, NX, NC * rows, units),
        grad_fc2.reshape(NZ, NY, NX, block, width),
        grad_out.reshape(NZ, NY, NX, NC, rows, width),
        grad_wq.reshape(NZ, NY, group, rows, 3 * part),
        packed,
    )
    grad_w1 = o1.reshape(NC, rows, chips, block).transpose(1, 2, 0, 3).reshape(rows, NC * units)
    grad_wqkv = oq.astype(F32).reshape(group, rows, 3, part).transpose(1, 2, 0, 3).reshape(rows, 3 * width)
    flat = ov.reshape(-1)
    end = a_len + f_len + w_len
    return (
        outputs,
        grad_tokens.reshape(1, span, width),
        grad_wqkv,
        oo,
        flat[:a_len].reshape(attn_vecs.shape),
        flat[end : end + head_count],
        grad_w1,
        o2,
        flat[a_len : a_len + f_len].reshape(ffn_vecs.shape),
        flat[a_len + f_len : end].reshape(ffn_wide.shape),
    )


def gelu_slope(u):
    return 0.5 * (1.0 + jax.scipy.special.erf(u * math.sqrt(0.5))) + u * jnp.exp(-0.5 * u * u) * (
        1.0 / math.sqrt(2.0 * math.pi)
    )


def solution(mesh):
    placed = (
        P("dp", "seq", None),
        P("dp", None),
        P("dp", "seq", None),
        P(("dp", "seq"), None),
        P(("dp", "seq"), None),
        P(None, ("dp", "seq")),
        P(),
        P(("dp", "seq"), None),
        P(("dp", "seq"), None),
        P(None, ("dp", "seq")),
        P(None, ("dp", "seq")),
    )
    results = (
        P("dp", "seq", None),
        P("dp", "seq", None),
        P(("dp", "seq"), None),
        P(("dp", "seq"), None),
        P(None, ("dp", "seq")),
        P(),
        P(("dp", "seq"), None),
        P(("dp", "seq"), None),
        P(None, ("dp", "seq")),
        P(None, ("dp", "seq")),
    )
    suits = mesh.shape["dp"] == NZ * NY and mesh.shape["seq"] == NX * NC
    return jax.shard_map(
        fast if suits else local, mesh=mesh, in_specs=placed, out_specs=results, check_vma=False
    )
```

```python
import functools
import math

import jax
import jax.numpy as jnp
from jax import lax
from jax.experimental import pallas as pl
from jax.experimental.pallas import tpu as pltpu
from jax.sharding import PartitionSpec as P

EPSILON = 1e-05
NEGATIVE = -1e30
MESH = pl.DeviceIdType.MESH
BF = jnp.bfloat16
F32 = jnp.float32
NZ, NY, NX, NC = 4, 2, 2, 2
HBM = pl.BlockSpec(memory_space=pl.ANY)
VM = pl.BlockSpec(memory_space=pltpu.VMEM)


def normalize(values):
    centre = jnp.mean(values, -1, keepdims=True)
    centred = values - centre
    scale_inv = lax.rsqrt(jnp.mean(centred * centred, -1, keepdims=True) + EPSILON)
    return (centred * scale_inv, scale_inv)


def norm_back(grad_normed, normed, scale_inv):
    return scale_inv * (
        grad_normed
        - jnp.mean(grad_normed, -1, keepdims=True)
        - normed * jnp.mean(grad_normed * normed, -1, keepdims=True)
    )


def gelu_exact(values):
    return 0.5 * values * (1.0 + jax.scipy.special.erf(values * math.sqrt(0.5)))


def left_grad(activations, gradients):
    return lax.dot_general(
        activations, gradients, (((0,), (0,)), ((), ())), preferred_element_type=jnp.float32
    )


def right_back(gradients, matrix):
    return lax.dot_general(
        gradients, matrix, (((1,), (1,)), ((), ())), preferred_element_type=jnp.float32
    )


def masked_scores(queries, keys_block, query_pos, key_pos, query_ids, key_ids):
    raw_scores = jnp.einsum(
        "rqhe,rkhe->rhqk", queries, keys_block, preferred_element_type=jnp.float32
    )
    allowed = (key_pos[None, None, :] <= query_pos[None, :, None]) & (
        key_ids[:, None, :] == query_ids[:, :, None]
    )
    return jnp.where(allowed[:, None], raw_scores * queries.shape[3] ** (-0.5), NEGATIVE)


def attend(queries, keys_all, values_all, query_pos, query_ids, doc_rows, block_len):
    block_count = keys_all.shape[1] // block_len
    stat_shape = (queries.shape[0], queries.shape[2], queries.shape[1])

    def slice_block(block_index):
        start = block_index * block_len
        keys_block = lax.dynamic_slice_in_dim(keys_all, start, block_len, 1)
        values_block = lax.dynamic_slice_in_dim(values_all, start, block_len, 1)
        key_ids = lax.dynamic_slice_in_dim(doc_rows, start, block_len, 1)
        key_pos = start + jnp.arange(block_len, dtype=jnp.int32)
        return (
            values_block,
            masked_scores(queries, keys_block, query_pos, key_pos, query_ids, key_ids),
        )

    def first_pass(carry, block_index):
        running_max, running_sum = carry
        _, scores = slice_block(block_index)
        new_max = jnp.maximum(running_max, jnp.max(scores, -1))
        running_sum = running_sum * jnp.exp(running_max - new_max) + jnp.sum(
            jnp.exp(scores - new_max[..., None]), -1
        )
        return ((new_max, running_sum), None)

    start_stats = (jnp.full(stat_shape, NEGATIVE, jnp.float32), jnp.zeros(stat_shape, jnp.float32))
    (row_max, row_sum), _ = lax.scan(
        first_pass, start_stats, jnp.arange(block_count, dtype=jnp.int32)
    )
    log_total = row_max + jnp.log(row_sum)

    def second_pass(total_out, block_index):
        values_block, scores = slice_block(block_index)
        probs = jnp.exp(scores - log_total[..., None]).astype(jnp.bfloat16)
        return (
            total_out
            + jnp.einsum(
                "rhqk,rkhe->rqhe", probs, values_block, preferred_element_type=jnp.float32
            ),
            None,
        )

    attended, _ = lax.scan(
        second_pass, jnp.zeros(queries.shape, jnp.float32), jnp.arange(block_count, dtype=jnp.int32)
    )
    return (attended, log_total)


def attend_back(
    queries,
    keys_all,
    values_all,
    grad_out,
    log_total,
    delta,
    query_pos,
    query_ids,
    doc_rows,
    block_len,
):
    block_count = keys_all.shape[1] // block_len
    scale = queries.shape[3] ** (-0.5)

    def step(grad_queries, block_index):
        start = block_index * block_len
        keys_block = lax.dynamic_slice_in_dim(keys_all, start, block_len, 1)
        values_block = lax.dynamic_slice_in_dim(values_all, start, block_len, 1)
        key_ids = lax.dynamic_slice_in_dim(doc_rows, start, block_len, 1)
        key_pos = start + jnp.arange(block_len, dtype=jnp.int32)
        scores = masked_scores(queries, keys_block, query_pos, key_pos, query_ids, key_ids)
        probs = jnp.exp(scores - log_total[..., None])
        grad_probs = jnp.einsum(
            "rqhe,rkhe->rhqk", grad_out, values_block, preferred_element_type=jnp.float32
        )
        grad_scores = (probs * (grad_probs - delta[..., None]) * scale).astype(jnp.bfloat16)
        grad_queries = grad_queries + jnp.einsum(
            "rhqk,rkhe->rqhe", grad_scores, keys_block, preferred_element_type=jnp.float32
        )
        grad_keys = jnp.einsum(
            "rhqk,rqhe->rkhe", grad_scores, queries, preferred_element_type=jnp.float32
        )
        grad_values = jnp.einsum(
            "rhqk,rqhe->rkhe",
            probs.astype(jnp.bfloat16),
            grad_out,
            preferred_element_type=jnp.float32,
        )
        return (grad_queries, (grad_keys, grad_values))

    return lax.scan(
        step, jnp.zeros(queries.shape, jnp.float32), jnp.arange(block_count, dtype=jnp.int32)
    )


def local(
    tokens,
    doc_ids,
    cotangent,
    w_qkv,
    w_out,
    attn_vecs,
    head_scale,
    w_fc1,
    w_fc2,
    ffn_vecs,
    ffn_wide,
):
    row_count, span_len, model_width = tokens.shape
    head_count = head_scale.shape[0]
    head_size = model_width // head_count
    token_count = row_count * span_len
    brain = jnp.bfloat16
    single = jnp.float32
    gathered_qkv, gathered_out, attn_rows = (
        lax.all_gather(w_qkv.astype(brain), ("dp", "seq"), axis=0, tiled=True),
        lax.all_gather(w_out.astype(brain), ("dp", "seq"), axis=0, tiled=True),
        lax.all_gather(attn_vecs.astype(brain), ("dp", "seq"), axis=1, tiled=True),
    )
    attn_rows = attn_rows.astype(single)
    inputs = tokens.astype(single).reshape(token_count, model_width)
    normed_one, inv_one = normalize(inputs)
    act_one = (normed_one * attn_rows[0] + attn_rows[1]).astype(brain)
    projected = jnp.dot(act_one, gathered_qkv, preferred_element_type=single)
    queries = (projected[:, :model_width] + attn_rows[2]).astype(brain)
    keys_own = projected[:, model_width : 2 * model_width].astype(brain)
    values_own = (projected[:, 2 * model_width :] + attn_rows[3]).astype(brain)
    keys_all, values_all = (
        lax.all_gather(
            keys_own.reshape(row_count, span_len, model_width), "seq", axis=1, tiled=True
        ),
        lax.all_gather(
            values_own.reshape(row_count, span_len, model_width), "seq", axis=1, tiled=True
        ),
    )
    offset = lax.axis_index("seq") * span_len
    query_pos = offset + jnp.arange(span_len, dtype=jnp.int32)
    query_ids = lax.dynamic_slice_in_dim(doc_ids, offset, span_len, 1)
    queries_four = queries.reshape(row_count, span_len, head_count, head_size)
    keys_four = keys_all.reshape(row_count, -1, head_count, head_size)
    values_four = values_all.reshape(row_count, -1, head_count, head_size)
    attended, log_total = attend(
        queries_four, keys_four, values_four, query_pos, query_ids, doc_ids, span_len
    )
    scaled = (
        (attended * head_scale[None, None, :, None]).reshape(token_count, model_width).astype(brain)
    )
    branch = jnp.dot(scaled, gathered_out, preferred_element_type=single) + attn_rows[4]
    normed_branch, inv_branch = normalize(branch)
    hidden = inputs + normed_branch * attn_rows[5] + attn_rows[6]
    gathered_fc1, gathered_fc2, ffn_rows, wide_rows = (
        lax.all_gather(w_fc1.astype(brain), ("dp", "seq"), axis=0, tiled=True),
        lax.all_gather(w_fc2.astype(brain), ("dp", "seq"), axis=0, tiled=True),
        lax.all_gather(ffn_vecs.astype(brain), ("dp", "seq"), axis=1, tiled=True),
        lax.all_gather(ffn_wide.astype(brain), ("dp", "seq"), axis=1, tiled=True),
    )
    ffn_rows = ffn_rows.astype(single)
    wide_rows = wide_rows.astype(single)
    normed_two, inv_two = normalize(hidden)
    act_two = (normed_two * ffn_rows[0] + ffn_rows[1]).astype(brain)
    inner_act = jnp.dot(act_two, gathered_fc1, preferred_element_type=single) + wide_rows[0]
    activated, gelu_pull = jax.vjp(gelu_exact, inner_act)
    normed_three, inv_three = normalize(activated)
    mixed_act = (normed_three * wide_rows[1] + wide_rows[2]).astype(brain)
    result = hidden + jnp.dot(mixed_act, gathered_fc2, preferred_element_type=single) + ffn_rows[2]
    outputs = result.astype(brain).reshape(row_count, span_len, model_width)
    back_set = (
        lax.all_gather(w_qkv.astype(brain), ("dp", "seq"), axis=0, tiled=True),
        lax.all_gather(w_out.astype(brain), ("dp", "seq"), axis=0, tiled=True),
        lax.all_gather(attn_vecs.astype(brain), ("dp", "seq"), axis=1, tiled=True),
        lax.all_gather(w_fc1.astype(brain), ("dp", "seq"), axis=0, tiled=True),
        lax.all_gather(w_fc2.astype(brain), ("dp", "seq"), axis=0, tiled=True),
        lax.all_gather(ffn_vecs.astype(brain), ("dp", "seq"), axis=1, tiled=True),
        lax.all_gather(ffn_wide.astype(brain), ("dp", "seq"), axis=1, tiled=True),
    )
    gathered_qkv, gathered_out, attn_back, gathered_fc1, gathered_fc2, ffn_back, wide_back = (
        back_set
    )
    attn_rows = attn_back.astype(single)
    ffn_rows = ffn_back.astype(single)
    wide_rows = wide_back.astype(single)
    grad_top = cotangent.astype(single).reshape(token_count, model_width)
    grad_branch_two = grad_top.astype(brain)
    grad_fc2 = left_grad(mixed_act, grad_branch_two)
    grad_bias_two = jnp.sum(grad_branch_two.astype(single), 0)
    grad_mixed = right_back(grad_branch_two, gathered_fc2)
    grad_inner_gain = jnp.sum(grad_mixed * normed_three, 0)
    grad_inner_bias = jnp.sum(grad_mixed, 0)
    grad_activated = norm_back(grad_mixed * wide_rows[1], normed_three, inv_three)
    grad_inner = gelu_pull(grad_activated)[0].astype(brain)
    grad_fc1 = left_grad(act_two, grad_inner)
    grad_bias_one = jnp.sum(grad_inner.astype(single), 0)
    grad_act_two = right_back(grad_inner, gathered_fc1)
    grad_gain_two = jnp.sum(grad_act_two * normed_two, 0)
    grad_shift_two = jnp.sum(grad_act_two, 0)
    grad_hidden = grad_top + norm_back(grad_act_two * ffn_rows[0], normed_two, inv_two)
    ffn_sums = (
        lax.psum_scatter(grad_fc1, ("dp", "seq"), scatter_dimension=0, tiled=True),
        lax.psum_scatter(grad_fc2, ("dp", "seq"), scatter_dimension=0, tiled=True),
        lax.psum_scatter(
            jnp.stack([grad_gain_two, grad_shift_two, grad_bias_two]),
            ("dp", "seq"),
            scatter_dimension=1,
            tiled=True,
        ),
        lax.psum_scatter(
            jnp.stack([grad_bias_one, grad_inner_gain, grad_inner_bias]),
            ("dp", "seq"),
            scatter_dimension=1,
            tiled=True,
        ),
    )
    grad_post_gain = jnp.sum(grad_hidden * normed_branch, 0)
    grad_post_shift = jnp.sum(grad_hidden, 0)
    grad_branch = norm_back(grad_hidden * attn_rows[5], normed_branch, inv_branch).astype(brain)
    grad_out_bias = jnp.sum(grad_branch.astype(single), 0)
    grad_out = left_grad(scaled, grad_branch)
    grad_scaled = right_back(grad_branch, gathered_out).reshape(
        row_count, span_len, head_count, head_size
    )
    grad_scale = jnp.sum(grad_scaled * attended, (0, 1, 3))
    grad_attended = (grad_scaled * head_scale[None, None, :, None]).astype(brain)
    delta = jnp.transpose(jnp.sum(grad_attended.astype(single) * attended, -1), (0, 2, 1))
    grad_queries, key_parts = attend_back(
        queries_four,
        keys_four,
        values_four,
        grad_attended,
        log_total,
        delta,
        query_pos,
        query_ids,
        doc_ids,
        span_len,
    )
    partial_keys = jnp.transpose(key_parts[0], (1, 0, 2, 3, 4)).reshape(row_count, -1, model_width)
    partial_values = jnp.transpose(key_parts[1], (1, 0, 2, 3, 4)).reshape(
        row_count, -1, model_width
    )
    grad_keys, grad_values = (
        lax.psum_scatter(
            partial_keys.astype(jnp.bfloat16), "seq", scatter_dimension=1, tiled=True
        ).astype(jnp.float32),
        lax.psum_scatter(
            partial_values.astype(jnp.bfloat16), "seq", scatter_dimension=1, tiled=True
        ).astype(jnp.float32),
    )
    grad_qkv = jnp.concatenate(
        [
            grad_queries.reshape(token_count, model_width).astype(brain),
            grad_keys.reshape(token_count, model_width).astype(brain),
            grad_values.reshape(token_count, model_width).astype(brain),
        ],
        1,
    )
    grad_w_qkv = left_grad(act_one, grad_qkv)
    grad_query_bias = jnp.sum(grad_qkv[:, :model_width].astype(single), 0)
    grad_value_bias = jnp.sum(grad_qkv[:, 2 * model_width :].astype(single), 0)
    grad_act_one = right_back(grad_qkv, gathered_qkv)
    grad_gain_one = jnp.sum(grad_act_one * normed_one, 0)
    grad_shift_one = jnp.sum(grad_act_one, 0)
    grad_tokens = (
        (grad_hidden + norm_back(grad_act_one * attn_rows[0], normed_one, inv_one))
        .astype(brain)
        .reshape(row_count, span_len, model_width)
    )
    attn_stack = jnp.stack(
        [
            grad_gain_one,
            grad_shift_one,
            grad_query_bias,
            grad_value_bias,
            grad_out_bias,
            grad_post_gain,
            grad_post_shift,
        ]
    )
    attn_sums = (
        lax.psum_scatter(grad_w_qkv, ("dp", "seq"), scatter_dimension=0, tiled=True),
        lax.psum_scatter(grad_out, ("dp", "seq"), scatter_dimension=0, tiled=True),
        lax.psum_scatter(attn_stack, ("dp", "seq"), scatter_dimension=1, tiled=True),
    )
    scale_total = lax.psum(grad_scale, ("dp", "seq"))
    return (
        outputs,
        grad_tokens,
        attn_sums[0],
        attn_sums[1],
        attn_sums[2],
        scale_total,
        ffn_sums[0],
        ffn_sums[1],
        ffn_sums[2],
        ffn_sums[3],
    )


class Place:
    def __init__(self):
        self.dp = lax.axis_index("dp")
        self.seq = lax.axis_index("seq")
        self.z, self.y = self.dp // NY, self.dp % NY
        self.x, self.c = self.seq // NC, self.seq % NC

    def at(self, z=None, y=None, x=None, c=None):
        z = self.z if z is None else z
        y = self.y if y is None else y
        x = self.x if x is None else x
        c = self.c if c is None else c
        return (z * NY + y, x * NC + c)

    def zup(self, k):
        return (self.z + k) % NZ

    def group(self):
        near = [self.at(c=1 - self.c), self.at(x=1 - self.x), self.at(x=1 - self.x, c=1 - self.c)]
        return near + [self.at(y=1 - self.y)] + [self.at(z=self.zup(k)) for k in range(1, NZ)]


class Copy:
    def __init__(self, desc):
        self.desc, self.sent = desc, False

    def go(self):
        self.desc.start()
        return self

    def wait_recv(self):
        self.desc.wait_recv()

    def wait_send(self):
        if not self.sent:
            self.desc.wait_send()
        self.sent = True


class Wire:
    def __init__(self, place, send, recv):
        self.place, self.send, self.recv, self.used, self.open = place, send, recv, 0, []

    def copy(self, src, dst, dev):
        n = self.used
        self.used += 1
        copy = Copy(
            pltpu.make_async_remote_copy(
                src_ref=src,
                dst_ref=dst,
                send_sem=self.send.at[n],
                recv_sem=self.recv.at[n],
                device_id=dev,
                device_id_type=MESH,
            )
        )
        self.open.append(copy)
        return copy

    def drain(self):
        for copy in self.open:
            copy.wait_send()


def greet(place):
    barrier = pltpu.get_barrier_semaphore()
    group = place.group()
    for dev in group:
        pl.semaphore_signal(barrier, inc=1, device_id=dev, device_id_type=MESH)
    pl.semaphore_wait(barrier, len(group))


def spread_zxy(wire, place, ref, swap=False):
    z, y, x = place.z, place.y, place.x
    own = ref.at[z, y, x]
    first = place.at(y=1 - y) if swap else place.at(x=1 - x)
    second = place.at(x=1 - x) if swap else place.at(y=1 - y)
    order = [(z - k + NZ) % NZ for k in range(NZ)]
    along_z = [wire.copy(own, own, place.at(z=place.zup(k))) for k in range(1, NZ)]
    firsts = [wire.copy(ref.at[zk, y, x], ref.at[zk, y, x], first) for zk in order]
    twos = [ref.at[zk, :, x] if swap else ref.at[zk, y] for zk in order]
    seconds = [wire.copy(two, two, second) for two in twos]
    yield
    for copy in along_z + firsts[:1]:
        copy.go()
    yield
    for k in range(1, NZ):
        along_z[k - 1].wait_recv()
        firsts[k].go()
        yield
    for k in range(NZ):
        firsts[k].wait_recv()
        seconds[k].go()
        yield
    for copy in seconds:
        copy.wait_recv()


def spread_xzy(wire, place, ref, swap=False):
    z, y, x = place.z, place.y, place.x
    own = ref.at[z, y, x]
    first = place.at(y=1 - y) if swap else place.at(x=1 - x)
    second = place.at(x=1 - x) if swap else place.at(y=1 - y)
    order = [(z - k + NZ) % NZ for k in range(NZ)]
    twos = [ref.at[zk, :, x] if swap else ref.at[zk, y] for zk in order]
    start = wire.copy(own, own, first)
    steps = [wire.copy(two, two, place.at(z=place.zup(1))) for two in twos[:-1]]
    seconds = [wire.copy(two, two, second) for two in twos]
    yield
    start.go()
    yield
    start.wait_recv()
    steps[0].go()
    seconds[0].go()
    yield
    for k in range(1, NZ):
        steps[k - 1].wait_recv()
        if k < NZ - 1:
            steps[k].go()
        seconds[k].go()
        yield
    for copy in seconds:
        copy.wait_recv()


def spread_pair(wire, place, ref):
    plane = ref.at[:, :, :, place.c]
    last = wire.copy(plane, plane, place.at(c=1 - place.c))
    yield from spread_xzy(wire, place, plane)
    last.go()
    yield
    last.wait_recv()


def spread_dp(wire, place, views):
    z, y = place.z, place.y
    at = [z * NY + y] + [((z - n + NZ) % NZ) * NY + y for n in range(1, NZ)]
    along_z = [[wire.copy(view(at[0]), view(at[0]), place.at(z=place.zup(n))) for view in views] for n in range(1, NZ)]
    ys = [[wire.copy(view(d), view(d), place.at(y=1 - y)) for view in views] for d in at]
    yield
    for copies in along_z + ys[:1]:
        for copy in copies:
            copy.go()
    yield
    for n in range(1, NZ):
        for copy in along_z[n - 1]:
            copy.wait_recv()
        for copy in ys[n]:
            copy.go()
        yield
    for copies in ys:
        for copy in copies:
            copy.wait_recv()


def spread_row(wire, place, tok, tok_all):
    s, other, core = place.seq, place.at(x=1 - place.x), place.at(c=1 - place.c)
    far = tok_all.at[s ^ 2]
    tok_x = wire.copy(tok, tok_all.at[s], other)
    tok_c = wire.copy(tok, tok_all.at[s], core)
    last = wire.copy(far, far, core)
    yield
    tok_c.go()
    tok_x.go()
    yield
    tok_c.wait_recv()
    yield
    tok_x.wait_recv()
    last.go()
    yield
    last.wait_recv()


class Plan:
    def __init__(self, tasks, order):
        self.tasks, self.order = tasks, list(order)
        for task in tasks.values():
            next(task)

    def hook(self):
        for name in self.order.pop(0):
            next(self.tasks[name], None)

    def finish(self):
        while self.order:
            self.hook()
        for task in self.tasks.values():
            for _ in task:
                pass


COPIES = 104


def nt(a, b):
    return lax.dot_general(a, b, (((1,), (1,)), ((), ())), preferred_element_type=F32)


def nn(a, b):
    return lax.dot_general(a, b, (((1,), (0,)), ((), ())), preferred_element_type=F32)


def pair_bias(idr, key_ids, qb, kb, size):
    qs = pl.multiple_of(qb * size, size)
    key_pos = kb * size + lax.broadcasted_iota(jnp.int32, (size, size), 0)
    query_pos = qs + lax.broadcasted_iota(jnp.int32, (size, size), 1)
    same = key_ids == idr[:, pl.ds(qs, size)]
    return jnp.where((key_pos <= query_pos) & same, 0.0, NEGATIVE)


def mask_heads(dst, src, heads, head):
    lane = lax.broadcasted_iota(jnp.int32, src.shape, 1) // head
    whole = src[...]
    for h in range(heads):
        dst[h] = jnp.where(lane == h, whole, jnp.zeros_like(whole))


FORWARD = (
    "tqbaoboqqqddaaaaaabqtt",
    "",
    "tao",
    "d",
    "",
    "bo",
    "",
    "d",
    "",
    "a",
    "b",
    "o",
    "",
    "d",
    "",
    "",
    "obod",
)


def forward_tasks(wire, place, tok, tok_all, wq, rows_all, wide_all, lane, wo_all, f1_all, f2_all):
    group = NX * NC
    half1 = f1_all.shape[4] // 2
    views = [
        lambda d: wq.at[d],
        lambda d: rows_all.at[:, pl.ds(pl.multiple_of(d * lane, lane), lane)],
        lambda d: wide_all.at[:, pl.ds(pl.multiple_of(d * lane * group, lane * group), lane * group)],
    ]
    return {
        "t": spread_row(wire, place, tok, tok_all),
        "q": spread_dp(wire, place, views),
        "a": spread_zxy(wire, place, f1_all.at[:, :, :, :, pl.ds(0, half1)]),
        "b": spread_xzy(wire, place, f1_all.at[:, :, :, :, pl.ds(half1, half1)], swap=True),
        "o": spread_pair(wire, place, wo_all),
        "d": spread_xzy(wire, place, f2_all),
    }


def forward_kernel(heads, *refs):
    tok, wq4, vec, wo, f1, f2, idr, idc, lanes = refs[:9]
    act, q, k, v, att, lse, own, wq, rows_all, wide_all, wo_all, f1_all, f2_all = refs[9:22]
    tok_all, actv, vecs, km, vt, bias, top, low, acc, scb, send, recv, local = refs[22:]
    place = Place()
    z, y, x, c, s, dp = place.z, place.y, place.x, place.c, place.seq, place.dp
    group = NX * NC
    wire = Wire(place, send, recv)
    core, other, across = place.at(c=1 - c), place.at(x=1 - x), place.at(x=1 - x, c=1 - c)
    span, width = tok.shape
    rows = f1.shape[1]
    length, part = q.shape
    head = part // heads

    greet(place)
    quarter = []
    for dev, peer in ((core, s ^ 1), (other, s ^ 2), (across, s ^ 3)):
        quarter.append(wire.copy(wq4.at[peer], wq.at[dp, s], dev).go())
        quarter.append(wire.copy(vec, vecs.at[s], dev).go())
    f1_c = wire.copy(f1.at[1 - c], f1_all.at[z, y, x, pl.ds(c * rows, rows)], core).go()
    here = [
        pltpu.make_async_copy(wq4.at[s], wq.at[dp, s], local.at[0]),
        pltpu.make_async_copy(vec, vecs.at[s], local.at[1]),
        pltpu.make_async_copy(tok, tok_all.at[s], local.at[2]),
        pltpu.make_async_copy(wo, wo_all.at[z, y, x, c], local.at[3]),
        pltpu.make_async_copy(f1.at[c], f1_all.at[z, y, x, pl.ds(c * rows, rows)], local.at[4]),
        pltpu.make_async_copy(f2, f2_all.at[z, y, x], local.at[5]),
    ]
    for desc in here:
        desc.start()
    for desc in here:
        desc.wait()
    for desc in quarter:
        desc.wait_recv()

    lane = vec.shape[2]
    blk = pl.multiple_of(dp * lane, lane)
    wide_blk = pl.multiple_of(dp * lane * group, lane * group)
    rows_all[:, pl.ds(blk, lane)] = (vecs[0, 0] + vecs[1, 0]) + (vecs[2, 0] + vecs[3, 0])
    for j in range(group):
        wide_all[:, pl.ds(pl.multiple_of(wide_blk + j * lane, lane), lane)] = vecs[j, 1]

    f1_c.wait_recv()
    plan = Plan(
        forward_tasks(wire, place, tok, tok_all, wq, rows_all, wide_all, lane, wo_all, f1_all, f2_all), FORWARD
    )
    plan.hook()

    shift = pl.multiple_of(s * part, part)
    bias_q = rows_all[2:3, pl.ds(shift, part)].astype(F32)
    bias_v = rows_all[3:4, pl.ds(shift, part)].astype(F32)
    gain, base = rows_all[0:1, :].astype(F32), rows_all[1:2, :].astype(F32)
    keep = []
    for m in range(group):
        j = s ^ m
        plan.hook()
        if m >= 2:
            keep[m - 2].wait()
        slot = actv.at[m % 2]
        step = 64

        def norm_rows(n, _, slot=slot, j=j):
            at = pl.ds(pl.multiple_of(n * step, step), step)
            values = tok_all[j, at, :].astype(F32)
            slot[at, :] = (normalize(values)[0] * gain + base).astype(BF)
            return 0

        lax.fori_loop(0, span // step, norm_rows, 0)
        at = pl.ds(pl.multiple_of(j * span, span), span)
        desc = pltpu.make_async_copy(slot, act.at[at], local.at[6 + m])
        desc.start()
        keep.append(desc)
        for n, (dst, add) in enumerate(((q, bias_q), (k, None), (v, bias_v))):
            weights = wq[:, :, :, n * part : (n + 1) * part].reshape(width, part)
            proj = nn(slot[...], weights)
            if add is not None:
                proj = proj + add
            if n == 0:
                proj = proj * (head**-0.5)
            dst[at, :] = proj.astype(BF)

    plan.hook()
    mask_heads(km, k, heads, head)
    vt[...] = v[...].T
    blocks = length // span
    returns = []
    for qb in reversed(range(blocks)):
        qs = slice(qb * span, (qb + 1) * span)
        top[...] = jnp.full(top.shape, NEGATIVE, F32)
        low[...] = jnp.zeros(low.shape, F32)
        acc[...] = jnp.zeros(acc.shape, F32)

        def keys(step, _, qb=qb, qs=qs):
            kb = qb - step
            ks = pl.ds(pl.multiple_of(kb * span, span), span)
            bias[...] = pair_bias(idr, idc[ks, :], qb, kb, span)
            for h in range(heads):
                scores = nt(km[h, ks, :], q[qs, :]) + bias[...]
                old = top[h : h + 1, :]
                new = jnp.maximum(old, jnp.max(scores, 0, keepdims=True))
                probs = jnp.exp(scores - new)
                shrink = jnp.exp(old - new)
                top[h : h + 1, :] = new
                low[h : h + 1, :] = low[h : h + 1, :] * shrink + jnp.sum(probs, 0, keepdims=True)
                hs = slice(h * head, (h + 1) * head)
                acc[hs, :] = acc[hs, :] * shrink + nn(vt[hs, ks], probs.astype(BF))
            for n in range(qb + 1):

                @pl.when(step == n)
                def _():
                    plan.hook()

            return 0

        lax.fori_loop(0, qb + 1, keys, 0)
        for h in range(heads):
            hs = slice(h * head, (h + 1) * head)
            acc[hs, :] = acc[hs, :] * (1.0 / low[h : h + 1, :])
        att[:, qs] = acc[...]
        lse[:, qs] = top[...] + jnp.log(low[...])
        scb[qb] = (acc[...].T * lanes[...]).astype(BF)
        view = own.at[:, pl.ds(shift, part)]
        back = pltpu.make_async_remote_copy(
            src_ref=scb.at[qb],
            dst_ref=view,
            send_sem=send.at[COPIES - 1 - qb],
            recv_sem=recv.at[COPIES - 4 + (s ^ qb)],
            device_id=(dp, qb),
            device_id_type=MESH,
        )
        mine = pltpu.make_async_copy(scb.at[qb], view, local.at[10])
        returns.append((qb, back, mine))

        @pl.when(s == qb)
        def _():
            mine.start()

        @pl.when(s != qb)
        def _():
            back.start()

    plan.finish()
    for desc in keep[-2:]:
        desc.wait()
    for qb, back, mine in returns:

        @pl.when(s == qb)
        def _():
            mine.wait()

        @pl.when(s != qb)
        def _():
            back.wait_send()

    for m in range(1, group):
        view = own.at[:, pl.ds(pl.multiple_of((s ^ m) * part, part), part)]
        pltpu.make_async_remote_copy(
            src_ref=scb.at[0],
            dst_ref=view,
            send_sem=send.at[COPIES - 1],
            recv_sem=recv.at[COPIES - 4 + m],
            device_id=core,
            device_id_type=MESH,
        ).wait_recv()
    wire.drain()


def forward(tok, wq4, vec, wo, f1, f2, ids, lanes, heads):
    span, width = tok.shape
    group, rows, triple = wq4.shape
    part = triple // 3
    length = span * group
    dps = NZ * NY
    lane = vec.shape[2]
    out = (
        (HBM, (length, width), BF),
        (VM, (length, part), BF),
        (VM, (length, part), BF),
        (VM, (length, part), BF),
        (VM, (part, length), F32),
        (VM, (8, length), F32),
        (VM, (span, width), BF),
        (VM, (dps, group, rows, triple), BF),
        (VM, (16, dps * lane), BF),
        (VM, (16, dps * group * lane), BF),
        (HBM, (NZ, NY, NX, NC) + wo.shape, BF),
        (HBM, (NZ, NY, NX, NC * f1.shape[1], f1.shape[2]), BF),
        (HBM, (NZ, NY, NX) + f2.shape, BF),
    )
    return pl.pallas_call(
        functools.partial(forward_kernel, heads),
        out_shape=tuple(jax.ShapeDtypeStruct(shape, dtype) for _, shape, dtype in out),
        in_specs=[VM] * 9,
        out_specs=[spec for spec, _, _ in out],
        scratch_shapes=[
            pltpu.VMEM((group, span, width), BF),
            pltpu.VMEM((2, span, width), BF),
            pltpu.VMEM((group,) + vec.shape, BF),
            pltpu.VMEM((heads, length, part), BF),
            pltpu.VMEM((part, length), BF),
            pltpu.VMEM((span, span), F32),
            pltpu.VMEM((8, span), F32),
            pltpu.VMEM((8, span), F32),
            pltpu.VMEM((part, span), F32),
            pltpu.VMEM((group, span, part), BF),
            pltpu.SemaphoreType.DMA((COPIES,)),
            pltpu.SemaphoreType.DMA((COPIES,)),
            pltpu.SemaphoreType.DMA((12,)),
        ],
        compiler_params=pltpu.CompilerParams(
            collective_id=1, has_side_effects=True, vmem_limit_bytes=56 * 1024 * 1024
        ),
        name="forward_row",
    )(tok, wq4, vec, wo, f1, f2, ids.reshape(1, length), ids.reshape(length, 1), lanes)


def lead_loop(total, fn, step=16):
    lead, rows = total.shape[:-2], total.shape[-2]
    per = rows // step

    def body(n, _):
        block = n // per
        at = []
        for dim in reversed(lead):
            at.append(block % dim)
            block = block // dim
        fn(tuple(reversed(at)) + (pl.ds(pl.multiple_of((n % per) * step, step), step), slice(None)))
        return 0

    lax.fori_loop(0, math.prod(lead) * per, body, 0)


def add_into(total, term):
    def fn(idx):
        total[idx] = (total[idx].astype(F32) + term[idx].astype(F32)).astype(total.dtype)

    lead_loop(total, fn, 16 if total.dtype == BF else 8)


def reduce_plane(wire, place, grad, own, got, got2, got3, out, local, swap=False):
    z, y, x = place.z, place.y, place.x
    first = place.at(x=1 - x) if swap else place.at(y=1 - y)
    second = place.at(y=1 - y) if swap else place.at(x=1 - x)
    keep, give = (y, 1 - y) if swap else (x, 1 - x)
    order = [place.zup(k) for k in (1, 2, 3, 0)]

    def two(zk, mine):
        if swap:
            return grad.at[zk, :, x if mine else 1 - x]
        return grad.at[zk, y if mine else 1 - y]

    def one(k, i):
        if own is not None:
            return own.at[k, i]
        return grad.at[order[k], i, x] if swap else grad.at[order[k], y, i]

    sends = [wire.copy(two(zk, False), got.at[k], first) for k, zk in enumerate(order)]
    loads = []
    if own is not None:
        loads = [pltpu.make_async_copy(two(zk, True), own.at[k], local.at[k]) for k, zk in enumerate(order)]
    gives = [one(k, give) for k in range(NZ)]
    keeps = [one(k, keep) for k in range(NZ)]
    seconds = [wire.copy(gives[k], got2.at[k], second) for k in range(NZ)]
    along = [wire.copy(keeps[k], got3.at[k], place.at(z=place.zup(k + 1))) for k in range(NZ - 1)]
    yield
    for copy in sends:
        copy.go()
    for desc in loads:
        desc.start()
    yield
    for k in range(NZ):
        if loads:
            loads[k].wait()
        sends[k].wait_recv()
        add_into(gives[k], got.at[k, give])
        seconds[k].go()
        add_into(keeps[k], got.at[k, keep])
        yield
    for k in range(NZ):
        seconds[k].wait_recv()
        add_into(keeps[k], got2.at[k])
        if k < NZ - 1:
            along[k].go()
        yield
    for copy in along:
        copy.wait_recv()
    add_up(out, keeps[NZ - 1], got3)


def plane_scratch(block):
    return [
        pltpu.VMEM((NZ, 2) + block, BF),
        pltpu.VMEM((NZ, 2) + block, BF),
        pltpu.VMEM((NZ,) + block, BF),
        pltpu.VMEM((NZ - 1,) + block, BF),
        pltpu.SemaphoreType.DMA((NZ,)),
    ]


def reduce_outer(wire, place, go, outp, outg, load, scratch, out):
    c = place.c
    swap_o = wire.copy(go.at[:, :, :, 1 - c], outg, place.at(c=1 - c))
    load_o = pltpu.make_async_copy(go.at[:, :, :, c], outp, load)
    rest = reduce_plane(wire, place, outp, *scratch[:4], out, scratch[4], swap=True)
    next(rest)
    yield
    swap_o.go()
    load_o.start()
    yield
    load_o.wait()
    swap_o.wait_recv()
    add_into(outp, outg)
    yield from rest


def reduce_first(wire, place, g1, buf, got, scratch, out):
    c = place.c
    rows = got.shape[0]
    part = wire.copy(buf.at[pl.ds((1 - c) * rows, rows)], got, place.at(c=1 - c))
    yield from reduce_plane(wire, place, g1, *scratch[:4], buf, scratch[4])
    part.go()
    lane = out.shape[1] // (NZ * NY * NX * NC)
    spread_columns(out, buf, pl.multiple_of(c * rows, rows), c, lane)
    yield
    part.wait_recv()
    spread_columns(out, got, 0, 1 - c, lane)


def spread_columns(out, src, row, c, lane):
    rows = out.shape[0]
    for n in range(NZ * NY * NX):
        at = pl.ds(pl.multiple_of((n * NC + c) * lane, lane), lane)
        out[:, at] = src[pl.ds(row, rows), n * lane : (n + 1) * lane]


def reduce_quarter(wire, place, gq, own, got, got2, total, buf, out, local):
    y, s = place.y, place.seq
    order = [place.zup(n) for n in (1, 2, 3, 0)]
    sends = [wire.copy(gq.at[zk, 1 - y], got.at[n], place.at(y=1 - y)) for n, zk in enumerate(order)]
    along = [wire.copy(own.at[n], got2.at[n], place.at(z=place.zup(n + 1))) for n in range(NZ - 1)]
    near = ((place.at(c=1 - place.c), 1), (place.at(x=1 - place.x), 2), (place.at(x=1 - place.x, c=1 - place.c), 3))
    parts = [wire.copy(total.at[s ^ m], buf.at[s], dev) for dev, m in near]
    loads = [pltpu.make_async_copy(gq.at[zk, y], own.at[n], local.at[n]) for n, zk in enumerate(order)]
    mine = pltpu.make_async_copy(total.at[s], buf.at[s], local.at[NZ])
    yield
    for copy in sends:
        copy.go()
    for desc in loads:
        desc.start()
    yield
    for n in range(NZ):
        loads[n].wait()
        sends[n].wait_recv()
        add_into(own.at[n], got.at[n])
        if n < NZ - 1:
            along[n].go()
        yield
    for copy in along:
        copy.wait_recv()
    add_up(total, own.at[NZ - 1], got2)
    for copy in parts:
        copy.go()
    mine.start()
    yield
    mine.wait()
    for copy in parts:
        copy.wait_recv()
    group = NX * NC
    part = buf.shape[2] // 3
    for j in range(group):
        for n in range(3):
            at = (n * group + j) * part
            out[:, at : at + part] = buf[j, :, n * part : (n + 1) * part].astype(F32)


def reduce_vectors(wire, place, pairs):
    z, y = place.z, place.y
    sizes = [g.shape[1] // (NZ * NY) for g, *_ in pairs]

    def cols(n, zk, yk):
        return pl.ds(pl.multiple_of((zk * NY + yk) * sizes[n], sizes[n]), sizes[n])

    cs = [wire.copy(g, t.at[0], place.at(c=1 - place.c)) for g, t, *_ in pairs]
    xs = [wire.copy(g, t.at[1], place.at(x=1 - place.x)) for g, t, *_ in pairs]
    ys, zs = [], []
    for n, (g, t, got, _) in enumerate(pairs):
        for zk in range(NZ):
            at = cols(n, zk, 1 - y)
            ys.append(wire.copy(g.at[:, at], t.at[2, :, at], place.at(y=1 - y)))
        for k in range(1, NZ):
            at = cols(n, place.zup(k), y)
            zs.append(wire.copy(g.at[:, at], got.at[z], place.at(z=place.zup(k))))
    yield
    for copy in cs:
        copy.go()
    yield
    for copies, slot in ((cs, 0), (xs, 1)):
        for copy, (g, t, *_) in zip(copies, pairs):
            copy.wait_recv()
            copy.wait_send()
            add_rows(g, t.at[slot])
        for copy in xs if slot == 0 else ys:
            copy.go()
        yield
    for copy in ys:
        copy.wait_recv()
    for n, (g, t, got, _) in enumerate(pairs):
        for zk in range(NZ):
            at = cols(n, zk, y)
            add_rows(g.at[:, at], t.at[2, :, at])
    for copy in zs:
        copy.go()
    for n, (g, t, got, _) in enumerate(pairs):
        keep_rows(got.at[z], g.at[:, cols(n, z, y)])
    yield
    for copy in zs:
        copy.wait_recv()
    for g, t, got, out in pairs:
        add_fixed(out, got)


def add_rows(total, term):
    total[...] += term[...]


def keep_rows(dst, src):
    dst[...] = src[...]


def add_fixed(out, got):
    total = got[0]
    for k in range(1, NZ):
        total = total + got[k]
    out[...] = total


def add_up(out, own, got):
    def fn(idx):
        value = own[idx].astype(F32)
        for k in range(NZ - 1):
            value = value + got[(k,) + idx].astype(F32)
        out[idx] = value.astype(out.dtype)

    lead_loop(out, fn)


BACKWARD = (
    "1o",
    "1o",
    "1o",
    "o",
    "oo",
    "1",
    "1111ooo",
    "o",
    "1",
    "",
    "",
    "1o",
    "q1",
    "",
    "qqqq",
    "vvqvqvv",
)


def backward_kernel(heads, *refs):
    q, k, v, att, lse, idr, wq, grad_hidden, rows_in, wide_in, gain = refs[:11]
    tok, give, act, g1, go = refs[11:16]
    grad_tok, out1, outo, outq, outr, outw = refs[16:22]
    (do, km, vm, qm, dm, kt, idc, bias, acck, accv, accq, accw, delta, blk, actb) = refs[22:37]
    (dap, dgot, dfin, ownq, gotq, gotqb, sumq, outq_buf, gq, gotp, f1buf, f1got) = refs[37:49]
    (rowg, rowt, rowz, wideg, widet, widez, outp, outg) = refs[49:57]
    plane1, planeo = refs[57:62], refs[62:67]
    send, recv, local, dsend, drecv = refs[67:]
    place = Place()
    z, y, x, c, s, dp = place.z, place.y, place.x, place.c, place.seq, place.dp
    group = NX * NC
    wire = Wire(place, send, recv)
    core, other, across = place.at(c=1 - c), place.at(x=1 - x), place.at(x=1 - x, c=1 - c)
    length, part = q.shape
    span, width = tok.shape
    head = part // heads
    blocks = length // span
    shift = pl.multiple_of(s * part, part)

    greet(place)
    mine_at = pl.ds(pl.multiple_of(s * span, span), span)
    incoming = [
        wire.copy(give.at[peer], do.at[mine_at], dev).go()
        for dev, peer in ((core, s ^ 1), (other, s ^ 2), (across, s ^ 3))
    ]
    mine = pltpu.make_async_copy(give.at[s], do.at[mine_at], local.at[0])
    mine.start()

    plan = Plan(
        {
            "1": reduce_first(wire, place, g1, f1buf, f1got, plane1, out1),
            "o": reduce_outer(wire, place, go, outp, outg, local.at[1], planeo, outo),
            "q": reduce_quarter(wire, place, gq, ownq, gotq, gotqb, sumq, outq_buf, outq, local.at[pl.ds(6, NZ + 1)]),
            "v": reduce_vectors(wire, place, ((rowg, rowt, rowz, outr), (wideg, widet, widez, outw))),
        },
        BACKWARD,
    )
    plan.hook()

    mask_heads(qm, q, heads, head)
    accq[...] = jnp.zeros(accq.shape, F32)
    accw[...] = jnp.zeros(accw.shape, F32)
    delta[...] = jnp.zeros(delta.shape, F32)
    mine.wait()
    for copy in incoming:
        copy.wait_recv()
    plan.hook()
    mask_heads(dm, do, heads, head)
    for b in range(blocks):
        at = slice(b * span, (b + 1) * span)
        weighted = do[at, :].T.astype(F32) * att[:, at]
        for h in range(heads):
            delta[h : h + 1, at] = jnp.sum(weighted[h * head : (h + 1) * head, :], 0, keepdims=True)

    hops = []
    for t in range(blocks):
        tx, tc = t // NC, t % NC
        inner = pltpu.make_async_remote_copy(
            src_ref=dap.at[t],
            dst_ref=dgot.at[tx],
            send_sem=dsend.at[2 * t],
            recv_sem=drecv.at[2 * t],
            device_id=core,
            device_id_type=MESH,
        )
        outerc = pltpu.make_async_remote_copy(
            src_ref=dap.at[t],
            dst_ref=dfin,
            send_sem=dsend.at[2 * t + 1],
            recv_sem=drecv.at[2 * t + 1],
            device_id=other,
            device_id_type=MESH,
        )
        hops.append((tx, tc, inner, outerc))

    def meet(t):
        tx, tc, inner, outerc = hops[t]

        @pl.when(c == tc)
        def _():
            inner.wait_recv()
            add_into(dap.at[t], dgot.at[tx])

            @pl.when(x != tx)
            def _():
                outerc.start()

    fetch = [
        pltpu.make_async_copy(act.at[pl.ds(b * span, span)], actb.at[b % 2], local.at[2 + b]) for b in range(blocks)
    ]
    fetch[0].start()

    for kb in range(blocks):
        ks = slice(kb * span, (kb + 1) * span)
        if kb + 1 < blocks:
            fetch[kb + 1].start()
        mask_heads(km, k.at[ks], heads, head)
        mask_heads(vm, v.at[ks], heads, head)
        kt[...] = k[ks, :].T
        idc[...] = jnp.broadcast_to(idr[:, ks], (8, span)).T
        acck[...] = jnp.zeros(acck.shape, F32)
        accv[...] = jnp.zeros(accv.shape, F32)

        def queries(qb, _, kb=kb, ks=ks):
            qs = pl.ds(pl.multiple_of(qb * span, span), span)
            bias[...] = pair_bias(idr, idc[:, 0:1], qb, kb, span)
            for h in range(heads):
                scores = nt(km[h], q[qs, :]) + bias[...]
                probs = jnp.exp(scores - lse[h : h + 1, qs])
                grad = nt(vm[h], do[qs, :])
                ds = (probs * (grad - delta[h : h + 1, qs])).astype(BF)
                accv[...] += nn(probs.astype(BF), dm[h, qs, :])
                acck[...] += nn(ds, qm[h, qs, :])
                hs = slice(h * head, (h + 1) * head)
                accq[hs, qs] += nn(kt[hs, :], ds)
            for n in range(kb, blocks):

                @pl.when(qb == n)
                def _():
                    if n == blocks - 1 and kb > 0:
                        meet(kb - 1)
                    plan.hook()

            return 0

        lax.fori_loop(kb, blocks, queries, 0)
        blk[:, :part] = (accq[:, ks].T * (head**-0.5)).astype(BF)
        blk[:, part : 2 * part] = acck[...].astype(BF)
        blk[:, 2 * part :] = accv[...].astype(BF)
        sums = jnp.sum(blk[...].astype(F32), 0, keepdims=True)
        if kb == 0:
            gotp[...] = jnp.zeros(gotp.shape, F32)
        gotp[0:1, :] += sums
        fetch[kb].wait()
        step = 256
        for n in range(0, width, step):
            accw[n : n + step, :] += lax.dot_general(
                actb[kb % 2, :, n : n + step], blk[...], (((0,), (0,)), ((), ())), preferred_element_type=F32
            )
        if kb == blocks - 1:
            gq[...] = accw[...].astype(BF).reshape(gq.shape)
            plan.hook()
        weights = wq[...].reshape(width, 3 * part)
        for n in range(0, width, step):
            dap[kb, :, n : n + step] = nt(blk[...], weights[n : n + step, :]).astype(BF)
        tx, tc, inner, outerc = hops[kb]

        @pl.when(c != tc)
        def _():
            inner.start()

    fetch_tok = pltpu.make_async_copy(tok, actb.at[0], local.at[11])
    fetch_tok.start()
    plan.hook()
    meet(blocks - 1)
    plan.hook()

    step = 64
    rowg[...] = rows_in[...]
    wideg[...] = wide_in[...]
    lane_sum = jnp.sum(delta[...], 1, keepdims=True)
    for j in range(group):
        rowg[16 + j * heads : 16 + (j + 1) * heads, :] = jnp.where(
            s == j, jnp.broadcast_to(lane_sum[:heads], (heads, width)), 0.0
        )
    rowg[2:3, pl.ds(shift, part)] = gotp[0:1, :part]
    rowg[3:4, pl.ds(shift, part)] = gotp[0:1, 2 * part :]
    for t in range(blocks):
        tx, tc, inner, outerc = hops[t]

        @pl.when((x == tx) & (c == tc))
        def _():
            outerc.wait_recv()

    fetch_tok.wait()

    def finish(n, carry):
        at = pl.ds(pl.multiple_of(n * step, step), step)
        da = dap[s, at, :].astype(F32) + dfin[at, :].astype(F32)
        normed, inv = normalize(actb[0, at, :].astype(F32))
        grad = norm_back(da * gain[...], normed, inv) + grad_hidden[at, :]
        grad_tok[at, :] = grad.astype(BF)
        return (
            carry[0] + jnp.sum(da * normed, 0, keepdims=True),
            carry[1] + jnp.sum(da, 0, keepdims=True),
        )

    zero = jnp.zeros((1, width), F32)
    gain_one, shift_one = lax.fori_loop(0, span // step, finish, (zero, zero))
    rowg[0:1, :] = gain_one
    rowg[1:2, :] = shift_one

    plan.finish()
    for t in range(blocks):
        tx, tc, inner, outerc = hops[t]

        @pl.when(c != tc)
        def _():
            inner.wait_send()

        @pl.when((c == tc) & (x != tx))
        def _():
            outerc.wait_send()

    wire.drain()


def backward(give, q, k, v, att, lse, ids, wq, tok, grad_hidden, rows_in, wide_in, gain, act, g1, go, heads):
    length, part = q.shape
    span, width = tok.shape
    group = length // span
    b1, bo = g1.shape[3:], go.shape[4:]
    rows, triple = wq.shape[2:]
    bq = (group, rows, triple)
    dps = NZ * NY
    out = (
        (VM, (span, width), BF),
        (VM, (b1[0] // NC, NC * b1[1]), F32),
        (VM, bo, F32),
        (VM, (rows, group * triple), F32),
        (VM, (rows_in.shape[0], width // dps), F32),
        (VM, (wide_in.shape[0], wide_in.shape[1] // dps), F32),
    )
    scratch = [
        pltpu.VMEM((length, part), BF),
        pltpu.VMEM((heads, span, part), BF),
        pltpu.VMEM((heads, span, part), BF),
        pltpu.VMEM((heads, length, part), BF),
        pltpu.VMEM((heads, length, part), BF),
        pltpu.VMEM((part, span), BF),
        pltpu.VMEM((span, 8), jnp.int32),
        pltpu.VMEM((span, span), F32),
        pltpu.VMEM((span, part), F32),
        pltpu.VMEM((span, part), F32),
        pltpu.VMEM((part, length), F32),
        pltpu.VMEM((width, triple), F32),
        pltpu.VMEM((8, length), F32),
        pltpu.VMEM((span, triple), BF),
        pltpu.VMEM((2, span, width), BF),
        pltpu.VMEM((group, span, width), BF),
        pltpu.VMEM((NX, span, width), BF),
        pltpu.VMEM((span, width), BF),
        pltpu.VMEM((NZ,) + bq, BF),
        pltpu.VMEM((NZ,) + bq, BF),
        pltpu.VMEM((NZ - 1,) + bq, BF),
        pltpu.VMEM(bq, BF),
        pltpu.VMEM(bq, BF),
        pltpu.VMEM((NZ, NY) + bq, BF),
        pltpu.VMEM((8, triple), F32),
        pltpu.VMEM(b1, F32),
        pltpu.VMEM((b1[0] // NC, b1[1]), F32),
        pltpu.VMEM(rows_in.shape, F32),
        pltpu.VMEM((3,) + rows_in.shape, F32),
        pltpu.VMEM((NZ, rows_in.shape[0], width // dps), F32),
        pltpu.VMEM(wide_in.shape, F32),
        pltpu.VMEM((3,) + wide_in.shape, F32),
        pltpu.VMEM((NZ, wide_in.shape[0], wide_in.shape[1] // dps), F32),
        pltpu.VMEM((NZ, NY, NX) + bo, BF),
        pltpu.VMEM((NZ, NY, NX) + bo, BF),
    ]
    scratch += plane_scratch(b1) + plane_scratch(bo)
    scratch += [
        pltpu.SemaphoreType.DMA((COPIES,)),
        pltpu.SemaphoreType.DMA((COPIES,)),
        pltpu.SemaphoreType.DMA((12,)),
        pltpu.SemaphoreType.DMA((2 * group,)),
        pltpu.SemaphoreType.DMA((2 * group,)),
    ]
    return pl.pallas_call(
        functools.partial(backward_kernel, heads),
        out_shape=tuple(jax.ShapeDtypeStruct(shape, dtype) for _, shape, dtype in out),
        in_specs=[VM] * 11 + [HBM] * 5,
        out_specs=[spec for spec, _, _ in out],
        scratch_shapes=scratch,
        compiler_params=pltpu.CompilerParams(
            collective_id=2, has_side_effects=True, vmem_limit_bytes=63 * 1024 * 1024
        ),
        name="backward_row",
    )(
        q, k, v, att, lse, ids.reshape(1, length), wq, grad_hidden, rows_in, wide_in, gain,
        tok, give, act, g1, go,
    )


MIDDLE = (
    "c",
    "",
    "",
    "",
    "cccc",
    "cccc2",
    "",
    "",
    "",
    "2",
    "",
    "2",
    "",
    "",
    "2222222",
)


def middle_tasks(wire, place, f2c, g2, scratch, out2):
    return {
        "c": spread_zxy(wire, place, f2c, swap=True),
        "2": reduce_plane(wire, place, g2, None, *scratch, out2, None, swap=True),
    }


def tn(a, b):
    return lax.dot_general(a, b, (((0,), (0,)), ((), ())), preferred_element_type=F32)


def row_steps(count, step, fn):
    def body(n, _):
        fn(pl.ds(pl.multiple_of(n * step, step), step))
        return 0

    lax.fori_loop(0, count // step, body, 0)


def ffn_kernel(*refs):
    own, rows_all, wide_all, lanes = refs[:4]
    tok, cot, f2own, f2d, wo, f1 = refs[4:10]
    out, give, gh, g1, go, out2, rows_g, wide_g = refs[10:18]
    wov, f1v, f2v, dt, act, buf, slope, mix, dm, br, hid, g2, dbuf, prb, prc, stg, wv = refs[18:35]
    stat, stat_got, back, back_got, sums, colsums = refs[35:41]
    plane2 = refs[41:44]
    send, recv, local = refs[44:]
    place = Place()
    z, y, x, c = place.z, place.y, place.x, place.c
    wire = Wire(place, send, recv)
    core = place.at(c=1 - c)
    span, width = own.shape
    units = f1v.shape[4]
    group = NX * NC
    tile = 512
    tiles = units // tile
    total_units = units * NC

    half = f2own.shape[0]
    f2c = f2v.at[:, :, :, pl.ds(0, half)]
    loads = [
        pltpu.make_async_copy(wo, wov, local.at[0]),
        pltpu.make_async_copy(f2own, f2c.at[z, y, x], local.at[1]),
        pltpu.make_async_copy(cot, dt.at[c], local.at[2]),
        pltpu.make_async_copy(f1, f1v, local.at[3]),
        pltpu.make_async_copy(f2d, f2v.at[:, :, :, pl.ds(half, half)], local.at[4]),
        pltpu.make_async_copy(tok, prc, local.at[5]),
    ]
    for desc in loads:
        desc.start()
    chunk = span // 4
    chunks = [pl.ds(n * chunk, chunk) for n in range(4)]
    dt_copy = wire.copy(cot, dt.at[c], core)
    act_copies = [wire.copy(act.at[c, at], act.at[c, at], core) for at in chunks]
    stat_copies = [wire.copy(stat.at[h], stat_got.at[h], core) for h in range(NC)]
    back_copies = [wire.copy(back.at[h], back_got.at[h], core) for h in range(NC)]
    out_copy = wire.copy(dbuf, prb, core)
    da_copy = wire.copy(prb, prc, core)
    loads[1].wait()
    greet(place)
    dt_copy.go()
    plan = Plan(middle_tasks(wire, place, f2c, g2, plane2, out2), MIDDLE)
    plan.hook()

    def row(ref, n):
        return ref[n : n + 1, :].astype(F32)

    lane = wide_all.shape[1] // (NZ * NY * NX * NC)
    for n in range(NZ * NY * NX):
        at = pl.ds(pl.multiple_of((n * NC + c) * lane, lane), lane)
        wv[0:3, n * lane : (n + 1) * lane] = wide_all[0:3, at].astype(F32)
    colsums[...] = jnp.zeros(colsums.shape, F32)
    sums[...] = jnp.zeros(sums.shape, F32)
    loads[0].wait()
    loads[5].wait()

    for at, copy in zip(chunks, act_copies):
        branch = nn(own[at, :], wov[...].reshape(width, width)) + row(rows_all, 4)
        br[at, :] = branch

        def fn(inner, at=at):
            rows = pl.ds(at.start + inner.start, inner.size)
            hidden = prc[rows, :].astype(F32) + normalize(br[rows, :])[0] * row(rows_all, 5) + row(rows_all, 6)
            hid[rows, :] = hidden
            act[c, rows, :] = (normalize(hidden)[0] * row(rows_all, 7) + row(rows_all, 8)).astype(BF)

        row_steps(chunk, 32, fn)
        copy.go()
    plan.hook()
    loads[3].wait()

    for h in range(NC):

        @pl.when(c != h)
        def _():
            for copy in act_copies:
                copy.wait_recv()

        for n in range(tiles):
            cols = slice(n * tile, (n + 1) * tile)
            weights = f1v[:, :, :, :, cols].reshape(width, tile)
            buf[h, :, cols] = nn(act[h], weights) + wv[0:1, cols]

        def fn(at, h=h):
            total = jnp.zeros((at.size, 1), F32)
            for n in range(tiles):
                cols = slice(n * tile, (n + 1) * tile)
                u = buf[h, at, cols]
                cdf = 0.5 + 0.5 * lax.erf(u * math.sqrt(0.5))
                value = u * cdf
                buf[h, at, cols] = value
                pdf = jnp.exp(-0.5 * u * u) * (1.0 / math.sqrt(2.0 * math.pi))
                slope[h, at, cols] = (cdf + u * pdf).astype(BF)
                total = total + jnp.sum(value, 1, keepdims=True)
            mean = total * (1.0 / units)
            square = jnp.zeros((at.size, 1), F32)
            for n in range(tiles):
                centred = buf[h, at, n * tile : (n + 1) * tile] - mean
                square = square + jnp.sum(centred * centred, 1, keepdims=True)
            column = lax.broadcasted_iota(jnp.int32, (at.size, 128), 1)
            stat[h, at, :] = jnp.where(column == 0, mean, square)

        row_steps(span, 16, fn)
        stat_copies[h].go()
        plan.hook()

    for h in range(NC):
        stat_copies[h].wait_recv()
        stat_copies[h].wait_send()

        def fn(at, h=h):
            mean_a, mean_b = stat[h, at, 0:1], stat_got[h, at, 0:1]
            gap = mean_a - mean_b
            square = stat[h, at, 1:2] + stat_got[h, at, 1:2] + gap * gap * (0.5 * units)
            mean = 0.5 * (mean_a + mean_b)
            inv = lax.rsqrt(square * (1.0 / total_units) + EPSILON)
            stat[h, at, :] = jnp.broadcast_to(inv, (at.size, 128))
            for n in range(tiles):
                cols = slice(n * tile, (n + 1) * tile)
                normed = (buf[h, at, cols] - mean) * inv
                buf[h, at, cols] = normed
                mix[h, at, cols] = (normed * wv[1:2, cols] + wv[2:3, cols]).astype(BF)

        row_steps(span, 16, fn)
    plan.hook()

    loads[2].wait()
    loads[4].wait()
    dt_copy.wait_recv()
    per = g2.shape[3]
    for n in range(units // (2 * per)):
        cols = slice(n * 2 * per, (n + 1) * 2 * per)
        part = tn(mix[0, :, cols], dt[0]) + tn(mix[1, :, cols], dt[1])
        g2[n // NY, n % NY] = part.astype(BF).reshape(NX, per, width)
    plan.hook()

    weights2 = f2v[...].reshape(units, width)
    for n in range(0, width, tile):
        dbuf[:, n : n + tile] = nn(mix[1 - c], weights2[:, n : n + tile]).astype(BF)
    out_copy.go()
    for n in range(0, width, tile):
        cols = slice(n, n + tile)
        gh[:, cols] = nn(mix[c], weights2[:, cols]) + hid[:, cols] + rows_all[9:10, cols].astype(F32)
    plan.hook()

    for h in range(NC):
        for n in range(tiles):
            cols = slice(n * tile, (n + 1) * tile)
            dm[:, cols] = nt(dt[h], weights2[cols, :])

        def fn(at, h=h):
            first = jnp.zeros((at.size, 1), F32)
            second = jnp.zeros((at.size, 1), F32)
            for n in range(tiles):
                cols = slice(n * tile, (n + 1) * tile)
                grad = dm[at, cols]
                normed = buf[h, at, cols]
                product = grad * normed
                colsums[1, :, cols] += product
                colsums[2, :, cols] += grad
                first = first + jnp.sum(grad * wv[1:2, cols], 1, keepdims=True)
                second = second + jnp.sum(product * wv[1:2, cols], 1, keepdims=True)
            column = lax.broadcasted_iota(jnp.int32, (at.size, 128), 1)
            back[h, at, :] = jnp.where(column == 0, first, second)

        row_steps(span, 16, fn)
        back_copies[h].go()
        plan.hook()
        back_copies[h].wait_recv()

        def fn(at, h=h):
            scale = 1.0 / total_units
            first = (back[h, at, 0:1] + back_got[h, at, 0:1]) * scale
            second = (back[h, at, 1:2] + back_got[h, at, 1:2]) * scale
            inv = stat[h, at, 0:1]
            for n in range(tiles):
                cols = slice(n * tile, (n + 1) * tile)
                grad = inv * (dm[at, cols] * wv[1:2, cols] - first - buf[h, at, cols] * second)
                inner = (grad * slope[h, at, cols].astype(F32)).astype(BF)
                mix[h, at, cols] = inner
                colsums[0, :, cols] += inner.astype(F32)

        row_steps(span, 16, fn)
        plan.hook()

    weights1 = f1v[...].reshape(width, units)
    out_copy.wait_recv()
    out[...] = (gh[...] + prb[...].astype(F32)).astype(BF)
    for n in range(0, width, tile):
        prb[:, n : n + tile] = nt(mix[1 - c], weights1[n : n + tile, :]).astype(BF)
    da_copy.go()
    for n in range(0, width, tile):
        gh[:, n : n + tile] = nt(mix[c], weights1[n : n + tile, :])
    plan.hook()
    size = stg.shape[1]
    writes = []

    def write(part, dst, wide):
        n = len(writes)
        if n >= 2:
            writes[n - 2].wait()
        stg[n % 2, :, 0:wide] = part.astype(BF)
        desc = pltpu.make_async_copy(stg.at[n % 2, :, pl.ds(0, wide)], dst, local.at[6 + n % 2])
        desc.start()
        writes.append(desc)

    for n in range(0, width, size):
        part = tn(act[0, :, n : n + size], mix[0]) + tn(act[1, :, n : n + size], mix[1])
        write(part, g1.at[pl.ds(n, size)], units)
    plan.hook()
    da_copy.wait_recv()
    out_copy.wait_send()

    def fn(at):
        da = gh[at, :] + prc[at, :].astype(F32)
        top = dt[c, at, :].astype(F32)
        normed, inv = normalize(hid[at, :])
        grad = top + norm_back(da * row(rows_all, 7), normed, inv)
        gh[at, :] = grad
        normed_b, inv_b = normalize(br[at, :])
        down = norm_back(grad * row(rows_all, 5), normed_b, inv_b).astype(BF)
        dbuf[at, :] = down
        for n, value in enumerate((down.astype(F32), grad * normed_b, grad, da * normed, da, top)):
            sums[n] += value

    row_steps(span, 16, fn)
    plan.hook()
    weights_o = wov[...].reshape(width, width)
    part_size = width // group
    for j in range(group):
        at = slice(j * part_size, (j + 1) * part_size)
        give[j] = (nt(dbuf[...], weights_o[at, :]) * lanes[:, at]).astype(BF)
    for n in range(0, width, size):
        write(tn(own[:, n : n + size], dbuf[...]), go.at[pl.ds(n, size)], width)
    rows_g[...] = jnp.zeros(rows_g.shape, F32)
    for n in range(6):
        rows_g[4 + n : 5 + n, :] = jnp.sum(sums[n], 0, keepdims=True)
    wide_g[...] = jnp.zeros(wide_g.shape, F32)
    for n in range(NZ * NY * NX):
        at = pl.ds(pl.multiple_of((n * NC + c) * lane, lane), lane)
        for j in range(3):
            wide_g[j : j + 1, at] = jnp.sum(colsums[j, :, n * lane : (n + 1) * lane], 0, keepdims=True)
    plan.finish()
    for desc in writes[-2:]:
        desc.wait()
    wire.drain()


def feed_forward(own, rows_all, wide_all, lanes, tok, cot, f2own, f2d, wo, f1):
    span, width = own.shape
    units = f1.shape[4]
    group = NX * NC
    per = 2 * f2own.shape[0]
    out = (
        (VM, (span, width), BF),
        (VM, (group, span, width // group), BF),
        (VM, (span, width), F32),
        (HBM, (width, units), BF),
        (HBM, (width, width), BF),
        (VM, (per, width), F32),
        (VM, (32, width), F32),
        (VM, (8, wide_all.shape[1]), F32),
    )
    scratch = [
        pltpu.VMEM(wo.shape, BF),
        pltpu.VMEM(f1.shape, BF),
        pltpu.VMEM((NZ, NY, NX) + (per, width), BF),
        pltpu.VMEM((NC, span, width), BF),
        pltpu.VMEM((NC, span, width), BF),
        pltpu.VMEM((NC, span, units), F32),
        pltpu.VMEM((NC, span, units), BF),
        pltpu.VMEM((NC, span, units), BF),
        pltpu.VMEM((span, units), F32),
        pltpu.VMEM((span, width), F32),
        pltpu.VMEM((span, width), F32),
        pltpu.VMEM((NZ, NY, NX) + (per, width), BF),
        pltpu.VMEM((span, width), BF),
        pltpu.VMEM((span, width), BF),
        pltpu.VMEM((span, width), BF),
        pltpu.VMEM((2, 128, units), BF),
        pltpu.VMEM((8, units), F32),
    ]
    scratch += [pltpu.VMEM((NC, span, 128), F32)] * 4
    scratch += [pltpu.VMEM((6, 16, width), F32), pltpu.VMEM((3, 16, units), F32)]
    scratch += plane_scratch((per, width))[1:4]
    scratch += [
        pltpu.SemaphoreType.DMA((COPIES,)),
        pltpu.SemaphoreType.DMA((COPIES,)),
        pltpu.SemaphoreType.DMA((8,)),
    ]
    return pl.pallas_call(
        ffn_kernel,
        out_shape=tuple(jax.ShapeDtypeStruct(shape, dtype) for _, shape, dtype in out),
        in_specs=[VM] * 4 + [HBM] * 6,
        out_specs=[spec for spec, _, _ in out],
        scratch_shapes=scratch,
        compiler_params=pltpu.CompilerParams(
            collective_id=3, has_side_effects=True, vmem_limit_bytes=63 * 1024 * 1024
        ),
        name="feed_forward",
    )(own, rows_all, wide_all, lanes, tok, cot, f2own, f2d, wo, f1)


def fast(tokens, doc_ids, cotangent, w_qkv, w_out, attn_vecs, head_scale, w_fc1, w_fc2, ffn_vecs, ffn_wide):
    _, span, width = tokens.shape
    group = NX * NC
    length = span * group
    head_count = head_scale.shape[0]
    head = width // head_count
    heads = head_count // group
    part = heads * head
    seq = lax.axis_index("seq")
    chips = NZ * NY * NX
    block = w_fc2.shape[0]
    units = chips * block

    rows = w_qkv.shape[0]
    wq4 = w_qkv.astype(BF).reshape(rows, 3, group, part).transpose(2, 0, 1, 3).reshape(group, rows, 3 * part)
    f1 = w_fc1.astype(BF).reshape(rows, chips, NC, block).transpose(2, 0, 1, 3).reshape(NC, rows, units)
    f2 = w_fc2.astype(BF)
    narrow = jnp.concatenate([attn_vecs, ffn_vecs], 0).astype(BF)
    count, each = narrow.shape
    lane = each * group
    narrow = lax.dynamic_update_slice(jnp.zeros((16, lane), BF), narrow, (0, seq * each))
    vec = jnp.stack([narrow, jnp.pad(ffn_wide.astype(BF), ((0, 16 - ffn_wide.shape[0]), (0, 0)))])
    tok = tokens.reshape(span, width)
    scale_own = lax.dynamic_slice_in_dim(head_scale, heads * seq, heads)
    scale_lanes = jnp.repeat(scale_own, head).reshape(1, part)
    ids = doc_ids.reshape(length)
    act_one, q, k, v, att, lse, scaled_own, wq, rows_all, wide_all, wo, fc1, fc2 = forward(
        tok, wq4, vec, w_out.astype(BF), f1, f2[block // 2 :], ids, scale_lanes, heads
    )
    outputs, give, grad_hidden, grad_fc1, grad_out, grad_w2, rows_in, wide_grads = feed_forward(
        scaled_own,
        rows_all,
        wide_all,
        jnp.repeat(head_scale, head).reshape(1, width),
        tok,
        cotangent.reshape(span, width),
        f2[: block // 2],
        fc2,
        wo,
        fc1,
    )
    grad_tokens, grad_w1, grad_wo, grad_wqkv, rows_out, wide_out = backward(
        give,
        q,
        k,
        v,
        att,
        lse,
        ids,
        wq,
        tok,
        grad_hidden,
        rows_in,
        wide_grads,
        rows_all[:1].astype(F32),
        act_one,
        grad_fc1.reshape(NZ, NY, NX, NC * rows, units),
        grad_out.reshape(NZ, NY, NX, NC, rows, width),
        heads,
    )
    mine = lax.dynamic_slice_in_dim(rows_out, seq * each, each, 1)
    wide_mine = lax.dynamic_slice_in_dim(wide_out, seq * block, block, 1)
    return (
        outputs.reshape(1, span, width),
        grad_tokens.reshape(1, span, width),
        grad_wqkv,
        grad_wo,
        mine[: attn_vecs.shape[0]],
        rows_out[16 : 16 + head_count, 0] / head_scale,
        grad_w1,
        grad_w2,
        mine[attn_vecs.shape[0] : count],
        wide_mine[: ffn_wide.shape[0]],
    )


def solution(mesh):
    placed = (
        P("dp", "seq", None),
        P("dp", None),
        P("dp", "seq", None),
        P(("dp", "seq"), None),
        P(("dp", "seq"), None),
        P(None, ("dp", "seq")),
        P(),
        P(("dp", "seq"), None),
        P(("dp", "seq"), None),
        P(None, ("dp", "seq")),
        P(None, ("dp", "seq")),
    )
    results = (
        P("dp", "seq", None),
        P("dp", "seq", None),
        P(("dp", "seq"), None),
        P(("dp", "seq"), None),
        P(None, ("dp", "seq")),
        P(),
        P(("dp", "seq"), None),
        P(("dp", "seq"), None),
        P(None, ("dp", "seq")),
        P(None, ("dp", "seq")),
    )
    suits = mesh.shape["dp"] == NZ * NY and mesh.shape["seq"] == NX * NC
    return jax.shard_map(
        fast if suits else local, mesh=mesh, in_specs=placed, out_specs=results, check_vma=False
    )
```

```python
import functools
import math

import jax
import jax.numpy as jnp
from jax import lax
from jax.experimental import pallas as pl
from jax.experimental.pallas import tpu as pltpu
from jax.sharding import PartitionSpec as P

EPSILON = 1e-05
NEGATIVE = -1e30
MESH = pl.DeviceIdType.MESH
BF = jnp.bfloat16
F32 = jnp.float32
NZ, NY, NX, NC = 4, 2, 2, 2
HBM = pl.BlockSpec(memory_space=pl.ANY)
VM = pl.BlockSpec(memory_space=pltpu.VMEM)


def normalize(values):
    centre = jnp.mean(values, -1, keepdims=True)
    centred = values - centre
    scale_inv = lax.rsqrt(jnp.mean(centred * centred, -1, keepdims=True) + EPSILON)
    return (centred * scale_inv, scale_inv)


def norm_back(grad_normed, normed, scale_inv):
    return scale_inv * (
        grad_normed
        - jnp.mean(grad_normed, -1, keepdims=True)
        - normed * jnp.mean(grad_normed * normed, -1, keepdims=True)
    )


def gelu_exact(values):
    return 0.5 * values * (1.0 + jax.scipy.special.erf(values * math.sqrt(0.5)))


def left_grad(activations, gradients):
    return lax.dot_general(
        activations, gradients, (((0,), (0,)), ((), ())), preferred_element_type=jnp.float32
    )


def right_back(gradients, matrix):
    return lax.dot_general(
        gradients, matrix, (((1,), (1,)), ((), ())), preferred_element_type=jnp.float32
    )


def masked_scores(queries, keys_block, query_pos, key_pos, query_ids, key_ids):
    raw_scores = jnp.einsum(
        "rqhe,rkhe->rhqk", queries, keys_block, preferred_element_type=jnp.float32
    )
    allowed = (key_pos[None, None, :] <= query_pos[None, :, None]) & (
        key_ids[:, None, :] == query_ids[:, :, None]
    )
    return jnp.where(allowed[:, None], raw_scores * queries.shape[3] ** (-0.5), NEGATIVE)


def attend(queries, keys_all, values_all, query_pos, query_ids, doc_rows, block_len):
    block_count = keys_all.shape[1] // block_len
    stat_shape = (queries.shape[0], queries.shape[2], queries.shape[1])

    def slice_block(block_index):
        start = block_index * block_len
        keys_block = lax.dynamic_slice_in_dim(keys_all, start, block_len, 1)
        values_block = lax.dynamic_slice_in_dim(values_all, start, block_len, 1)
        key_ids = lax.dynamic_slice_in_dim(doc_rows, start, block_len, 1)
        key_pos = start + jnp.arange(block_len, dtype=jnp.int32)
        return (
            values_block,
            masked_scores(queries, keys_block, query_pos, key_pos, query_ids, key_ids),
        )

    def first_pass(carry, block_index):
        running_max, running_sum = carry
        _, scores = slice_block(block_index)
        new_max = jnp.maximum(running_max, jnp.max(scores, -1))
        running_sum = running_sum * jnp.exp(running_max - new_max) + jnp.sum(
            jnp.exp(scores - new_max[..., None]), -1
        )
        return ((new_max, running_sum), None)

    start_stats = (jnp.full(stat_shape, NEGATIVE, jnp.float32), jnp.zeros(stat_shape, jnp.float32))
    (row_max, row_sum), _ = lax.scan(
        first_pass, start_stats, jnp.arange(block_count, dtype=jnp.int32)
    )
    log_total = row_max + jnp.log(row_sum)

    def second_pass(total_out, block_index):
        values_block, scores = slice_block(block_index)
        probs = jnp.exp(scores - log_total[..., None]).astype(jnp.bfloat16)
        return (
            total_out
            + jnp.einsum(
                "rhqk,rkhe->rqhe", probs, values_block, preferred_element_type=jnp.float32
            ),
            None,
        )

    attended, _ = lax.scan(
        second_pass, jnp.zeros(queries.shape, jnp.float32), jnp.arange(block_count, dtype=jnp.int32)
    )
    return (attended, log_total)


def attend_back(
    queries,
    keys_all,
    values_all,
    grad_out,
    log_total,
    delta,
    query_pos,
    query_ids,
    doc_rows,
    block_len,
):
    block_count = keys_all.shape[1] // block_len
    scale = queries.shape[3] ** (-0.5)

    def step(grad_queries, block_index):
        start = block_index * block_len
        keys_block = lax.dynamic_slice_in_dim(keys_all, start, block_len, 1)
        values_block = lax.dynamic_slice_in_dim(values_all, start, block_len, 1)
        key_ids = lax.dynamic_slice_in_dim(doc_rows, start, block_len, 1)
        key_pos = start + jnp.arange(block_len, dtype=jnp.int32)
        scores = masked_scores(queries, keys_block, query_pos, key_pos, query_ids, key_ids)
        probs = jnp.exp(scores - log_total[..., None])
        grad_probs = jnp.einsum(
            "rqhe,rkhe->rhqk", grad_out, values_block, preferred_element_type=jnp.float32
        )
        grad_scores = (probs * (grad_probs - delta[..., None]) * scale).astype(jnp.bfloat16)
        grad_queries = grad_queries + jnp.einsum(
            "rhqk,rkhe->rqhe", grad_scores, keys_block, preferred_element_type=jnp.float32
        )
        grad_keys = jnp.einsum(
            "rhqk,rqhe->rkhe", grad_scores, queries, preferred_element_type=jnp.float32
        )
        grad_values = jnp.einsum(
            "rhqk,rqhe->rkhe",
            probs.astype(jnp.bfloat16),
            grad_out,
            preferred_element_type=jnp.float32,
        )
        return (grad_queries, (grad_keys, grad_values))

    return lax.scan(
        step, jnp.zeros(queries.shape, jnp.float32), jnp.arange(block_count, dtype=jnp.int32)
    )


def local(
    tokens,
    doc_ids,
    cotangent,
    w_qkv,
    w_out,
    attn_vecs,
    head_scale,
    w_fc1,
    w_fc2,
    ffn_vecs,
    ffn_wide,
):
    row_count, span_len, model_width = tokens.shape
    head_count = head_scale.shape[0]
    head_size = model_width // head_count
    token_count = row_count * span_len
    brain = jnp.bfloat16
    single = jnp.float32
    gathered_qkv, gathered_out, attn_rows = (
        lax.all_gather(w_qkv.astype(brain), ("dp", "seq"), axis=0, tiled=True),
        lax.all_gather(w_out.astype(brain), ("dp", "seq"), axis=0, tiled=True),
        lax.all_gather(attn_vecs.astype(brain), ("dp", "seq"), axis=1, tiled=True),
    )
    attn_rows = attn_rows.astype(single)
    inputs = tokens.astype(single).reshape(token_count, model_width)
    normed_one, inv_one = normalize(inputs)
    act_one = (normed_one * attn_rows[0] + attn_rows[1]).astype(brain)
    projected = jnp.dot(act_one, gathered_qkv, preferred_element_type=single)
    queries = (projected[:, :model_width] + attn_rows[2]).astype(brain)
    keys_own = projected[:, model_width : 2 * model_width].astype(brain)
    values_own = (projected[:, 2 * model_width :] + attn_rows[3]).astype(brain)
    keys_all, values_all = (
        lax.all_gather(
            keys_own.reshape(row_count, span_len, model_width), "seq", axis=1, tiled=True
        ),
        lax.all_gather(
            values_own.reshape(row_count, span_len, model_width), "seq", axis=1, tiled=True
        ),
    )
    offset = lax.axis_index("seq") * span_len
    query_pos = offset + jnp.arange(span_len, dtype=jnp.int32)
    query_ids = lax.dynamic_slice_in_dim(doc_ids, offset, span_len, 1)
    queries_four = queries.reshape(row_count, span_len, head_count, head_size)
    keys_four = keys_all.reshape(row_count, -1, head_count, head_size)
    values_four = values_all.reshape(row_count, -1, head_count, head_size)
    attended, log_total = attend(
        queries_four, keys_four, values_four, query_pos, query_ids, doc_ids, span_len
    )
    scaled = (
        (attended * head_scale[None, None, :, None]).reshape(token_count, model_width).astype(brain)
    )
    branch = jnp.dot(scaled, gathered_out, preferred_element_type=single) + attn_rows[4]
    normed_branch, inv_branch = normalize(branch)
    hidden = inputs + normed_branch * attn_rows[5] + attn_rows[6]
    gathered_fc1, gathered_fc2, ffn_rows, wide_rows = (
        lax.all_gather(w_fc1.astype(brain), ("dp", "seq"), axis=0, tiled=True),
        lax.all_gather(w_fc2.astype(brain), ("dp", "seq"), axis=0, tiled=True),
        lax.all_gather(ffn_vecs.astype(brain), ("dp", "seq"), axis=1, tiled=True),
        lax.all_gather(ffn_wide.astype(brain), ("dp", "seq"), axis=1, tiled=True),
    )
    ffn_rows = ffn_rows.astype(single)
    wide_rows = wide_rows.astype(single)
    normed_two, inv_two = normalize(hidden)
    act_two = (normed_two * ffn_rows[0] + ffn_rows[1]).astype(brain)
    inner_act = jnp.dot(act_two, gathered_fc1, preferred_element_type=single) + wide_rows[0]
    activated, gelu_pull = jax.vjp(gelu_exact, inner_act)
    normed_three, inv_three = normalize(activated)
    mixed_act = (normed_three * wide_rows[1] + wide_rows[2]).astype(brain)
    result = hidden + jnp.dot(mixed_act, gathered_fc2, preferred_element_type=single) + ffn_rows[2]
    outputs = result.astype(brain).reshape(row_count, span_len, model_width)
    back_set = (
        lax.all_gather(w_qkv.astype(brain), ("dp", "seq"), axis=0, tiled=True),
        lax.all_gather(w_out.astype(brain), ("dp", "seq"), axis=0, tiled=True),
        lax.all_gather(attn_vecs.astype(brain), ("dp", "seq"), axis=1, tiled=True),
        lax.all_gather(w_fc1.astype(brain), ("dp", "seq"), axis=0, tiled=True),
        lax.all_gather(w_fc2.astype(brain), ("dp", "seq"), axis=0, tiled=True),
        lax.all_gather(ffn_vecs.astype(brain), ("dp", "seq"), axis=1, tiled=True),
        lax.all_gather(ffn_wide.astype(brain), ("dp", "seq"), axis=1, tiled=True),
    )
    gathered_qkv, gathered_out, attn_back, gathered_fc1, gathered_fc2, ffn_back, wide_back = (
        back_set
    )
    attn_rows = attn_back.astype(single)
    ffn_rows = ffn_back.astype(single)
    wide_rows = wide_back.astype(single)
    grad_top = cotangent.astype(single).reshape(token_count, model_width)
    grad_branch_two = grad_top.astype(brain)
    grad_fc2 = left_grad(mixed_act, grad_branch_two)
    grad_bias_two = jnp.sum(grad_branch_two.astype(single), 0)
    grad_mixed = right_back(grad_branch_two, gathered_fc2)
    grad_inner_gain = jnp.sum(grad_mixed * normed_three, 0)
    grad_inner_bias = jnp.sum(grad_mixed, 0)
    grad_activated = norm_back(grad_mixed * wide_rows[1], normed_three, inv_three)
    grad_inner = gelu_pull(grad_activated)[0].astype(brain)
    grad_fc1 = left_grad(act_two, grad_inner)
    grad_bias_one = jnp.sum(grad_inner.astype(single), 0)
    grad_act_two = right_back(grad_inner, gathered_fc1)
    grad_gain_two = jnp.sum(grad_act_two * normed_two, 0)
    grad_shift_two = jnp.sum(grad_act_two, 0)
    grad_hidden = grad_top + norm_back(grad_act_two * ffn_rows[0], normed_two, inv_two)
    ffn_sums = (
        lax.psum_scatter(grad_fc1, ("dp", "seq"), scatter_dimension=0, tiled=True),
        lax.psum_scatter(grad_fc2, ("dp", "seq"), scatter_dimension=0, tiled=True),
        lax.psum_scatter(
            jnp.stack([grad_gain_two, grad_shift_two, grad_bias_two]),
            ("dp", "seq"),
            scatter_dimension=1,
            tiled=True,
        ),
        lax.psum_scatter(
            jnp.stack([grad_bias_one, grad_inner_gain, grad_inner_bias]),
            ("dp", "seq"),
            scatter_dimension=1,
            tiled=True,
        ),
    )
    grad_post_gain = jnp.sum(grad_hidden * normed_branch, 0)
    grad_post_shift = jnp.sum(grad_hidden, 0)
    grad_branch = norm_back(grad_hidden * attn_rows[5], normed_branch, inv_branch).astype(brain)
    grad_out_bias = jnp.sum(grad_branch.astype(single), 0)
    grad_out = left_grad(scaled, grad_branch)
    grad_scaled = right_back(grad_branch, gathered_out).reshape(
        row_count, span_len, head_count, head_size
    )
    grad_scale = jnp.sum(grad_scaled * attended, (0, 1, 3))
    grad_attended = (grad_scaled * head_scale[None, None, :, None]).astype(brain)
    delta = jnp.transpose(jnp.sum(grad_attended.astype(single) * attended, -1), (0, 2, 1))
    grad_queries, key_parts = attend_back(
        queries_four,
        keys_four,
        values_four,
        grad_attended,
        log_total,
        delta,
        query_pos,
        query_ids,
        doc_ids,
        span_len,
    )
    partial_keys = jnp.transpose(key_parts[0], (1, 0, 2, 3, 4)).reshape(row_count, -1, model_width)
    partial_values = jnp.transpose(key_parts[1], (1, 0, 2, 3, 4)).reshape(
        row_count, -1, model_width
    )
    grad_keys, grad_values = (
        lax.psum_scatter(
            partial_keys.astype(jnp.bfloat16), "seq", scatter_dimension=1, tiled=True
        ).astype(jnp.float32),
        lax.psum_scatter(
            partial_values.astype(jnp.bfloat16), "seq", scatter_dimension=1, tiled=True
        ).astype(jnp.float32),
    )
    grad_qkv = jnp.concatenate(
        [
            grad_queries.reshape(token_count, model_width).astype(brain),
            grad_keys.reshape(token_count, model_width).astype(brain),
            grad_values.reshape(token_count, model_width).astype(brain),
        ],
        1,
    )
    grad_w_qkv = left_grad(act_one, grad_qkv)
    grad_query_bias = jnp.sum(grad_qkv[:, :model_width].astype(single), 0)
    grad_value_bias = jnp.sum(grad_qkv[:, 2 * model_width :].astype(single), 0)
    grad_act_one = right_back(grad_qkv, gathered_qkv)
    grad_gain_one = jnp.sum(grad_act_one * normed_one, 0)
    grad_shift_one = jnp.sum(grad_act_one, 0)
    grad_tokens = (
        (grad_hidden + norm_back(grad_act_one * attn_rows[0], normed_one, inv_one))
        .astype(brain)
        .reshape(row_count, span_len, model_width)
    )
    attn_stack = jnp.stack(
        [
            grad_gain_one,
            grad_shift_one,
            grad_query_bias,
            grad_value_bias,
            grad_out_bias,
            grad_post_gain,
            grad_post_shift,
        ]
    )
    attn_sums = (
        lax.psum_scatter(grad_w_qkv, ("dp", "seq"), scatter_dimension=0, tiled=True),
        lax.psum_scatter(grad_out, ("dp", "seq"), scatter_dimension=0, tiled=True),
        lax.psum_scatter(attn_stack, ("dp", "seq"), scatter_dimension=1, tiled=True),
    )
    scale_total = lax.psum(grad_scale, ("dp", "seq"))
    return (
        outputs,
        grad_tokens,
        attn_sums[0],
        attn_sums[1],
        attn_sums[2],
        scale_total,
        ffn_sums[0],
        ffn_sums[1],
        ffn_sums[2],
        ffn_sums[3],
    )


class Place:
    def __init__(self):
        self.dp = lax.axis_index("dp")
        self.seq = lax.axis_index("seq")
        self.z, self.y = self.dp // NY, self.dp % NY
        self.x, self.c = self.seq // NC, self.seq % NC

    def at(self, z=None, y=None, x=None, c=None):
        z = self.z if z is None else z
        y = self.y if y is None else y
        x = self.x if x is None else x
        c = self.c if c is None else c
        return (z * NY + y, x * NC + c)

    def zup(self, k):
        return (self.z + k) % NZ

    def group(self):
        near = [self.at(c=1 - self.c), self.at(x=1 - self.x), self.at(x=1 - self.x, c=1 - self.c)]
        return near + [self.at(y=1 - self.y)] + [self.at(z=self.zup(k)) for k in range(1, NZ)]


class Copy:
    def __init__(self, desc):
        self.desc, self.sent = desc, False

    def go(self):
        self.desc.start()
        return self

    def wait_recv(self):
        self.desc.wait_recv()

    def wait_send(self):
        if not self.sent:
            self.desc.wait_send()
        self.sent = True


class Wire:
    def __init__(self, place, send, recv):
        self.place, self.send, self.recv, self.used, self.open = place, send, recv, 0, []

    def copy(self, src, dst, dev):
        n = self.used
        self.used += 1
        copy = Copy(
            pltpu.make_async_remote_copy(
                src_ref=src,
                dst_ref=dst,
                send_sem=self.send.at[n],
                recv_sem=self.recv.at[n],
                device_id=dev,
                device_id_type=MESH,
            )
        )
        self.open.append(copy)
        return copy

    def drain(self):
        for copy in self.open:
            copy.wait_send()


def greet(place):
    barrier = pltpu.get_barrier_semaphore()
    group = place.group()
    for dev in group:
        pl.semaphore_signal(barrier, inc=1, device_id=dev, device_id_type=MESH)
    pl.semaphore_wait(barrier, len(group))


def spread_zxy(wire, place, ref, swap=False):
    z, y, x = place.z, place.y, place.x
    own = ref.at[z, y, x]
    first = place.at(y=1 - y) if swap else place.at(x=1 - x)
    second = place.at(x=1 - x) if swap else place.at(y=1 - y)
    order = [(z - k + NZ) % NZ for k in range(NZ)]
    along_z = [wire.copy(own, own, place.at(z=place.zup(k))) for k in range(1, NZ)]
    firsts = [wire.copy(ref.at[zk, y, x], ref.at[zk, y, x], first) for zk in order]
    twos = [ref.at[zk, :, x] if swap else ref.at[zk, y] for zk in order]
    seconds = [wire.copy(two, two, second) for two in twos]
    yield
    for copy in along_z + firsts[:1]:
        copy.go()
    yield
    for k in range(1, NZ):
        along_z[k - 1].wait_recv()
        firsts[k].go()
        yield
    for k in range(NZ):
        firsts[k].wait_recv()
        seconds[k].go()
        yield
    for copy in seconds:
        copy.wait_recv()


def spread_xzy(wire, place, ref, swap=False):
    z, y, x = place.z, place.y, place.x
    own = ref.at[z, y, x]
    first = place.at(y=1 - y) if swap else place.at(x=1 - x)
    second = place.at(x=1 - x) if swap else place.at(y=1 - y)
    order = [(z - k + NZ) % NZ for k in range(NZ)]
    twos = [ref.at[zk, :, x] if swap else ref.at[zk, y] for zk in order]
    start = wire.copy(own, own, first)
    steps = [wire.copy(two, two, place.at(z=place.zup(1))) for two in twos[:-1]]
    seconds = [wire.copy(two, two, second) for two in twos]
    yield
    start.go()
    yield
    start.wait_recv()
    steps[0].go()
    seconds[0].go()
    yield
    for k in range(1, NZ):
        steps[k - 1].wait_recv()
        if k < NZ - 1:
            steps[k].go()
        seconds[k].go()
        yield
    for copy in seconds:
        copy.wait_recv()


def spread_pair(wire, place, ref):
    plane = ref.at[:, :, :, place.c]
    last = wire.copy(plane, plane, place.at(c=1 - place.c))
    yield from spread_xzy(wire, place, plane)
    last.go()
    yield
    last.wait_recv()


def spread_dp(wire, place, views):
    z, y = place.z, place.y
    at = [z * NY + y] + [((z - n + NZ) % NZ) * NY + y for n in range(1, NZ)]
    along_z = [[wire.copy(view(at[0]), view(at[0]), place.at(z=place.zup(n))) for view in views] for n in range(1, NZ)]
    ys = [[wire.copy(view(d), view(d), place.at(y=1 - y)) for view in views] for d in at]
    yield
    for copies in along_z + ys[:1]:
        for copy in copies:
            copy.go()
    yield
    for n in range(1, NZ):
        for copy in along_z[n - 1]:
            copy.wait_recv()
        for copy in ys[n]:
            copy.go()
        yield
    for copies in ys:
        for copy in copies:
            copy.wait_recv()


def spread_row(wire, place, tok, tok_all):
    s, other, core = place.seq, place.at(x=1 - place.x), place.at(c=1 - place.c)
    far = tok_all.at[s ^ 2]
    tok_x = wire.copy(tok, tok_all.at[s], other)
    tok_c = wire.copy(tok, tok_all.at[s], core)
    last = wire.copy(far, far, core)
    yield
    tok_c.go()
    tok_x.go()
    yield
    tok_c.wait_recv()
    yield
    tok_x.wait_recv()
    last.go()
    yield
    last.wait_recv()


class Plan:
    def __init__(self, tasks, order):
        self.tasks, self.order = tasks, list(order)
        for task in tasks.values():
            next(task)

    def hook(self):
        for name in self.order.pop(0):
            next(self.tasks[name], None)

    def finish(self):
        while self.order:
            self.hook()
        for task in self.tasks.values():
            for _ in task:
                pass


COPIES = 104


def nt(a, b):
    return lax.dot_general(a, b, (((1,), (1,)), ((), ())), preferred_element_type=F32)


def nn(a, b):
    return lax.dot_general(a, b, (((1,), (0,)), ((), ())), preferred_element_type=F32)


def pair_bias(idr, key_ids, qb, kb, size):
    qs = pl.multiple_of(qb * size, size)
    key_pos = kb * size + lax.broadcasted_iota(jnp.int32, (size, size), 0)
    query_pos = qs + lax.broadcasted_iota(jnp.int32, (size, size), 1)
    same = key_ids == idr[:, pl.ds(qs, size)]
    return jnp.where((key_pos <= query_pos) & same, 0.0, NEGATIVE)


def mask_heads(dst, src, heads, head):
    lane = lax.broadcasted_iota(jnp.int32, src.shape, 1) // head
    whole = src[...]
    for h in range(heads):
        dst[h] = jnp.where(lane == h, whole, jnp.zeros_like(whole))


FORWARD = (
    "tqbaoboqqqddaaaaaabqtt",
    "",
    "tao",
    "d",
    "",
    "bo",
    "",
    "d",
    "",
    "a",
    "b",
    "o",
    "",
    "d",
    "",
    "",
    "obod",
)


def forward_tasks(wire, place, tok, tok_all, wq, rows_all, wide_all, lane, wo_all, f1_all, f2_all):
    group = NX * NC
    half1 = f1_all.shape[4] // 2
    views = [
        lambda d: wq.at[d],
        lambda d: rows_all.at[:, pl.ds(pl.multiple_of(d * lane, lane), lane)],
        lambda d: wide_all.at[:, pl.ds(pl.multiple_of(d * lane * group, lane * group), lane * group)],
    ]
    return {
        "t": spread_row(wire, place, tok, tok_all),
        "q": spread_dp(wire, place, views),
        "a": spread_zxy(wire, place, f1_all.at[:, :, :, :, pl.ds(0, half1)]),
        "b": spread_xzy(wire, place, f1_all.at[:, :, :, :, pl.ds(half1, half1)], swap=True),
        "o": spread_pair(wire, place, wo_all),
        "d": spread_xzy(wire, place, f2_all),
    }


def forward_kernel(heads, *refs):
    tok, wq4, vec, wo, f1, f2, idr, idc, lanes = refs[:9]
    act, q, k, v, att, lse, own, wq, rows_all, wide_all, wo_all, f1_all, f2_all = refs[9:22]
    tok_all, actv, vecs, km, vt, bias, top, low, acc, scb, send, recv, local = refs[22:]
    place = Place()
    z, y, x, c, s, dp = place.z, place.y, place.x, place.c, place.seq, place.dp
    group = NX * NC
    wire = Wire(place, send, recv)
    core, other, across = place.at(c=1 - c), place.at(x=1 - x), place.at(x=1 - x, c=1 - c)
    span, width = tok.shape
    rows = f1.shape[1]
    length, part = q.shape
    head = part // heads

    greet(place)
    quarter = []
    for dev, peer in ((core, s ^ 1), (other, s ^ 2), (across, s ^ 3)):
        quarter.append(wire.copy(wq4.at[peer], wq.at[dp, s], dev).go())
        quarter.append(wire.copy(vec, vecs.at[s], dev).go())
    f1_c = wire.copy(f1.at[1 - c], f1_all.at[z, y, x, pl.ds(c * rows, rows)], core).go()
    here = [
        pltpu.make_async_copy(wq4.at[s], wq.at[dp, s], local.at[0]),
        pltpu.make_async_copy(vec, vecs.at[s], local.at[1]),
        pltpu.make_async_copy(tok, tok_all.at[s], local.at[2]),
        pltpu.make_async_copy(wo, wo_all.at[z, y, x, c], local.at[3]),
        pltpu.make_async_copy(f1.at[c], f1_all.at[z, y, x, pl.ds(c * rows, rows)], local.at[4]),
        pltpu.make_async_copy(f2, f2_all.at[z, y, x], local.at[5]),
    ]
    for desc in here:
        desc.start()
    for desc in here:
        desc.wait()
    for desc in quarter:
        desc.wait_recv()

    lane = vec.shape[2]
    blk = pl.multiple_of(dp * lane, lane)
    wide_blk = pl.multiple_of(dp * lane * group, lane * group)
    rows_all[:, pl.ds(blk, lane)] = (vecs[0, 0] + vecs[1, 0]) + (vecs[2, 0] + vecs[3, 0])
    for j in range(group):
        wide_all[:, pl.ds(pl.multiple_of(wide_blk + j * lane, lane), lane)] = vecs[j, 1]

    f1_c.wait_recv()
    plan = Plan(
        forward_tasks(wire, place, tok, tok_all, wq, rows_all, wide_all, lane, wo_all, f1_all, f2_all), FORWARD
    )
    plan.hook()

    shift = pl.multiple_of(s * part, part)
    bias_q = rows_all[2:3, pl.ds(shift, part)].astype(F32)
    bias_v = rows_all[3:4, pl.ds(shift, part)].astype(F32)
    gain, base = rows_all[0:1, :].astype(F32), rows_all[1:2, :].astype(F32)
    keep = []
    for m in range(group):
        j = s ^ m
        plan.hook()
        if m >= 2:
            keep[m - 2].wait()
        slot = actv.at[m % 2]
        step = 64

        def norm_rows(n, _, slot=slot, j=j):
            at = pl.ds(pl.multiple_of(n * step, step), step)
            values = tok_all[j, at, :].astype(F32)
            slot[at, :] = (normalize(values)[0] * gain + base).astype(BF)
            return 0

        lax.fori_loop(0, span // step, norm_rows, 0)
        at = pl.ds(pl.multiple_of(j * span, span), span)
        desc = pltpu.make_async_copy(slot, act.at[at], local.at[6 + m])
        desc.start()
        keep.append(desc)
        for n, (dst, add) in enumerate(((q, bias_q), (k, None), (v, bias_v))):
            weights = wq[:, :, :, n * part : (n + 1) * part].reshape(width, part)
            proj = nn(slot[...], weights)
            if add is not None:
                proj = proj + add
            if n == 0:
                proj = proj * (head**-0.5)
            dst[at, :] = proj.astype(BF)

    plan.hook()
    mask_heads(km, k, heads, head)
    vt[...] = v[...].T
    blocks = length // span
    returns = []
    for qb in reversed(range(blocks)):
        qs = slice(qb * span, (qb + 1) * span)
        top[...] = jnp.full(top.shape, NEGATIVE, F32)
        low[...] = jnp.zeros(low.shape, F32)
        acc[...] = jnp.zeros(acc.shape, F32)

        def keys(step, _, qb=qb, qs=qs):
            kb = qb - step
            ks = pl.ds(pl.multiple_of(kb * span, span), span)
            bias[...] = pair_bias(idr, idc[ks, :], qb, kb, span)
            for h in range(heads):
                scores = nt(km[h, ks, :], q[qs, :]) + bias[...]
                old = top[h : h + 1, :]
                new = jnp.maximum(old, jnp.max(scores, 0, keepdims=True))
                probs = jnp.exp(scores - new)
                shrink = jnp.exp(old - new)
                top[h : h + 1, :] = new
                low[h : h + 1, :] = low[h : h + 1, :] * shrink + jnp.sum(probs, 0, keepdims=True)
                hs = slice(h * head, (h + 1) * head)
                acc[hs, :] = acc[hs, :] * shrink + nn(vt[hs, ks], probs.astype(BF))
            for n in range(qb + 1):

                @pl.when(step == n)
                def _():
                    plan.hook()

            return 0

        lax.fori_loop(0, qb + 1, keys, 0)
        for h in range(heads):
            hs = slice(h * head, (h + 1) * head)
            acc[hs, :] = acc[hs, :] * (1.0 / low[h : h + 1, :])
        att[:, qs] = acc[...]
        lse[:, qs] = top[...] + jnp.log(low[...])
        scb[qb] = (acc[...].T * lanes[...]).astype(BF)
        view = own.at[:, pl.ds(shift, part)]
        back = pltpu.make_async_remote_copy(
            src_ref=scb.at[qb],
            dst_ref=view,
            send_sem=send.at[COPIES - 1 - qb],
            recv_sem=recv.at[COPIES - 4 + (s ^ qb)],
            device_id=(dp, qb),
            device_id_type=MESH,
        )
        mine = pltpu.make_async_copy(scb.at[qb], view, local.at[10])
        returns.append((qb, back, mine))

        @pl.when(s == qb)
        def _():
            mine.start()

        @pl.when(s != qb)
        def _():
            back.start()

    plan.finish()
    for desc in keep[-2:]:
        desc.wait()
    for qb, back, mine in returns:

        @pl.when(s == qb)
        def _():
            mine.wait()

        @pl.when(s != qb)
        def _():
            back.wait_send()

    for m in range(1, group):
        view = own.at[:, pl.ds(pl.multiple_of((s ^ m) * part, part), part)]
        pltpu.make_async_remote_copy(
            src_ref=scb.at[0],
            dst_ref=view,
            send_sem=send.at[COPIES - 1],
            recv_sem=recv.at[COPIES - 4 + m],
            device_id=core,
            device_id_type=MESH,
        ).wait_recv()
    wire.drain()


def forward(tok, wq4, vec, wo, f1, f2, ids, lanes, heads):
    span, width = tok.shape
    group, rows, triple = wq4.shape
    part = triple // 3
    length = span * group
    dps = NZ * NY
    lane = vec.shape[2]
    out = (
        (HBM, (length, width), BF),
        (VM, (length, part), BF),
        (VM, (length, part), BF),
        (VM, (length, part), BF),
        (VM, (part, length), F32),
        (VM, (8, length), F32),
        (VM, (span, width), BF),
        (VM, (dps, group, rows, triple), BF),
        (VM, (16, dps * lane), BF),
        (VM, (16, dps * group * lane), BF),
        (HBM, (NZ, NY, NX, NC) + wo.shape, BF),
        (HBM, (NZ, NY, NX, NC * f1.shape[1], f1.shape[2]), BF),
        (HBM, (NZ, NY, NX) + f2.shape, BF),
    )
    return pl.pallas_call(
        functools.partial(forward_kernel, heads),
        out_shape=tuple(jax.ShapeDtypeStruct(shape, dtype) for _, shape, dtype in out),
        in_specs=[VM] * 9,
        out_specs=[spec for spec, _, _ in out],
        scratch_shapes=[
            pltpu.VMEM((group, span, width), BF),
            pltpu.VMEM((2, span, width), BF),
            pltpu.VMEM((group,) + vec.shape, BF),
            pltpu.VMEM((heads, length, part), BF),
            pltpu.VMEM((part, length), BF),
            pltpu.VMEM((span, span), F32),
            pltpu.VMEM((8, span), F32),
            pltpu.VMEM((8, span), F32),
            pltpu.VMEM((part, span), F32),
            pltpu.VMEM((group, span, part), BF),
            pltpu.SemaphoreType.DMA((COPIES,)),
            pltpu.SemaphoreType.DMA((COPIES,)),
            pltpu.SemaphoreType.DMA((12,)),
        ],
        compiler_params=pltpu.CompilerParams(
            collective_id=1, has_side_effects=True, vmem_limit_bytes=56 * 1024 * 1024
        ),
        name="forward_row",
    )(tok, wq4, vec, wo, f1, f2, ids.reshape(1, length), ids.reshape(length, 1), lanes)


def lead_loop(total, fn, step=16):
    lead, rows = total.shape[:-2], total.shape[-2]
    per = rows // step

    def body(n, _):
        block = n // per
        at = []
        for dim in reversed(lead):
            at.append(block % dim)
            block = block // dim
        fn(tuple(reversed(at)) + (pl.ds(pl.multiple_of((n % per) * step, step), step), slice(None)))
        return 0

    lax.fori_loop(0, math.prod(lead) * per, body, 0)


def add_into(total, term):
    def fn(idx):
        total[idx] = (total[idx].astype(F32) + term[idx].astype(F32)).astype(total.dtype)

    lead_loop(total, fn, 16 if total.dtype == BF else 8)


def reduce_plane(wire, place, grad, own, got, got2, got3, out, local, swap=False):
    z, y, x = place.z, place.y, place.x
    first = place.at(x=1 - x) if swap else place.at(y=1 - y)
    second = place.at(y=1 - y) if swap else place.at(x=1 - x)
    keep, give = (y, 1 - y) if swap else (x, 1 - x)
    order = [place.zup(k) for k in (1, 2, 3, 0)]

    def two(zk, mine):
        if swap:
            return grad.at[zk, :, x if mine else 1 - x]
        return grad.at[zk, y if mine else 1 - y]

    def one(k, i):
        if own is not None:
            return own.at[k, i]
        return grad.at[order[k], i, x] if swap else grad.at[order[k], y, i]

    sends = [wire.copy(two(zk, False), got.at[k], first) for k, zk in enumerate(order)]
    loads = []
    if own is not None:
        loads = [pltpu.make_async_copy(two(zk, True), own.at[k], local.at[k]) for k, zk in enumerate(order)]
    gives = [one(k, give) for k in range(NZ)]
    keeps = [one(k, keep) for k in range(NZ)]
    seconds = [wire.copy(gives[k], got2.at[k], second) for k in range(NZ)]
    along = [wire.copy(keeps[k], got3.at[k], place.at(z=place.zup(k + 1))) for k in range(NZ - 1)]
    yield
    for copy in sends:
        copy.go()
    for desc in loads:
        desc.start()
    yield
    for k in range(NZ):
        if loads:
            loads[k].wait()
        sends[k].wait_recv()
        add_into(gives[k], got.at[k, give])
        seconds[k].go()
        add_into(keeps[k], got.at[k, keep])
        yield
    for k in range(NZ):
        seconds[k].wait_recv()
        add_into(keeps[k], got2.at[k])
        if k < NZ - 1:
            along[k].go()
        yield
    for copy in along:
        copy.wait_recv()
    add_up(out, keeps[NZ - 1], got3)


def plane_scratch(block):
    return [
        pltpu.VMEM((NZ, 2) + block, BF),
        pltpu.VMEM((NZ, 2) + block, BF),
        pltpu.VMEM((NZ,) + block, BF),
        pltpu.VMEM((NZ - 1,) + block, BF),
        pltpu.SemaphoreType.DMA((NZ,)),
    ]


def reduce_outer(wire, place, go, outp, outg, load, scratch, out):
    c = place.c
    swap_o = wire.copy(go.at[:, :, :, 1 - c], outg, place.at(c=1 - c))
    load_o = pltpu.make_async_copy(go.at[:, :, :, c], outp, load)
    rest = reduce_plane(wire, place, outp, *scratch[:4], out, scratch[4], swap=True)
    next(rest)
    yield
    swap_o.go()
    load_o.start()
    yield
    load_o.wait()
    swap_o.wait_recv()
    add_into(outp, outg)
    yield from rest


def reduce_first(wire, place, g1, buf, got, scratch, out):
    c = place.c
    rows = got.shape[0]
    part = wire.copy(buf.at[pl.ds((1 - c) * rows, rows)], got, place.at(c=1 - c))
    yield from reduce_plane(wire, place, g1, *scratch[:4], buf, scratch[4])
    part.go()
    lane = out.shape[1] // (NZ * NY * NX * NC)
    spread_columns(out, buf, pl.multiple_of(c * rows, rows), c, lane)
    yield
    part.wait_recv()
    spread_columns(out, got, 0, 1 - c, lane)


def spread_columns(out, src, row, c, lane):
    rows = out.shape[0]
    for n in range(NZ * NY * NX):
        at = pl.ds(pl.multiple_of((n * NC + c) * lane, lane), lane)
        out[:, at] = src[pl.ds(row, rows), n * lane : (n + 1) * lane]


def reduce_quarter(wire, place, gq, own, got, got2, total, buf, out, local):
    y, s = place.y, place.seq
    order = [place.zup(n) for n in (1, 2, 3, 0)]
    sends = [wire.copy(gq.at[zk, 1 - y], got.at[n], place.at(y=1 - y)) for n, zk in enumerate(order)]
    along = [wire.copy(own.at[n], got2.at[n], place.at(z=place.zup(n + 1))) for n in range(NZ - 1)]
    near = ((place.at(c=1 - place.c), 1), (place.at(x=1 - place.x), 2), (place.at(x=1 - place.x, c=1 - place.c), 3))
    parts = [wire.copy(total.at[s ^ m], buf.at[s], dev) for dev, m in near]
    loads = [pltpu.make_async_copy(gq.at[zk, y], own.at[n], local.at[n]) for n, zk in enumerate(order)]
    mine = pltpu.make_async_copy(total.at[s], buf.at[s], local.at[NZ])
    yield
    for copy in sends:
        copy.go()
    for desc in loads:
        desc.start()
    yield
    for n in range(NZ):
        loads[n].wait()
        sends[n].wait_recv()
        add_into(own.at[n], got.at[n])
        if n < NZ - 1:
            along[n].go()
        yield
    for copy in along:
        copy.wait_recv()
    add_up(total, own.at[NZ - 1], got2)
    for copy in parts:
        copy.go()
    mine.start()
    yield
    mine.wait()
    for copy in parts:
        copy.wait_recv()
    group = NX * NC
    part = buf.shape[2] // 3
    for j in range(group):
        for n in range(3):
            at = (n * group + j) * part
            out[:, at : at + part] = buf[j, :, n * part : (n + 1) * part].astype(F32)


def reduce_vectors(wire, place, pairs):
    z, y = place.z, place.y
    sizes = [g.shape[1] // (NZ * NY) for g, *_ in pairs]

    def cols(n, zk, yk):
        return pl.ds(pl.multiple_of((zk * NY + yk) * sizes[n], sizes[n]), sizes[n])

    cs = [wire.copy(g, t.at[0], place.at(c=1 - place.c)) for g, t, *_ in pairs]
    xs = [wire.copy(g, t.at[1], place.at(x=1 - place.x)) for g, t, *_ in pairs]
    ys, zs = [], []
    for n, (g, t, got, _) in enumerate(pairs):
        for zk in range(NZ):
            at = cols(n, zk, 1 - y)
            ys.append(wire.copy(g.at[:, at], t.at[2, :, at], place.at(y=1 - y)))
        for k in range(1, NZ):
            at = cols(n, place.zup(k), y)
            zs.append(wire.copy(g.at[:, at], got.at[z], place.at(z=place.zup(k))))
    yield
    for copy in cs:
        copy.go()
    yield
    for copies, slot in ((cs, 0), (xs, 1)):
        for copy, (g, t, *_) in zip(copies, pairs):
            copy.wait_recv()
            copy.wait_send()
            add_rows(g, t.at[slot])
        for copy in xs if slot == 0 else ys:
            copy.go()
        yield
    for copy in ys:
        copy.wait_recv()
    for n, (g, t, got, _) in enumerate(pairs):
        for zk in range(NZ):
            at = cols(n, zk, y)
            add_rows(g.at[:, at], t.at[2, :, at])
    for copy in zs:
        copy.go()
    for n, (g, t, got, _) in enumerate(pairs):
        keep_rows(got.at[z], g.at[:, cols(n, z, y)])
    yield
    for copy in zs:
        copy.wait_recv()
    for g, t, got, out in pairs:
        add_fixed(out, got)


def add_rows(total, term):
    total[...] += term[...]


def keep_rows(dst, src):
    dst[...] = src[...]


def add_fixed(out, got):
    total = got[0]
    for k in range(1, NZ):
        total = total + got[k]
    out[...] = total


def add_up(out, own, got):
    def fn(idx):
        value = own[idx].astype(F32)
        for k in range(NZ - 1):
            value = value + got[(k,) + idx].astype(F32)
        out[idx] = value.astype(out.dtype)

    lead_loop(out, fn)


BACKWARD = (
    "o1",
    "o",
    "oo1o",
    "o",
    "",
    "1",
    "1",
    "",
    "",
    "oooo1111",
    "",
    "o1",
    "q",
    "",
    "q11qqq",
    "vvqvqvv",
)


def backward_kernel(heads, *refs):
    q, k, v, att, lse, do, idr, wq, grad_hidden, rows_in, wide_in, gain = refs[:12]
    tok, act, g1, go = refs[12:16]
    grad_tok, out1, outo, outq, outr, outw = refs[16:22]
    (km, vm, qm, dm, kt, idc, bias, acck, accv, accq, accw, delta, blk, actb) = refs[22:36]
    (dap, dgot, dfin, ownq, gotq, gotqb, sumq, outq_buf, gq, gotp, f1buf, f1got) = refs[36:48]
    (rowg, rowt, rowz, wideg, widet, widez, outp, outg) = refs[48:56]
    plane1, planeo = refs[56:61], refs[61:66]
    send, recv, local, dsend, drecv = refs[66:]
    place = Place()
    z, y, x, c, s, dp = place.z, place.y, place.x, place.c, place.seq, place.dp
    group = NX * NC
    wire = Wire(place, send, recv)
    core, other, across = place.at(c=1 - c), place.at(x=1 - x), place.at(x=1 - x, c=1 - c)
    length, part = q.shape
    span, width = tok.shape
    head = part // heads
    blocks = length // span
    shift = pl.multiple_of(s * part, part)

    greet(place)
    plan = Plan(
        {
            "1": reduce_first(wire, place, g1, f1buf, f1got, plane1, out1),
            "o": reduce_outer(wire, place, go, outp, outg, local.at[1], planeo, outo),
            "q": reduce_quarter(wire, place, gq, ownq, gotq, gotqb, sumq, outq_buf, outq, local.at[pl.ds(6, NZ + 1)]),
            "v": reduce_vectors(wire, place, ((rowg, rowt, rowz, outr), (wideg, widet, widez, outw))),
        },
        BACKWARD,
    )
    plan.hook()

    mask_heads(qm, q, heads, head)
    accq[...] = jnp.zeros(accq.shape, F32)
    accw[...] = jnp.zeros(accw.shape, F32)
    delta[...] = jnp.zeros(delta.shape, F32)
    plan.hook()
    mask_heads(dm, do, heads, head)
    for b in range(blocks):
        at = slice(b * span, (b + 1) * span)
        weighted = do[at, :].T.astype(F32) * att[:, at]
        for h in range(heads):
            delta[h : h + 1, at] = jnp.sum(weighted[h * head : (h + 1) * head, :], 0, keepdims=True)

    hops = []
    for t in range(blocks):
        tx, tc = t // NC, t % NC
        inner = pltpu.make_async_remote_copy(
            src_ref=dap.at[t],
            dst_ref=dgot.at[tx],
            send_sem=dsend.at[2 * t],
            recv_sem=drecv.at[2 * t],
            device_id=core,
            device_id_type=MESH,
        )
        outerc = pltpu.make_async_remote_copy(
            src_ref=dap.at[t],
            dst_ref=dfin,
            send_sem=dsend.at[2 * t + 1],
            recv_sem=drecv.at[2 * t + 1],
            device_id=other,
            device_id_type=MESH,
        )
        hops.append((tx, tc, inner, outerc))

    def meet(t):
        tx, tc, inner, outerc = hops[t]

        @pl.when(c == tc)
        def _():
            inner.wait_recv()
            add_into(dap.at[t], dgot.at[tx])

            @pl.when(x != tx)
            def _():
                outerc.start()

    fetch = [
        pltpu.make_async_copy(act.at[pl.ds(b * span, span)], actb.at[b % 2], local.at[2 + b]) for b in range(blocks)
    ]
    fetch[0].start()

    for kb in range(blocks):
        ks = slice(kb * span, (kb + 1) * span)
        if kb + 1 < blocks:
            fetch[kb + 1].start()
        mask_heads(km, k.at[ks], heads, head)
        mask_heads(vm, v.at[ks], heads, head)
        kt[...] = k[ks, :].T
        idc[...] = jnp.broadcast_to(idr[:, ks], (8, span)).T
        acck[...] = jnp.zeros(acck.shape, F32)
        accv[...] = jnp.zeros(accv.shape, F32)

        def queries(qb, _, kb=kb, ks=ks):
            qs = pl.ds(pl.multiple_of(qb * span, span), span)
            bias[...] = pair_bias(idr, idc[:, 0:1], qb, kb, span)
            for h in range(heads):
                scores = nt(km[h], q[qs, :]) + bias[...]
                probs = jnp.exp(scores - lse[h : h + 1, qs])
                grad = nt(vm[h], do[qs, :])
                ds = (probs * (grad - delta[h : h + 1, qs])).astype(BF)
                accv[...] += nn(probs.astype(BF), dm[h, qs, :])
                acck[...] += nn(ds, qm[h, qs, :])
                hs = slice(h * head, (h + 1) * head)
                accq[hs, qs] += nn(kt[hs, :], ds)
            for n in range(kb, blocks):

                @pl.when(qb == n)
                def _():
                    if n == blocks - 1 and kb > 0:
                        meet(kb - 1)
                    plan.hook()

            return 0

        lax.fori_loop(kb, blocks, queries, 0)
        blk[:, :part] = (accq[:, ks].T * (head**-0.5)).astype(BF)
        blk[:, part : 2 * part] = acck[...].astype(BF)
        blk[:, 2 * part :] = accv[...].astype(BF)
        sums = jnp.sum(blk[...].astype(F32), 0, keepdims=True)
        if kb == 0:
            gotp[...] = jnp.zeros(gotp.shape, F32)
        gotp[0:1, :] += sums
        fetch[kb].wait()
        step = 256
        for n in range(0, width, step):
            accw[n : n + step, :] += lax.dot_general(
                actb[kb % 2, :, n : n + step], blk[...], (((0,), (0,)), ((), ())), preferred_element_type=F32
            )
        if kb == blocks - 1:
            gq[...] = accw[...].astype(BF).reshape(gq.shape)
            plan.hook()
        weights = wq[...].reshape(width, 3 * part)
        for n in range(0, width, step):
            dap[kb, :, n : n + step] = nt(blk[...], weights[n : n + step, :]).astype(BF)
        tx, tc, inner, outerc = hops[kb]

        @pl.when(c != tc)
        def _():
            inner.start()

    fetch_tok = pltpu.make_async_copy(tok, actb.at[0], local.at[11])
    fetch_tok.start()
    plan.hook()
    meet(blocks - 1)
    plan.hook()

    step = 64
    rowg[...] = rows_in[...]
    wideg[...] = wide_in[...]
    lane_sum = jnp.sum(delta[...], 1, keepdims=True)
    for j in range(group):
        rowg[16 + j * heads : 16 + (j + 1) * heads, :] = jnp.where(
            s == j, jnp.broadcast_to(lane_sum[:heads], (heads, width)), 0.0
        )
    rowg[2:3, pl.ds(shift, part)] = gotp[0:1, :part]
    rowg[3:4, pl.ds(shift, part)] = gotp[0:1, 2 * part :]
    for t in range(blocks):
        tx, tc, inner, outerc = hops[t]

        @pl.when((x == tx) & (c == tc))
        def _():
            outerc.wait_recv()

    fetch_tok.wait()

    def finish(n, carry):
        at = pl.ds(pl.multiple_of(n * step, step), step)
        da = dap[s, at, :].astype(F32) + dfin[at, :].astype(F32)
        normed, inv = normalize(actb[0, at, :].astype(F32))
        grad = norm_back(da * gain[...], normed, inv) + grad_hidden[at, :]
        grad_tok[at, :] = grad.astype(BF)
        return (
            carry[0] + jnp.sum(da * normed, 0, keepdims=True),
            carry[1] + jnp.sum(da, 0, keepdims=True),
        )

    zero = jnp.zeros((1, width), F32)
    gain_one, shift_one = lax.fori_loop(0, span // step, finish, (zero, zero))
    rowg[0:1, :] = gain_one
    rowg[1:2, :] = shift_one

    plan.finish()
    for t in range(blocks):
        tx, tc, inner, outerc = hops[t]

        @pl.when(c != tc)
        def _():
            inner.wait_send()

        @pl.when((c == tc) & (x != tx))
        def _():
            outerc.wait_send()

    wire.drain()


def backward(do, q, k, v, att, lse, ids, wq, tok, grad_hidden, rows_in, wide_in, gain, act, g1, go, heads):
    length, part = q.shape
    span, width = tok.shape
    group = length // span
    b1, bo = g1.shape[3:], go.shape[4:]
    rows, triple = wq.shape[2:]
    bq = (group, rows, triple)
    dps = NZ * NY
    out = (
        (VM, (span, width), BF),
        (VM, (b1[0] // NC, NC * b1[1]), F32),
        (VM, bo, F32),
        (VM, (rows, group * triple), F32),
        (VM, (rows_in.shape[0], width // dps), F32),
        (VM, (wide_in.shape[0], wide_in.shape[1] // dps), F32),
    )
    scratch = [
        pltpu.VMEM((heads, span, part), BF),
        pltpu.VMEM((heads, span, part), BF),
        pltpu.VMEM((heads, length, part), BF),
        pltpu.VMEM((heads, length, part), BF),
        pltpu.VMEM((part, span), BF),
        pltpu.VMEM((span, 8), jnp.int32),
        pltpu.VMEM((span, span), F32),
        pltpu.VMEM((span, part), F32),
        pltpu.VMEM((span, part), F32),
        pltpu.VMEM((part, length), F32),
        pltpu.VMEM((width, triple), F32),
        pltpu.VMEM((8, length), F32),
        pltpu.VMEM((span, triple), BF),
        pltpu.VMEM((2, span, width), BF),
        pltpu.VMEM((group, span, width), BF),
        pltpu.VMEM((NX, span, width), BF),
        pltpu.VMEM((span, width), BF),
        pltpu.VMEM((NZ,) + bq, BF),
        pltpu.VMEM((NZ,) + bq, BF),
        pltpu.VMEM((NZ - 1,) + bq, BF),
        pltpu.VMEM(bq, BF),
        pltpu.VMEM(bq, BF),
        pltpu.VMEM((NZ, NY) + bq, BF),
        pltpu.VMEM((8, triple), F32),
        pltpu.VMEM(b1, F32),
        pltpu.VMEM((b1[0] // NC, b1[1]), F32),
        pltpu.VMEM(rows_in.shape, F32),
        pltpu.VMEM((3,) + rows_in.shape, F32),
        pltpu.VMEM((NZ, rows_in.shape[0], width // dps), F32),
        pltpu.VMEM(wide_in.shape, F32),
        pltpu.VMEM((3,) + wide_in.shape, F32),
        pltpu.VMEM((NZ, wide_in.shape[0], wide_in.shape[1] // dps), F32),
        pltpu.VMEM((NZ, NY, NX) + bo, BF),
        pltpu.VMEM((NZ, NY, NX) + bo, BF),
    ]
    scratch += plane_scratch(b1) + plane_scratch(bo)
    scratch += [
        pltpu.SemaphoreType.DMA((COPIES,)),
        pltpu.SemaphoreType.DMA((COPIES,)),
        pltpu.SemaphoreType.DMA((12,)),
        pltpu.SemaphoreType.DMA((2 * group,)),
        pltpu.SemaphoreType.DMA((2 * group,)),
    ]
    return pl.pallas_call(
        functools.partial(backward_kernel, heads),
        out_shape=tuple(jax.ShapeDtypeStruct(shape, dtype) for _, shape, dtype in out),
        in_specs=[VM] * 12 + [HBM] * 4,
        out_specs=[spec for spec, _, _ in out],
        scratch_shapes=scratch,
        compiler_params=pltpu.CompilerParams(
            collective_id=2, has_side_effects=True, vmem_limit_bytes=63 * 1024 * 1024
        ),
        name="backward_row",
    )(
        q, k, v, att, lse, do, ids.reshape(1, length), wq, grad_hidden, rows_in, wide_in, gain,
        tok, act, g1, go,
    )


MIDDLE = (
    "ce",
    "",
    "cccc",
    "ccceeee",
    "",
    "23ceee232323232e",
    "22332",
    "33",
    "",
    "2",
    "",
    "",
    "3",
    "",
    "",
    "",
)


def middle_tasks(wire, place, f2c, g2, scratch, out2):
    some = f2c.shape[3] // 2
    half = g2.shape[3] // 2
    one, two = pl.ds(0, half), pl.ds(half, half)
    upper, lower = scratch[:3], scratch[3:]
    return {
        "c": spread_zxy(wire, place, f2c.at[:, :, :, pl.ds(0, some)]),
        "e": spread_zxy(wire, place, f2c.at[:, :, :, pl.ds(some, some)], swap=True),
        "2": reduce_plane(wire, place, g2.at[:, :, :, one], None, *upper, out2.at[one], None, swap=True),
        "3": reduce_plane(wire, place, g2.at[:, :, :, two], None, *lower, out2.at[two], None),
    }


def tn(a, b):
    return lax.dot_general(a, b, (((0,), (0,)), ((), ())), preferred_element_type=F32)


def fold(value, rows=16):
    total = value[:rows]
    for n in range(1, value.shape[0] // rows):
        total = total + value[n * rows : (n + 1) * rows]
    return total


def lanes_of(value):
    total = value[:, :128]
    for n in range(1, value.shape[1] // 128):
        total = total + value[:, n * 128 : (n + 1) * 128]
    return total


def row_steps(count, step, fn):
    def body(n, _):
        fn(pl.ds(pl.multiple_of(n * step, step), step))
        return 0

    lax.fori_loop(0, count // step, body, 0)


def ffn_kernel(*refs):
    own, rows_all, wide_all, lanes = refs[:4]
    tok, cot, f2own, f2d, wo, f1 = refs[4:10]
    out, do, gh, g1, go, out2, rows_g, wide_g = refs[10:18]
    wov, f1v, f2v, dt, act, buf, slope, mix, dm, br, hid, g2, dbuf, prb, prc, stg, wv = refs[18:35]
    stat, stat_got, back, back_got, sums, colsums = refs[35:41]
    plane2 = refs[41:47]
    send, recv, local = refs[47:50]
    lane_mean, lane_square = dm.at[:, pl.ds(0, 128)], dm.at[:, pl.ds(128, 128)]
    place = Place()
    z, y, x, c, s = place.z, place.y, place.x, place.c, place.seq
    wire = Wire(place, send, recv)
    core = place.at(c=1 - c)
    span, width = own.shape
    units = f1v.shape[4]
    group = NX * NC
    tile = 512
    tiles = units // tile
    total_units = units * NC

    half = f2own.shape[0]
    f2c = f2v.at[:, :, :, pl.ds(0, half)]
    loads = [
        pltpu.make_async_copy(wo, wov, local.at[0]),
        pltpu.make_async_copy(f2own, f2c.at[z, y, x], local.at[1]),
        pltpu.make_async_copy(cot, dt.at[c], local.at[2]),
        pltpu.make_async_copy(f1, f1v, local.at[3]),
        pltpu.make_async_copy(f2d, f2v.at[:, :, :, pl.ds(half, half)], local.at[4]),
        pltpu.make_async_copy(tok, prc, local.at[5]),
    ]
    for desc in loads:
        desc.start()
    chunk = span // 4
    chunks = [pl.ds(n * chunk, chunk) for n in range(4)]
    dt_copy = wire.copy(cot, dt.at[c], core)
    act_copies = [wire.copy(act.at[c, at], act.at[c, at], core) for at in chunks]
    stat_copies = [wire.copy(stat.at[h], stat_got.at[h], core) for h in range(NC)]
    back_copies = [wire.copy(back.at[h], back_got.at[h], core) for h in range(NC)]
    out_copy = wire.copy(dbuf, prb, core)
    da_copy = wire.copy(prb, prc, core)
    mine_at = pl.ds(pl.multiple_of(s * span, span), span)
    part_size = width // group

    def give(j):
        return prb.at[:, pl.ds(pl.multiple_of(j * part_size, part_size), part_size)]

    outgoing = [
        wire.copy(give(s ^ m), do.at[mine_at], dev)
        for dev, m in ((core, 1), (place.at(x=1 - x), 2), (place.at(x=1 - x, c=1 - c), 3))
    ]
    loads[1].wait()
    greet(place)
    dt_copy.go()
    plan = Plan(middle_tasks(wire, place, f2c, g2, plane2, out2), MIDDLE)
    plan.hook()

    def row(ref, n):
        return ref[n : n + 1, :].astype(F32)

    lane = wide_all.shape[1] // (NZ * NY * NX * NC)
    for n in range(NZ * NY * NX):
        at = pl.ds(pl.multiple_of((n * NC + c) * lane, lane), lane)
        wv[0:3, n * lane : (n + 1) * lane] = wide_all[0:3, at].astype(F32)
    colsums[...] = jnp.zeros(colsums.shape, F32)
    sums[...] = jnp.zeros(sums.shape, F32)
    loads[0].wait()
    loads[5].wait()

    for at, copy in zip(chunks, act_copies):
        branch = nn(own[at, :], wov[...].reshape(width, width)) + row(rows_all, 4)
        br[at, :] = branch

        def fn(inner, at=at):
            rows = pl.ds(at.start + inner.start, inner.size)
            hidden = prc[rows, :].astype(F32) + normalize(br[rows, :])[0] * row(rows_all, 5) + row(rows_all, 6)
            hid[rows, :] = hidden
            act[c, rows, :] = (normalize(hidden)[0] * row(rows_all, 7) + row(rows_all, 8)).astype(BF)

        row_steps(chunk, 64, fn)
        copy.go()
    plan.hook()
    loads[3].wait()

    for h in range(NC):

        @pl.when(c != h)
        def _():
            for copy in act_copies:
                copy.wait_recv()

        for n in range(tiles):
            cols = slice(n * tile, (n + 1) * tile)
            weights = f1v[:, :, :, :, cols].reshape(width, tile)
            buf[h, :, cols] = nn(act[h], weights) + wv[0:1, cols]

        def fn(at, h=h):
            count = units // 128
            pivot = None
            for n in range(tiles):
                cols = slice(n * tile, (n + 1) * tile)
                u = buf[h, at, cols]
                cdf = 0.5 + 0.5 * lax.erf(u * math.sqrt(0.5))
                value = u * cdf
                buf[h, at, cols] = value
                pdf = jnp.exp(-0.5 * u * u) * (1.0 / math.sqrt(2.0 * math.pi))
                slope[h, at, cols] = (cdf + u * pdf).astype(BF)
                if pivot is None:
                    pivot = value[:, :128]
                    total, square = jnp.zeros_like(pivot), jnp.zeros_like(pivot)
                for j in range(tile // 128):
                    gap = value[:, j * 128 : (j + 1) * 128] - pivot
                    total = total + gap
                    square = square + gap * gap
            shift = total * (1.0 / count)
            lane_mean[at, :] = pivot + shift
            lane_square[at, :] = square - total * shift

        row_steps(span, 32, fn)

        def fn(at, h=h):
            count = units // 128
            means = lane_mean[at, :]
            mean = jnp.mean(means, 1, keepdims=True)
            gap = means - mean
            square = jnp.sum(lane_square[at, :] + count * (gap * gap), 1, keepdims=True)
            column = lax.broadcasted_iota(jnp.int32, (at.size, 128), 1)
            stat[h, at, :] = jnp.where(column == 0, mean, square)

        row_steps(span, 128, fn)
        stat_copies[h].go()
        plan.hook()

    for h in range(NC):
        stat_copies[h].wait_recv()
        stat_copies[h].wait_send()

        def fn(at, h=h):
            mean_a, mean_b = stat[h, at, 0:1], stat_got[h, at, 0:1]
            gap = mean_a - mean_b
            square = stat[h, at, 1:2] + stat_got[h, at, 1:2] + gap * gap * (0.5 * units)
            mean = 0.5 * (mean_a + mean_b)
            inv = lax.rsqrt(square * (1.0 / total_units) + EPSILON)
            stat[h, at, :] = jnp.broadcast_to(inv, (at.size, 128))
            for n in range(tiles):
                cols = slice(n * tile, (n + 1) * tile)
                normed = (buf[h, at, cols] - mean) * inv
                buf[h, at, cols] = normed
                mix[h, at, cols] = (normed * wv[1:2, cols] + wv[2:3, cols]).astype(BF)

        row_steps(span, 64, fn)
    plan.hook()

    loads[2].wait()
    loads[4].wait()
    dt_copy.wait_recv()
    per = g2.shape[3]
    for n in range(units // (2 * per)):
        cols = slice(n * 2 * per, (n + 1) * 2 * per)
        part = tn(mix[0, :, cols], dt[0]) + tn(mix[1, :, cols], dt[1])
        g2[n // NY, n % NY] = part.astype(BF).reshape(NX, per, width)
    plan.hook()

    weights2 = f2v[...].reshape(units, width)
    for n in range(0, width, tile):
        dbuf[:, n : n + tile] = nn(mix[1 - c], weights2[:, n : n + tile]).astype(BF)
    out_copy.go()
    for n in range(0, width, tile):
        cols = slice(n, n + tile)
        gh[:, cols] = nn(mix[c], weights2[:, cols]) + hid[:, cols] + rows_all[9:10, cols].astype(F32)
    plan.hook()

    for h in range(NC):
        for n in range(tiles):
            cols = slice(n * tile, (n + 1) * tile)
            dm[:, cols] = nt(dt[h], weights2[cols, :])

        def fn(at, h=h):
            first = jnp.zeros((at.size, 128), F32)
            second = jnp.zeros((at.size, 128), F32)
            for n in range(tiles):
                cols = slice(n * tile, (n + 1) * tile)
                grad = dm[at, cols]
                product = grad * buf[h, at, cols]
                colsums[1, :, cols] += fold(product)
                colsums[2, :, cols] += fold(grad)
                first = first + lanes_of(grad * wv[1:2, cols])
                second = second + lanes_of(product * wv[1:2, cols])
            column = lax.broadcasted_iota(jnp.int32, (at.size, 128), 1)
            first = jnp.sum(first, 1, keepdims=True)
            second = jnp.sum(second, 1, keepdims=True)
            back[h, at, :] = jnp.where(column == 0, first, second)

        row_steps(span, 64, fn)
        back_copies[h].go()
        plan.hook()
        back_copies[h].wait_recv()

        def fn(at, h=h):
            scale = 1.0 / total_units
            first = (back[h, at, 0:1] + back_got[h, at, 0:1]) * scale
            second = (back[h, at, 1:2] + back_got[h, at, 1:2]) * scale
            inv = stat[h, at, 0:1]
            for n in range(tiles):
                cols = slice(n * tile, (n + 1) * tile)
                grad = inv * (dm[at, cols] * wv[1:2, cols] - first - buf[h, at, cols] * second)
                inner = (grad * slope[h, at, cols].astype(F32)).astype(BF)
                mix[h, at, cols] = inner
                colsums[0, :, cols] += fold(inner.astype(F32))

        row_steps(span, 64, fn)
        plan.hook()

    weights1 = f1v[...].reshape(width, units)
    out_copy.wait_recv()
    out[...] = (gh[...] + prb[...].astype(F32)).astype(BF)
    for n in range(0, width, tile):
        prb[:, n : n + tile] = nt(mix[1 - c], weights1[n : n + tile, :]).astype(BF)
    da_copy.go()
    for n in range(0, width, tile):
        gh[:, n : n + tile] = nt(mix[c], weights1[n : n + tile, :])
    plan.hook()
    size = stg.shape[1]
    writes = []

    def write(part, dst, wide):
        n = len(writes)
        if n >= 2:
            writes[n - 2].wait()
        stg[n % 2, :, 0:wide] = part.astype(BF)
        desc = pltpu.make_async_copy(stg.at[n % 2, :, pl.ds(0, wide)], dst, local.at[6 + n % 2])
        desc.start()
        writes.append(desc)

    for n in range(0, width, size):
        part = tn(act[0, :, n : n + size], mix[0]) + tn(act[1, :, n : n + size], mix[1])
        write(part, g1.at[pl.ds(n, size)], units)
    plan.hook()
    da_copy.wait_recv()
    out_copy.wait_send()

    def fn(at):
        da = gh[at, :] + prc[at, :].astype(F32)
        top = dt[c, at, :].astype(F32)
        normed, inv = normalize(hid[at, :])
        grad = top + norm_back(da * row(rows_all, 7), normed, inv)
        gh[at, :] = grad
        normed_b, inv_b = normalize(br[at, :])
        down = norm_back(grad * row(rows_all, 5), normed_b, inv_b).astype(BF)
        dbuf[at, :] = down
        for n, value in enumerate((down.astype(F32), grad * normed_b, grad, da * normed, da, top)):
            sums[n] += fold(value)

    row_steps(span, 64, fn)
    plan.hook()
    weights_o = wov[...].reshape(width, width)
    da_copy.wait_send()
    for j in range(group):
        at = slice(j * part_size, (j + 1) * part_size)
        prb[:, at] = (nt(dbuf[...], weights_o[at, :]) * lanes[:, at]).astype(BF)
    for copy in outgoing:
        copy.go()
    keep = pltpu.make_async_copy(give(s), do.at[mine_at], local.at[8])
    keep.start()
    plan.hook()
    for n in range(0, width, size):
        write(tn(own[:, n : n + size], dbuf[...]), go.at[pl.ds(n, size)], width)
    rows_g[...] = jnp.zeros(rows_g.shape, F32)
    for n in range(6):
        rows_g[4 + n : 5 + n, :] = jnp.sum(sums[n], 0, keepdims=True)
    wide_g[...] = jnp.zeros(wide_g.shape, F32)
    for n in range(NZ * NY * NX):
        at = pl.ds(pl.multiple_of((n * NC + c) * lane, lane), lane)
        for j in range(3):
            wide_g[j : j + 1, at] = jnp.sum(colsums[j, :, n * lane : (n + 1) * lane], 0, keepdims=True)
    plan.finish()
    keep.wait()
    for copy in outgoing:
        copy.wait_recv()
    for desc in writes[-2:]:
        desc.wait()
    wire.drain()


def feed_forward(own, rows_all, wide_all, lanes, tok, cot, f2own, f2d, wo, f1):
    span, width = own.shape
    units = f1.shape[4]
    group = NX * NC
    per = 2 * f2own.shape[0]
    out = (
        (VM, (span, width), BF),
        (HBM, (group * span, width // group), BF),
        (VM, (span, width), F32),
        (HBM, (width, units), BF),
        (HBM, (width, width), BF),
        (VM, (per, width), F32),
        (VM, (32, width), F32),
        (VM, (8, wide_all.shape[1]), F32),
    )
    scratch = [
        pltpu.VMEM(wo.shape, BF),
        pltpu.VMEM(f1.shape, BF),
        pltpu.VMEM((NZ, NY, NX) + (per, width), BF),
        pltpu.VMEM((NC, span, width), BF),
        pltpu.VMEM((NC, span, width), BF),
        pltpu.VMEM((NC, span, units), F32),
        pltpu.VMEM((NC, span, units), BF),
        pltpu.VMEM((NC, span, units), BF),
        pltpu.VMEM((span, units), F32),
        pltpu.VMEM((span, width), F32),
        pltpu.VMEM((span, width), F32),
        pltpu.VMEM((NZ, NY, NX) + (per, width), BF),
        pltpu.VMEM((span, width), BF),
        pltpu.VMEM((span, width), BF),
        pltpu.VMEM((span, width), BF),
        pltpu.VMEM((2, 128, units), BF),
        pltpu.VMEM((8, units), F32),
    ]
    scratch += [pltpu.VMEM((NC, span, 128), F32)] * 4
    scratch += [pltpu.VMEM((6, 16, width), F32), pltpu.VMEM((3, 16, units), F32)]
    scratch += plane_scratch((per // 2, width))[1:4] * 2
    scratch += [
        pltpu.SemaphoreType.DMA((COPIES,)),
        pltpu.SemaphoreType.DMA((COPIES,)),
        pltpu.SemaphoreType.DMA((9,)),
    ]
    return pl.pallas_call(
        ffn_kernel,
        out_shape=tuple(jax.ShapeDtypeStruct(shape, dtype) for _, shape, dtype in out),
        in_specs=[VM] * 4 + [HBM] * 6,
        out_specs=[spec for spec, _, _ in out],
        scratch_shapes=scratch,
        compiler_params=pltpu.CompilerParams(
            collective_id=3, has_side_effects=True, vmem_limit_bytes=63 * 1024 * 1024
        ),
        name="feed_forward",
    )(own, rows_all, wide_all, lanes, tok, cot, f2own, f2d, wo, f1)


def fast(tokens, doc_ids, cotangent, w_qkv, w_out, attn_vecs, head_scale, w_fc1, w_fc2, ffn_vecs, ffn_wide):
    _, span, width = tokens.shape
    group = NX * NC
    length = span * group
    head_count = head_scale.shape[0]
    head = width // head_count
    heads = head_count // group
    part = heads * head
    seq = lax.axis_index("seq")
    chips = NZ * NY * NX
    block = w_fc2.shape[0]
    units = chips * block

    rows = w_qkv.shape[0]
    wq4 = w_qkv.astype(BF).reshape(rows, 3, group, part).transpose(2, 0, 1, 3).reshape(group, rows, 3 * part)
    f1 = w_fc1.astype(BF).reshape(rows, chips, NC, block).transpose(2, 0, 1, 3).reshape(NC, rows, units)
    f2 = w_fc2.astype(BF)
    narrow = jnp.concatenate([attn_vecs, ffn_vecs], 0).astype(BF)
    count, each = narrow.shape
    lane = each * group
    narrow = lax.dynamic_update_slice(jnp.zeros((16, lane), BF), narrow, (0, seq * each))
    vec = jnp.stack([narrow, jnp.pad(ffn_wide.astype(BF), ((0, 16 - ffn_wide.shape[0]), (0, 0)))])
    tok = tokens.reshape(span, width)
    scale_own = lax.dynamic_slice_in_dim(head_scale, heads * seq, heads)
    scale_lanes = jnp.repeat(scale_own, head).reshape(1, part)
    ids = doc_ids.reshape(length)
    act_one, q, k, v, att, lse, scaled_own, wq, rows_all, wide_all, wo, fc1, fc2 = forward(
        tok, wq4, vec, w_out.astype(BF), f1, f2[block // 2 :], ids, scale_lanes, heads
    )
    outputs, do, grad_hidden, grad_fc1, grad_out, grad_w2, rows_in, wide_grads = feed_forward(
        scaled_own,
        rows_all,
        wide_all,
        jnp.repeat(head_scale, head).reshape(1, width),
        tok,
        cotangent.reshape(span, width),
        f2[: block // 2],
        fc2,
        wo,
        fc1,
    )
    grad_tokens, grad_w1, grad_wo, grad_wqkv, rows_out, wide_out = backward(
        do,
        q,
        k,
        v,
        att,
        lse,
        ids,
        wq,
        tok,
        grad_hidden,
        rows_in,
        wide_grads,
        rows_all[:1].astype(F32),
        act_one,
        grad_fc1.reshape(NZ, NY, NX, NC * rows, units),
        grad_out.reshape(NZ, NY, NX, NC, rows, width),
        heads,
    )
    mine = lax.dynamic_slice_in_dim(rows_out, seq * each, each, 1)
    wide_mine = lax.dynamic_slice_in_dim(wide_out, seq * block, block, 1)
    return (
        outputs.reshape(1, span, width),
        grad_tokens.reshape(1, span, width),
        grad_wqkv,
        grad_wo,
        mine[: attn_vecs.shape[0]],
        rows_out[16 : 16 + head_count, 0] / head_scale,
        grad_w1,
        grad_w2,
        mine[attn_vecs.shape[0] : count],
        wide_mine[: ffn_wide.shape[0]],
    )


def solution(mesh):
    placed = (
        P("dp", "seq", None),
        P("dp", None),
        P("dp", "seq", None),
        P(("dp", "seq"), None),
        P(("dp", "seq"), None),
        P(None, ("dp", "seq")),
        P(),
        P(("dp", "seq"), None),
        P(("dp", "seq"), None),
        P(None, ("dp", "seq")),
        P(None, ("dp", "seq")),
    )
    results = (
        P("dp", "seq", None),
        P("dp", "seq", None),
        P(("dp", "seq"), None),
        P(("dp", "seq"), None),
        P(None, ("dp", "seq")),
        P(),
        P(("dp", "seq"), None),
        P(("dp", "seq"), None),
        P(None, ("dp", "seq")),
        P(None, ("dp", "seq")),
    )
    suits = mesh.shape["dp"] == NZ * NY and mesh.shape["seq"] == NX * NC
    return jax.shard_map(
        fast if suits else local, mesh=mesh, in_specs=placed, out_specs=results, check_vma=False
    )
```

```python
import functools
import math

import jax
import jax.numpy as jnp
from jax import lax
from jax.experimental import pallas as pl
from jax.experimental.pallas import tpu as pltpu
from jax.sharding import PartitionSpec as P

EPSILON = 1e-05
NEGATIVE = -1e30
MESH = pl.DeviceIdType.MESH
BF = jnp.bfloat16
F32 = jnp.float32
NZ, NY, NX, NC = 4, 2, 2, 2
HBM = pl.BlockSpec(memory_space=pl.ANY)
VM = pl.BlockSpec(memory_space=pltpu.VMEM)


def normalize(values):
    centre = jnp.mean(values, -1, keepdims=True)
    centred = values - centre
    scale_inv = lax.rsqrt(jnp.mean(centred * centred, -1, keepdims=True) + EPSILON)
    return (centred * scale_inv, scale_inv)


def norm_back(grad_normed, normed, scale_inv):
    return scale_inv * (
        grad_normed
        - jnp.mean(grad_normed, -1, keepdims=True)
        - normed * jnp.mean(grad_normed * normed, -1, keepdims=True)
    )


def gelu_exact(values):
    return 0.5 * values * (1.0 + jax.scipy.special.erf(values * math.sqrt(0.5)))


def left_grad(activations, gradients):
    return lax.dot_general(
        activations, gradients, (((0,), (0,)), ((), ())), preferred_element_type=jnp.float32
    )


def right_back(gradients, matrix):
    return lax.dot_general(
        gradients, matrix, (((1,), (1,)), ((), ())), preferred_element_type=jnp.float32
    )


def masked_scores(queries, keys_block, query_pos, key_pos, query_ids, key_ids):
    raw_scores = jnp.einsum(
        "rqhe,rkhe->rhqk", queries, keys_block, preferred_element_type=jnp.float32
    )
    allowed = (key_pos[None, None, :] <= query_pos[None, :, None]) & (
        key_ids[:, None, :] == query_ids[:, :, None]
    )
    return jnp.where(allowed[:, None], raw_scores * queries.shape[3] ** (-0.5), NEGATIVE)


def attend(queries, keys_all, values_all, query_pos, query_ids, doc_rows, block_len):
    block_count = keys_all.shape[1] // block_len
    stat_shape = (queries.shape[0], queries.shape[2], queries.shape[1])

    def slice_block(block_index):
        start = block_index * block_len
        keys_block = lax.dynamic_slice_in_dim(keys_all, start, block_len, 1)
        values_block = lax.dynamic_slice_in_dim(values_all, start, block_len, 1)
        key_ids = lax.dynamic_slice_in_dim(doc_rows, start, block_len, 1)
        key_pos = start + jnp.arange(block_len, dtype=jnp.int32)
        return (
            values_block,
            masked_scores(queries, keys_block, query_pos, key_pos, query_ids, key_ids),
        )

    def first_pass(carry, block_index):
        running_max, running_sum = carry
        _, scores = slice_block(block_index)
        new_max = jnp.maximum(running_max, jnp.max(scores, -1))
        running_sum = running_sum * jnp.exp(running_max - new_max) + jnp.sum(
            jnp.exp(scores - new_max[..., None]), -1
        )
        return ((new_max, running_sum), None)

    start_stats = (jnp.full(stat_shape, NEGATIVE, jnp.float32), jnp.zeros(stat_shape, jnp.float32))
    (row_max, row_sum), _ = lax.scan(
        first_pass, start_stats, jnp.arange(block_count, dtype=jnp.int32)
    )
    log_total = row_max + jnp.log(row_sum)

    def second_pass(total_out, block_index):
        values_block, scores = slice_block(block_index)
        probs = jnp.exp(scores - log_total[..., None]).astype(jnp.bfloat16)
        return (
            total_out
            + jnp.einsum(
                "rhqk,rkhe->rqhe", probs, values_block, preferred_element_type=jnp.float32
            ),
            None,
        )

    attended, _ = lax.scan(
        second_pass, jnp.zeros(queries.shape, jnp.float32), jnp.arange(block_count, dtype=jnp.int32)
    )
    return (attended, log_total)


def attend_back(
    queries,
    keys_all,
    values_all,
    grad_out,
    log_total,
    delta,
    query_pos,
    query_ids,
    doc_rows,
    block_len,
):
    block_count = keys_all.shape[1] // block_len
    scale = queries.shape[3] ** (-0.5)

    def step(grad_queries, block_index):
        start = block_index * block_len
        keys_block = lax.dynamic_slice_in_dim(keys_all, start, block_len, 1)
        values_block = lax.dynamic_slice_in_dim(values_all, start, block_len, 1)
        key_ids = lax.dynamic_slice_in_dim(doc_rows, start, block_len, 1)
        key_pos = start + jnp.arange(block_len, dtype=jnp.int32)
        scores = masked_scores(queries, keys_block, query_pos, key_pos, query_ids, key_ids)
        probs = jnp.exp(scores - log_total[..., None])
        grad_probs = jnp.einsum(
            "rqhe,rkhe->rhqk", grad_out, values_block, preferred_element_type=jnp.float32
        )
        grad_scores = (probs * (grad_probs - delta[..., None]) * scale).astype(jnp.bfloat16)
        grad_queries = grad_queries + jnp.einsum(
            "rhqk,rkhe->rqhe", grad_scores, keys_block, preferred_element_type=jnp.float32
        )
        grad_keys = jnp.einsum(
            "rhqk,rqhe->rkhe", grad_scores, queries, preferred_element_type=jnp.float32
        )
        grad_values = jnp.einsum(
            "rhqk,rqhe->rkhe",
            probs.astype(jnp.bfloat16),
            grad_out,
            preferred_element_type=jnp.float32,
        )
        return (grad_queries, (grad_keys, grad_values))

    return lax.scan(
        step, jnp.zeros(queries.shape, jnp.float32), jnp.arange(block_count, dtype=jnp.int32)
    )


def local(
    tokens,
    doc_ids,
    cotangent,
    w_qkv,
    w_out,
    attn_vecs,
    head_scale,
    w_fc1,
    w_fc2,
    ffn_vecs,
    ffn_wide,
):
    row_count, span_len, model_width = tokens.shape
    head_count = head_scale.shape[0]
    head_size = model_width // head_count
    token_count = row_count * span_len
    brain = jnp.bfloat16
    single = jnp.float32
    gathered_qkv, gathered_out, attn_rows = (
        lax.all_gather(w_qkv.astype(brain), ("dp", "seq"), axis=0, tiled=True),
        lax.all_gather(w_out.astype(brain), ("dp", "seq"), axis=0, tiled=True),
        lax.all_gather(attn_vecs.astype(brain), ("dp", "seq"), axis=1, tiled=True),
    )
    attn_rows = attn_rows.astype(single)
    inputs = tokens.astype(single).reshape(token_count, model_width)
    normed_one, inv_one = normalize(inputs)
    act_one = (normed_one * attn_rows[0] + attn_rows[1]).astype(brain)
    projected = jnp.dot(act_one, gathered_qkv, preferred_element_type=single)
    queries = (projected[:, :model_width] + attn_rows[2]).astype(brain)
    keys_own = projected[:, model_width : 2 * model_width].astype(brain)
    values_own = (projected[:, 2 * model_width :] + attn_rows[3]).astype(brain)
    keys_all, values_all = (
        lax.all_gather(
            keys_own.reshape(row_count, span_len, model_width), "seq", axis=1, tiled=True
        ),
        lax.all_gather(
            values_own.reshape(row_count, span_len, model_width), "seq", axis=1, tiled=True
        ),
    )
    offset = lax.axis_index("seq") * span_len
    query_pos = offset + jnp.arange(span_len, dtype=jnp.int32)
    query_ids = lax.dynamic_slice_in_dim(doc_ids, offset, span_len, 1)
    queries_four = queries.reshape(row_count, span_len, head_count, head_size)
    keys_four = keys_all.reshape(row_count, -1, head_count, head_size)
    values_four = values_all.reshape(row_count, -1, head_count, head_size)
    attended, log_total = attend(
        queries_four, keys_four, values_four, query_pos, query_ids, doc_ids, span_len
    )
    scaled = (
        (attended * head_scale[None, None, :, None]).reshape(token_count, model_width).astype(brain)
    )
    branch = jnp.dot(scaled, gathered_out, preferred_element_type=single) + attn_rows[4]
    normed_branch, inv_branch = normalize(branch)
    hidden = inputs + normed_branch * attn_rows[5] + attn_rows[6]
    gathered_fc1, gathered_fc2, ffn_rows, wide_rows = (
        lax.all_gather(w_fc1.astype(brain), ("dp", "seq"), axis=0, tiled=True),
        lax.all_gather(w_fc2.astype(brain), ("dp", "seq"), axis=0, tiled=True),
        lax.all_gather(ffn_vecs.astype(brain), ("dp", "seq"), axis=1, tiled=True),
        lax.all_gather(ffn_wide.astype(brain), ("dp", "seq"), axis=1, tiled=True),
    )
    ffn_rows = ffn_rows.astype(single)
    wide_rows = wide_rows.astype(single)
    normed_two, inv_two = normalize(hidden)
    act_two = (normed_two * ffn_rows[0] + ffn_rows[1]).astype(brain)
    inner_act = jnp.dot(act_two, gathered_fc1, preferred_element_type=single) + wide_rows[0]
    activated, gelu_pull = jax.vjp(gelu_exact, inner_act)
    normed_three, inv_three = normalize(activated)
    mixed_act = (normed_three * wide_rows[1] + wide_rows[2]).astype(brain)
    result = hidden + jnp.dot(mixed_act, gathered_fc2, preferred_element_type=single) + ffn_rows[2]
    outputs = result.astype(brain).reshape(row_count, span_len, model_width)
    back_set = (
        lax.all_gather(w_qkv.astype(brain), ("dp", "seq"), axis=0, tiled=True),
        lax.all_gather(w_out.astype(brain), ("dp", "seq"), axis=0, tiled=True),
        lax.all_gather(attn_vecs.astype(brain), ("dp", "seq"), axis=1, tiled=True),
        lax.all_gather(w_fc1.astype(brain), ("dp", "seq"), axis=0, tiled=True),
        lax.all_gather(w_fc2.astype(brain), ("dp", "seq"), axis=0, tiled=True),
        lax.all_gather(ffn_vecs.astype(brain), ("dp", "seq"), axis=1, tiled=True),
        lax.all_gather(ffn_wide.astype(brain), ("dp", "seq"), axis=1, tiled=True),
    )
    gathered_qkv, gathered_out, attn_back, gathered_fc1, gathered_fc2, ffn_back, wide_back = (
        back_set
    )
    attn_rows = attn_back.astype(single)
    ffn_rows = ffn_back.astype(single)
    wide_rows = wide_back.astype(single)
    grad_top = cotangent.astype(single).reshape(token_count, model_width)
    grad_branch_two = grad_top.astype(brain)
    grad_fc2 = left_grad(mixed_act, grad_branch_two)
    grad_bias_two = jnp.sum(grad_branch_two.astype(single), 0)
    grad_mixed = right_back(grad_branch_two, gathered_fc2)
    grad_inner_gain = jnp.sum(grad_mixed * normed_three, 0)
    grad_inner_bias = jnp.sum(grad_mixed, 0)
    grad_activated = norm_back(grad_mixed * wide_rows[1], normed_three, inv_three)
    grad_inner = gelu_pull(grad_activated)[0].astype(brain)
    grad_fc1 = left_grad(act_two, grad_inner)
    grad_bias_one = jnp.sum(grad_inner.astype(single), 0)
    grad_act_two = right_back(grad_inner, gathered_fc1)
    grad_gain_two = jnp.sum(grad_act_two * normed_two, 0)
    grad_shift_two = jnp.sum(grad_act_two, 0)
    grad_hidden = grad_top + norm_back(grad_act_two * ffn_rows[0], normed_two, inv_two)
    ffn_sums = (
        lax.psum_scatter(grad_fc1, ("dp", "seq"), scatter_dimension=0, tiled=True),
        lax.psum_scatter(grad_fc2, ("dp", "seq"), scatter_dimension=0, tiled=True),
        lax.psum_scatter(
            jnp.stack([grad_gain_two, grad_shift_two, grad_bias_two]),
            ("dp", "seq"),
            scatter_dimension=1,
            tiled=True,
        ),
        lax.psum_scatter(
            jnp.stack([grad_bias_one, grad_inner_gain, grad_inner_bias]),
            ("dp", "seq"),
            scatter_dimension=1,
            tiled=True,
        ),
    )
    grad_post_gain = jnp.sum(grad_hidden * normed_branch, 0)
    grad_post_shift = jnp.sum(grad_hidden, 0)
    grad_branch = norm_back(grad_hidden * attn_rows[5], normed_branch, inv_branch).astype(brain)
    grad_out_bias = jnp.sum(grad_branch.astype(single), 0)
    grad_out = left_grad(scaled, grad_branch)
    grad_scaled = right_back(grad_branch, gathered_out).reshape(
        row_count, span_len, head_count, head_size
    )
    grad_scale = jnp.sum(grad_scaled * attended, (0, 1, 3))
    grad_attended = (grad_scaled * head_scale[None, None, :, None]).astype(brain)
    delta = jnp.transpose(jnp.sum(grad_attended.astype(single) * attended, -1), (0, 2, 1))
    grad_queries, key_parts = attend_back(
        queries_four,
        keys_four,
        values_four,
        grad_attended,
        log_total,
        delta,
        query_pos,
        query_ids,
        doc_ids,
        span_len,
    )
    partial_keys = jnp.transpose(key_parts[0], (1, 0, 2, 3, 4)).reshape(row_count, -1, model_width)
    partial_values = jnp.transpose(key_parts[1], (1, 0, 2, 3, 4)).reshape(
        row_count, -1, model_width
    )
    grad_keys, grad_values = (
        lax.psum_scatter(
            partial_keys.astype(jnp.bfloat16), "seq", scatter_dimension=1, tiled=True
        ).astype(jnp.float32),
        lax.psum_scatter(
            partial_values.astype(jnp.bfloat16), "seq", scatter_dimension=1, tiled=True
        ).astype(jnp.float32),
    )
    grad_qkv = jnp.concatenate(
        [
            grad_queries.reshape(token_count, model_width).astype(brain),
            grad_keys.reshape(token_count, model_width).astype(brain),
            grad_values.reshape(token_count, model_width).astype(brain),
        ],
        1,
    )
    grad_w_qkv = left_grad(act_one, grad_qkv)
    grad_query_bias = jnp.sum(grad_qkv[:, :model_width].astype(single), 0)
    grad_value_bias = jnp.sum(grad_qkv[:, 2 * model_width :].astype(single), 0)
    grad_act_one = right_back(grad_qkv, gathered_qkv)
    grad_gain_one = jnp.sum(grad_act_one * normed_one, 0)
    grad_shift_one = jnp.sum(grad_act_one, 0)
    grad_tokens = (
        (grad_hidden + norm_back(grad_act_one * attn_rows[0], normed_one, inv_one))
        .astype(brain)
        .reshape(row_count, span_len, model_width)
    )
    attn_stack = jnp.stack(
        [
            grad_gain_one,
            grad_shift_one,
            grad_query_bias,
            grad_value_bias,
            grad_out_bias,
            grad_post_gain,
            grad_post_shift,
        ]
    )
    attn_sums = (
        lax.psum_scatter(grad_w_qkv, ("dp", "seq"), scatter_dimension=0, tiled=True),
        lax.psum_scatter(grad_out, ("dp", "seq"), scatter_dimension=0, tiled=True),
        lax.psum_scatter(attn_stack, ("dp", "seq"), scatter_dimension=1, tiled=True),
    )
    scale_total = lax.psum(grad_scale, ("dp", "seq"))
    return (
        outputs,
        grad_tokens,
        attn_sums[0],
        attn_sums[1],
        attn_sums[2],
        scale_total,
        ffn_sums[0],
        ffn_sums[1],
        ffn_sums[2],
        ffn_sums[3],
    )


class Place:
    def __init__(self):
        self.dp = lax.axis_index("dp")
        self.seq = lax.axis_index("seq")
        self.z, self.y = self.dp // NY, self.dp % NY
        self.x, self.c = self.seq // NC, self.seq % NC

    def at(self, z=None, y=None, x=None, c=None):
        z = self.z if z is None else z
        y = self.y if y is None else y
        x = self.x if x is None else x
        c = self.c if c is None else c
        return (z * NY + y, x * NC + c)

    def zup(self, k):
        return (self.z + k) % NZ

    def group(self):
        near = [self.at(c=1 - self.c), self.at(x=1 - self.x), self.at(x=1 - self.x, c=1 - self.c)]
        return near + [self.at(y=1 - self.y)] + [self.at(z=self.zup(k)) for k in range(1, NZ)]


class Copy:
    def __init__(self, desc):
        self.desc, self.sent = desc, False

    def go(self):
        self.desc.start()
        return self

    def wait_recv(self):
        self.desc.wait_recv()

    def wait_send(self):
        if not self.sent:
            self.desc.wait_send()
        self.sent = True


class Wire:
    def __init__(self, place, send, recv):
        self.place, self.send, self.recv, self.used, self.open = place, send, recv, 0, []

    def copy(self, src, dst, dev):
        n = self.used
        self.used += 1
        copy = Copy(
            pltpu.make_async_remote_copy(
                src_ref=src,
                dst_ref=dst,
                send_sem=self.send.at[n],
                recv_sem=self.recv.at[n],
                device_id=dev,
                device_id_type=MESH,
            )
        )
        self.open.append(copy)
        return copy

    def drain(self):
        for copy in self.open:
            copy.wait_send()


def greet(place):
    barrier = pltpu.get_barrier_semaphore()
    group = place.group()
    for dev in group:
        pl.semaphore_signal(barrier, inc=1, device_id=dev, device_id_type=MESH)
    pl.semaphore_wait(barrier, len(group))


def spread_zxy(wire, place, ref, swap=False):
    z, y, x = place.z, place.y, place.x
    own = ref.at[z, y, x]
    first = place.at(y=1 - y) if swap else place.at(x=1 - x)
    second = place.at(x=1 - x) if swap else place.at(y=1 - y)
    order = [(z - k + NZ) % NZ for k in range(NZ)]
    along_z = [wire.copy(own, own, place.at(z=place.zup(k))) for k in range(1, NZ)]
    firsts = [wire.copy(ref.at[zk, y, x], ref.at[zk, y, x], first) for zk in order]
    twos = [ref.at[zk, :, x] if swap else ref.at[zk, y] for zk in order]
    seconds = [wire.copy(two, two, second) for two in twos]
    yield
    for copy in along_z + firsts[:1]:
        copy.go()
    yield
    for k in range(1, NZ):
        along_z[k - 1].wait_recv()
        firsts[k].go()
        yield
    for k in range(NZ):
        firsts[k].wait_recv()
        seconds[k].go()
        yield
    for copy in seconds:
        copy.wait_recv()


def spread_xzy(wire, place, ref, swap=False):
    z, y, x = place.z, place.y, place.x
    own = ref.at[z, y, x]
    first = place.at(y=1 - y) if swap else place.at(x=1 - x)
    second = place.at(x=1 - x) if swap else place.at(y=1 - y)
    order = [(z - k + NZ) % NZ for k in range(NZ)]
    twos = [ref.at[zk, :, x] if swap else ref.at[zk, y] for zk in order]
    start = wire.copy(own, own, first)
    steps = [wire.copy(two, two, place.at(z=place.zup(1))) for two in twos[:-1]]
    seconds = [wire.copy(two, two, second) for two in twos]
    yield
    start.go()
    yield
    start.wait_recv()
    steps[0].go()
    seconds[0].go()
    yield
    for k in range(1, NZ):
        steps[k - 1].wait_recv()
        if k < NZ - 1:
            steps[k].go()
        seconds[k].go()
        yield
    for copy in seconds:
        copy.wait_recv()


def spread_zx(wire, place, ref, swap=False):
    z, y, x = place.z, place.y, place.x
    first = place.at(y=1 - y) if swap else place.at(x=1 - x)
    order = [(z - k + NZ) % NZ for k in range(NZ)]
    own = ref.at[z, y, x]
    along_z = [wire.copy(own, own, place.at(z=place.zup(k))) for k in range(1, NZ)]
    firsts = [wire.copy(ref.at[zk, y, x], ref.at[zk, y, x], first) for zk in order]
    yield
    for copy in along_z + firsts[:1]:
        copy.go()
    yield
    for k in range(1, NZ):
        along_z[k - 1].wait_recv()
        firsts[k].go()
        yield
    for copy in firsts:
        copy.wait_recv()


def spread_last(wire, place, src, dst, swap=False):
    z, y, x = place.z, place.y, place.x
    second = place.at(x=1 - x) if swap else place.at(y=1 - y)
    seconds = []
    for k in range(NZ):
        zk = (z - k + NZ) % NZ
        here, there = (src.at[zk, :, x], dst.at[zk, :, x]) if swap else (src.at[zk, y], dst.at[zk, y])
        seconds.append(wire.copy(here, there, second))
    yield
    for copy in seconds:
        copy.go()
    yield
    for copy in seconds:
        copy.wait_recv()


def spread_pair(wire, place, ref):
    plane = ref.at[:, :, :, place.c]
    last = wire.copy(plane, plane, place.at(c=1 - place.c))
    yield from spread_xzy(wire, place, plane)
    last.go()
    yield
    last.wait_recv()


def spread_dp(wire, place, views):
    z, y = place.z, place.y
    at = [z * NY + y] + [((z - n + NZ) % NZ) * NY + y for n in range(1, NZ)]
    along_z = [[wire.copy(view(at[0]), view(at[0]), place.at(z=place.zup(n))) for view in views] for n in range(1, NZ)]
    ys = [[wire.copy(view(d), view(d), place.at(y=1 - y)) for view in views] for d in at]
    yield
    for copies in along_z + ys[:1]:
        for copy in copies:
            copy.go()
    yield
    for n in range(1, NZ):
        for copy in along_z[n - 1]:
            copy.wait_recv()
        for copy in ys[n]:
            copy.go()
        yield
    for copies in ys:
        for copy in copies:
            copy.wait_recv()


def spread_row(wire, place, tok, tok_all):
    s, other, core = place.seq, place.at(x=1 - place.x), place.at(c=1 - place.c)
    far = tok_all.at[s ^ 2]
    tok_x = wire.copy(tok, tok_all.at[s], other)
    tok_c = wire.copy(tok, tok_all.at[s], core)
    last = wire.copy(far, far, core)
    yield
    tok_c.go()
    tok_x.go()
    yield
    tok_c.wait_recv()
    yield
    tok_x.wait_recv()
    last.go()
    yield
    last.wait_recv()


class Plan:
    def __init__(self, tasks, order):
        self.tasks, self.order = tasks, list(order)
        for task in tasks.values():
            next(task)

    def hook(self):
        for name in self.order.pop(0):
            next(self.tasks[name], None)

    def finish(self):
        while self.order:
            self.hook()
        for task in self.tasks.values():
            for _ in task:
                pass


COPIES = 104


def nt(a, b):
    return lax.dot_general(a, b, (((1,), (1,)), ((), ())), preferred_element_type=F32)


def nn(a, b):
    return lax.dot_general(a, b, (((1,), (0,)), ((), ())), preferred_element_type=F32)


def pair_bias(idr, key_ids, qb, kb, size):
    qs = pl.multiple_of(qb * size, size)
    key_pos = kb * size + lax.broadcasted_iota(jnp.int32, (size, size), 0)
    query_pos = qs + lax.broadcasted_iota(jnp.int32, (size, size), 1)
    same = key_ids == idr[:, pl.ds(qs, size)]
    return jnp.where((key_pos <= query_pos) & same, 0.0, NEGATIVE)


def mask_heads(dst, src, heads, head):
    lane = lax.broadcasted_iota(jnp.int32, src.shape, 1) // head
    whole = src[...]
    for h in range(heads):
        dst[h] = jnp.where(lane == h, whole, jnp.zeros_like(whole))


FORWARD = (
    "tqoabcboqqqdaaaaaaqtt",
    "",
    "accc",
    "t",
    "",
    "b",
    "oc",
    "",
    "",
    "",
    "ddd",
    "a",
    "",
    "b",
    "o",
    "",
    "dbooob",
)


def forward_tasks(wire, place, tok, tok_all, wq, rows_all, wide_all, lane, wo_all, f1_all, f2_all):
    group = NX * NC
    half1 = f1_all.shape[4] // 2
    half2 = f2_all.shape[3] // 2
    views = [
        lambda d: wq.at[d],
        lambda d: rows_all.at[:, pl.ds(pl.multiple_of(d * lane, lane), lane)],
        lambda d: wide_all.at[:, pl.ds(pl.multiple_of(d * lane * group, lane * group), lane * group)],
    ]
    return {
        "t": spread_row(wire, place, tok, tok_all),
        "q": spread_dp(wire, place, views),
        "a": spread_zxy(wire, place, f1_all.at[:, :, :, :, pl.ds(0, half1)]),
        "b": spread_xzy(wire, place, f1_all.at[:, :, :, :, pl.ds(half1, half1)], swap=True),
        "o": spread_pair(wire, place, wo_all),
        "c": spread_zx(wire, place, f2_all.at[:, :, :, pl.ds(0, half2)]),
        "d": spread_zx(wire, place, f2_all.at[:, :, :, pl.ds(half2, half2)], swap=True),
    }


def forward_kernel(heads, *refs):
    tok, wq4, vec, wo, f1, f2, idr, lanes = refs[:8]
    act, q, k, v, att, lse, own, wq, rows_all, wide_all, wo_all, f1_all, f2_all = refs[8:21]
    tok_all, actv, vecs, km, vt, idc, bias, top, low, acc, scb, send, recv, local = refs[21:]
    place = Place()
    z, y, x, c, s, dp = place.z, place.y, place.x, place.c, place.seq, place.dp
    group = NX * NC
    wire = Wire(place, send, recv)
    core, other, across = place.at(c=1 - c), place.at(x=1 - x), place.at(x=1 - x, c=1 - c)
    span, width = tok.shape
    rows = f1.shape[1]
    length, part = q.shape
    head = part // heads

    greet(place)
    quarter = []
    for dev, peer in ((core, s ^ 1), (other, s ^ 2), (across, s ^ 3)):
        quarter.append(wire.copy(wq4.at[peer], wq.at[dp, s], dev).go())
        quarter.append(wire.copy(vec, vecs.at[s], dev).go())
    f1_c = wire.copy(f1.at[1 - c], f1_all.at[z, y, x, pl.ds(c * rows, rows)], core).go()
    here = [
        pltpu.make_async_copy(wq4.at[s], wq.at[dp, s], local.at[0]),
        pltpu.make_async_copy(vec, vecs.at[s], local.at[1]),
        pltpu.make_async_copy(tok, tok_all.at[s], local.at[2]),
        pltpu.make_async_copy(wo, wo_all.at[z, y, x, c], local.at[3]),
        pltpu.make_async_copy(f1.at[c], f1_all.at[z, y, x, pl.ds(c * rows, rows)], local.at[4]),
        pltpu.make_async_copy(f2, f2_all.at[z, y, x], local.at[5]),
    ]
    for desc in here:
        desc.start()
    for desc in here:
        desc.wait()
    for desc in quarter:
        desc.wait_recv()

    lane = vec.shape[2]
    blk = pl.multiple_of(dp * lane, lane)
    wide_blk = pl.multiple_of(dp * lane * group, lane * group)
    rows_all[:, pl.ds(blk, lane)] = (vecs[0, 0] + vecs[1, 0]) + (vecs[2, 0] + vecs[3, 0])
    for j in range(group):
        wide_all[:, pl.ds(pl.multiple_of(wide_blk + j * lane, lane), lane)] = vecs[j, 1]

    f1_c.wait_recv()
    plan = Plan(
        forward_tasks(wire, place, tok, tok_all, wq, rows_all, wide_all, lane, wo_all, f1_all, f2_all), FORWARD
    )
    plan.hook()

    shift = pl.multiple_of(s * part, part)
    bias_q = rows_all[2:3, pl.ds(shift, part)].astype(F32)
    bias_v = rows_all[3:4, pl.ds(shift, part)].astype(F32)
    gain, base = rows_all[0:1, :].astype(F32), rows_all[1:2, :].astype(F32)
    keep = []
    for m in range(group):
        j = s ^ m
        plan.hook()
        if m >= 2:
            keep[m - 2].wait()
        slot = actv.at[m % 2]
        step = 64

        def norm_rows(n, _, slot=slot, j=j):
            at = pl.ds(pl.multiple_of(n * step, step), step)
            values = tok_all[j, at, :].astype(F32)
            slot[at, :] = (normalize(values)[0] * gain + base).astype(BF)
            return 0

        lax.fori_loop(0, span // step, norm_rows, 0)
        at = pl.ds(pl.multiple_of(j * span, span), span)
        desc = pltpu.make_async_copy(slot, act.at[at], local.at[6 + m])
        desc.start()
        keep.append(desc)
        for n, (dst, add) in enumerate(((q, bias_q), (k, None), (v, bias_v))):
            weights = wq[:, :, :, n * part : (n + 1) * part].reshape(width, part)
            proj = nn(slot[...], weights)
            if add is not None:
                proj = proj + add
            if n == 0:
                proj = proj * (head**-0.5)
            dst[at, :] = proj.astype(BF)

    plan.hook()
    mask_heads(km, k, heads, head)
    vt[...] = v[...].T
    idc[...] = jnp.broadcast_to(idr[...], (8, length)).T
    blocks = length // span
    returns = []
    for qb in reversed(range(blocks)):
        qs = slice(qb * span, (qb + 1) * span)
        top[...] = jnp.full(top.shape, NEGATIVE, F32)
        low[...] = jnp.zeros(low.shape, F32)
        acc[...] = jnp.zeros(acc.shape, F32)

        def keys(step, _, qb=qb, qs=qs):
            kb = qb - step
            ks = pl.ds(pl.multiple_of(kb * span, span), span)
            bias[...] = pair_bias(idr, idc[ks, 0:1], qb, kb, span)
            for h in range(heads):
                scores = nt(km[h, ks, :], q[qs, :]) + bias[...]
                old = top[h : h + 1, :]
                new = jnp.maximum(old, jnp.max(scores, 0, keepdims=True))
                probs = jnp.exp(scores - new)
                shrink = jnp.exp(old - new)
                top[h : h + 1, :] = new
                low[h : h + 1, :] = low[h : h + 1, :] * shrink + jnp.sum(probs, 0, keepdims=True)
                hs = slice(h * head, (h + 1) * head)
                acc[hs, :] = acc[hs, :] * shrink + nn(vt[hs, ks], probs.astype(BF))
            for n in range(qb + 1):

                @pl.when(step == n)
                def _():
                    plan.hook()

            return 0

        lax.fori_loop(0, qb + 1, keys, 0)
        for h in range(heads):
            hs = slice(h * head, (h + 1) * head)
            acc[hs, :] = acc[hs, :] * (1.0 / low[h : h + 1, :])
        att[:, qs] = acc[...]
        lse[:, qs] = top[...] + jnp.log(low[...])
        scb[qb] = (acc[...].T * lanes[...]).astype(BF)
        view = own.at[:, pl.ds(shift, part)]
        back = pltpu.make_async_remote_copy(
            src_ref=scb.at[qb],
            dst_ref=view,
            send_sem=send.at[COPIES - 1 - qb],
            recv_sem=recv.at[COPIES - 4 + (s ^ qb)],
            device_id=(dp, qb),
            device_id_type=MESH,
        )
        mine = pltpu.make_async_copy(scb.at[qb], view, local.at[10])
        returns.append((qb, back, mine))

        @pl.when(s == qb)
        def _():
            mine.start()

        @pl.when(s != qb)
        def _():
            back.start()

    plan.finish()
    for desc in keep[-2:]:
        desc.wait()
    for qb, back, mine in returns:

        @pl.when(s == qb)
        def _():
            mine.wait()

        @pl.when(s != qb)
        def _():
            back.wait_send()

    for m in range(1, group):
        view = own.at[:, pl.ds(pl.multiple_of((s ^ m) * part, part), part)]
        pltpu.make_async_remote_copy(
            src_ref=scb.at[0],
            dst_ref=view,
            send_sem=send.at[COPIES - 1],
            recv_sem=recv.at[COPIES - 4 + m],
            device_id=core,
            device_id_type=MESH,
        ).wait_recv()
    wire.drain()


def forward(tok, wq4, vec, wo, f1, f2, ids, lanes, heads):
    span, width = tok.shape
    group, rows, triple = wq4.shape
    part = triple // 3
    length = span * group
    dps = NZ * NY
    lane = vec.shape[2]
    out = (
        (HBM, (length, width), BF),
        (VM, (length, part), BF),
        (VM, (length, part), BF),
        (VM, (length, part), BF),
        (VM, (part, length), F32),
        (VM, (8, length), F32),
        (VM, (span, width), BF),
        (VM, (dps, group, rows, triple), BF),
        (VM, (16, dps * lane), BF),
        (VM, (16, dps * group * lane), BF),
        (HBM, (NZ, NY, NX, NC) + wo.shape, BF),
        (HBM, (NZ, NY, NX, NC * f1.shape[1], f1.shape[2]), BF),
        (HBM, (NZ, NY, NX) + f2.shape, BF),
    )
    return pl.pallas_call(
        functools.partial(forward_kernel, heads),
        out_shape=tuple(jax.ShapeDtypeStruct(shape, dtype) for _, shape, dtype in out),
        in_specs=[VM] * 8,
        out_specs=[spec for spec, _, _ in out],
        scratch_shapes=[
            pltpu.VMEM((group, span, width), BF),
            pltpu.VMEM((2, span, width), BF),
            pltpu.VMEM((group,) + vec.shape, BF),
            pltpu.VMEM((heads, length, part), BF),
            pltpu.VMEM((part, length), BF),
            pltpu.VMEM((length, 8), jnp.int32),
            pltpu.VMEM((span, span), F32),
            pltpu.VMEM((8, span), F32),
            pltpu.VMEM((8, span), F32),
            pltpu.VMEM((part, span), F32),
            pltpu.VMEM((group, span, part), BF),
            pltpu.SemaphoreType.DMA((COPIES,)),
            pltpu.SemaphoreType.DMA((COPIES,)),
            pltpu.SemaphoreType.DMA((12,)),
        ],
        compiler_params=pltpu.CompilerParams(
            collective_id=1, has_side_effects=True, vmem_limit_bytes=56 * 1024 * 1024
        ),
        name="forward_row",
    )(tok, wq4, vec, wo, f1, f2, ids.reshape(1, length), lanes)


def lead_loop(total, fn, step=16):
    lead, rows = total.shape[:-2], total.shape[-2]
    per = rows // step

    def body(n, _):
        block = n // per
        at = []
        for dim in reversed(lead):
            at.append(block % dim)
            block = block // dim
        fn(tuple(reversed(at)) + (pl.ds(pl.multiple_of((n % per) * step, step), step), slice(None)))
        return 0

    lax.fori_loop(0, math.prod(lead) * per, body, 0)


def add_into(total, term):
    def fn(idx):
        total[idx] = (total[idx].astype(F32) + term[idx].astype(F32)).astype(total.dtype)

    lead_loop(total, fn, 16 if total.dtype == BF else 8)


def reduce_plane(wire, place, grad, own, got, got2, got3, out, local, swap=False):
    z, y, x = place.z, place.y, place.x
    first = place.at(x=1 - x) if swap else place.at(y=1 - y)
    order = [place.zup(k) for k in (1, 2, 3, 0)]

    def two(zk, mine):
        if swap:
            return grad.at[zk, :, x if mine else 1 - x]
        return grad.at[zk, y if mine else 1 - y]

    sends = [wire.copy(two(zk, False), got.at[k], first) for k, zk in enumerate(order)]
    loads = [pltpu.make_async_copy(two(zk, True), own.at[k], local.at[k]) for k, zk in enumerate(order)]
    rest = reduce_tail(wire, place, own, got2, got3, out, swap)
    next(rest)
    yield
    for copy in sends:
        copy.go()
    for desc in loads:
        desc.start()
    yield
    for k in range(NZ):
        loads[k].wait()
        sends[k].wait_recv()
        add_into(own.at[k], got.at[k])
        next(rest)
        yield
    yield from rest


def reduce_head(wire, place, grad, got, got2, swap=False):
    y, x = place.y, place.x
    first = place.at(x=1 - x) if swap else place.at(y=1 - y)
    second = place.at(y=1 - y) if swap else place.at(x=1 - x)
    keep, give = (y, 1 - y) if swap else (x, 1 - x)
    order = [place.zup(k) for k in (1, 2, 3, 0)]
    mine = [grad.at[zk, :, x] if swap else grad.at[zk, y] for zk in order]
    others = [grad.at[zk, :, 1 - x] if swap else grad.at[zk, 1 - y] for zk in order]
    keeps = [grad.at[zk, keep, x] if swap else grad.at[zk, y, keep] for zk in order]
    gives = [grad.at[zk, give, x] if swap else grad.at[zk, y, give] for zk in order]
    sends = [wire.copy(others[k], got.at[k], first) for k in range(NZ)]
    seconds = [wire.copy(gives[k], got2.at[k], second) for k in range(NZ)]
    yield
    for copy in sends:
        copy.go()
    yield
    for k in range(NZ):
        sends[k].wait_recv()
        add_into(mine[k], got.at[k])
        seconds[k].go()
        yield
    for k in range(NZ):
        seconds[k].wait_recv()
        add_into(keeps[k], got2.at[k])
        yield


def reduce_line(wire, place, own, got, out):
    along = [wire.copy(own.at[k], got.at[k], place.at(z=place.zup(k + 1))) for k in range(NZ - 1)]
    yield
    for copy in along:
        copy.go()
    yield
    for copy in along:
        copy.wait_recv()
    add_up(out, own.at[NZ - 1], got)


def reduce_tail(wire, place, own, got2, got3, out, swap=False):
    y, x = place.y, place.x
    second = place.at(y=1 - y) if swap else place.at(x=1 - x)
    keep, give = (y, 1 - y) if swap else (x, 1 - x)
    keeps = [own.at[k, keep] for k in range(NZ)]
    seconds = [wire.copy(own.at[k, give], got2.at[k], second) for k in range(NZ)]
    along = [wire.copy(keeps[k], got3.at[k], place.at(z=place.zup(k + 1))) for k in range(NZ - 1)]
    yield
    for copy in seconds:
        copy.go()
        yield
    for k in range(NZ):
        seconds[k].wait_recv()
        add_into(keeps[k], got2.at[k])
        if k < NZ - 1:
            along[k].go()
        yield
    for copy in along:
        copy.wait_recv()
    add_up(out, keeps[NZ - 1], got3)


def plane_scratch(block):
    return [
        pltpu.VMEM((NZ, 2) + block, BF),
        pltpu.VMEM((NZ, 2) + block, BF),
        pltpu.VMEM((NZ,) + block, BF),
        pltpu.VMEM((NZ - 1,) + block, BF),
        pltpu.SemaphoreType.DMA((NZ,)),
    ]


def reduce_outer(wire, place, go, outp, outg, load, scratch, out):
    c = place.c
    swap_o = wire.copy(go.at[:, :, :, 1 - c], outg, place.at(c=1 - c))
    load_o = pltpu.make_async_copy(go.at[:, :, :, c], outp, load)
    rest = reduce_plane(wire, place, outp, *scratch[:4], out, scratch[4])
    next(rest)
    yield
    swap_o.go()
    load_o.start()
    yield
    load_o.wait()
    swap_o.wait_recv()
    add_into(outp, outg)
    yield from rest


def reduce_first(wire, place, half, g1, buf, got, scratch, out, swap=False):
    c = place.c
    rows = got.shape[0]
    size = buf.shape[1] // 2
    cols = pl.ds(half * size, size)
    mine, theirs = buf.at[:, cols], got.at[:, cols]
    part = wire.copy(mine.at[pl.ds((1 - c) * rows, rows)], theirs, place.at(c=1 - c))
    yield from reduce_plane(
        wire, place, g1.at[:, :, :, :, cols], *scratch[:4], mine, scratch[4], swap=swap
    )
    part.go()
    lane = out.shape[1] // (NZ * NY * NX * NC)
    spread_columns(out, buf, pl.multiple_of(c * rows, rows), c, lane, half)
    yield
    part.wait_recv()
    spread_columns(out, got, 0, 1 - c, lane, half)


def spread_columns(out, src, row, c, lane, half):
    rows = out.shape[0]
    chips = NZ * NY * NX // 2
    for n in range(half * chips, (half + 1) * chips):
        at = pl.ds(pl.multiple_of((n * NC + c) * lane, lane), lane)
        out[:, at] = src[pl.ds(row, rows), n * lane : (n + 1) * lane]


def reduce_quarter(wire, place, gq, own, got, got2, total, buf, out, local):
    y, s = place.y, place.seq
    order = [place.zup(n) for n in (1, 2, 3, 0)]
    sends = [wire.copy(gq.at[zk, 1 - y], got.at[n], place.at(y=1 - y)) for n, zk in enumerate(order)]
    along = [wire.copy(own.at[n], got2.at[n], place.at(z=place.zup(n + 1))) for n in range(NZ - 1)]
    near = ((place.at(c=1 - place.c), 1), (place.at(x=1 - place.x), 2), (place.at(x=1 - place.x, c=1 - place.c), 3))
    parts = [wire.copy(total.at[s ^ m], buf.at[s], dev) for dev, m in near]
    loads = [pltpu.make_async_copy(gq.at[zk, y], own.at[n], local.at[n]) for n, zk in enumerate(order)]
    mine = pltpu.make_async_copy(total.at[s], buf.at[s], local.at[NZ])
    yield
    for copy in sends:
        copy.go()
    for desc in loads:
        desc.start()
    yield
    for n in range(NZ):
        loads[n].wait()
        sends[n].wait_recv()
        add_into(own.at[n], got.at[n])
        if n < NZ - 1:
            along[n].go()
        yield
    for copy in along:
        copy.wait_recv()
    add_up(total, own.at[NZ - 1], got2)
    for copy in parts:
        copy.go()
    mine.start()
    yield
    mine.wait()
    for copy in parts:
        copy.wait_recv()
    group = NX * NC
    part = buf.shape[2] // 3
    for j in range(group):
        for n in range(3):
            at = (n * group + j) * part
            out[:, at : at + part] = buf[j, :, n * part : (n + 1) * part].astype(F32)


def reduce_vectors(wire, place, pairs):
    z, y = place.z, place.y
    sizes = [g.shape[1] // (NZ * NY) for g, *_ in pairs]

    def cols(n, zk, yk):
        return pl.ds(pl.multiple_of((zk * NY + yk) * sizes[n], sizes[n]), sizes[n])

    cs = [wire.copy(g, t.at[0], place.at(c=1 - place.c)) for g, t, *_ in pairs]
    xs = [wire.copy(g, t.at[1], place.at(x=1 - place.x)) for g, t, *_ in pairs]
    ys, zs = [], []
    for n, (g, t, got, _) in enumerate(pairs):
        for zk in range(NZ):
            at = cols(n, zk, 1 - y)
            ys.append(wire.copy(g.at[:, at], t.at[2, :, at], place.at(y=1 - y)))
        for k in range(1, NZ):
            at = cols(n, place.zup(k), y)
            zs.append(wire.copy(g.at[:, at], got.at[z], place.at(z=place.zup(k))))
    yield
    for copy in cs:
        copy.go()
    yield
    for copies, slot in ((cs, 0), (xs, 1)):
        for copy, (g, t, *_) in zip(copies, pairs):
            copy.wait_recv()
            copy.wait_send()
            add_rows(g, t.at[slot])
        for copy in xs if slot == 0 else ys:
            copy.go()
        yield
    for copy in ys:
        copy.wait_recv()
    for n, (g, t, got, _) in enumerate(pairs):
        for zk in range(NZ):
            at = cols(n, zk, y)
            add_rows(g.at[:, at], t.at[2, :, at])
    for copy in zs:
        copy.go()
    for n, (g, t, got, _) in enumerate(pairs):
        keep_rows(got.at[z], g.at[:, cols(n, z, y)])
    yield
    for copy in zs:
        copy.wait_recv()
    for g, t, got, out in pairs:
        add_fixed(out, got)


def add_rows(total, term):
    total[...] += term[...]


def keep_rows(dst, src):
    dst[...] = src[...]


def add_fixed(out, got):
    total = got[0]
    for k in range(1, NZ):
        total = total + got[k]
    out[...] = total


def add_up(out, own, got):
    def fn(idx):
        value = own[idx].astype(F32)
        for k in range(NZ - 1):
            value = value + got[(k,) + idx].astype(F32)
        out[idx] = value.astype(out.dtype)

    lead_loop(out, fn)


BACKWARD = (
    "2314",
    "",
    "1",
    "4",
    "",
    "14o",
    "214o",
    "14",
    "144",
    "31114oo",
    "o",
    "4ooo",
    "qo",
    "",
    "14qo14qoqq",
    "vvqvqvv",
)


def backward_kernel(heads, *refs):
    q, k, v, att, lse, do, idr, wq, grad_hidden, rows_in, wide_in, gain = refs[:12]
    tok, act, g1, go, in2, in3 = refs[12:18]
    grad_tok, out1, out2, outo, outq, outr, outw = refs[18:25]
    (km, vm, qm, dm, kt, idc, bias, acck, accv, accq, accw, delta, blk, actb) = refs[25:39]
    (dap, dgot, dfin, ownq, gotq, gotqb, sumq, outq_buf, gq, gotp, f1buf, f1got) = refs[39:51]
    (rowg, rowt, rowz, wideg, widet, widez, outp, outg) = refs[51:59]
    plane1, plane4, planeo = refs[59:64], refs[64:69], refs[69:74]
    own2, own3, half2, half3 = refs[74:78]
    send, recv, local, dsend, drecv = refs[78:]
    place = Place()
    z, y, x, c, s, dp = place.z, place.y, place.x, place.c, place.seq, place.dp
    group = NX * NC
    wire = Wire(place, send, recv)
    core, other, across = place.at(c=1 - c), place.at(x=1 - x), place.at(x=1 - x, c=1 - c)
    length, part = q.shape
    span, width = tok.shape
    head = part // heads
    blocks = length // span
    shift = pl.multiple_of(s * part, part)

    greet(place)
    load2 = pltpu.make_async_copy(in2, own2, local.at[0])
    load3 = pltpu.make_async_copy(in3, own3, local.at[1])
    load2.start()
    load3.start()
    per = in2.shape[1]
    load2.wait()
    load3.wait()
    plan = Plan(
        {
            "1": reduce_first(wire, place, 0, g1, f1buf, f1got, plane1, out1),
            "4": reduce_first(wire, place, 1, g1, f1buf, f1got, plane4, out1, swap=True),
            "o": reduce_outer(wire, place, go, outp, outg, local.at[12], planeo, outo),
            "2": reduce_line(wire, place, own2, half2, out2.at[pl.ds(0, per)]),
            "3": reduce_line(wire, place, own3, half3, out2.at[pl.ds(per, per)]),
            "q": reduce_quarter(wire, place, gq, ownq, gotq, gotqb, sumq, outq_buf, outq, local.at[pl.ds(6, NZ + 1)]),
            "v": reduce_vectors(wire, place, ((rowg, rowt, rowz, outr), (wideg, widet, widez, outw))),
        },
        BACKWARD,
    )
    plan.hook()

    mask_heads(qm, q, heads, head)
    accq[...] = jnp.zeros(accq.shape, F32)
    accw[...] = jnp.zeros(accw.shape, F32)
    delta[...] = jnp.zeros(delta.shape, F32)
    plan.hook()
    mask_heads(dm, do, heads, head)
    for b in range(blocks):
        at = slice(b * span, (b + 1) * span)
        weighted = do[at, :].T.astype(F32) * att[:, at]
        for h in range(heads):
            delta[h : h + 1, at] = jnp.sum(weighted[h * head : (h + 1) * head, :], 0, keepdims=True)

    hops = []
    for t in range(blocks):
        tx, tc = t // NC, t % NC
        inner = pltpu.make_async_remote_copy(
            src_ref=dap.at[t],
            dst_ref=dgot.at[tx],
            send_sem=dsend.at[2 * t],
            recv_sem=drecv.at[2 * t],
            device_id=core,
            device_id_type=MESH,
        )
        outerc = pltpu.make_async_remote_copy(
            src_ref=dap.at[t],
            dst_ref=dfin,
            send_sem=dsend.at[2 * t + 1],
            recv_sem=drecv.at[2 * t + 1],
            device_id=other,
            device_id_type=MESH,
        )
        hops.append((tx, tc, inner, outerc))

    def meet(t):
        tx, tc, inner, outerc = hops[t]

        @pl.when(c == tc)
        def _():
            inner.wait_recv()
            add_into(dap.at[t], dgot.at[tx])

            @pl.when(x != tx)
            def _():
                outerc.start()

    fetch = [
        pltpu.make_async_copy(act.at[pl.ds(b * span, span)], actb.at[b % 2], local.at[2 + b]) for b in range(blocks)
    ]
    fetch[0].start()

    for kb in range(blocks):
        ks = slice(kb * span, (kb + 1) * span)
        if kb + 1 < blocks:
            fetch[kb + 1].start()
        mask_heads(km, k.at[ks], heads, head)
        mask_heads(vm, v.at[ks], heads, head)
        kt[...] = k[ks, :].T
        idc[...] = jnp.broadcast_to(idr[:, ks], (8, span)).T
        acck[...] = jnp.zeros(acck.shape, F32)
        accv[...] = jnp.zeros(accv.shape, F32)

        def queries(qb, _, kb=kb, ks=ks):
            qs = pl.ds(pl.multiple_of(qb * span, span), span)
            bias[...] = pair_bias(idr, idc[:, 0:1], qb, kb, span)
            for h in range(heads):
                scores = nt(km[h], q[qs, :]) + bias[...]
                probs = jnp.exp(scores - lse[h : h + 1, qs])
                grad = nt(vm[h], do[qs, :])
                ds = (probs * (grad - delta[h : h + 1, qs])).astype(BF)
                accv[...] += nn(probs.astype(BF), dm[h, qs, :])
                acck[...] += nn(ds, qm[h, qs, :])
                hs = slice(h * head, (h + 1) * head)
                accq[hs, qs] += nn(kt[hs, :], ds)
            for n in range(kb, blocks):

                @pl.when(qb == n)
                def _():
                    if n == blocks - 1 and kb > 0:
                        meet(kb - 1)
                    plan.hook()

            return 0

        lax.fori_loop(kb, blocks, queries, 0)
        blk[:, :part] = (accq[:, ks].T * (head**-0.5)).astype(BF)
        blk[:, part : 2 * part] = acck[...].astype(BF)
        blk[:, 2 * part :] = accv[...].astype(BF)
        sums = jnp.sum(blk[...].astype(F32), 0, keepdims=True)
        if kb == 0:
            gotp[...] = jnp.zeros(gotp.shape, F32)
        gotp[0:1, :] += sums
        fetch[kb].wait()
        step = 256
        for n in range(0, width, step):
            accw[n : n + step, :] += lax.dot_general(
                actb[kb % 2, :, n : n + step], blk[...], (((0,), (0,)), ((), ())), preferred_element_type=F32
            )
        if kb == blocks - 1:
            gq[...] = accw[...].astype(BF).reshape(gq.shape)
            plan.hook()
        weights = wq[...].reshape(width, 3 * part)
        for n in range(0, width, step):
            dap[kb, :, n : n + step] = nt(blk[...], weights[n : n + step, :]).astype(BF)
        tx, tc, inner, outerc = hops[kb]

        @pl.when(c != tc)
        def _():
            inner.start()

    fetch_tok = pltpu.make_async_copy(tok, actb.at[0], local.at[11])
    fetch_tok.start()
    plan.hook()
    meet(blocks - 1)
    plan.hook()

    step = 64
    rowg[...] = rows_in[...]
    wideg[...] = wide_in[...]
    lane_sum = jnp.sum(delta[...], 1, keepdims=True)
    for j in range(group):
        rowg[16 + j * heads : 16 + (j + 1) * heads, :] = jnp.where(
            s == j, jnp.broadcast_to(lane_sum[:heads], (heads, width)), 0.0
        )
    rowg[2:3, pl.ds(shift, part)] = gotp[0:1, :part]
    rowg[3:4, pl.ds(shift, part)] = gotp[0:1, 2 * part :]
    for t in range(blocks):
        tx, tc, inner, outerc = hops[t]

        @pl.when((x == tx) & (c == tc))
        def _():
            outerc.wait_recv()

    fetch_tok.wait()

    def finish(n, carry):
        at = pl.ds(pl.multiple_of(n * step, step), step)
        da = dap[s, at, :].astype(F32) + dfin[at, :].astype(F32)
        normed, inv = normalize(actb[0, at, :].astype(F32))
        grad = norm_back(da * gain[...], normed, inv) + grad_hidden[at, :]
        grad_tok[at, :] = grad.astype(BF)
        return (
            carry[0] + jnp.sum(da * normed, 0, keepdims=True),
            carry[1] + jnp.sum(da, 0, keepdims=True),
        )

    zero = jnp.zeros((1, width), F32)
    gain_one, shift_one = lax.fori_loop(0, span // step, finish, (zero, zero))
    rowg[0:1, :] = gain_one
    rowg[1:2, :] = shift_one

    plan.finish()
    for t in range(blocks):
        tx, tc, inner, outerc = hops[t]

        @pl.when(c != tc)
        def _():
            inner.wait_send()

        @pl.when((c == tc) & (x != tx))
        def _():
            outerc.wait_send()

    wire.drain()


def backward(do, q, k, v, att, lse, ids, wq, tok, grad_hidden, rows_in, wide_in, gain, act, g1, go, in2, in3, heads):
    length, part = q.shape
    span, width = tok.shape
    group = length // span
    b1, bo = g1.shape[3:], go.shape[4:]
    rows, triple = wq.shape[2:]
    bq = (group, rows, triple)
    dps = NZ * NY
    out = (
        (VM, (span, width), BF),
        (VM, (b1[0] // NC, NC * b1[1]), F32),
        (VM, (2 * in2.shape[1], width), F32),
        (VM, bo, F32),
        (VM, (rows, group * triple), F32),
        (VM, (rows_in.shape[0], width // dps), F32),
        (VM, (wide_in.shape[0], wide_in.shape[1] // dps), F32),
    )
    scratch = [
        pltpu.VMEM((heads, span, part), BF),
        pltpu.VMEM((heads, span, part), BF),
        pltpu.VMEM((heads, length, part), BF),
        pltpu.VMEM((heads, length, part), BF),
        pltpu.VMEM((part, span), BF),
        pltpu.VMEM((span, 8), jnp.int32),
        pltpu.VMEM((span, span), F32),
        pltpu.VMEM((span, part), F32),
        pltpu.VMEM((span, part), F32),
        pltpu.VMEM((part, length), F32),
        pltpu.VMEM((width, triple), F32),
        pltpu.VMEM((8, length), F32),
        pltpu.VMEM((span, triple), BF),
        pltpu.VMEM((2, span, width), BF),
        pltpu.VMEM((group, span, width), BF),
        pltpu.VMEM((NX, span, width), BF),
        pltpu.VMEM((span, width), BF),
        pltpu.VMEM((NZ,) + bq, BF),
        pltpu.VMEM((NZ,) + bq, BF),
        pltpu.VMEM((NZ - 1,) + bq, BF),
        pltpu.VMEM(bq, BF),
        pltpu.VMEM(bq, BF),
        pltpu.VMEM((NZ, NY) + bq, BF),
        pltpu.VMEM((8, triple), F32),
        pltpu.VMEM(b1, F32),
        pltpu.VMEM((b1[0] // NC, b1[1]), F32),
        pltpu.VMEM(rows_in.shape, F32),
        pltpu.VMEM((3,) + rows_in.shape, F32),
        pltpu.VMEM((NZ, rows_in.shape[0], width // dps), F32),
        pltpu.VMEM(wide_in.shape, F32),
        pltpu.VMEM((3,) + wide_in.shape, F32),
        pltpu.VMEM((NZ, wide_in.shape[0], wide_in.shape[1] // dps), F32),
        pltpu.VMEM((NZ, NY, NX) + bo, BF),
        pltpu.VMEM((NZ, NY, NX) + bo, BF),
    ]
    scratch += plane_scratch((b1[0], b1[1] // 2)) * 2 + plane_scratch(bo)
    scratch += [pltpu.VMEM(in2.shape, BF)] * 2 + plane_scratch(in2.shape[1:])[3:4] * 2
    scratch += [
        pltpu.SemaphoreType.DMA((COPIES,)),
        pltpu.SemaphoreType.DMA((COPIES,)),
        pltpu.SemaphoreType.DMA((13,)),
        pltpu.SemaphoreType.DMA((2 * group,)),
        pltpu.SemaphoreType.DMA((2 * group,)),
    ]
    return pl.pallas_call(
        functools.partial(backward_kernel, heads),
        out_shape=tuple(jax.ShapeDtypeStruct(shape, dtype) for _, shape, dtype in out),
        in_specs=[VM] * 12 + [HBM] * 6,
        out_specs=[spec for spec, _, _ in out],
        scratch_shapes=scratch,
        compiler_params=pltpu.CompilerParams(
            collective_id=2, has_side_effects=True, vmem_limit_bytes=63 * 1024 * 1024
        ),
        name="backward_row",
    )(
        q, k, v, att, lse, do, ids.reshape(1, length), wq, grad_hidden, rows_in, wide_in, gain,
        tok, act, g1, go, in2, in3,
    )


MIDDLE = (
    "ce",
    "",
    "",
    "",
    "",
    "23ce",
    "",
    "23",
    "23",
    "",
    "23",
    "2233",
    "2233",
    "2233",
    "",
    "",
)


def middle_tasks(wire, place, f2, f2v, g2, got2, got2b, got3, got3b):
    half = g2.shape[3] // 2
    one, two = pl.ds(0, half), pl.ds(half, half)
    return {
        "c": spread_last(wire, place, f2.at[:, :, :, one], f2v.at[:, :, :, one]),
        "e": spread_last(wire, place, f2.at[:, :, :, two], f2v.at[:, :, :, two], swap=True),
        "2": reduce_head(wire, place, g2.at[:, :, :, one], got2, got2b, swap=True),
        "3": reduce_head(wire, place, g2.at[:, :, :, two], got3, got3b),
    }


def tn(a, b):
    return lax.dot_general(a, b, (((0,), (0,)), ((), ())), preferred_element_type=F32)


def fold(value, rows=16):
    total = value[:rows]
    for n in range(1, value.shape[0] // rows):
        total = total + value[n * rows : (n + 1) * rows]
    return total


def lanes_of(value):
    total = value[:, :128]
    for n in range(1, value.shape[1] // 128):
        total = total + value[:, n * 128 : (n + 1) * 128]
    return total


def row_steps(count, step, fn):
    def body(n, _):
        fn(pl.ds(pl.multiple_of(n * step, step), step))
        return 0

    lax.fori_loop(0, count // step, body, 0)


def ffn_kernel(*refs):
    own, rows_all, wide_all, lanes = refs[:4]
    tok, cot, f2, wo, f1 = refs[4:9]
    out, do, gh, g1, go, half2, half3, rows_g, wide_g = refs[9:18]
    wov, f1v, f2v, dt, act, buf, slope, mix, dm, br, hid, g2, dbuf, prb, prc, stg, wv = refs[18:35]
    stat, stat_got, back, back_got, sums, colsums = refs[35:41]
    gots = refs[41:45]
    send, recv, local = refs[45:48]
    lane_mean, lane_square = dm.at[:, pl.ds(0, 128)], dm.at[:, pl.ds(128, 128)]
    place = Place()
    z, y, x, c, s = place.z, place.y, place.x, place.c, place.seq
    wire = Wire(place, send, recv)
    core = place.at(c=1 - c)
    span, width = own.shape
    units = f1v.shape[4]
    group = NX * NC
    tile = 512
    tiles = units // tile
    total_units = units * NC

    half = f2.shape[3] // 2
    one, two = pl.ds(0, half), pl.ds(half, half)
    loads = [
        pltpu.make_async_copy(wo, wov, local.at[0]),
        pltpu.make_async_copy(f2.at[:, y, :, one], f2v.at[:, y, :, one], local.at[1]),
        pltpu.make_async_copy(cot, dt.at[c], local.at[2]),
        pltpu.make_async_copy(f1, f1v, local.at[3]),
        pltpu.make_async_copy(f2.at[:, :, x, two], f2v.at[:, :, x, two], local.at[4]),
        pltpu.make_async_copy(tok, prc, local.at[5]),
    ]
    for desc in loads:
        desc.start()
    chunk = span // 4
    chunks = [pl.ds(n * chunk, chunk) for n in range(4)]
    dt_copy = wire.copy(cot, dt.at[c], core)
    act_copies = [wire.copy(act.at[c, at], act.at[c, at], core) for at in chunks]
    stat_copies = [wire.copy(stat.at[h], stat_got.at[h], core) for h in range(NC)]
    back_copies = [wire.copy(back.at[h], back_got.at[h], core) for h in range(NC)]
    out_copy = wire.copy(dbuf, prb, core)
    da_copy = wire.copy(prb, prc, core)
    mine_at = pl.ds(pl.multiple_of(s * span, span), span)
    part_size = width // group

    def give(j):
        return prb.at[:, pl.ds(pl.multiple_of(j * part_size, part_size), part_size)]

    outgoing = [
        wire.copy(give(s ^ m), do.at[mine_at], dev)
        for dev, m in ((core, 1), (place.at(x=1 - x), 2), (place.at(x=1 - x, c=1 - c), 3))
    ]
    greet(place)
    dt_copy.go()
    plan = Plan(middle_tasks(wire, place, f2, f2v, g2, *gots), MIDDLE)
    plan.hook()

    def row(ref, n):
        return ref[n : n + 1, :].astype(F32)

    lane = wide_all.shape[1] // (NZ * NY * NX * NC)
    for n in range(NZ * NY * NX):
        at = pl.ds(pl.multiple_of((n * NC + c) * lane, lane), lane)
        wv[0:3, n * lane : (n + 1) * lane] = wide_all[0:3, at].astype(F32)
    colsums[...] = jnp.zeros(colsums.shape, F32)
    sums[...] = jnp.zeros(sums.shape, F32)
    loads[0].wait()
    loads[5].wait()

    for at, copy in zip(chunks, act_copies):
        branch = nn(own[at, :], wov[...].reshape(width, width)) + row(rows_all, 4)
        br[at, :] = branch

        def fn(inner, at=at):
            rows = pl.ds(at.start + inner.start, inner.size)
            hidden = prc[rows, :].astype(F32) + normalize(br[rows, :])[0] * row(rows_all, 5) + row(rows_all, 6)
            hid[rows, :] = hidden
            act[c, rows, :] = (normalize(hidden)[0] * row(rows_all, 7) + row(rows_all, 8)).astype(BF)

        row_steps(chunk, 64, fn)
        copy.go()
    plan.hook()
    loads[3].wait()

    for h in range(NC):

        @pl.when(c != h)
        def _():
            for copy in act_copies:
                copy.wait_recv()

        for n in range(tiles):
            cols = slice(n * tile, (n + 1) * tile)
            weights = f1v[:, :, :, :, cols].reshape(width, tile)
            buf[h, :, cols] = nn(act[h], weights) + wv[0:1, cols]

        def fn(at, h=h):
            count = units // 128
            pivot = None
            for n in range(tiles):
                cols = slice(n * tile, (n + 1) * tile)
                u = buf[h, at, cols]
                cdf = 0.5 + 0.5 * lax.erf(u * math.sqrt(0.5))
                value = u * cdf
                buf[h, at, cols] = value
                pdf = jnp.exp(-0.5 * u * u) * (1.0 / math.sqrt(2.0 * math.pi))
                slope[h, at, cols] = (cdf + u * pdf).astype(BF)
                if pivot is None:
                    pivot = value[:, :128]
                    total, square = jnp.zeros_like(pivot), jnp.zeros_like(pivot)
                for j in range(tile // 128):
                    gap = value[:, j * 128 : (j + 1) * 128] - pivot
                    total = total + gap
                    square = square + gap * gap
            shift = total * (1.0 / count)
            lane_mean[at, :] = pivot + shift
            lane_square[at, :] = square - total * shift

        row_steps(span, 32, fn)

        def fn(at, h=h):
            count = units // 128
            means = lane_mean[at, :]
            mean = jnp.mean(means, 1, keepdims=True)
            gap = means - mean
            square = jnp.sum(lane_square[at, :] + count * (gap * gap), 1, keepdims=True)
            column = lax.broadcasted_iota(jnp.int32, (at.size, 128), 1)
            stat[h, at, :] = jnp.where(column == 0, mean, square)

        row_steps(span, 128, fn)
        stat_copies[h].go()
        plan.hook()

    for h in range(NC):
        stat_copies[h].wait_recv()
        stat_copies[h].wait_send()

        def fn(at, h=h):
            mean_a, mean_b = stat[h, at, 0:1], stat_got[h, at, 0:1]
            gap = mean_a - mean_b
            square = stat[h, at, 1:2] + stat_got[h, at, 1:2] + gap * gap * (0.5 * units)
            mean = 0.5 * (mean_a + mean_b)
            inv = lax.rsqrt(square * (1.0 / total_units) + EPSILON)
            stat[h, at, :] = jnp.broadcast_to(inv, (at.size, 128))
            for n in range(tiles):
                cols = slice(n * tile, (n + 1) * tile)
                normed = (buf[h, at, cols] - mean) * inv
                buf[h, at, cols] = normed
                mix[h, at, cols] = (normed * wv[1:2, cols] + wv[2:3, cols]).astype(BF)

        row_steps(span, 64, fn)
    plan.hook()

    loads[2].wait()
    loads[1].wait()
    loads[4].wait()
    dt_copy.wait_recv()
    per = g2.shape[3]
    for n in range(units // (2 * per)):
        cols = slice(n * 2 * per, (n + 1) * 2 * per)
        part = tn(mix[0, :, cols], dt[0]) + tn(mix[1, :, cols], dt[1])
        g2[n // NY, n % NY] = part.astype(BF).reshape(NX, per, width)
    plan.hook()

    weights2 = f2v[...].reshape(units, width)
    for n in range(0, width, tile):
        dbuf[:, n : n + tile] = nn(mix[1 - c], weights2[:, n : n + tile]).astype(BF)
    out_copy.go()
    for n in range(0, width, tile):
        cols = slice(n, n + tile)
        gh[:, cols] = nn(mix[c], weights2[:, cols]) + hid[:, cols] + rows_all[9:10, cols].astype(F32)
    plan.hook()

    for h in range(NC):
        for n in range(tiles):
            cols = slice(n * tile, (n + 1) * tile)
            dm[:, cols] = nt(dt[h], weights2[cols, :])

        def fn(at, h=h):
            first = jnp.zeros((at.size, 128), F32)
            second = jnp.zeros((at.size, 128), F32)
            for n in range(tiles):
                cols = slice(n * tile, (n + 1) * tile)
                grad = dm[at, cols]
                product = grad * buf[h, at, cols]
                colsums[1, :, cols] += fold(product)
                colsums[2, :, cols] += fold(grad)
                first = first + lanes_of(grad * wv[1:2, cols])
                second = second + lanes_of(product * wv[1:2, cols])
            column = lax.broadcasted_iota(jnp.int32, (at.size, 128), 1)
            first = jnp.sum(first, 1, keepdims=True)
            second = jnp.sum(second, 1, keepdims=True)
            back[h, at, :] = jnp.where(column == 0, first, second)

        row_steps(span, 64, fn)
        back_copies[h].go()
        plan.hook()
        back_copies[h].wait_recv()

        def fn(at, h=h):
            scale = 1.0 / total_units
            first = (back[h, at, 0:1] + back_got[h, at, 0:1]) * scale
            second = (back[h, at, 1:2] + back_got[h, at, 1:2]) * scale
            inv = stat[h, at, 0:1]
            for n in range(tiles):
                cols = slice(n * tile, (n + 1) * tile)
                grad = inv * (dm[at, cols] * wv[1:2, cols] - first - buf[h, at, cols] * second)
                inner = (grad * slope[h, at, cols].astype(F32)).astype(BF)
                mix[h, at, cols] = inner
                colsums[0, :, cols] += fold(inner.astype(F32))

        row_steps(span, 64, fn)
        plan.hook()

    weights1 = f1v[...].reshape(width, units)
    out_copy.wait_recv()
    out[...] = (gh[...] + prb[...].astype(F32)).astype(BF)
    for n in range(0, width, tile):
        prb[:, n : n + tile] = nt(mix[1 - c], weights1[n : n + tile, :]).astype(BF)
    da_copy.go()
    for n in range(0, width, tile):
        gh[:, n : n + tile] = nt(mix[c], weights1[n : n + tile, :])
    plan.hook()
    size = stg.shape[1]
    writes = []

    def write(part, dst, wide):
        n = len(writes)
        if n >= 2:
            writes[n - 2].wait()
        stg[n % 2, :, 0:wide] = part.astype(BF)
        desc = pltpu.make_async_copy(stg.at[n % 2, :, pl.ds(0, wide)], dst, local.at[6 + n % 2])
        desc.start()
        writes.append(desc)

    for n in range(0, width, size):
        part = tn(act[0, :, n : n + size], mix[0]) + tn(act[1, :, n : n + size], mix[1])
        write(part, g1.at[pl.ds(n, size)], units)
    plan.hook()
    da_copy.wait_recv()
    out_copy.wait_send()

    def fn(at):
        da = gh[at, :] + prc[at, :].astype(F32)
        top = dt[c, at, :].astype(F32)
        normed, inv = normalize(hid[at, :])
        grad = top + norm_back(da * row(rows_all, 7), normed, inv)
        gh[at, :] = grad
        normed_b, inv_b = normalize(br[at, :])
        down = norm_back(grad * row(rows_all, 5), normed_b, inv_b).astype(BF)
        dbuf[at, :] = down
        for n, value in enumerate((down.astype(F32), grad * normed_b, grad, da * normed, da, top)):
            sums[n] += fold(value)

    row_steps(span, 64, fn)
    plan.hook()
    weights_o = wov[...].reshape(width, width)
    da_copy.wait_send()
    for j in range(group):
        at = slice(j * part_size, (j + 1) * part_size)
        prb[:, at] = (nt(dbuf[...], weights_o[at, :]) * lanes[:, at]).astype(BF)
    for copy in outgoing:
        copy.go()
    keep = pltpu.make_async_copy(give(s), do.at[mine_at], local.at[8])
    keep.start()
    plan.hook()
    for n in range(0, width, size):
        write(tn(own[:, n : n + size], dbuf[...]), go.at[pl.ds(n, size)], width)
    rows_g[...] = jnp.zeros(rows_g.shape, F32)
    for n in range(6):
        rows_g[4 + n : 5 + n, :] = jnp.sum(sums[n], 0, keepdims=True)
    wide_g[...] = jnp.zeros(wide_g.shape, F32)
    for n in range(NZ * NY * NX):
        at = pl.ds(pl.multiple_of((n * NC + c) * lane, lane), lane)
        for j in range(3):
            wide_g[j : j + 1, at] = jnp.sum(colsums[j, :, n * lane : (n + 1) * lane], 0, keepdims=True)
    plan.finish()
    for k in range(NZ):
        zk = place.zup((1, 2, 3, 0)[k])
        for src, dst, n in ((g2.at[zk, y, x, one], half2, 9), (g2.at[zk, y, x, two], half3, 10)):
            desc = pltpu.make_async_copy(src, dst.at[k], local.at[n + 2 * k])
            desc.start()
            writes.append(desc)
    for desc in writes[-2 * NZ :]:
        desc.wait()
    writes = writes[: -2 * NZ]
    keep.wait()
    for copy in outgoing:
        copy.wait_recv()
    for desc in writes[-2:]:
        desc.wait()
    wire.drain()


def feed_forward(own, rows_all, wide_all, lanes, tok, cot, f2, wo, f1):
    span, width = own.shape
    units = f1.shape[4]
    group = NX * NC
    per = f2.shape[3]
    out = (
        (VM, (span, width), BF),
        (HBM, (group * span, width // group), BF),
        (VM, (span, width), F32),
        (HBM, (width, units), BF),
        (HBM, (width, width), BF),
        (HBM, (NZ, per // 2, width), BF),
        (HBM, (NZ, per // 2, width), BF),
        (VM, (32, width), F32),
        (VM, (8, wide_all.shape[1]), F32),
    )
    scratch = [
        pltpu.VMEM(wo.shape, BF),
        pltpu.VMEM(f1.shape, BF),
        pltpu.VMEM((NZ, NY, NX) + (per, width), BF),
        pltpu.VMEM((NC, span, width), BF),
        pltpu.VMEM((NC, span, width), BF),
        pltpu.VMEM((NC, span, units), F32),
        pltpu.VMEM((NC, span, units), BF),
        pltpu.VMEM((NC, span, units), BF),
        pltpu.VMEM((span, units), F32),
        pltpu.VMEM((span, width), F32),
        pltpu.VMEM((span, width), F32),
        pltpu.VMEM((NZ, NY, NX) + (per, width), BF),
        pltpu.VMEM((span, width), BF),
        pltpu.VMEM((span, width), BF),
        pltpu.VMEM((span, width), BF),
        pltpu.VMEM((2, 128, units), BF),
        pltpu.VMEM((8, units), F32),
    ]
    scratch += [pltpu.VMEM((NC, span, 128), F32)] * 4
    scratch += [pltpu.VMEM((6, 16, width), F32), pltpu.VMEM((3, 16, units), F32)]
    scratch += plane_scratch((per // 2, width))[1:3] * 2
    scratch += [
        pltpu.SemaphoreType.DMA((COPIES,)),
        pltpu.SemaphoreType.DMA((COPIES,)),
        pltpu.SemaphoreType.DMA((17,)),
    ]
    return pl.pallas_call(
        ffn_kernel,
        out_shape=tuple(jax.ShapeDtypeStruct(shape, dtype) for _, shape, dtype in out),
        in_specs=[VM] * 4 + [HBM] * 5,
        out_specs=[spec for spec, _, _ in out],
        scratch_shapes=scratch,
        compiler_params=pltpu.CompilerParams(
            collective_id=3, has_side_effects=True, vmem_limit_bytes=63 * 1024 * 1024
        ),
        name="feed_forward",
    )(own, rows_all, wide_all, lanes, tok, cot, f2, wo, f1)


def fast(tokens, doc_ids, cotangent, w_qkv, w_out, attn_vecs, head_scale, w_fc1, w_fc2, ffn_vecs, ffn_wide):
    _, span, width = tokens.shape
    group = NX * NC
    length = span * group
    head_count = head_scale.shape[0]
    head = width // head_count
    heads = head_count // group
    part = heads * head
    seq = lax.axis_index("seq")
    chips = NZ * NY * NX
    block = w_fc2.shape[0]
    units = chips * block

    rows = w_qkv.shape[0]
    wq4 = w_qkv.astype(BF).reshape(rows, 3, group, part).transpose(2, 0, 1, 3).reshape(group, rows, 3 * part)
    f1 = w_fc1.astype(BF).reshape(rows, chips, NC, block).transpose(2, 0, 1, 3).reshape(NC, rows, units)
    f2 = w_fc2.astype(BF)
    narrow = jnp.concatenate([attn_vecs, ffn_vecs], 0).astype(BF)
    count, each = narrow.shape
    lane = each * group
    narrow = lax.dynamic_update_slice(jnp.zeros((16, lane), BF), narrow, (0, seq * each))
    vec = jnp.stack([narrow, jnp.pad(ffn_wide.astype(BF), ((0, 16 - ffn_wide.shape[0]), (0, 0)))])
    tok = tokens.reshape(span, width)
    scale_own = lax.dynamic_slice_in_dim(head_scale, heads * seq, heads)
    scale_lanes = jnp.repeat(scale_own, head).reshape(1, part)
    ids = doc_ids.reshape(length)
    act_one, q, k, v, att, lse, scaled_own, wq, rows_all, wide_all, wo, fc1, fc2 = forward(
        tok, wq4, vec, w_out.astype(BF), f1, f2, ids, scale_lanes, heads
    )
    outputs, do, grad_hidden, grad_fc1, grad_out, half2, half3, rows_in, wide_grads = feed_forward(
        scaled_own,
        rows_all,
        wide_all,
        jnp.repeat(head_scale, head).reshape(1, width),
        tok,
        cotangent.reshape(span, width),
        fc2,
        wo,
        fc1,
    )
    grad_tokens, grad_w1, grad_w2, grad_wo, grad_wqkv, rows_out, wide_out = backward(
        do,
        q,
        k,
        v,
        att,
        lse,
        ids,
        wq,
        tok,
        grad_hidden,
        rows_in,
        wide_grads,
        rows_all[:1].astype(F32),
        act_one,
        grad_fc1.reshape(NZ, NY, NX, NC * rows, units),
        grad_out.reshape(NZ, NY, NX, NC, rows, width),
        half2,
        half3,
        heads,
    )
    mine = lax.dynamic_slice_in_dim(rows_out, seq * each, each, 1)
    wide_mine = lax.dynamic_slice_in_dim(wide_out, seq * block, block, 1)
    return (
        outputs.reshape(1, span, width),
        grad_tokens.reshape(1, span, width),
        grad_wqkv,
        grad_wo,
        mine[: attn_vecs.shape[0]],
        rows_out[16 : 16 + head_count, 0] / head_scale,
        grad_w1,
        grad_w2,
        mine[attn_vecs.shape[0] : count],
        wide_mine[: ffn_wide.shape[0]],
    )


def solution(mesh):
    placed = (
        P("dp", "seq", None),
        P("dp", None),
        P("dp", "seq", None),
        P(("dp", "seq"), None),
        P(("dp", "seq"), None),
        P(None, ("dp", "seq")),
        P(),
        P(("dp", "seq"), None),
        P(("dp", "seq"), None),
        P(None, ("dp", "seq")),
        P(None, ("dp", "seq")),
    )
    results = (
        P("dp", "seq", None),
        P("dp", "seq", None),
        P(("dp", "seq"), None),
        P(("dp", "seq"), None),
        P(None, ("dp", "seq")),
        P(),
        P(("dp", "seq"), None),
        P(("dp", "seq"), None),
        P(None, ("dp", "seq")),
        P(None, ("dp", "seq")),
    )
    suits = mesh.shape["dp"] == NZ * NY and mesh.shape["seq"] == NX * NC
    return jax.shard_map(
        fast if suits else local, mesh=mesh, in_specs=placed, out_specs=results, check_vma=False
    )
```

```python
import functools
import math

import jax
import jax.numpy as jnp
from jax import lax
from jax.experimental import pallas as pl
from jax.experimental.pallas import tpu as pltpu
from jax.sharding import PartitionSpec as P

EPSILON = 1e-05
NEGATIVE = -1e30
MESH = pl.DeviceIdType.MESH
BF = jnp.bfloat16
F32 = jnp.float32
NZ, NY, NX, NC = 4, 2, 2, 2
HBM = pl.BlockSpec(memory_space=pl.ANY)
VM = pl.BlockSpec(memory_space=pltpu.VMEM)


def normalize(values):
    centre = jnp.mean(values, -1, keepdims=True)
    centred = values - centre
    scale_inv = lax.rsqrt(jnp.mean(centred * centred, -1, keepdims=True) + EPSILON)
    return (centred * scale_inv, scale_inv)


def norm_back(grad_normed, normed, scale_inv):
    return scale_inv * (
        grad_normed
        - jnp.mean(grad_normed, -1, keepdims=True)
        - normed * jnp.mean(grad_normed * normed, -1, keepdims=True)
    )


def gelu_exact(values):
    return 0.5 * values * (1.0 + jax.scipy.special.erf(values * math.sqrt(0.5)))


def left_grad(activations, gradients):
    return lax.dot_general(
        activations, gradients, (((0,), (0,)), ((), ())), preferred_element_type=jnp.float32
    )


def right_back(gradients, matrix):
    return lax.dot_general(
        gradients, matrix, (((1,), (1,)), ((), ())), preferred_element_type=jnp.float32
    )


def masked_scores(queries, keys_block, query_pos, key_pos, query_ids, key_ids):
    raw_scores = jnp.einsum(
        "rqhe,rkhe->rhqk", queries, keys_block, preferred_element_type=jnp.float32
    )
    allowed = (key_pos[None, None, :] <= query_pos[None, :, None]) & (
        key_ids[:, None, :] == query_ids[:, :, None]
    )
    return jnp.where(allowed[:, None], raw_scores * queries.shape[3] ** (-0.5), NEGATIVE)


def attend(queries, keys_all, values_all, query_pos, query_ids, doc_rows, block_len):
    block_count = keys_all.shape[1] // block_len
    stat_shape = (queries.shape[0], queries.shape[2], queries.shape[1])

    def slice_block(block_index):
        start = block_index * block_len
        keys_block = lax.dynamic_slice_in_dim(keys_all, start, block_len, 1)
        values_block = lax.dynamic_slice_in_dim(values_all, start, block_len, 1)
        key_ids = lax.dynamic_slice_in_dim(doc_rows, start, block_len, 1)
        key_pos = start + jnp.arange(block_len, dtype=jnp.int32)
        return (
            values_block,
            masked_scores(queries, keys_block, query_pos, key_pos, query_ids, key_ids),
        )

    def first_pass(carry, block_index):
        running_max, running_sum = carry
        _, scores = slice_block(block_index)
        new_max = jnp.maximum(running_max, jnp.max(scores, -1))
        running_sum = running_sum * jnp.exp(running_max - new_max) + jnp.sum(
            jnp.exp(scores - new_max[..., None]), -1
        )
        return ((new_max, running_sum), None)

    start_stats = (jnp.full(stat_shape, NEGATIVE, jnp.float32), jnp.zeros(stat_shape, jnp.float32))
    (row_max, row_sum), _ = lax.scan(
        first_pass, start_stats, jnp.arange(block_count, dtype=jnp.int32)
    )
    log_total = row_max + jnp.log(row_sum)

    def second_pass(total_out, block_index):
        values_block, scores = slice_block(block_index)
        probs = jnp.exp(scores - log_total[..., None]).astype(jnp.bfloat16)
        return (
            total_out
            + jnp.einsum(
                "rhqk,rkhe->rqhe", probs, values_block, preferred_element_type=jnp.float32
            ),
            None,
        )

    attended, _ = lax.scan(
        second_pass, jnp.zeros(queries.shape, jnp.float32), jnp.arange(block_count, dtype=jnp.int32)
    )
    return (attended, log_total)


def attend_back(
    queries,
    keys_all,
    values_all,
    grad_out,
    log_total,
    delta,
    query_pos,
    query_ids,
    doc_rows,
    block_len,
):
    block_count = keys_all.shape[1] // block_len
    scale = queries.shape[3] ** (-0.5)

    def step(grad_queries, block_index):
        start = block_index * block_len
        keys_block = lax.dynamic_slice_in_dim(keys_all, start, block_len, 1)
        values_block = lax.dynamic_slice_in_dim(values_all, start, block_len, 1)
        key_ids = lax.dynamic_slice_in_dim(doc_rows, start, block_len, 1)
        key_pos = start + jnp.arange(block_len, dtype=jnp.int32)
        scores = masked_scores(queries, keys_block, query_pos, key_pos, query_ids, key_ids)
        probs = jnp.exp(scores - log_total[..., None])
        grad_probs = jnp.einsum(
            "rqhe,rkhe->rhqk", grad_out, values_block, preferred_element_type=jnp.float32
        )
        grad_scores = (probs * (grad_probs - delta[..., None]) * scale).astype(jnp.bfloat16)
        grad_queries = grad_queries + jnp.einsum(
            "rhqk,rkhe->rqhe", grad_scores, keys_block, preferred_element_type=jnp.float32
        )
        grad_keys = jnp.einsum(
            "rhqk,rqhe->rkhe", grad_scores, queries, preferred_element_type=jnp.float32
        )
        grad_values = jnp.einsum(
            "rhqk,rqhe->rkhe",
            probs.astype(jnp.bfloat16),
            grad_out,
            preferred_element_type=jnp.float32,
        )
        return (grad_queries, (grad_keys, grad_values))

    return lax.scan(
        step, jnp.zeros(queries.shape, jnp.float32), jnp.arange(block_count, dtype=jnp.int32)
    )


def local(
    tokens,
    doc_ids,
    cotangent,
    w_qkv,
    w_out,
    attn_vecs,
    head_scale,
    w_fc1,
    w_fc2,
    ffn_vecs,
    ffn_wide,
):
    row_count, span_len, model_width = tokens.shape
    head_count = head_scale.shape[0]
    head_size = model_width // head_count
    token_count = row_count * span_len
    brain = jnp.bfloat16
    single = jnp.float32
    gathered_qkv, gathered_out, attn_rows = (
        lax.all_gather(w_qkv.astype(brain), ("dp", "seq"), axis=0, tiled=True),
        lax.all_gather(w_out.astype(brain), ("dp", "seq"), axis=0, tiled=True),
        lax.all_gather(attn_vecs.astype(brain), ("dp", "seq"), axis=1, tiled=True),
    )
    attn_rows = attn_rows.astype(single)
    inputs = tokens.astype(single).reshape(token_count, model_width)
    normed_one, inv_one = normalize(inputs)
    act_one = (normed_one * attn_rows[0] + attn_rows[1]).astype(brain)
    projected = jnp.dot(act_one, gathered_qkv, preferred_element_type=single)
    queries = (projected[:, :model_width] + attn_rows[2]).astype(brain)
    keys_own = projected[:, model_width : 2 * model_width].astype(brain)
    values_own = (projected[:, 2 * model_width :] + attn_rows[3]).astype(brain)
    keys_all, values_all = (
        lax.all_gather(
            keys_own.reshape(row_count, span_len, model_width), "seq", axis=1, tiled=True
        ),
        lax.all_gather(
            values_own.reshape(row_count, span_len, model_width), "seq", axis=1, tiled=True
        ),
    )
    offset = lax.axis_index("seq") * span_len
    query_pos = offset + jnp.arange(span_len, dtype=jnp.int32)
    query_ids = lax.dynamic_slice_in_dim(doc_ids, offset, span_len, 1)
    queries_four = queries.reshape(row_count, span_len, head_count, head_size)
    keys_four = keys_all.reshape(row_count, -1, head_count, head_size)
    values_four = values_all.reshape(row_count, -1, head_count, head_size)
    attended, log_total = attend(
        queries_four, keys_four, values_four, query_pos, query_ids, doc_ids, span_len
    )
    scaled = (
        (attended * head_scale[None, None, :, None]).reshape(token_count, model_width).astype(brain)
    )
    branch = jnp.dot(scaled, gathered_out, preferred_element_type=single) + attn_rows[4]
    normed_branch, inv_branch = normalize(branch)
    hidden = inputs + normed_branch * attn_rows[5] + attn_rows[6]
    gathered_fc1, gathered_fc2, ffn_rows, wide_rows = (
        lax.all_gather(w_fc1.astype(brain), ("dp", "seq"), axis=0, tiled=True),
        lax.all_gather(w_fc2.astype(brain), ("dp", "seq"), axis=0, tiled=True),
        lax.all_gather(ffn_vecs.astype(brain), ("dp", "seq"), axis=1, tiled=True),
        lax.all_gather(ffn_wide.astype(brain), ("dp", "seq"), axis=1, tiled=True),
    )
    ffn_rows = ffn_rows.astype(single)
    wide_rows = wide_rows.astype(single)
    normed_two, inv_two = normalize(hidden)
    act_two = (normed_two * ffn_rows[0] + ffn_rows[1]).astype(brain)
    inner_act = jnp.dot(act_two, gathered_fc1, preferred_element_type=single) + wide_rows[0]
    activated, gelu_pull = jax.vjp(gelu_exact, inner_act)
    normed_three, inv_three = normalize(activated)
    mixed_act = (normed_three * wide_rows[1] + wide_rows[2]).astype(brain)
    result = hidden + jnp.dot(mixed_act, gathered_fc2, preferred_element_type=single) + ffn_rows[2]
    outputs = result.astype(brain).reshape(row_count, span_len, model_width)
    back_set = (
        lax.all_gather(w_qkv.astype(brain), ("dp", "seq"), axis=0, tiled=True),
        lax.all_gather(w_out.astype(brain), ("dp", "seq"), axis=0, tiled=True),
        lax.all_gather(attn_vecs.astype(brain), ("dp", "seq"), axis=1, tiled=True),
        lax.all_gather(w_fc1.astype(brain), ("dp", "seq"), axis=0, tiled=True),
        lax.all_gather(w_fc2.astype(brain), ("dp", "seq"), axis=0, tiled=True),
        lax.all_gather(ffn_vecs.astype(brain), ("dp", "seq"), axis=1, tiled=True),
        lax.all_gather(ffn_wide.astype(brain), ("dp", "seq"), axis=1, tiled=True),
    )
    gathered_qkv, gathered_out, attn_back, gathered_fc1, gathered_fc2, ffn_back, wide_back = (
        back_set
    )
    attn_rows = attn_back.astype(single)
    ffn_rows = ffn_back.astype(single)
    wide_rows = wide_back.astype(single)
    grad_top = cotangent.astype(single).reshape(token_count, model_width)
    grad_branch_two = grad_top.astype(brain)
    grad_fc2 = left_grad(mixed_act, grad_branch_two)
    grad_bias_two = jnp.sum(grad_branch_two.astype(single), 0)
    grad_mixed = right_back(grad_branch_two, gathered_fc2)
    grad_inner_gain = jnp.sum(grad_mixed * normed_three, 0)
    grad_inner_bias = jnp.sum(grad_mixed, 0)
    grad_activated = norm_back(grad_mixed * wide_rows[1], normed_three, inv_three)
    grad_inner = gelu_pull(grad_activated)[0].astype(brain)
    grad_fc1 = left_grad(act_two, grad_inner)
    grad_bias_one = jnp.sum(grad_inner.astype(single), 0)
    grad_act_two = right_back(grad_inner, gathered_fc1)
    grad_gain_two = jnp.sum(grad_act_two * normed_two, 0)
    grad_shift_two = jnp.sum(grad_act_two, 0)
    grad_hidden = grad_top + norm_back(grad_act_two * ffn_rows[0], normed_two, inv_two)
    ffn_sums = (
        lax.psum_scatter(grad_fc1, ("dp", "seq"), scatter_dimension=0, tiled=True),
        lax.psum_scatter(grad_fc2, ("dp", "seq"), scatter_dimension=0, tiled=True),
        lax.psum_scatter(
            jnp.stack([grad_gain_two, grad_shift_two, grad_bias_two]),
            ("dp", "seq"),
            scatter_dimension=1,
            tiled=True,
        ),
        lax.psum_scatter(
            jnp.stack([grad_bias_one, grad_inner_gain, grad_inner_bias]),
            ("dp", "seq"),
            scatter_dimension=1,
            tiled=True,
        ),
    )
    grad_post_gain = jnp.sum(grad_hidden * normed_branch, 0)
    grad_post_shift = jnp.sum(grad_hidden, 0)
    grad_branch = norm_back(grad_hidden * attn_rows[5], normed_branch, inv_branch).astype(brain)
    grad_out_bias = jnp.sum(grad_branch.astype(single), 0)
    grad_out = left_grad(scaled, grad_branch)
    grad_scaled = right_back(grad_branch, gathered_out).reshape(
        row_count, span_len, head_count, head_size
    )
    grad_scale = jnp.sum(grad_scaled * attended, (0, 1, 3))
    grad_attended = (grad_scaled * head_scale[None, None, :, None]).astype(brain)
    delta = jnp.transpose(jnp.sum(grad_attended.astype(single) * attended, -1), (0, 2, 1))
    grad_queries, key_parts = attend_back(
        queries_four,
        keys_four,
        values_four,
        grad_attended,
        log_total,
        delta,
        query_pos,
        query_ids,
        doc_ids,
        span_len,
    )
    partial_keys = jnp.transpose(key_parts[0], (1, 0, 2, 3, 4)).reshape(row_count, -1, model_width)
    partial_values = jnp.transpose(key_parts[1], (1, 0, 2, 3, 4)).reshape(
        row_count, -1, model_width
    )
    grad_keys, grad_values = (
        lax.psum_scatter(
            partial_keys.astype(jnp.bfloat16), "seq", scatter_dimension=1, tiled=True
        ).astype(jnp.float32),
        lax.psum_scatter(
            partial_values.astype(jnp.bfloat16), "seq", scatter_dimension=1, tiled=True
        ).astype(jnp.float32),
    )
    grad_qkv = jnp.concatenate(
        [
            grad_queries.reshape(token_count, model_width).astype(brain),
            grad_keys.reshape(token_count, model_width).astype(brain),
            grad_values.reshape(token_count, model_width).astype(brain),
        ],
        1,
    )
    grad_w_qkv = left_grad(act_one, grad_qkv)
    grad_query_bias = jnp.sum(grad_qkv[:, :model_width].astype(single), 0)
    grad_value_bias = jnp.sum(grad_qkv[:, 2 * model_width :].astype(single), 0)
    grad_act_one = right_back(grad_qkv, gathered_qkv)
    grad_gain_one = jnp.sum(grad_act_one * normed_one, 0)
    grad_shift_one = jnp.sum(grad_act_one, 0)
    grad_tokens = (
        (grad_hidden + norm_back(grad_act_one * attn_rows[0], normed_one, inv_one))
        .astype(brain)
        .reshape(row_count, span_len, model_width)
    )
    attn_stack = jnp.stack(
        [
            grad_gain_one,
            grad_shift_one,
            grad_query_bias,
            grad_value_bias,
            grad_out_bias,
            grad_post_gain,
            grad_post_shift,
        ]
    )
    attn_sums = (
        lax.psum_scatter(grad_w_qkv, ("dp", "seq"), scatter_dimension=0, tiled=True),
        lax.psum_scatter(grad_out, ("dp", "seq"), scatter_dimension=0, tiled=True),
        lax.psum_scatter(attn_stack, ("dp", "seq"), scatter_dimension=1, tiled=True),
    )
    scale_total = lax.psum(grad_scale, ("dp", "seq"))
    return (
        outputs,
        grad_tokens,
        attn_sums[0],
        attn_sums[1],
        attn_sums[2],
        scale_total,
        ffn_sums[0],
        ffn_sums[1],
        ffn_sums[2],
        ffn_sums[3],
    )


class Place:
    def __init__(self):
        self.dp = lax.axis_index("dp")
        self.seq = lax.axis_index("seq")
        self.z, self.y = self.dp // NY, self.dp % NY
        self.x, self.c = self.seq // NC, self.seq % NC

    def at(self, z=None, y=None, x=None, c=None):
        z = self.z if z is None else z
        y = self.y if y is None else y
        x = self.x if x is None else x
        c = self.c if c is None else c
        return (z * NY + y, x * NC + c)

    def zup(self, k):
        return (self.z + k) % NZ

    def group(self):
        near = [self.at(c=1 - self.c), self.at(x=1 - self.x), self.at(x=1 - self.x, c=1 - self.c)]
        return near + [self.at(y=1 - self.y)] + [self.at(z=self.zup(k)) for k in range(1, NZ)]


class Copy:
    def __init__(self, desc):
        self.desc, self.sent = desc, False

    def go(self):
        self.desc.start()
        return self

    def wait_recv(self):
        self.desc.wait_recv()

    def wait_send(self):
        if not self.sent:
            self.desc.wait_send()
        self.sent = True


class Wire:
    def __init__(self, place, send, recv):
        self.place, self.send, self.recv, self.used, self.open = place, send, recv, 0, []

    def copy(self, src, dst, dev):
        n = self.used
        self.used += 1
        copy = Copy(
            pltpu.make_async_remote_copy(
                src_ref=src,
                dst_ref=dst,
                send_sem=self.send.at[n],
                recv_sem=self.recv.at[n],
                device_id=dev,
                device_id_type=MESH,
            )
        )
        self.open.append(copy)
        return copy

    def drain(self):
        for copy in self.open:
            copy.wait_send()


def greet(place):
    barrier = pltpu.get_barrier_semaphore()
    group = place.group()
    for dev in group:
        pl.semaphore_signal(barrier, inc=1, device_id=dev, device_id_type=MESH)
    pl.semaphore_wait(barrier, len(group))


def spread_zxy(wire, place, ref, swap=False):
    z, y, x = place.z, place.y, place.x
    own = ref.at[z, y, x]
    first = place.at(y=1 - y) if swap else place.at(x=1 - x)
    second = place.at(x=1 - x) if swap else place.at(y=1 - y)
    order = [(z - k + NZ) % NZ for k in range(NZ)]
    along_z = [wire.copy(own, own, place.at(z=place.zup(k))) for k in range(1, NZ)]
    firsts = [wire.copy(ref.at[zk, y, x], ref.at[zk, y, x], first) for zk in order]
    twos = [ref.at[zk, :, x] if swap else ref.at[zk, y] for zk in order]
    seconds = [wire.copy(two, two, second) for two in twos]
    yield
    for copy in along_z + firsts[:1]:
        copy.go()
    yield
    for k in range(1, NZ):
        along_z[k - 1].wait_recv()
        firsts[k].go()
        yield
    for k in range(NZ):
        firsts[k].wait_recv()
        seconds[k].go()
        yield
    for copy in seconds:
        copy.wait_recv()


def spread_xzy(wire, place, ref, swap=False):
    z, y, x = place.z, place.y, place.x
    own = ref.at[z, y, x]
    first = place.at(y=1 - y) if swap else place.at(x=1 - x)
    second = place.at(x=1 - x) if swap else place.at(y=1 - y)
    order = [(z - k + NZ) % NZ for k in range(NZ)]
    twos = [ref.at[zk, :, x] if swap else ref.at[zk, y] for zk in order]
    start = wire.copy(own, own, first)
    steps = [wire.copy(two, two, place.at(z=place.zup(1))) for two in twos[:-1]]
    seconds = [wire.copy(two, two, second) for two in twos]
    yield
    start.go()
    yield
    start.wait_recv()
    steps[0].go()
    seconds[0].go()
    yield
    for k in range(1, NZ):
        steps[k - 1].wait_recv()
        if k < NZ - 1:
            steps[k].go()
        seconds[k].go()
        yield
    for copy in seconds:
        copy.wait_recv()


def spread_zx(wire, place, ref, swap=False):
    z, y, x = place.z, place.y, place.x
    first = place.at(y=1 - y) if swap else place.at(x=1 - x)
    order = [(z - k + NZ) % NZ for k in range(NZ)]
    own = ref.at[z, y, x]
    along_z = [wire.copy(own, own, place.at(z=place.zup(k))) for k in range(1, NZ)]
    firsts = [wire.copy(ref.at[zk, y, x], ref.at[zk, y, x], first) for zk in order]
    yield
    for copy in along_z + firsts[:1]:
        copy.go()
    yield
    for k in range(1, NZ):
        along_z[k - 1].wait_recv()
        firsts[k].go()
        yield
    for copy in firsts:
        copy.wait_recv()


def spread_last(wire, place, src, dst, swap=False):
    z, y, x = place.z, place.y, place.x
    second = place.at(x=1 - x) if swap else place.at(y=1 - y)
    seconds = []
    for k in range(NZ):
        zk = (z - k + NZ) % NZ
        here, there = (src.at[zk, :, x], dst.at[zk, :, x]) if swap else (src.at[zk, y], dst.at[zk, y])
        seconds.append(wire.copy(here, there, second))
    yield
    for copy in seconds:
        copy.go()
    yield
    for copy in seconds:
        copy.wait_recv()


def spread_pair(wire, place, ref):
    plane = ref.at[:, :, :, place.c]
    last = wire.copy(plane, plane, place.at(c=1 - place.c))
    yield from spread_xzy(wire, place, plane)
    last.go()
    yield
    last.wait_recv()


def spread_dp(wire, place, views):
    z, y = place.z, place.y
    at = [z * NY + y] + [((z - n + NZ) % NZ) * NY + y for n in range(1, NZ)]
    along_z = [[wire.copy(view(at[0]), view(at[0]), place.at(z=place.zup(n))) for view in views] for n in range(1, NZ)]
    ys = [[wire.copy(view(d), view(d), place.at(y=1 - y)) for view in views] for d in at]
    yield
    for copies in along_z + ys[:1]:
        for copy in copies:
            copy.go()
    yield
    for n in range(1, NZ):
        for copy in along_z[n - 1]:
            copy.wait_recv()
        for copy in ys[n]:
            copy.go()
        yield
    for copies in ys:
        for copy in copies:
            copy.wait_recv()


def spread_row(wire, place, tok, tok_all):
    s, other, core = place.seq, place.at(x=1 - place.x), place.at(c=1 - place.c)
    far = tok_all.at[s ^ 2]
    tok_x = wire.copy(tok, tok_all.at[s], other)
    tok_c = wire.copy(tok, tok_all.at[s], core)
    last = wire.copy(far, far, core)
    yield
    tok_c.go()
    tok_x.go()
    yield
    tok_c.wait_recv()
    yield
    tok_x.wait_recv()
    last.go()
    yield
    last.wait_recv()


class Plan:
    def __init__(self, tasks, order):
        self.tasks, self.order = tasks, list(order)
        for task in tasks.values():
            next(task)

    def hook(self):
        for name in self.order.pop(0):
            next(self.tasks[name], None)

    def finish(self):
        while self.order:
            self.hook()
        for task in self.tasks.values():
            for _ in task:
                pass


COPIES = 104


def nt(a, b):
    return lax.dot_general(a, b, (((1,), (1,)), ((), ())), preferred_element_type=F32)


def nn(a, b):
    return lax.dot_general(a, b, (((1,), (0,)), ((), ())), preferred_element_type=F32)


def pair_bias(idr, key_ids, qb, kb, size):
    qs = pl.multiple_of(qb * size, size)
    key_pos = kb * size + lax.broadcasted_iota(jnp.int32, (size, size), 0)
    query_pos = qs + lax.broadcasted_iota(jnp.int32, (size, size), 1)
    same = key_ids == idr[:, pl.ds(qs, size)]
    return jnp.where((key_pos <= query_pos) & same, 0.0, NEGATIVE)


def mask_heads(dst, src, heads, head):
    lane = lax.broadcasted_iota(jnp.int32, src.shape, 1) // head
    whole = src[...]
    for h in range(heads):
        dst[h] = jnp.where(lane == h, whole, jnp.zeros_like(whole))


FORWARD = (
    "tqocaoaqqqbdcccoacqtt",
    "",
    "",
    "t",
    "bbbb",
    "",
    "",
    "b",
    "bddd",
    "bo",
    "",
    "",
    "a",
    "od",
    "",
    "b",
    "aooa",
)


def forward_tasks(wire, place, tok, tok_all, wq, rows_all, wide_all, lane, wo_all, f1_all, f2_all):
    group = NX * NC
    half1 = f1_all.shape[4] // 2
    half2 = f2_all.shape[3] // 2
    views = [
        lambda d: wq.at[d],
        lambda d: rows_all.at[:, pl.ds(pl.multiple_of(d * lane, lane), lane)],
        lambda d: wide_all.at[:, pl.ds(pl.multiple_of(d * lane * group, lane * group), lane * group)],
    ]
    return {
        "t": spread_row(wire, place, tok, tok_all),
        "q": spread_dp(wire, place, views),
        "a": spread_xzy(wire, place, f1_all.at[:, :, :, :, pl.ds(0, half1)]),
        "b": spread_zxy(wire, place, f1_all.at[:, :, :, :, pl.ds(half1, half1)], swap=True),
        "o": spread_pair(wire, place, wo_all),
        "c": spread_zx(wire, place, f2_all.at[:, :, :, pl.ds(0, half2)]),
        "d": spread_zx(wire, place, f2_all.at[:, :, :, pl.ds(half2, half2)], swap=True),
    }


def forward_kernel(heads, *refs):
    tok, w_qkv, vec, w_out, w_fc1, w_fc2, idr, lanes = refs[:8]
    act, q, k, v, att, lse, own, wq, rows_all, wide_all, wo_all, f1_all, f2_all = refs[8:21]
    tok_all, actv, vecs, km, vt, idc, bias, top, low, acc, scb, wq4, wo, f1, f2, send, recv, local = refs[21:]
    place = Place()
    z, y, x, c, s, dp = place.z, place.y, place.x, place.c, place.seq, place.dp
    group = NX * NC
    wire = Wire(place, send, recv)
    core, other, across = place.at(c=1 - c), place.at(x=1 - x), place.at(x=1 - x, c=1 - c)
    span, width = tok.shape
    rows = f1.shape[1]
    length, part = q.shape
    head = part // heads

    for j in range(group):
        for n in range(3):
            at = n * width + j * part
            wq4[j, :, n * part : (n + 1) * part] = w_qkv[:, at : at + part].astype(BF)
    greet(place)
    quarter = []
    for dev, peer in ((core, s ^ 1), (other, s ^ 2), (across, s ^ 3)):
        quarter.append(wire.copy(wq4.at[peer], wq.at[dp, s], dev).go())
        quarter.append(wire.copy(vec, vecs.at[s], dev).go())
    cut = vec.shape[2]
    for n in range(NZ * NY * NX):
        for j in range(NC):
            at = (n * NC + j) * cut
            f1[j, :, n * cut : (n + 1) * cut] = w_fc1[:, at : at + cut].astype(BF)
    wo[...] = w_out[...].astype(BF)
    f2[...] = w_fc2[...].astype(BF)
    f1_c = wire.copy(f1.at[1 - c], f1_all.at[z, y, x, pl.ds(c * rows, rows)], core).go()
    here = [
        pltpu.make_async_copy(wq4.at[s], wq.at[dp, s], local.at[0]),
        pltpu.make_async_copy(vec, vecs.at[s], local.at[1]),
        pltpu.make_async_copy(tok, tok_all.at[s], local.at[2]),
        pltpu.make_async_copy(wo, wo_all.at[z, y, x, c], local.at[3]),
        pltpu.make_async_copy(f1.at[c], f1_all.at[z, y, x, pl.ds(c * rows, rows)], local.at[4]),
        pltpu.make_async_copy(f2, f2_all.at[z, y, x], local.at[5]),
    ]
    for desc in here:
        desc.start()
    for desc in here:
        desc.wait()
    for desc in quarter:
        desc.wait_recv()

    lane = vec.shape[2]
    blk = pl.multiple_of(dp * lane, lane)
    wide_blk = pl.multiple_of(dp * lane * group, lane * group)
    rows_all[:, pl.ds(blk, lane)] = (vecs[0, 0] + vecs[1, 0]) + (vecs[2, 0] + vecs[3, 0])
    for j in range(group):
        wide_all[:, pl.ds(pl.multiple_of(wide_blk + j * lane, lane), lane)] = vecs[j, 1]

    f1_c.wait_recv()
    plan = Plan(
        forward_tasks(wire, place, tok, tok_all, wq, rows_all, wide_all, lane, wo_all, f1_all, f2_all), FORWARD
    )
    plan.hook()

    shift = pl.multiple_of(s * part, part)
    bias_q = rows_all[2:3, pl.ds(shift, part)].astype(F32)
    bias_v = rows_all[3:4, pl.ds(shift, part)].astype(F32)
    gain, base = rows_all[0:1, :].astype(F32), rows_all[1:2, :].astype(F32)
    keep = []
    for m in range(group):
        j = s ^ m
        plan.hook()
        if m >= 2:
            keep[m - 2].wait()
        slot = actv.at[m % 2]
        step = 64

        def norm_rows(n, _, slot=slot, j=j):
            at = pl.ds(pl.multiple_of(n * step, step), step)
            values = tok_all[j, at, :].astype(F32)
            slot[at, :] = (normalize(values)[0] * gain + base).astype(BF)
            return 0

        lax.fori_loop(0, span // step, norm_rows, 0)
        at = pl.ds(pl.multiple_of(j * span, span), span)
        desc = pltpu.make_async_copy(slot, act.at[at], local.at[6 + m])
        desc.start()
        keep.append(desc)
        for n, (dst, add) in enumerate(((q, bias_q), (k, None), (v, bias_v))):
            weights = wq[:, :, :, n * part : (n + 1) * part].reshape(width, part)
            proj = nn(slot[...], weights)
            if add is not None:
                proj = proj + add
            if n == 0:
                proj = proj * (head**-0.5)
            dst[at, :] = proj.astype(BF)

    plan.hook()
    mask_heads(km, k, heads, head)
    vt[...] = v[...].T
    idc[...] = jnp.broadcast_to(idr[...], (8, length)).T
    blocks = length // span
    returns = []
    for qb in reversed(range(blocks)):
        qs = slice(qb * span, (qb + 1) * span)
        top[...] = jnp.full(top.shape, NEGATIVE, F32)
        low[...] = jnp.zeros(low.shape, F32)
        acc[...] = jnp.zeros(acc.shape, F32)

        def keys(step, _, qb=qb, qs=qs):
            kb = qb - step
            ks = pl.ds(pl.multiple_of(kb * span, span), span)
            bias[...] = pair_bias(idr, idc[ks, 0:1], qb, kb, span)
            for h in range(heads):
                scores = nt(km[h, ks, :], q[qs, :]) + bias[...]
                old = top[h : h + 1, :]
                new = jnp.maximum(old, jnp.max(scores, 0, keepdims=True))
                probs = jnp.exp(scores - new)
                shrink = jnp.exp(old - new)
                top[h : h + 1, :] = new
                low[h : h + 1, :] = low[h : h + 1, :] * shrink + jnp.sum(probs, 0, keepdims=True)
                hs = slice(h * head, (h + 1) * head)
                acc[hs, :] = acc[hs, :] * shrink + nn(vt[hs, ks], probs.astype(BF))
            for n in range(qb + 1):

                @pl.when(step == n)
                def _():
                    plan.hook()

            return 0

        lax.fori_loop(0, qb + 1, keys, 0)
        for h in range(heads):
            hs = slice(h * head, (h + 1) * head)
            acc[hs, :] = acc[hs, :] * (1.0 / low[h : h + 1, :])
        att[:, qs] = acc[...]
        lse[:, qs] = top[...] + jnp.log(low[...])
        scb[qb] = (acc[...].T * lanes[:, pl.ds(shift, part)]).astype(BF)
        view = own.at[:, pl.ds(shift, part)]
        back = pltpu.make_async_remote_copy(
            src_ref=scb.at[qb],
            dst_ref=view,
            send_sem=send.at[COPIES - 1 - qb],
            recv_sem=recv.at[COPIES - 4 + (s ^ qb)],
            device_id=(dp, qb),
            device_id_type=MESH,
        )
        mine = pltpu.make_async_copy(scb.at[qb], view, local.at[10])
        returns.append((qb, back, mine))

        @pl.when(s == qb)
        def _():
            mine.start()

        @pl.when(s != qb)
        def _():
            back.start()

    plan.finish()
    for desc in keep[-2:]:
        desc.wait()
    for qb, back, mine in returns:

        @pl.when(s == qb)
        def _():
            mine.wait()

        @pl.when(s != qb)
        def _():
            back.wait_send()

    for m in range(1, group):
        view = own.at[:, pl.ds(pl.multiple_of((s ^ m) * part, part), part)]
        pltpu.make_async_remote_copy(
            src_ref=scb.at[0],
            dst_ref=view,
            send_sem=send.at[COPIES - 1],
            recv_sem=recv.at[COPIES - 4 + m],
            device_id=core,
            device_id_type=MESH,
        ).wait_recv()
    wire.drain()


def forward(tok, w_qkv, vec, w_out, w_fc1, w_fc2, ids, lanes, heads):
    span, width = tok.shape
    group = NX * NC
    rows = w_qkv.shape[0]
    part = width // group
    triple = 3 * part
    f1_shape = (NC, rows, w_fc1.shape[1] // NC)
    length = span * group
    dps = NZ * NY
    lane = vec.shape[2]
    out = (
        (HBM, (length, width), BF),
        (VM, (length, part), BF),
        (VM, (length, part), BF),
        (VM, (length, part), BF),
        (VM, (part, length), F32),
        (VM, (8, length), F32),
        (VM, (span, width), BF),
        (VM, (dps, group, rows, triple), BF),
        (VM, (16, dps * lane), BF),
        (VM, (16, dps * group * lane), BF),
        (HBM, (NZ, NY, NX, NC) + w_out.shape, BF),
        (HBM, (NZ, NY, NX, NC * rows, f1_shape[2]), BF),
        (HBM, (NZ, NY, NX) + w_fc2.shape, BF),
    )
    return pl.pallas_call(
        functools.partial(forward_kernel, heads),
        out_shape=tuple(jax.ShapeDtypeStruct(shape, dtype) for _, shape, dtype in out),
        in_specs=[VM] * 8,
        out_specs=[spec for spec, _, _ in out],
        scratch_shapes=[
            pltpu.VMEM((group, span, width), BF),
            pltpu.VMEM((2, span, width), BF),
            pltpu.VMEM((group,) + vec.shape, BF),
            pltpu.VMEM((heads, length, part), BF),
            pltpu.VMEM((part, length), BF),
            pltpu.VMEM((length, 8), jnp.int32),
            pltpu.VMEM((span, span), F32),
            pltpu.VMEM((8, span), F32),
            pltpu.VMEM((8, span), F32),
            pltpu.VMEM((part, span), F32),
            pltpu.VMEM((group, span, part), BF),
            pltpu.VMEM((group, rows, triple), BF),
            pltpu.VMEM(w_out.shape, BF),
            pltpu.VMEM(f1_shape, BF),
            pltpu.VMEM(w_fc2.shape, BF),
            pltpu.SemaphoreType.DMA((COPIES,)),
            pltpu.SemaphoreType.DMA((COPIES,)),
            pltpu.SemaphoreType.DMA((12,)),
        ],
        compiler_params=pltpu.CompilerParams(
            collective_id=1, has_side_effects=True, vmem_limit_bytes=56 * 1024 * 1024
        ),
        name="forward_row",
    )(tok, w_qkv, vec, w_out, w_fc1, w_fc2, ids.reshape(1, length), lanes)


def lead_loop(total, fn, step=16):
    lead, rows = total.shape[:-2], total.shape[-2]
    per = rows // step

    def body(n, _):
        block = n // per
        at = []
        for dim in reversed(lead):
            at.append(block % dim)
            block = block // dim
        fn(tuple(reversed(at)) + (pl.ds(pl.multiple_of((n % per) * step, step), step), slice(None)))
        return 0

    lax.fori_loop(0, math.prod(lead) * per, body, 0)


def add_into(total, term):
    def fn(idx):
        total[idx] = (total[idx].astype(F32) + term[idx].astype(F32)).astype(total.dtype)

    lead_loop(total, fn, 16 if total.dtype == BF else 8)


def reduce_plane(wire, place, grad, own, got, got2, got3, out, local, swap=False):
    z, y, x = place.z, place.y, place.x
    first = place.at(x=1 - x) if swap else place.at(y=1 - y)
    order = [place.zup(k) for k in (1, 2, 3, 0)]

    def two(zk, mine):
        if swap:
            return grad.at[zk, :, x if mine else 1 - x]
        return grad.at[zk, y if mine else 1 - y]

    sends = [wire.copy(two(zk, False), got.at[k], first) for k, zk in enumerate(order)]
    loads = [pltpu.make_async_copy(two(zk, True), own.at[k], local.at[k]) for k, zk in enumerate(order)]
    rest = reduce_tail(wire, place, own, got2, got3, out, swap)
    next(rest)
    yield
    for copy in sends:
        copy.go()
    for desc in loads:
        desc.start()
    yield
    for k in range(NZ):
        loads[k].wait()
        sends[k].wait_recv()
        add_into(own.at[k], got.at[k])
        next(rest)
        yield
    yield from rest


def reduce_head(wire, place, grad, got, got2, swap=False):
    y, x = place.y, place.x
    first = place.at(x=1 - x) if swap else place.at(y=1 - y)
    second = place.at(y=1 - y) if swap else place.at(x=1 - x)
    keep, give = (y, 1 - y) if swap else (x, 1 - x)
    order = [place.zup(k) for k in (1, 2, 3, 0)]
    mine = [grad.at[zk, :, x] if swap else grad.at[zk, y] for zk in order]
    others = [grad.at[zk, :, 1 - x] if swap else grad.at[zk, 1 - y] for zk in order]
    keeps = [grad.at[zk, keep, x] if swap else grad.at[zk, y, keep] for zk in order]
    gives = [grad.at[zk, give, x] if swap else grad.at[zk, y, give] for zk in order]
    sends = [wire.copy(others[k], got.at[k], first) for k in range(NZ)]
    seconds = [wire.copy(gives[k], got2.at[k], second) for k in range(NZ)]
    yield
    for copy in sends:
        copy.go()
    yield
    for k in range(NZ):
        sends[k].wait_recv()
        add_into(mine[k], got.at[k])
        seconds[k].go()
        yield
    for k in range(NZ):
        seconds[k].wait_recv()
        add_into(keeps[k], got2.at[k])
        yield


def reduce_line(wire, place, own, got, out):
    along = [wire.copy(own.at[k], got.at[k], place.at(z=place.zup(k + 1))) for k in range(NZ - 1)]
    yield
    for copy in along:
        copy.go()
    yield
    for copy in along:
        copy.wait_recv()
    add_up(out, own.at[NZ - 1], got)


def reduce_tail(wire, place, own, got2, got3, out, swap=False):
    y, x = place.y, place.x
    second = place.at(y=1 - y) if swap else place.at(x=1 - x)
    keep, give = (y, 1 - y) if swap else (x, 1 - x)
    keeps = [own.at[k, keep] for k in range(NZ)]
    seconds = [wire.copy(own.at[k, give], got2.at[k], second) for k in range(NZ)]
    along = [wire.copy(keeps[k], got3.at[k], place.at(z=place.zup(k + 1))) for k in range(NZ - 1)]
    yield
    for copy in seconds:
        copy.go()
        yield
    for k in range(NZ):
        seconds[k].wait_recv()
        add_into(keeps[k], got2.at[k])
        if k < NZ - 1:
            along[k].go()
        yield
    for copy in along:
        copy.wait_recv()
    add_up(out, keeps[NZ - 1], got3)


def plane_scratch(block):
    return [
        pltpu.VMEM((NZ, 2) + block, BF),
        pltpu.VMEM((NZ, 2) + block, BF),
        pltpu.VMEM((NZ,) + block, BF),
        pltpu.VMEM((NZ - 1,) + block, BF),
        pltpu.SemaphoreType.DMA((NZ,)),
    ]


def reduce_outer(wire, place, go, outp, outg, load, scratch, out):
    c = place.c
    swap_o = wire.copy(go.at[:, :, :, 1 - c], outg, place.at(c=1 - c))
    load_o = pltpu.make_async_copy(go.at[:, :, :, c], outp, load)
    rest = reduce_plane(wire, place, outp, *scratch[:4], out, scratch[4])
    next(rest)
    yield
    swap_o.go()
    load_o.start()
    yield
    load_o.wait()
    swap_o.wait_recv()
    add_into(outp, outg)
    yield from rest


def reduce_first(wire, place, half, g1, buf, got, scratch, out, swap=False):
    c = place.c
    rows = got.shape[0]
    size = buf.shape[1] // 2
    cols = pl.ds(half * size, size)
    mine, theirs = buf.at[:, cols], got.at[:, cols]
    part = wire.copy(mine.at[pl.ds((1 - c) * rows, rows)], theirs, place.at(c=1 - c))
    yield from reduce_plane(
        wire, place, g1.at[:, :, :, :, cols], *scratch[:4], mine, scratch[4], swap=swap
    )
    part.go()
    lane = out.shape[1] // (NZ * NY * NX * NC)
    spread_columns(out, buf, pl.multiple_of(c * rows, rows), c, lane, half)
    yield
    part.wait_recv()
    spread_columns(out, got, 0, 1 - c, lane, half)


def spread_columns(out, src, row, c, lane, half):
    rows = out.shape[0]
    chips = NZ * NY * NX // 2
    for n in range(half * chips, (half + 1) * chips):
        at = pl.ds(pl.multiple_of((n * NC + c) * lane, lane), lane)
        out[:, at] = src[pl.ds(row, rows), n * lane : (n + 1) * lane]


def send_rows(wire, place, total, buf, cols, local):
    s = place.seq
    near = ((place.at(c=1 - place.c), 1), (place.at(x=1 - place.x), 2), (place.at(x=1 - place.x, c=1 - place.c), 3))
    parts = [wire.copy(total.at[s ^ m, :, cols], buf.at[s, :, cols], dev) for dev, m in near]
    mine = pltpu.make_async_copy(total.at[s, :, cols], buf.at[s, :, cols], local)
    return parts, mine


def place_rows(out, buf, first, count):
    group, part = buf.shape[0], buf.shape[2] // 3
    step = 128
    for j in range(group):
        for m in range(first // step, (first + count) // step):
            n, rest = m * step // part, m * step % part
            at = (n * group + j) * part + rest
            out[:, at : at + step] = buf[j, :, m * step : (m + 1) * step].astype(F32)


def reduce_quarter(wire, place, gq, own, got, got2, total, buf, out, local):
    y = place.y
    size = total.shape[2] // 2
    cols = pl.ds(0, size)
    order = [place.zup(n) for n in (1, 2, 3, 0)]
    sends = [wire.copy(gq.at[zk, 1 - y, :, :, cols], got.at[n], place.at(y=1 - y)) for n, zk in enumerate(order)]
    along = [wire.copy(own.at[n], got2.at[n], place.at(z=place.zup(n + 1))) for n in range(NZ - 1)]
    loads = [pltpu.make_async_copy(gq.at[zk, y, :, :, cols], own.at[n], local.at[n]) for n, zk in enumerate(order)]
    parts, mine = send_rows(wire, place, total, buf, cols, local.at[NZ])
    yield
    for copy in sends:
        copy.go()
    for desc in loads:
        desc.start()
    yield
    for n in range(NZ):
        loads[n].wait()
        sends[n].wait_recv()
        add_into(own.at[n], got.at[n])
        if n < NZ - 1:
            along[n].go()
        yield
    for copy in along:
        copy.wait_recv()
    add_up(total.at[:, :, cols], own.at[NZ - 1], got2)
    for copy in parts:
        copy.go()
    mine.start()
    yield
    mine.wait()
    for copy in parts:
        copy.wait_recv()
    place_rows(out, buf, 0, size)


def reduce_quarter_zy(wire, place, gq, got, give, gave, total, buf, out, local):
    z, y = place.z, place.y
    size = total.shape[2] // 2
    cols = pl.ds(size, size)
    along = [
        wire.copy(gq.at[place.zup(n), :, :, :, cols], got.at[n - 1], place.at(z=place.zup(n))) for n in range(1, NZ)
    ]
    other = wire.copy(give, gave, place.at(y=1 - y))
    parts, mine = send_rows(wire, place, total, buf, cols, local)
    yield
    for copy in along:
        copy.go()
    yield
    for copy in along:
        copy.wait_recv()
    add_up(give, gq.at[z, 1 - y, :, :, cols], got.at[:, 1 - y])
    other.go()
    add_up(total.at[:, :, cols], gq.at[z, y, :, :, cols], got.at[:, y])
    yield
    other.wait_recv()
    add_into(total.at[:, :, cols], gave)
    for copy in parts:
        copy.go()
    mine.start()
    yield
    mine.wait()
    for copy in parts:
        copy.wait_recv()
    place_rows(out, buf, size, size)


def reduce_vectors(wire, place, pairs):
    z, y = place.z, place.y
    sizes = [g.shape[1] // (NZ * NY) for g, *_ in pairs]

    def cols(n, zk, yk):
        return pl.ds(pl.multiple_of((zk * NY + yk) * sizes[n], sizes[n]), sizes[n])

    cs = [wire.copy(g, t.at[0], place.at(c=1 - place.c)) for g, t, *_ in pairs]
    xs = [wire.copy(g, t.at[1], place.at(x=1 - place.x)) for g, t, *_ in pairs]
    ys, zs = [], []
    for n, (g, t, got, _) in enumerate(pairs):
        for zk in range(NZ):
            at = cols(n, zk, 1 - y)
            ys.append(wire.copy(g.at[:, at], t.at[2, :, at], place.at(y=1 - y)))
        for k in range(1, NZ):
            at = cols(n, place.zup(k), y)
            zs.append(wire.copy(g.at[:, at], got.at[z], place.at(z=place.zup(k))))
    yield
    for copy in cs:
        copy.go()
    yield
    for copies, slot in ((cs, 0), (xs, 1)):
        for copy, (g, t, *_) in zip(copies, pairs):
            copy.wait_recv()
            copy.wait_send()
            add_rows(g, t.at[slot])
        for copy in xs if slot == 0 else ys:
            copy.go()
        yield
    for copy in ys:
        copy.wait_recv()
    for n, (g, t, got, _) in enumerate(pairs):
        for zk in range(NZ):
            at = cols(n, zk, y)
            add_rows(g.at[:, at], t.at[2, :, at])
    for copy in zs:
        copy.go()
    for n, (g, t, got, _) in enumerate(pairs):
        keep_rows(got.at[z], g.at[:, cols(n, z, y)])
    yield
    for copy in zs:
        copy.wait_recv()
    for g, t, got, out in pairs:
        add_fixed(out, got)


def add_rows(total, term):
    total[...] += term[...]


def keep_rows(dst, src):
    dst[...] = src[...]


def add_fixed(out, got):
    total = got[0]
    for k in range(1, NZ):
        total = total + got[k]
    out[...] = total


def add_up(out, own, got):
    def fn(idx):
        value = own[idx].astype(F32)
        for k in range(NZ - 1):
            value = value + got[(k,) + idx].astype(F32)
        out[idx] = value.astype(out.dtype)

    lead_loop(out, fn)


BACKWARD = (
    "4321",
    "",
    "",
    "41",
    "",
    "4o",
    "4o311",
    "4",
    "141",
    "44211o",
    "o",
    "ooo1",
    "rq44o",
    "",
    "q4qoqo1q1",
    "vvrrvorqvqv",
)


def backward_kernel(heads, *refs):
    q, k, v, att, lse, do, idr, wq, grad_hidden, rows_in, wide_in, gain = refs[:12]
    tok, act, g1, go, in2, in3 = refs[12:18]
    grad_tok, out1, out2, outo, outq, outr, outw = refs[18:25]
    (km, vm, qm, dm, kt, idc, bias, acck, accv, accq, accw, delta, blk, actb) = refs[25:39]
    (dap, dgot, dfin, ownq, gotq, gotqb, sumq, outq_buf, gq, gotp, f1buf, f1got) = refs[39:51]
    (rowg, rowt, rowz, wideg, widet, widez, outp, outg) = refs[51:59]
    plane1, plane4, planeo = refs[59:64], refs[64:69], refs[69:74]
    own2, own3, half2, half3, zgot, zgive, zgave = refs[74:81]
    send, recv, local, dsend, drecv = refs[81:]
    place = Place()
    z, y, x, c, s, dp = place.z, place.y, place.x, place.c, place.seq, place.dp
    group = NX * NC
    wire = Wire(place, send, recv)
    core, other, across = place.at(c=1 - c), place.at(x=1 - x), place.at(x=1 - x, c=1 - c)
    length, part = q.shape
    span, width = tok.shape
    head = part // heads
    blocks = length // span
    shift = pl.multiple_of(s * part, part)

    greet(place)
    load2 = pltpu.make_async_copy(in2, own2, local.at[0])
    load3 = pltpu.make_async_copy(in3, own3, local.at[1])
    load2.start()
    load3.start()
    per = in2.shape[1]
    load2.wait()
    load3.wait()
    plan = Plan(
        {
            "1": reduce_first(wire, place, 0, g1, f1buf, f1got, plane1, out1),
            "4": reduce_first(wire, place, 1, g1, f1buf, f1got, plane4, out1, swap=True),
            "o": reduce_outer(wire, place, go, outp, outg, local.at[12], planeo, outo),
            "2": reduce_line(wire, place, own2, half2, out2.at[pl.ds(0, per)]),
            "3": reduce_line(wire, place, own3, half3, out2.at[pl.ds(per, per)]),
            "q": reduce_quarter(wire, place, gq, ownq, gotq, gotqb, sumq, outq_buf, outq, local.at[pl.ds(6, NZ + 1)]),
            "r": reduce_quarter_zy(wire, place, gq, zgot, zgive, zgave, sumq, outq_buf, outq, local.at[13]),
            "v": reduce_vectors(wire, place, ((rowg, rowt, rowz, outr), (wideg, widet, widez, outw))),
        },
        BACKWARD,
    )
    plan.hook()

    mask_heads(qm, q, heads, head)
    accq[...] = jnp.zeros(accq.shape, F32)
    accw[...] = jnp.zeros(accw.shape, F32)
    delta[...] = jnp.zeros(delta.shape, F32)
    plan.hook()
    mask_heads(dm, do, heads, head)
    for b in range(blocks):
        at = slice(b * span, (b + 1) * span)
        weighted = do[at, :].T.astype(F32) * att[:, at]
        for h in range(heads):
            delta[h : h + 1, at] = jnp.sum(weighted[h * head : (h + 1) * head, :], 0, keepdims=True)

    hops = []
    for t in range(blocks):
        tx, tc = t // NC, t % NC
        inner = pltpu.make_async_remote_copy(
            src_ref=dap.at[t],
            dst_ref=dgot.at[tx],
            send_sem=dsend.at[2 * t],
            recv_sem=drecv.at[2 * t],
            device_id=core,
            device_id_type=MESH,
        )
        outerc = pltpu.make_async_remote_copy(
            src_ref=dap.at[t],
            dst_ref=dfin,
            send_sem=dsend.at[2 * t + 1],
            recv_sem=drecv.at[2 * t + 1],
            device_id=other,
            device_id_type=MESH,
        )
        hops.append((tx, tc, inner, outerc))

    def meet(t):
        tx, tc, inner, outerc = hops[t]

        @pl.when(c == tc)
        def _():
            inner.wait_recv()
            add_into(dap.at[t], dgot.at[tx])

            @pl.when(x != tx)
            def _():
                outerc.start()

    fetch = [
        pltpu.make_async_copy(act.at[pl.ds(b * span, span)], actb.at[b % 2], local.at[2 + b]) for b in range(blocks)
    ]
    fetch[0].start()

    for kb in range(blocks):
        ks = slice(kb * span, (kb + 1) * span)
        if kb + 1 < blocks:
            fetch[kb + 1].start()
        mask_heads(km, k.at[ks], heads, head)
        mask_heads(vm, v.at[ks], heads, head)
        kt[...] = k[ks, :].T
        idc[...] = jnp.broadcast_to(idr[:, ks], (8, span)).T
        acck[...] = jnp.zeros(acck.shape, F32)
        accv[...] = jnp.zeros(accv.shape, F32)

        def queries(qb, _, kb=kb, ks=ks):
            qs = pl.ds(pl.multiple_of(qb * span, span), span)
            bias[...] = pair_bias(idr, idc[:, 0:1], qb, kb, span)
            for h in range(heads):
                scores = nt(km[h], q[qs, :]) + bias[...]
                probs = jnp.exp(scores - lse[h : h + 1, qs])
                grad = nt(vm[h], do[qs, :])
                ds = (probs * (grad - delta[h : h + 1, qs])).astype(BF)
                accv[...] += nn(probs.astype(BF), dm[h, qs, :])
                acck[...] += nn(ds, qm[h, qs, :])
                hs = slice(h * head, (h + 1) * head)
                accq[hs, qs] += nn(kt[hs, :], ds)
            for n in range(kb, blocks):

                @pl.when(qb == n)
                def _():
                    if n == blocks - 1 and kb > 0:
                        meet(kb - 1)
                    plan.hook()

            return 0

        lax.fori_loop(kb, blocks, queries, 0)
        blk[:, :part] = (accq[:, ks].T * (head**-0.5)).astype(BF)
        blk[:, part : 2 * part] = acck[...].astype(BF)
        blk[:, 2 * part :] = accv[...].astype(BF)
        sums = jnp.sum(blk[...].astype(F32), 0, keepdims=True)
        if kb == 0:
            gotp[...] = jnp.zeros(gotp.shape, F32)
        gotp[0:1, :] += sums
        fetch[kb].wait()
        step = 256
        for n in range(0, width, step):
            accw[n : n + step, :] += lax.dot_general(
                actb[kb % 2, :, n : n + step], blk[...], (((0,), (0,)), ((), ())), preferred_element_type=F32
            )
        if kb == blocks - 1:
            gq[...] = accw[...].astype(BF).reshape(gq.shape)
            plan.hook()
        weights = wq[...].reshape(width, 3 * part)
        for n in range(0, width, step):
            dap[kb, :, n : n + step] = nt(blk[...], weights[n : n + step, :]).astype(BF)
        tx, tc, inner, outerc = hops[kb]

        @pl.when(c != tc)
        def _():
            inner.start()

    fetch_tok = pltpu.make_async_copy(tok, actb.at[0], local.at[11])
    fetch_tok.start()
    plan.hook()
    meet(blocks - 1)
    plan.hook()

    step = 64
    rowg[...] = rows_in[...]
    wideg[...] = wide_in[...]
    lane_sum = jnp.sum(delta[...], 1, keepdims=True)
    for j in range(group):
        rowg[16 + j * heads : 16 + (j + 1) * heads, :] = jnp.where(
            s == j, jnp.broadcast_to(lane_sum[:heads], (heads, width)), 0.0
        )
    rowg[2:3, pl.ds(shift, part)] = gotp[0:1, :part]
    rowg[3:4, pl.ds(shift, part)] = gotp[0:1, 2 * part :]
    for t in range(blocks):
        tx, tc, inner, outerc = hops[t]

        @pl.when((x == tx) & (c == tc))
        def _():
            outerc.wait_recv()

    fetch_tok.wait()

    def finish(n, carry):
        at = pl.ds(pl.multiple_of(n * step, step), step)
        da = dap[s, at, :].astype(F32) + dfin[at, :].astype(F32)
        normed, inv = normalize(actb[0, at, :].astype(F32))
        grad = norm_back(da * gain[0:1, :].astype(F32), normed, inv) + grad_hidden[at, :]
        grad_tok[at, :] = grad.astype(BF)
        return (
            carry[0] + jnp.sum(da * normed, 0, keepdims=True),
            carry[1] + jnp.sum(da, 0, keepdims=True),
        )

    zero = jnp.zeros((1, width), F32)
    gain_one, shift_one = lax.fori_loop(0, span // step, finish, (zero, zero))
    rowg[0:1, :] = gain_one
    rowg[1:2, :] = shift_one

    plan.finish()
    for t in range(blocks):
        tx, tc, inner, outerc = hops[t]

        @pl.when(c != tc)
        def _():
            inner.wait_send()

        @pl.when((c == tc) & (x != tx))
        def _():
            outerc.wait_send()

    wire.drain()


def backward(do, q, k, v, att, lse, ids, wq, tok, grad_hidden, rows_in, wide_in, gain, act, g1, go, in2, in3, heads):
    length, part = q.shape
    span, width = tok.shape
    group = length // span
    b1, bo = g1.shape[3:], go.shape[4:]
    rows, triple = wq.shape[2:]
    bq = (group, rows, triple)
    bh = (group, rows, triple // 2)
    dps = NZ * NY
    out = (
        (VM, (span, width), BF),
        (VM, (b1[0] // NC, NC * b1[1]), F32),
        (VM, (2 * in2.shape[1], width), F32),
        (VM, bo, F32),
        (VM, (rows, group * triple), F32),
        (VM, (rows_in.shape[0], width // dps), F32),
        (VM, (wide_in.shape[0], wide_in.shape[1] // dps), F32),
    )
    scratch = [
        pltpu.VMEM((heads, span, part), BF),
        pltpu.VMEM((heads, span, part), BF),
        pltpu.VMEM((heads, length, part), BF),
        pltpu.VMEM((heads, length, part), BF),
        pltpu.VMEM((part, span), BF),
        pltpu.VMEM((span, 8), jnp.int32),
        pltpu.VMEM((span, span), F32),
        pltpu.VMEM((span, part), F32),
        pltpu.VMEM((span, part), F32),
        pltpu.VMEM((part, length), F32),
        pltpu.VMEM((width, triple), F32),
        pltpu.VMEM((8, length), F32),
        pltpu.VMEM((span, triple), BF),
        pltpu.VMEM((2, span, width), BF),
        pltpu.VMEM((group, span, width), BF),
        pltpu.VMEM((NX, span, width), BF),
        pltpu.VMEM((span, width), BF),
        pltpu.VMEM((NZ,) + bh, BF),
        pltpu.VMEM((NZ,) + bh, BF),
        pltpu.VMEM((NZ - 1,) + bh, BF),
        pltpu.VMEM(bq, BF),
        pltpu.VMEM(bq, BF),
        pltpu.VMEM((NZ, NY) + bq, BF),
        pltpu.VMEM((8, triple), F32),
        pltpu.VMEM(b1, F32),
        pltpu.VMEM((b1[0] // NC, b1[1]), F32),
        pltpu.VMEM(rows_in.shape, F32),
        pltpu.VMEM((3,) + rows_in.shape, F32),
        pltpu.VMEM((NZ, rows_in.shape[0], width // dps), F32),
        pltpu.VMEM(wide_in.shape, F32),
        pltpu.VMEM((3,) + wide_in.shape, F32),
        pltpu.VMEM((NZ, wide_in.shape[0], wide_in.shape[1] // dps), F32),
        pltpu.VMEM((NZ, NY, NX) + bo, BF),
        pltpu.VMEM((NZ, NY, NX) + bo, BF),
    ]
    scratch += plane_scratch((b1[0], b1[1] // 2)) * 2 + plane_scratch(bo)
    scratch += [pltpu.VMEM(in2.shape, BF)] * 2 + plane_scratch(in2.shape[1:])[3:4] * 2
    scratch += [pltpu.VMEM((NZ - 1, NY) + bh, BF), pltpu.VMEM(bh, BF), pltpu.VMEM(bh, BF)]
    scratch += [
        pltpu.SemaphoreType.DMA((COPIES,)),
        pltpu.SemaphoreType.DMA((COPIES,)),
        pltpu.SemaphoreType.DMA((14,)),
        pltpu.SemaphoreType.DMA((2 * group,)),
        pltpu.SemaphoreType.DMA((2 * group,)),
    ]
    return pl.pallas_call(
        functools.partial(backward_kernel, heads),
        out_shape=tuple(jax.ShapeDtypeStruct(shape, dtype) for _, shape, dtype in out),
        in_specs=[VM] * 12 + [HBM] * 6,
        out_specs=[spec for spec, _, _ in out],
        scratch_shapes=scratch,
        compiler_params=pltpu.CompilerParams(
            collective_id=2, has_side_effects=True, vmem_limit_bytes=63 * 1024 * 1024
        ),
        name="backward_row",
    )(
        q, k, v, att, lse, do, ids.reshape(1, length), wq, grad_hidden, rows_in, wide_in, gain,
        tok, act, g1, go, in2, in3,
    )


MIDDLE = (
    "ce",
    "",
    "",
    "",
    "",
    "23ce",
    "",
    "23",
    "23",
    "",
    "23",
    "2233",
    "2233",
    "2233",
    "",
    "",
)


def middle_tasks(wire, place, f2, f2v, g2, got2, got2b, got3, got3b):
    half = g2.shape[3] // 2
    one, two = pl.ds(0, half), pl.ds(half, half)
    return {
        "c": spread_last(wire, place, f2.at[:, :, :, one], f2v.at[:, :, :, one]),
        "e": spread_last(wire, place, f2.at[:, :, :, two], f2v.at[:, :, :, two], swap=True),
        "2": reduce_head(wire, place, g2.at[:, :, :, one], got2, got2b, swap=True),
        "3": reduce_head(wire, place, g2.at[:, :, :, two], got3, got3b),
    }


def tn(a, b):
    return lax.dot_general(a, b, (((0,), (0,)), ((), ())), preferred_element_type=F32)


def fold(value, rows=16):
    total = value[:rows]
    for n in range(1, value.shape[0] // rows):
        total = total + value[n * rows : (n + 1) * rows]
    return total


def lanes_of(value):
    total = value[:, :128]
    for n in range(1, value.shape[1] // 128):
        total = total + value[:, n * 128 : (n + 1) * 128]
    return total


def row_steps(count, step, fn):
    def body(n, _):
        fn(pl.ds(pl.multiple_of(n * step, step), step))
        return 0

    lax.fori_loop(0, count // step, body, 0)


def ffn_kernel(*refs):
    own, rows_all, wide_all, lanes = refs[:4]
    tok, cot, f2, wo, f1 = refs[4:9]
    out, do, gh, g1, go, half2, half3, rows_g, wide_g = refs[9:18]
    wov, f1v, f2v, dt, act, buf, slope, mix, dm, br, hid, g2, dbuf, prb, prc, stg, wv = refs[18:35]
    stat, stat_got, back, back_got, sums, colsums = refs[35:41]
    gots = refs[41:45]
    send, recv, local = refs[45:48]
    lane_mean, lane_square = dm.at[:, pl.ds(0, 128)], dm.at[:, pl.ds(128, 128)]
    place = Place()
    z, y, x, c, s = place.z, place.y, place.x, place.c, place.seq
    wire = Wire(place, send, recv)
    core = place.at(c=1 - c)
    span, width = own.shape
    units = f1v.shape[4]
    group = NX * NC
    tile = 512
    tiles = units // tile
    total_units = units * NC

    half = f2.shape[3] // 2
    one, two = pl.ds(0, half), pl.ds(half, half)
    loads = [
        pltpu.make_async_copy(wo, wov, local.at[0]),
        pltpu.make_async_copy(f2.at[:, y, :, one], f2v.at[:, y, :, one], local.at[1]),
        pltpu.make_async_copy(cot, dt.at[c], local.at[2]),
        pltpu.make_async_copy(f1, f1v, local.at[3]),
        pltpu.make_async_copy(f2.at[:, :, x, two], f2v.at[:, :, x, two], local.at[4]),
        pltpu.make_async_copy(tok, prc, local.at[5]),
    ]
    for desc in loads:
        desc.start()
    chunk = span // 4
    chunks = [pl.ds(n * chunk, chunk) for n in range(4)]
    dt_copy = wire.copy(cot, dt.at[c], core)
    act_copies = [wire.copy(act.at[c, at], act.at[c, at], core) for at in chunks]
    stat_copies = [wire.copy(stat.at[h], stat_got.at[h], core) for h in range(NC)]
    back_copies = [wire.copy(back.at[h], back_got.at[h], core) for h in range(NC)]
    out_copy = wire.copy(dbuf, prb, core)
    da_copy = wire.copy(prb, prc, core)
    mine_at = pl.ds(pl.multiple_of(s * span, span), span)
    part_size = width // group

    def give(j):
        return prb.at[:, pl.ds(pl.multiple_of(j * part_size, part_size), part_size)]

    outgoing = [
        wire.copy(give(s ^ m), do.at[mine_at], dev)
        for dev, m in ((core, 1), (place.at(x=1 - x), 2), (place.at(x=1 - x, c=1 - c), 3))
    ]
    greet(place)
    dt_copy.go()
    plan = Plan(middle_tasks(wire, place, f2, f2v, g2, *gots), MIDDLE)
    plan.hook()

    def row(ref, n):
        return ref[n : n + 1, :].astype(F32)

    lane = wide_all.shape[1] // (NZ * NY * NX * NC)
    for n in range(NZ * NY * NX):
        at = pl.ds(pl.multiple_of((n * NC + c) * lane, lane), lane)
        wv[0:3, n * lane : (n + 1) * lane] = wide_all[0:3, at].astype(F32)
    colsums[...] = jnp.zeros(colsums.shape, F32)
    sums[...] = jnp.zeros(sums.shape, F32)
    loads[0].wait()
    loads[5].wait()

    for at, copy in zip(chunks, act_copies):
        branch = nn(own[at, :], wov[...].reshape(width, width)) + row(rows_all, 4)
        br[at, :] = branch

        def fn(inner, at=at):
            rows = pl.ds(at.start + inner.start, inner.size)
            hidden = prc[rows, :].astype(F32) + normalize(br[rows, :])[0] * row(rows_all, 5) + row(rows_all, 6)
            hid[rows, :] = hidden
            act[c, rows, :] = (normalize(hidden)[0] * row(rows_all, 7) + row(rows_all, 8)).astype(BF)

        row_steps(chunk, 64, fn)
        copy.go()
    plan.hook()
    loads[3].wait()

    for h in range(NC):

        @pl.when(c != h)
        def _():
            for copy in act_copies:
                copy.wait_recv()

        for n in range(tiles):
            cols = slice(n * tile, (n + 1) * tile)
            weights = f1v[:, :, :, :, cols].reshape(width, tile)
            buf[h, :, cols] = nn(act[h], weights) + wv[0:1, cols]

        def fn(at, h=h):
            count = units // 128
            pivot = None
            for n in range(tiles):
                cols = slice(n * tile, (n + 1) * tile)
                u = buf[h, at, cols]
                cdf = 0.5 + 0.5 * lax.erf(u * math.sqrt(0.5))
                value = u * cdf
                buf[h, at, cols] = value
                pdf = jnp.exp(-0.5 * u * u) * (1.0 / math.sqrt(2.0 * math.pi))
                slope[h, at, cols] = (cdf + u * pdf).astype(BF)
                if pivot is None:
                    pivot = value[:, :128]
                    total, square = jnp.zeros_like(pivot), jnp.zeros_like(pivot)
                for j in range(tile // 128):
                    gap = value[:, j * 128 : (j + 1) * 128] - pivot
                    total = total + gap
                    square = square + gap * gap
            shift = total * (1.0 / count)
            lane_mean[at, :] = pivot + shift
            lane_square[at, :] = square - total * shift

        row_steps(span, 32, fn)

        def fn(at, h=h):
            count = units // 128
            means = lane_mean[at, :]
            mean = jnp.mean(means, 1, keepdims=True)
            gap = means - mean
            square = jnp.sum(lane_square[at, :] + count * (gap * gap), 1, keepdims=True)
            column = lax.broadcasted_iota(jnp.int32, (at.size, 128), 1)
            stat[h, at, :] = jnp.where(column == 0, mean, square)

        row_steps(span, 128, fn)
        stat_copies[h].go()
        plan.hook()

    for h in range(NC):
        stat_copies[h].wait_recv()
        stat_copies[h].wait_send()

        def fn(at, h=h):
            mean_a, mean_b = stat[h, at, 0:1], stat_got[h, at, 0:1]
            gap = mean_a - mean_b
            square = stat[h, at, 1:2] + stat_got[h, at, 1:2] + gap * gap * (0.5 * units)
            mean = 0.5 * (mean_a + mean_b)
            inv = lax.rsqrt(square * (1.0 / total_units) + EPSILON)
            stat[h, at, :] = jnp.broadcast_to(inv, (at.size, 128))
            for n in range(tiles):
                cols = slice(n * tile, (n + 1) * tile)
                normed = (buf[h, at, cols] - mean) * inv
                buf[h, at, cols] = normed
                mix[h, at, cols] = (normed * wv[1:2, cols] + wv[2:3, cols]).astype(BF)

        row_steps(span, 64, fn)
    plan.hook()

    loads[2].wait()
    loads[1].wait()
    loads[4].wait()
    dt_copy.wait_recv()
    per = g2.shape[3]
    for n in range(units // (2 * per)):
        cols = slice(n * 2 * per, (n + 1) * 2 * per)
        part = tn(mix[0, :, cols], dt[0]) + tn(mix[1, :, cols], dt[1])
        g2[n // NY, n % NY] = part.astype(BF).reshape(NX, per, width)
    plan.hook()

    weights2 = f2v[...].reshape(units, width)
    for n in range(0, width, tile):
        dbuf[:, n : n + tile] = nn(mix[1 - c], weights2[:, n : n + tile]).astype(BF)
    out_copy.go()
    for n in range(0, width, tile):
        cols = slice(n, n + tile)
        gh[:, cols] = nn(mix[c], weights2[:, cols]) + hid[:, cols] + rows_all[9:10, cols].astype(F32)
    plan.hook()

    for h in range(NC):
        for n in range(tiles):
            cols = slice(n * tile, (n + 1) * tile)
            dm[:, cols] = nt(dt[h], weights2[cols, :])

        def fn(at, h=h):
            first = jnp.zeros((at.size, 128), F32)
            second = jnp.zeros((at.size, 128), F32)
            for n in range(tiles):
                cols = slice(n * tile, (n + 1) * tile)
                grad = dm[at, cols]
                product = grad * buf[h, at, cols]
                colsums[1, :, cols] += fold(product)
                colsums[2, :, cols] += fold(grad)
                first = first + lanes_of(grad * wv[1:2, cols])
                second = second + lanes_of(product * wv[1:2, cols])
            column = lax.broadcasted_iota(jnp.int32, (at.size, 128), 1)
            first = jnp.sum(first, 1, keepdims=True)
            second = jnp.sum(second, 1, keepdims=True)
            back[h, at, :] = jnp.where(column == 0, first, second)

        row_steps(span, 64, fn)
        back_copies[h].go()
        plan.hook()
        back_copies[h].wait_recv()

        def fn(at, h=h):
            scale = 1.0 / total_units
            first = (back[h, at, 0:1] + back_got[h, at, 0:1]) * scale
            second = (back[h, at, 1:2] + back_got[h, at, 1:2]) * scale
            inv = stat[h, at, 0:1]
            for n in range(tiles):
                cols = slice(n * tile, (n + 1) * tile)
                grad = inv * (dm[at, cols] * wv[1:2, cols] - first - buf[h, at, cols] * second)
                inner = (grad * slope[h, at, cols].astype(F32)).astype(BF)
                mix[h, at, cols] = inner
                colsums[0, :, cols] += fold(inner.astype(F32))

        row_steps(span, 64, fn)
        plan.hook()

    weights1 = f1v[...].reshape(width, units)
    out_copy.wait_recv()
    out[...] = (gh[...] + prb[...].astype(F32)).astype(BF)
    for n in range(0, width, tile):
        prb[:, n : n + tile] = nt(mix[1 - c], weights1[n : n + tile, :]).astype(BF)
    da_copy.go()
    for n in range(0, width, tile):
        gh[:, n : n + tile] = nt(mix[c], weights1[n : n + tile, :])
    plan.hook()
    size = stg.shape[1]
    writes = []

    def write(part, dst, wide):
        n = len(writes)
        if n >= 2:
            writes[n - 2].wait()
        stg[n % 2, :, 0:wide] = part.astype(BF)
        desc = pltpu.make_async_copy(stg.at[n % 2, :, pl.ds(0, wide)], dst, local.at[6 + n % 2])
        desc.start()
        writes.append(desc)

    for n in range(0, width, size):
        part = tn(act[0, :, n : n + size], mix[0]) + tn(act[1, :, n : n + size], mix[1])
        write(part, g1.at[pl.ds(n, size)], units)
    plan.hook()
    da_copy.wait_recv()
    out_copy.wait_send()

    def fn(at):
        da = gh[at, :] + prc[at, :].astype(F32)
        top = dt[c, at, :].astype(F32)
        normed, inv = normalize(hid[at, :])
        grad = top + norm_back(da * row(rows_all, 7), normed, inv)
        gh[at, :] = grad
        normed_b, inv_b = normalize(br[at, :])
        down = norm_back(grad * row(rows_all, 5), normed_b, inv_b).astype(BF)
        dbuf[at, :] = down
        for n, value in enumerate((down.astype(F32), grad * normed_b, grad, da * normed, da, top)):
            sums[n] += fold(value)

    row_steps(span, 64, fn)
    plan.hook()
    weights_o = wov[...].reshape(width, width)
    da_copy.wait_send()
    for j in range(group):
        at = slice(j * part_size, (j + 1) * part_size)
        prb[:, at] = (nt(dbuf[...], weights_o[at, :]) * lanes[:, at]).astype(BF)
    for copy in outgoing:
        copy.go()
    keep = pltpu.make_async_copy(give(s), do.at[mine_at], local.at[8])
    keep.start()
    plan.hook()
    for n in range(0, width, size):
        write(tn(own[:, n : n + size], dbuf[...]), go.at[pl.ds(n, size)], width)
    rows_g[...] = jnp.zeros(rows_g.shape, F32)
    for n in range(6):
        rows_g[4 + n : 5 + n, :] = jnp.sum(sums[n], 0, keepdims=True)
    wide_g[...] = jnp.zeros(wide_g.shape, F32)
    for n in range(NZ * NY * NX):
        at = pl.ds(pl.multiple_of((n * NC + c) * lane, lane), lane)
        for j in range(3):
            wide_g[j : j + 1, at] = jnp.sum(colsums[j, :, n * lane : (n + 1) * lane], 0, keepdims=True)
    plan.finish()
    for k in range(NZ):
        zk = place.zup((1, 2, 3, 0)[k])
        for src, dst, n in ((g2.at[zk, y, x, one], half2, 9), (g2.at[zk, y, x, two], half3, 10)):
            desc = pltpu.make_async_copy(src, dst.at[k], local.at[n + 2 * k])
            desc.start()
            writes.append(desc)
    for desc in writes[-2 * NZ :]:
        desc.wait()
    writes = writes[: -2 * NZ]
    keep.wait()
    for copy in outgoing:
        copy.wait_recv()
    for desc in writes[-2:]:
        desc.wait()
    wire.drain()


def feed_forward(own, rows_all, wide_all, lanes, tok, cot, f2, wo, f1):
    span, width = own.shape
    units = f1.shape[4]
    group = NX * NC
    per = f2.shape[3]
    out = (
        (VM, (span, width), BF),
        (HBM, (group * span, width // group), BF),
        (VM, (span, width), F32),
        (HBM, (width, units), BF),
        (HBM, (width, width), BF),
        (HBM, (NZ, per // 2, width), BF),
        (HBM, (NZ, per // 2, width), BF),
        (VM, (32, width), F32),
        (VM, (8, wide_all.shape[1]), F32),
    )
    scratch = [
        pltpu.VMEM(wo.shape, BF),
        pltpu.VMEM(f1.shape, BF),
        pltpu.VMEM((NZ, NY, NX) + (per, width), BF),
        pltpu.VMEM((NC, span, width), BF),
        pltpu.VMEM((NC, span, width), BF),
        pltpu.VMEM((NC, span, units), F32),
        pltpu.VMEM((NC, span, units), BF),
        pltpu.VMEM((NC, span, units), BF),
        pltpu.VMEM((span, units), F32),
        pltpu.VMEM((span, width), F32),
        pltpu.VMEM((span, width), F32),
        pltpu.VMEM((NZ, NY, NX) + (per, width), BF),
        pltpu.VMEM((span, width), BF),
        pltpu.VMEM((span, width), BF),
        pltpu.VMEM((span, width), BF),
        pltpu.VMEM((2, 128, units), BF),
        pltpu.VMEM((8, units), F32),
    ]
    scratch += [pltpu.VMEM((NC, span, 128), F32)] * 4
    scratch += [pltpu.VMEM((6, 16, width), F32), pltpu.VMEM((3, 16, units), F32)]
    scratch += plane_scratch((per // 2, width))[1:3] * 2
    scratch += [
        pltpu.SemaphoreType.DMA((COPIES,)),
        pltpu.SemaphoreType.DMA((COPIES,)),
        pltpu.SemaphoreType.DMA((17,)),
    ]
    return pl.pallas_call(
        ffn_kernel,
        out_shape=tuple(jax.ShapeDtypeStruct(shape, dtype) for _, shape, dtype in out),
        in_specs=[VM] * 4 + [HBM] * 5,
        out_specs=[spec for spec, _, _ in out],
        scratch_shapes=scratch,
        compiler_params=pltpu.CompilerParams(
            collective_id=3, has_side_effects=True, vmem_limit_bytes=63 * 1024 * 1024
        ),
        name="feed_forward",
    )(own, rows_all, wide_all, lanes, tok, cot, f2, wo, f1)


def fast(tokens, doc_ids, cotangent, w_qkv, w_out, attn_vecs, head_scale, w_fc1, w_fc2, ffn_vecs, ffn_wide):
    _, span, width = tokens.shape
    group = NX * NC
    length = span * group
    head_count = head_scale.shape[0]
    head = width // head_count
    heads = head_count // group
    part = heads * head
    seq = lax.axis_index("seq")
    chips = NZ * NY * NX
    block = w_fc2.shape[0]
    units = chips * block

    rows = w_qkv.shape[0]
    narrow = jnp.concatenate([attn_vecs, ffn_vecs], 0)
    count, each = narrow.shape
    lane = each * group
    column = lax.broadcasted_iota(jnp.int32, (16, lane), 1) // each
    narrow = jnp.pad(jnp.tile(narrow, (1, group)), ((0, 16 - count), (0, 0)))
    narrow = jnp.where(column == seq, narrow, 0.0)
    vec = jnp.stack([narrow, jnp.pad(ffn_wide, ((0, 16 - ffn_wide.shape[0]), (0, 0)))]).astype(BF)
    tok = tokens.reshape(span, width)
    lanes = jnp.repeat(head_scale, head).reshape(1, width)
    ids = doc_ids.reshape(length)
    act_one, q, k, v, att, lse, scaled_own, wq, rows_all, wide_all, wo, fc1, fc2 = forward(
        tok, w_qkv, vec, w_out, w_fc1, w_fc2, ids, lanes, heads
    )
    outputs, do, grad_hidden, grad_fc1, grad_out, half2, half3, rows_in, wide_grads = feed_forward(
        scaled_own,
        rows_all,
        wide_all,
        lanes,
        tok,
        cotangent.reshape(span, width),
        fc2,
        wo,
        fc1,
    )
    grad_tokens, grad_w1, grad_w2, grad_wo, grad_wqkv, rows_out, wide_out = backward(
        do,
        q,
        k,
        v,
        att,
        lse,
        ids,
        wq,
        tok,
        grad_hidden,
        rows_in,
        wide_grads,
        rows_all,
        act_one,
        grad_fc1.reshape(NZ, NY, NX, NC * rows, units),
        grad_out.reshape(NZ, NY, NX, NC, rows, width),
        half2,
        half3,
        heads,
    )
    mine = lax.dynamic_slice_in_dim(rows_out, seq * each, each, 1)
    wide_mine = lax.dynamic_slice_in_dim(wide_out, seq * block, block, 1)
    return (
        outputs.reshape(1, span, width),
        grad_tokens.reshape(1, span, width),
        grad_wqkv,
        grad_wo,
        mine[: attn_vecs.shape[0]],
        rows_out[16 : 16 + head_count, 0] / head_scale,
        grad_w1,
        grad_w2,
        mine[attn_vecs.shape[0] : count],
        wide_mine[: ffn_wide.shape[0]],
    )


def solution(mesh):
    placed = (
        P("dp", "seq", None),
        P("dp", None),
        P("dp", "seq", None),
        P(("dp", "seq"), None),
        P(("dp", "seq"), None),
        P(None, ("dp", "seq")),
        P(),
        P(("dp", "seq"), None),
        P(("dp", "seq"), None),
        P(None, ("dp", "seq")),
        P(None, ("dp", "seq")),
    )
    results = (
        P("dp", "seq", None),
        P("dp", "seq", None),
        P(("dp", "seq"), None),
        P(("dp", "seq"), None),
        P(None, ("dp", "seq")),
        P(),
        P(("dp", "seq"), None),
        P(("dp", "seq"), None),
        P(None, ("dp", "seq")),
        P(None, ("dp", "seq")),
    )
    suits = mesh.shape["dp"] == NZ * NY and mesh.shape["seq"] == NX * NC
    return jax.shard_map(
        fast if suits else local, mesh=mesh, in_specs=placed, out_specs=results, check_vma=False
    )
```

```python
import functools
import math

import jax
import jax.numpy as jnp
from jax import lax
from jax.experimental import pallas as pl
from jax.experimental.pallas import tpu as pltpu
from jax.sharding import PartitionSpec as P

EPSILON = 1e-05
NEGATIVE = -1e30
MESH = pl.DeviceIdType.MESH
BF = jnp.bfloat16
F32 = jnp.float32
NZ, NY, NX, NC = 4, 2, 2, 2
HBM = pl.BlockSpec(memory_space=pl.ANY)
VM = pl.BlockSpec(memory_space=pltpu.VMEM)


def normalize(values):
    centre = jnp.mean(values, -1, keepdims=True)
    centred = values - centre
    scale_inv = lax.rsqrt(jnp.mean(centred * centred, -1, keepdims=True) + EPSILON)
    return (centred * scale_inv, scale_inv)


def norm_back(grad_normed, normed, scale_inv):
    return scale_inv * (
        grad_normed
        - jnp.mean(grad_normed, -1, keepdims=True)
        - normed * jnp.mean(grad_normed * normed, -1, keepdims=True)
    )


def gelu_exact(values):
    return 0.5 * values * (1.0 + jax.scipy.special.erf(values * math.sqrt(0.5)))


def left_grad(activations, gradients):
    return lax.dot_general(
        activations, gradients, (((0,), (0,)), ((), ())), preferred_element_type=jnp.float32
    )


def right_back(gradients, matrix):
    return lax.dot_general(
        gradients, matrix, (((1,), (1,)), ((), ())), preferred_element_type=jnp.float32
    )


def masked_scores(queries, keys_block, query_pos, key_pos, query_ids, key_ids):
    raw_scores = jnp.einsum(
        "rqhe,rkhe->rhqk", queries, keys_block, preferred_element_type=jnp.float32
    )
    allowed = (key_pos[None, None, :] <= query_pos[None, :, None]) & (
        key_ids[:, None, :] == query_ids[:, :, None]
    )
    return jnp.where(allowed[:, None], raw_scores * queries.shape[3] ** (-0.5), NEGATIVE)


def attend(queries, keys_all, values_all, query_pos, query_ids, doc_rows, block_len):
    block_count = keys_all.shape[1] // block_len
    stat_shape = (queries.shape[0], queries.shape[2], queries.shape[1])

    def slice_block(block_index):
        start = block_index * block_len
        keys_block = lax.dynamic_slice_in_dim(keys_all, start, block_len, 1)
        values_block = lax.dynamic_slice_in_dim(values_all, start, block_len, 1)
        key_ids = lax.dynamic_slice_in_dim(doc_rows, start, block_len, 1)
        key_pos = start + jnp.arange(block_len, dtype=jnp.int32)
        return (
            values_block,
            masked_scores(queries, keys_block, query_pos, key_pos, query_ids, key_ids),
        )

    def first_pass(carry, block_index):
        running_max, running_sum = carry
        _, scores = slice_block(block_index)
        new_max = jnp.maximum(running_max, jnp.max(scores, -1))
        running_sum = running_sum * jnp.exp(running_max - new_max) + jnp.sum(
            jnp.exp(scores - new_max[..., None]), -1
        )
        return ((new_max, running_sum), None)

    start_stats = (jnp.full(stat_shape, NEGATIVE, jnp.float32), jnp.zeros(stat_shape, jnp.float32))
    (row_max, row_sum), _ = lax.scan(
        first_pass, start_stats, jnp.arange(block_count, dtype=jnp.int32)
    )
    log_total = row_max + jnp.log(row_sum)

    def second_pass(total_out, block_index):
        values_block, scores = slice_block(block_index)
        probs = jnp.exp(scores - log_total[..., None]).astype(jnp.bfloat16)
        return (
            total_out
            + jnp.einsum(
                "rhqk,rkhe->rqhe", probs, values_block, preferred_element_type=jnp.float32
            ),
            None,
        )

    attended, _ = lax.scan(
        second_pass, jnp.zeros(queries.shape, jnp.float32), jnp.arange(block_count, dtype=jnp.int32)
    )
    return (attended, log_total)


def attend_back(
    queries,
    keys_all,
    values_all,
    grad_out,
    log_total,
    delta,
    query_pos,
    query_ids,
    doc_rows,
    block_len,
):
    block_count = keys_all.shape[1] // block_len
    scale = queries.shape[3] ** (-0.5)

    def step(grad_queries, block_index):
        start = block_index * block_len
        keys_block = lax.dynamic_slice_in_dim(keys_all, start, block_len, 1)
        values_block = lax.dynamic_slice_in_dim(values_all, start, block_len, 1)
        key_ids = lax.dynamic_slice_in_dim(doc_rows, start, block_len, 1)
        key_pos = start + jnp.arange(block_len, dtype=jnp.int32)
        scores = masked_scores(queries, keys_block, query_pos, key_pos, query_ids, key_ids)
        probs = jnp.exp(scores - log_total[..., None])
        grad_probs = jnp.einsum(
            "rqhe,rkhe->rhqk", grad_out, values_block, preferred_element_type=jnp.float32
        )
        grad_scores = (probs * (grad_probs - delta[..., None]) * scale).astype(jnp.bfloat16)
        grad_queries = grad_queries + jnp.einsum(
            "rhqk,rkhe->rqhe", grad_scores, keys_block, preferred_element_type=jnp.float32
        )
        grad_keys = jnp.einsum(
            "rhqk,rqhe->rkhe", grad_scores, queries, preferred_element_type=jnp.float32
        )
        grad_values = jnp.einsum(
            "rhqk,rqhe->rkhe",
            probs.astype(jnp.bfloat16),
            grad_out,
            preferred_element_type=jnp.float32,
        )
        return (grad_queries, (grad_keys, grad_values))

    return lax.scan(
        step, jnp.zeros(queries.shape, jnp.float32), jnp.arange(block_count, dtype=jnp.int32)
    )


def local(
    tokens,
    doc_ids,
    cotangent,
    w_qkv,
    w_out,
    attn_vecs,
    head_scale,
    w_fc1,
    w_fc2,
    ffn_vecs,
    ffn_wide,
):
    row_count, span_len, model_width = tokens.shape
    head_count = head_scale.shape[0]
    head_size = model_width // head_count
    token_count = row_count * span_len
    brain = jnp.bfloat16
    single = jnp.float32
    gathered_qkv, gathered_out, attn_rows = (
        lax.all_gather(w_qkv.astype(brain), ("dp", "seq"), axis=0, tiled=True),
        lax.all_gather(w_out.astype(brain), ("dp", "seq"), axis=0, tiled=True),
        lax.all_gather(attn_vecs.astype(brain), ("dp", "seq"), axis=1, tiled=True),
    )
    attn_rows = attn_rows.astype(single)
    inputs = tokens.astype(single).reshape(token_count, model_width)
    normed_one, inv_one = normalize(inputs)
    act_one = (normed_one * attn_rows[0] + attn_rows[1]).astype(brain)
    projected = jnp.dot(act_one, gathered_qkv, preferred_element_type=single)
    queries = (projected[:, :model_width] + attn_rows[2]).astype(brain)
    keys_own = projected[:, model_width : 2 * model_width].astype(brain)
    values_own = (projected[:, 2 * model_width :] + attn_rows[3]).astype(brain)
    keys_all, values_all = (
        lax.all_gather(
            keys_own.reshape(row_count, span_len, model_width), "seq", axis=1, tiled=True
        ),
        lax.all_gather(
            values_own.reshape(row_count, span_len, model_width), "seq", axis=1, tiled=True
        ),
    )
    offset = lax.axis_index("seq") * span_len
    query_pos = offset + jnp.arange(span_len, dtype=jnp.int32)
    query_ids = lax.dynamic_slice_in_dim(doc_ids, offset, span_len, 1)
    queries_four = queries.reshape(row_count, span_len, head_count, head_size)
    keys_four = keys_all.reshape(row_count, -1, head_count, head_size)
    values_four = values_all.reshape(row_count, -1, head_count, head_size)
    attended, log_total = attend(
        queries_four, keys_four, values_four, query_pos, query_ids, doc_ids, span_len
    )
    scaled = (
        (attended * head_scale[None, None, :, None]).reshape(token_count, model_width).astype(brain)
    )
    branch = jnp.dot(scaled, gathered_out, preferred_element_type=single) + attn_rows[4]
    normed_branch, inv_branch = normalize(branch)
    hidden = inputs + normed_branch * attn_rows[5] + attn_rows[6]
    gathered_fc1, gathered_fc2, ffn_rows, wide_rows = (
        lax.all_gather(w_fc1.astype(brain), ("dp", "seq"), axis=0, tiled=True),
        lax.all_gather(w_fc2.astype(brain), ("dp", "seq"), axis=0, tiled=True),
        lax.all_gather(ffn_vecs.astype(brain), ("dp", "seq"), axis=1, tiled=True),
        lax.all_gather(ffn_wide.astype(brain), ("dp", "seq"), axis=1, tiled=True),
    )
    ffn_rows = ffn_rows.astype(single)
    wide_rows = wide_rows.astype(single)
    normed_two, inv_two = normalize(hidden)
    act_two = (normed_two * ffn_rows[0] + ffn_rows[1]).astype(brain)
    inner_act = jnp.dot(act_two, gathered_fc1, preferred_element_type=single) + wide_rows[0]
    activated, gelu_pull = jax.vjp(gelu_exact, inner_act)
    normed_three, inv_three = normalize(activated)
    mixed_act = (normed_three * wide_rows[1] + wide_rows[2]).astype(brain)
    result = hidden + jnp.dot(mixed_act, gathered_fc2, preferred_element_type=single) + ffn_rows[2]
    outputs = result.astype(brain).reshape(row_count, span_len, model_width)
    back_set = (
        lax.all_gather(w_qkv.astype(brain), ("dp", "seq"), axis=0, tiled=True),
        lax.all_gather(w_out.astype(brain), ("dp", "seq"), axis=0, tiled=True),
        lax.all_gather(attn_vecs.astype(brain), ("dp", "seq"), axis=1, tiled=True),
        lax.all_gather(w_fc1.astype(brain), ("dp", "seq"), axis=0, tiled=True),
        lax.all_gather(w_fc2.astype(brain), ("dp", "seq"), axis=0, tiled=True),
        lax.all_gather(ffn_vecs.astype(brain), ("dp", "seq"), axis=1, tiled=True),
        lax.all_gather(ffn_wide.astype(brain), ("dp", "seq"), axis=1, tiled=True),
    )
    gathered_qkv, gathered_out, attn_back, gathered_fc1, gathered_fc2, ffn_back, wide_back = (
        back_set
    )
    attn_rows = attn_back.astype(single)
    ffn_rows = ffn_back.astype(single)
    wide_rows = wide_back.astype(single)
    grad_top = cotangent.astype(single).reshape(token_count, model_width)
    grad_branch_two = grad_top.astype(brain)
    grad_fc2 = left_grad(mixed_act, grad_branch_two)
    grad_bias_two = jnp.sum(grad_branch_two.astype(single), 0)
    grad_mixed = right_back(grad_branch_two, gathered_fc2)
    grad_inner_gain = jnp.sum(grad_mixed * normed_three, 0)
    grad_inner_bias = jnp.sum(grad_mixed, 0)
    grad_activated = norm_back(grad_mixed * wide_rows[1], normed_three, inv_three)
    grad_inner = gelu_pull(grad_activated)[0].astype(brain)
    grad_fc1 = left_grad(act_two, grad_inner)
    grad_bias_one = jnp.sum(grad_inner.astype(single), 0)
    grad_act_two = right_back(grad_inner, gathered_fc1)
    grad_gain_two = jnp.sum(grad_act_two * normed_two, 0)
    grad_shift_two = jnp.sum(grad_act_two, 0)
    grad_hidden = grad_top + norm_back(grad_act_two * ffn_rows[0], normed_two, inv_two)
    ffn_sums = (
        lax.psum_scatter(grad_fc1, ("dp", "seq"), scatter_dimension=0, tiled=True),
        lax.psum_scatter(grad_fc2, ("dp", "seq"), scatter_dimension=0, tiled=True),
        lax.psum_scatter(
            jnp.stack([grad_gain_two, grad_shift_two, grad_bias_two]),
            ("dp", "seq"),
            scatter_dimension=1,
            tiled=True,
        ),
        lax.psum_scatter(
            jnp.stack([grad_bias_one, grad_inner_gain, grad_inner_bias]),
            ("dp", "seq"),
            scatter_dimension=1,
            tiled=True,
        ),
    )
    grad_post_gain = jnp.sum(grad_hidden * normed_branch, 0)
    grad_post_shift = jnp.sum(grad_hidden, 0)
    grad_branch = norm_back(grad_hidden * attn_rows[5], normed_branch, inv_branch).astype(brain)
    grad_out_bias = jnp.sum(grad_branch.astype(single), 0)
    grad_out = left_grad(scaled, grad_branch)
    grad_scaled = right_back(grad_branch, gathered_out).reshape(
        row_count, span_len, head_count, head_size
    )
    grad_scale = jnp.sum(grad_scaled * attended, (0, 1, 3))
    grad_attended = (grad_scaled * head_scale[None, None, :, None]).astype(brain)
    delta = jnp.transpose(jnp.sum(grad_attended.astype(single) * attended, -1), (0, 2, 1))
    grad_queries, key_parts = attend_back(
        queries_four,
        keys_four,
        values_four,
        grad_attended,
        log_total,
        delta,
        query_pos,
        query_ids,
        doc_ids,
        span_len,
    )
    partial_keys = jnp.transpose(key_parts[0], (1, 0, 2, 3, 4)).reshape(row_count, -1, model_width)
    partial_values = jnp.transpose(key_parts[1], (1, 0, 2, 3, 4)).reshape(
        row_count, -1, model_width
    )
    grad_keys, grad_values = (
        lax.psum_scatter(
            partial_keys.astype(jnp.bfloat16), "seq", scatter_dimension=1, tiled=True
        ).astype(jnp.float32),
        lax.psum_scatter(
            partial_values.astype(jnp.bfloat16), "seq", scatter_dimension=1, tiled=True
        ).astype(jnp.float32),
    )
    grad_qkv = jnp.concatenate(
        [
            grad_queries.reshape(token_count, model_width).astype(brain),
            grad_keys.reshape(token_count, model_width).astype(brain),
            grad_values.reshape(token_count, model_width).astype(brain),
        ],
        1,
    )
    grad_w_qkv = left_grad(act_one, grad_qkv)
    grad_query_bias = jnp.sum(grad_qkv[:, :model_width].astype(single), 0)
    grad_value_bias = jnp.sum(grad_qkv[:, 2 * model_width :].astype(single), 0)
    grad_act_one = right_back(grad_qkv, gathered_qkv)
    grad_gain_one = jnp.sum(grad_act_one * normed_one, 0)
    grad_shift_one = jnp.sum(grad_act_one, 0)
    grad_tokens = (
        (grad_hidden + norm_back(grad_act_one * attn_rows[0], normed_one, inv_one))
        .astype(brain)
        .reshape(row_count, span_len, model_width)
    )
    attn_stack = jnp.stack(
        [
            grad_gain_one,
            grad_shift_one,
            grad_query_bias,
            grad_value_bias,
            grad_out_bias,
            grad_post_gain,
            grad_post_shift,
        ]
    )
    attn_sums = (
        lax.psum_scatter(grad_w_qkv, ("dp", "seq"), scatter_dimension=0, tiled=True),
        lax.psum_scatter(grad_out, ("dp", "seq"), scatter_dimension=0, tiled=True),
        lax.psum_scatter(attn_stack, ("dp", "seq"), scatter_dimension=1, tiled=True),
    )
    scale_total = lax.psum(grad_scale, ("dp", "seq"))
    return (
        outputs,
        grad_tokens,
        attn_sums[0],
        attn_sums[1],
        attn_sums[2],
        scale_total,
        ffn_sums[0],
        ffn_sums[1],
        ffn_sums[2],
        ffn_sums[3],
    )


class Place:
    def __init__(self):
        self.dp = lax.axis_index("dp")
        self.seq = lax.axis_index("seq")
        self.z, self.y = self.dp // NY, self.dp % NY
        self.x, self.c = self.seq // NC, self.seq % NC

    def at(self, z=None, y=None, x=None, c=None):
        z = self.z if z is None else z
        y = self.y if y is None else y
        x = self.x if x is None else x
        c = self.c if c is None else c
        return (z * NY + y, x * NC + c)

    def zup(self, k):
        return (self.z + k) % NZ

    def group(self):
        near = [self.at(c=1 - self.c), self.at(x=1 - self.x), self.at(x=1 - self.x, c=1 - self.c)]
        return near + [self.at(y=1 - self.y)] + [self.at(z=self.zup(k)) for k in range(1, NZ)]


class Copy:
    def __init__(self, desc):
        self.desc, self.sent = desc, False

    def go(self):
        self.desc.start()
        return self

    def wait_recv(self):
        self.desc.wait_recv()

    def wait_send(self):
        if not self.sent:
            self.desc.wait_send()
        self.sent = True


class Wire:
    def __init__(self, place, send, recv):
        self.place, self.send, self.recv, self.used, self.open = place, send, recv, 0, []

    def copy(self, src, dst, dev):
        n = self.used
        self.used += 1
        copy = Copy(
            pltpu.make_async_remote_copy(
                src_ref=src,
                dst_ref=dst,
                send_sem=self.send.at[n],
                recv_sem=self.recv.at[n],
                device_id=dev,
                device_id_type=MESH,
            )
        )
        self.open.append(copy)
        return copy

    def drain(self):
        for copy in self.open:
            copy.wait_send()


def greet(place):
    barrier = pltpu.get_barrier_semaphore()
    group = place.group()
    for dev in group:
        pl.semaphore_signal(barrier, inc=1, device_id=dev, device_id_type=MESH)
    pl.semaphore_wait(barrier, len(group))


def spread_zxy(wire, place, ref, swap=False):
    z, y, x = place.z, place.y, place.x
    own = ref.at[z, y, x]
    first = place.at(y=1 - y) if swap else place.at(x=1 - x)
    second = place.at(x=1 - x) if swap else place.at(y=1 - y)
    order = [(z - k + NZ) % NZ for k in range(NZ)]
    along_z = [wire.copy(own, own, place.at(z=place.zup(k))) for k in range(1, NZ)]
    firsts = [wire.copy(ref.at[zk, y, x], ref.at[zk, y, x], first) for zk in order]
    twos = [ref.at[zk, :, x] if swap else ref.at[zk, y] for zk in order]
    seconds = [wire.copy(two, two, second) for two in twos]
    yield
    for copy in along_z + firsts[:1]:
        copy.go()
    yield
    for k in range(1, NZ):
        along_z[k - 1].wait_recv()
        firsts[k].go()
        yield
    for k in range(NZ):
        firsts[k].wait_recv()
        seconds[k].go()
        yield
    for copy in seconds:
        copy.wait_recv()


def spread_xzy(wire, place, ref, swap=False):
    z, y, x = place.z, place.y, place.x
    own = ref.at[z, y, x]
    first = place.at(y=1 - y) if swap else place.at(x=1 - x)
    second = place.at(x=1 - x) if swap else place.at(y=1 - y)
    order = [(z - k + NZ) % NZ for k in range(NZ)]
    twos = [ref.at[zk, :, x] if swap else ref.at[zk, y] for zk in order]
    start = wire.copy(own, own, first)
    steps = [wire.copy(two, two, place.at(z=place.zup(1))) for two in twos[:-1]]
    seconds = [wire.copy(two, two, second) for two in twos]
    yield
    start.go()
    yield
    start.wait_recv()
    steps[0].go()
    seconds[0].go()
    yield
    for k in range(1, NZ):
        steps[k - 1].wait_recv()
        if k < NZ - 1:
            steps[k].go()
        seconds[k].go()
        yield
    for copy in seconds:
        copy.wait_recv()


def spread_zx(wire, place, ref, swap=False):
    z, y, x = place.z, place.y, place.x
    first = place.at(y=1 - y) if swap else place.at(x=1 - x)
    order = [(z - k + NZ) % NZ for k in range(NZ)]
    own = ref.at[z, y, x]
    along_z = [wire.copy(own, own, place.at(z=place.zup(k))) for k in range(1, NZ)]
    firsts = [wire.copy(ref.at[zk, y, x], ref.at[zk, y, x], first) for zk in order]
    yield
    for copy in along_z + firsts[:1]:
        copy.go()
    yield
    for k in range(1, NZ):
        along_z[k - 1].wait_recv()
        firsts[k].go()
        yield
    for copy in firsts:
        copy.wait_recv()


def spread_last(wire, place, src, dst, swap=False):
    z, y, x = place.z, place.y, place.x
    second = place.at(x=1 - x) if swap else place.at(y=1 - y)
    seconds = []
    for k in range(NZ):
        zk = (z - k + NZ) % NZ
        here, there = (src.at[zk, :, x], dst.at[zk, :, x]) if swap else (src.at[zk, y], dst.at[zk, y])
        seconds.append(wire.copy(here, there, second))
    yield
    for copy in seconds:
        copy.go()
    yield
    for copy in seconds:
        copy.wait_recv()


def spread_pair(wire, place, ref):
    plane = ref.at[:, :, :, place.c]
    last = wire.copy(plane, plane, place.at(c=1 - place.c))
    yield from spread_xzy(wire, place, plane)
    last.go()
    yield
    last.wait_recv()


def spread_dp(wire, place, views):
    z, y = place.z, place.y
    at = [z * NY + y] + [((z - n + NZ) % NZ) * NY + y for n in range(1, NZ)]
    along_z = [[wire.copy(view(at[0]), view(at[0]), place.at(z=place.zup(n))) for view in views] for n in range(1, NZ)]
    ys = [[wire.copy(view(d), view(d), place.at(y=1 - y)) for view in views] for d in at]
    yield
    for copies in along_z + ys[:1]:
        for copy in copies:
            copy.go()
    yield
    for n in range(1, NZ):
        for copy in along_z[n - 1]:
            copy.wait_recv()
        for copy in ys[n]:
            copy.go()
        yield
    for copies in ys:
        for copy in copies:
            copy.wait_recv()


def spread_row(wire, place, tok, tok_all):
    s, other, core = place.seq, place.at(x=1 - place.x), place.at(c=1 - place.c)
    far = tok_all.at[s ^ 2]
    tok_x = wire.copy(tok, tok_all.at[s], other)
    tok_c = wire.copy(tok, tok_all.at[s], core)
    last = wire.copy(far, far, core)
    yield
    tok_c.go()
    tok_x.go()
    yield
    tok_c.wait_recv()
    yield
    tok_x.wait_recv()
    last.go()
    yield
    last.wait_recv()


class Plan:
    def __init__(self, tasks, order):
        self.tasks, self.order = tasks, list(order)
        for task in tasks.values():
            next(task)

    def hook(self):
        for name in self.order.pop(0):
            next(self.tasks[name], None)

    def finish(self):
        while self.order:
            self.hook()
        for task in self.tasks.values():
            for _ in task:
                pass


COPIES = 104


def nt(a, b):
    return lax.dot_general(a, b, (((1,), (1,)), ((), ())), preferred_element_type=F32)


def nn(a, b):
    return lax.dot_general(a, b, (((1,), (0,)), ((), ())), preferred_element_type=F32)


def pair_bias(idr, key_ids, qb, kb, size):
    qs = pl.multiple_of(qb * size, size)
    key_pos = kb * size + lax.broadcasted_iota(jnp.int32, (size, size), 0)
    query_pos = qs + lax.broadcasted_iota(jnp.int32, (size, size), 1)
    same = key_ids == idr[:, pl.ds(qs, size)]
    return jnp.where((key_pos <= query_pos) & same, 0.0, NEGATIVE)


def mask_heads(dst, src, heads, head):
    lane = lax.broadcasted_iota(jnp.int32, src.shape, 1) // head
    whole = src[...]
    for h in range(heads):
        dst[h] = jnp.where(lane == h, whole, jnp.zeros_like(whole))


FORWARD = (
    "tqocaoaqqqbdcccoacqtt",
    "",
    "",
    "t",
    "bbbb",
    "",
    "",
    "b",
    "bddd",
    "bo",
    "",
    "",
    "a",
    "od",
    "",
    "b",
    "aooa",
)


def forward_tasks(wire, place, tok, tok_all, wq, rows_all, wide_all, lane, wo_all, f1_all, f2_all):
    group = NX * NC
    half1 = f1_all.shape[4] // 2
    half2 = f2_all.shape[3] // 2
    views = [
        lambda d: wq.at[d],
        lambda d: rows_all.at[:, pl.ds(pl.multiple_of(d * lane, lane), lane)],
        lambda d: wide_all.at[:, pl.ds(pl.multiple_of(d * lane * group, lane * group), lane * group)],
    ]
    return {
        "t": spread_row(wire, place, tok, tok_all),
        "q": spread_dp(wire, place, views),
        "a": spread_xzy(wire, place, f1_all.at[:, :, :, :, pl.ds(0, half1)]),
        "b": spread_zxy(wire, place, f1_all.at[:, :, :, :, pl.ds(half1, half1)], swap=True),
        "o": spread_pair(wire, place, wo_all),
        "c": spread_zx(wire, place, f2_all.at[:, :, :, pl.ds(0, half2)]),
        "d": spread_zx(wire, place, f2_all.at[:, :, :, pl.ds(half2, half2)], swap=True),
    }


def forward_kernel(heads, *refs):
    tok, w_qkv, vec, w_out, w_fc1, w_fc2, idr, lanes = refs[:8]
    act, q, k, v, att, lse, own, wq, rows_all, wide_all, wo_all, f1_all, f2_all = refs[8:21]
    tok_all, actv, vecs, km, vt, idc, bias, top, low, acc, scb, wq4, wo, f1, f2, send, recv, local = refs[21:]
    place = Place()
    z, y, x, c, s, dp = place.z, place.y, place.x, place.c, place.seq, place.dp
    group = NX * NC
    wire = Wire(place, send, recv)
    core, other, across = place.at(c=1 - c), place.at(x=1 - x), place.at(x=1 - x, c=1 - c)
    span, width = tok.shape
    rows = f1.shape[1]
    length, part = q.shape
    head = part // heads

    for j in range(group):
        for n in range(3):
            at = n * width + j * part
            wq4[j, :, n * part : (n + 1) * part] = w_qkv[:, at : at + part].astype(BF)
    greet(place)
    quarter = []
    for dev, peer in ((core, s ^ 1), (other, s ^ 2), (across, s ^ 3)):
        quarter.append(wire.copy(wq4.at[peer], wq.at[dp, s], dev).go())
        quarter.append(wire.copy(vec, vecs.at[s], dev).go())
    cut = vec.shape[2]
    for n in range(NZ * NY * NX):
        for j in range(NC):
            at = (n * NC + j) * cut
            f1[j, :, n * cut : (n + 1) * cut] = w_fc1[:, at : at + cut].astype(BF)
    wo[...] = w_out[...].astype(BF)
    f2[...] = w_fc2[...].astype(BF)
    f1_c = wire.copy(f1.at[1 - c], f1_all.at[z, y, x, pl.ds(c * rows, rows)], core).go()
    here = [
        pltpu.make_async_copy(wq4.at[s], wq.at[dp, s], local.at[0]),
        pltpu.make_async_copy(vec, vecs.at[s], local.at[1]),
        pltpu.make_async_copy(tok, tok_all.at[s], local.at[2]),
        pltpu.make_async_copy(wo, wo_all.at[z, y, x, c], local.at[3]),
        pltpu.make_async_copy(f1.at[c], f1_all.at[z, y, x, pl.ds(c * rows, rows)], local.at[4]),
        pltpu.make_async_copy(f2, f2_all.at[z, y, x], local.at[5]),
    ]
    for desc in here:
        desc.start()
    for desc in here:
        desc.wait()
    for desc in quarter:
        desc.wait_recv()

    lane = vec.shape[2]
    blk = pl.multiple_of(dp * lane, lane)
    wide_blk = pl.multiple_of(dp * lane * group, lane * group)
    rows_all[:, pl.ds(blk, lane)] = (vecs[0, 0] + vecs[1, 0]) + (vecs[2, 0] + vecs[3, 0])
    for j in range(group):
        wide_all[:, pl.ds(pl.multiple_of(wide_blk + j * lane, lane), lane)] = vecs[j, 1]

    f1_c.wait_recv()
    plan = Plan(
        forward_tasks(wire, place, tok, tok_all, wq, rows_all, wide_all, lane, wo_all, f1_all, f2_all), FORWARD
    )
    plan.hook()

    shift = pl.multiple_of(s * part, part)
    bias_q = rows_all[2:3, pl.ds(shift, part)].astype(F32)
    bias_v = rows_all[3:4, pl.ds(shift, part)].astype(F32)
    gain, base = rows_all[0:1, :].astype(F32), rows_all[1:2, :].astype(F32)
    keep = []
    for m in range(group):
        j = s ^ m
        plan.hook()
        if m >= 2:
            keep[m - 2].wait()
        slot = actv.at[m % 2]
        step = 64

        def norm_rows(n, _, slot=slot, j=j):
            at = pl.ds(pl.multiple_of(n * step, step), step)
            values = tok_all[j, at, :].astype(F32)
            slot[at, :] = (normalize(values)[0] * gain + base).astype(BF)
            return 0

        lax.fori_loop(0, span // step, norm_rows, 0)
        at = pl.ds(pl.multiple_of(j * span, span), span)
        desc = pltpu.make_async_copy(slot, act.at[at], local.at[6 + m])
        desc.start()
        keep.append(desc)
        for n, (dst, add) in enumerate(((q, bias_q), (k, None), (v, bias_v))):
            weights = wq[:, :, :, n * part : (n + 1) * part].reshape(width, part)
            proj = nn(slot[...], weights)
            if add is not None:
                proj = proj + add
            if n == 0:
                proj = proj * (head**-0.5)
            dst[at, :] = proj.astype(BF)

    plan.hook()
    mask_heads(km, k, heads, head)
    vt[...] = v[...].T
    idc[...] = jnp.broadcast_to(idr[...], (8, length)).T
    blocks = length // span
    returns = []
    for qb in reversed(range(blocks)):
        qs = slice(qb * span, (qb + 1) * span)
        top[...] = jnp.full(top.shape, NEGATIVE, F32)
        low[...] = jnp.zeros(low.shape, F32)
        acc[...] = jnp.zeros(acc.shape, F32)

        def keys(step, _, qb=qb, qs=qs):
            kb = qb - step
            ks = pl.ds(pl.multiple_of(kb * span, span), span)
            bias[...] = pair_bias(idr, idc[ks, 0:1], qb, kb, span)
            for h in range(heads):
                scores = nt(km[h, ks, :], q[qs, :]) + bias[...]
                old = top[h : h + 1, :]
                new = jnp.maximum(old, jnp.max(scores, 0, keepdims=True))
                probs = jnp.exp(scores - new)
                shrink = jnp.exp(old - new)
                top[h : h + 1, :] = new
                low[h : h + 1, :] = low[h : h + 1, :] * shrink + jnp.sum(probs, 0, keepdims=True)
                hs = slice(h * head, (h + 1) * head)
                acc[hs, :] = acc[hs, :] * shrink + nn(vt[hs, ks], probs.astype(BF))
            for n in range(qb + 1):

                @pl.when(step == n)
                def _():
                    plan.hook()

            return 0

        lax.fori_loop(0, qb + 1, keys, 0)
        for h in range(heads):
            hs = slice(h * head, (h + 1) * head)
            acc[hs, :] = acc[hs, :] * (1.0 / low[h : h + 1, :])
        att[:, qs] = acc[...]
        lse[:, qs] = top[...] + jnp.log(low[...])
        scb[qb] = (acc[...].T * lanes[:, pl.ds(shift, part)]).astype(BF)
        view = own.at[:, pl.ds(shift, part)]
        back = pltpu.make_async_remote_copy(
            src_ref=scb.at[qb],
            dst_ref=view,
            send_sem=send.at[COPIES - 1 - qb],
            recv_sem=recv.at[COPIES - 4 + (s ^ qb)],
            device_id=(dp, qb),
            device_id_type=MESH,
        )
        mine = pltpu.make_async_copy(scb.at[qb], view, local.at[10])
        returns.append((qb, back, mine))

        @pl.when(s == qb)
        def _():
            mine.start()

        @pl.when(s != qb)
        def _():
            back.start()

    plan.finish()
    for desc in keep[-2:]:
        desc.wait()
    for qb, back, mine in returns:

        @pl.when(s == qb)
        def _():
            mine.wait()

        @pl.when(s != qb)
        def _():
            back.wait_send()

    for m in range(1, group):
        view = own.at[:, pl.ds(pl.multiple_of((s ^ m) * part, part), part)]
        pltpu.make_async_remote_copy(
            src_ref=scb.at[0],
            dst_ref=view,
            send_sem=send.at[COPIES - 1],
            recv_sem=recv.at[COPIES - 4 + m],
            device_id=core,
            device_id_type=MESH,
        ).wait_recv()
    wire.drain()


def forward(tok, w_qkv, vec, w_out, w_fc1, w_fc2, ids, lanes, heads):
    span, width = tok.shape
    group = NX * NC
    rows = w_qkv.shape[0]
    part = width // group
    triple = 3 * part
    f1_shape = (NC, rows, w_fc1.shape[1] // NC)
    length = span * group
    dps = NZ * NY
    lane = vec.shape[2]
    out = (
        (HBM, (length, width), BF),
        (VM, (length, part), BF),
        (VM, (length, part), BF),
        (VM, (length, part), BF),
        (VM, (part, length), F32),
        (VM, (8, length), F32),
        (VM, (span, width), BF),
        (VM, (dps, group, rows, triple), BF),
        (VM, (16, dps * lane), BF),
        (VM, (16, dps * group * lane), BF),
        (HBM, (NZ, NY, NX, NC) + w_out.shape, BF),
        (HBM, (NZ, NY, NX, NC * rows, f1_shape[2]), BF),
        (HBM, (NZ, NY, NX) + w_fc2.shape, BF),
    )
    return pl.pallas_call(
        functools.partial(forward_kernel, heads),
        out_shape=tuple(jax.ShapeDtypeStruct(shape, dtype) for _, shape, dtype in out),
        in_specs=[VM] * 8,
        out_specs=[spec for spec, _, _ in out],
        scratch_shapes=[
            pltpu.VMEM((group, span, width), BF),
            pltpu.VMEM((2, span, width), BF),
            pltpu.VMEM((group,) + vec.shape, BF),
            pltpu.VMEM((heads, length, part), BF),
            pltpu.VMEM((part, length), BF),
            pltpu.VMEM((length, 8), jnp.int32),
            pltpu.VMEM((span, span), F32),
            pltpu.VMEM((8, span), F32),
            pltpu.VMEM((8, span), F32),
            pltpu.VMEM((part, span), F32),
            pltpu.VMEM((group, span, part), BF),
            pltpu.VMEM((group, rows, triple), BF),
            pltpu.VMEM(w_out.shape, BF),
            pltpu.VMEM(f1_shape, BF),
            pltpu.VMEM(w_fc2.shape, BF),
            pltpu.SemaphoreType.DMA((COPIES,)),
            pltpu.SemaphoreType.DMA((COPIES,)),
            pltpu.SemaphoreType.DMA((12,)),
        ],
        compiler_params=pltpu.CompilerParams(
            collective_id=1, has_side_effects=True, vmem_limit_bytes=56 * 1024 * 1024
        ),
        name="forward_row",
    )(tok, w_qkv, vec, w_out, w_fc1, w_fc2, ids.reshape(1, length), lanes)


def lead_loop(total, fn, step=16):
    lead, rows = total.shape[:-2], total.shape[-2]
    per = rows // step

    def body(n, _):
        block = n // per
        at = []
        for dim in reversed(lead):
            at.append(block % dim)
            block = block // dim
        fn(tuple(reversed(at)) + (pl.ds(pl.multiple_of((n % per) * step, step), step), slice(None)))
        return 0

    lax.fori_loop(0, math.prod(lead) * per, body, 0)


def add_into(total, term):
    def fn(idx):
        total[idx] = (total[idx].astype(F32) + term[idx].astype(F32)).astype(total.dtype)

    lead_loop(total, fn, 16 if total.dtype == BF else 8)


def reduce_plane(wire, place, grad, own, got, got2, got3, out, local, swap=False):
    z, y, x = place.z, place.y, place.x
    first = place.at(x=1 - x) if swap else place.at(y=1 - y)
    order = [place.zup(k) for k in (1, 2, 3, 0)]

    def two(zk, mine):
        if swap:
            return grad.at[zk, :, x if mine else 1 - x]
        return grad.at[zk, y if mine else 1 - y]

    sends = [wire.copy(two(zk, False), got.at[k], first) for k, zk in enumerate(order)]
    loads = [pltpu.make_async_copy(two(zk, True), own.at[k], local.at[k]) for k, zk in enumerate(order)]
    rest = reduce_tail(wire, place, own, got2, got3, out, swap)
    next(rest)
    yield
    for copy in sends:
        copy.go()
    for desc in loads:
        desc.start()
    yield
    for k in range(NZ):
        loads[k].wait()
        sends[k].wait_recv()
        add_into(own.at[k], got.at[k])
        next(rest)
        yield
    yield from rest


def reduce_head(wire, place, grad, got, got2, swap=False):
    y, x = place.y, place.x
    first = place.at(x=1 - x) if swap else place.at(y=1 - y)
    second = place.at(y=1 - y) if swap else place.at(x=1 - x)
    keep, give = (y, 1 - y) if swap else (x, 1 - x)
    order = [place.zup(k) for k in (1, 2, 3, 0)]
    mine = [grad.at[zk, :, x] if swap else grad.at[zk, y] for zk in order]
    others = [grad.at[zk, :, 1 - x] if swap else grad.at[zk, 1 - y] for zk in order]
    keeps = [grad.at[zk, keep, x] if swap else grad.at[zk, y, keep] for zk in order]
    gives = [grad.at[zk, give, x] if swap else grad.at[zk, y, give] for zk in order]
    sends = [wire.copy(others[k], got.at[k], first) for k in range(NZ)]
    seconds = [wire.copy(gives[k], got2.at[k], second) for k in range(NZ)]
    yield
    for copy in sends:
        copy.go()
    yield
    for k in range(NZ):
        sends[k].wait_recv()
        add_into(mine[k], got.at[k])
        seconds[k].go()
        yield
    for k in range(NZ):
        seconds[k].wait_recv()
        add_into(keeps[k], got2.at[k])
        yield


def reduce_line(wire, place, own, got, out):
    along = [wire.copy(own.at[k], got.at[k], place.at(z=place.zup(k + 1))) for k in range(NZ - 1)]
    yield
    for copy in along:
        copy.go()
    yield
    for copy in along:
        copy.wait_recv()
    add_up(out, own.at[NZ - 1], got)


def reduce_tail(wire, place, own, got2, got3, out, swap=False):
    y, x = place.y, place.x
    second = place.at(y=1 - y) if swap else place.at(x=1 - x)
    keep, give = (y, 1 - y) if swap else (x, 1 - x)
    keeps = [own.at[k, keep] for k in range(NZ)]
    seconds = [wire.copy(own.at[k, give], got2.at[k], second) for k in range(NZ)]
    along = [wire.copy(keeps[k], got3.at[k], place.at(z=place.zup(k + 1))) for k in range(NZ - 1)]
    yield
    for copy in seconds:
        copy.go()
        yield
    for k in range(NZ):
        seconds[k].wait_recv()
        add_into(keeps[k], got2.at[k])
        if k < NZ - 1:
            along[k].go()
        yield
    for copy in along:
        copy.wait_recv()
    add_up(out, keeps[NZ - 1], got3)


def plane_scratch(block):
    return [
        pltpu.VMEM((NZ, 2) + block, BF),
        pltpu.VMEM((NZ, 2) + block, BF),
        pltpu.VMEM((NZ,) + block, BF),
        pltpu.VMEM((NZ - 1,) + block, BF),
        pltpu.SemaphoreType.DMA((NZ,)),
    ]


def reduce_outer(wire, place, go, outp, outg, load, scratch, out):
    c = place.c
    swap_o = wire.copy(go.at[:, :, :, 1 - c], outg, place.at(c=1 - c))
    load_o = pltpu.make_async_copy(go.at[:, :, :, c], outp, load)
    rest = reduce_plane(wire, place, outp, *scratch[:4], out, scratch[4])
    next(rest)
    yield
    swap_o.go()
    load_o.start()
    yield
    load_o.wait()
    swap_o.wait_recv()
    add_into(outp, outg)
    yield from rest


def reduce_first(wire, place, half, g1, buf, got, scratch, out, swap=False):
    c = place.c
    rows = got.shape[0]
    size = buf.shape[1] // 2
    cols = pl.ds(half * size, size)
    mine, theirs = buf.at[:, cols], got.at[:, cols]
    part = wire.copy(mine.at[pl.ds((1 - c) * rows, rows)], theirs, place.at(c=1 - c))
    yield from reduce_plane(
        wire, place, g1.at[:, :, :, :, cols], *scratch[:4], mine, scratch[4], swap=swap
    )
    part.go()
    lane = out.shape[1] // (NZ * NY * NX * NC)
    spread_columns(out, buf, pl.multiple_of(c * rows, rows), c, lane, half)
    yield
    part.wait_recv()
    spread_columns(out, got, 0, 1 - c, lane, half)


def spread_columns(out, src, row, c, lane, half):
    rows = out.shape[0]
    chips = NZ * NY * NX // 2
    for n in range(half * chips, (half + 1) * chips):
        at = pl.ds(pl.multiple_of((n * NC + c) * lane, lane), lane)
        out[:, at] = src[pl.ds(row, rows), n * lane : (n + 1) * lane]


def send_rows(wire, place, total, buf, cols, local):
    s = place.seq
    near = ((place.at(c=1 - place.c), 1), (place.at(x=1 - place.x), 2), (place.at(x=1 - place.x, c=1 - place.c), 3))
    parts = [wire.copy(total.at[s ^ m, :, cols], buf.at[s, :, cols], dev) for dev, m in near]
    mine = pltpu.make_async_copy(total.at[s, :, cols], buf.at[s, :, cols], local)
    return parts, mine


def place_rows(out, buf, first, count):
    group, part = buf.shape[0], buf.shape[2] // 3
    step = 128
    for j in range(group):
        for m in range(first // step, (first + count) // step):
            n, rest = m * step // part, m * step % part
            at = (n * group + j) * part + rest
            out[:, at : at + step] = buf[j, :, m * step : (m + 1) * step].astype(F32)


def reduce_quarter(wire, place, gq, own, got, got2, total, buf, out, local):
    y = place.y
    size = total.shape[2] // 2
    cols = pl.ds(0, size)
    order = [place.zup(n) for n in (1, 2, 3, 0)]
    sends = [wire.copy(gq.at[zk, 1 - y, :, :, cols], got.at[n], place.at(y=1 - y)) for n, zk in enumerate(order)]
    along = [wire.copy(own.at[n], got2.at[n], place.at(z=place.zup(n + 1))) for n in range(NZ - 1)]
    loads = [pltpu.make_async_copy(gq.at[zk, y, :, :, cols], own.at[n], local.at[n]) for n, zk in enumerate(order)]
    parts, mine = send_rows(wire, place, total, buf, cols, local.at[NZ])
    yield
    for copy in sends:
        copy.go()
    for desc in loads:
        desc.start()
    yield
    for n in range(NZ):
        loads[n].wait()
        sends[n].wait_recv()
        add_into(own.at[n], got.at[n])
        if n < NZ - 1:
            along[n].go()
        yield
    for copy in along:
        copy.wait_recv()
    add_up(total.at[:, :, cols], own.at[NZ - 1], got2)
    for copy in parts:
        copy.go()
    mine.start()
    yield
    mine.wait()
    for copy in parts:
        copy.wait_recv()
    place_rows(out, buf, 0, size)


def reduce_quarter_zy(wire, place, gq, got, give, gave, total, buf, out, local):
    z, y = place.z, place.y
    size = total.shape[2] // 2
    cols = pl.ds(size, size)
    along = [
        wire.copy(gq.at[place.zup(n), :, :, :, cols], got.at[n - 1], place.at(z=place.zup(n))) for n in range(1, NZ)
    ]
    other = wire.copy(give, gave, place.at(y=1 - y))
    parts, mine = send_rows(wire, place, total, buf, cols, local)
    yield
    for copy in along:
        copy.go()
    yield
    for copy in along:
        copy.wait_recv()
    add_up(give, gq.at[z, 1 - y, :, :, cols], got.at[:, 1 - y])
    other.go()
    add_up(total.at[:, :, cols], gq.at[z, y, :, :, cols], got.at[:, y])
    yield
    other.wait_recv()
    add_into(total.at[:, :, cols], gave)
    for copy in parts:
        copy.go()
    mine.start()
    yield
    mine.wait()
    for copy in parts:
        copy.wait_recv()
    place_rows(out, buf, size, size)


def reduce_vectors(wire, place, pairs):
    z, y = place.z, place.y
    sizes = [g.shape[1] // (NZ * NY) for g, *_ in pairs]

    def cols(n, zk, yk):
        return pl.ds(pl.multiple_of((zk * NY + yk) * sizes[n], sizes[n]), sizes[n])

    cs = [wire.copy(g, t.at[0], place.at(c=1 - place.c)) for g, t, *_ in pairs]
    xs = [wire.copy(g, t.at[1], place.at(x=1 - place.x)) for g, t, *_ in pairs]
    ys, zs = [], []
    for n, (g, t, got, _) in enumerate(pairs):
        for zk in range(NZ):
            at = cols(n, zk, 1 - y)
            ys.append(wire.copy(g.at[:, at], t.at[2, :, at], place.at(y=1 - y)))
        for k in range(1, NZ):
            at = cols(n, place.zup(k), y)
            zs.append(wire.copy(g.at[:, at], got.at[z], place.at(z=place.zup(k))))
    yield
    for copy in cs:
        copy.go()
    yield
    for copies, slot in ((cs, 0), (xs, 1)):
        for copy, (g, t, *_) in zip(copies, pairs):
            copy.wait_recv()
            copy.wait_send()
            add_rows(g, t.at[slot])
        for copy in xs if slot == 0 else ys:
            copy.go()
        yield
    for copy in ys:
        copy.wait_recv()
    for n, (g, t, got, _) in enumerate(pairs):
        for zk in range(NZ):
            at = cols(n, zk, y)
            add_rows(g.at[:, at], t.at[2, :, at])
    for copy in zs:
        copy.go()
    for n, (g, t, got, _) in enumerate(pairs):
        keep_rows(got.at[z], g.at[:, cols(n, z, y)])
    yield
    for copy in zs:
        copy.wait_recv()
    for g, t, got, out in pairs:
        add_fixed(out, got)


def add_rows(total, term):
    total[...] += term[...]


def keep_rows(dst, src):
    dst[...] = src[...]


def add_fixed(out, got):
    total = got[0]
    for k in range(1, NZ):
        total = total + got[k]
    out[...] = total


def add_up(out, own, got):
    def fn(idx):
        value = own[idx].astype(F32)
        for k in range(NZ - 1):
            value = value + got[(k,) + idx].astype(F32)
        out[idx] = value.astype(out.dtype)

    lead_loop(out, fn)


BACKWARD = (
    "431",
    "",
    "",
    "41",
    "",
    "421o",
    "413o",
    "41",
    "411",
    "44211o",
    "o",
    "4ooo",
    "rqo",
    "v4",
    "v4qq1qooq1",
    "wwvwrvwrqorqvw",
)


def backward_kernel(heads, *refs):
    q, k, v, att, lse, do, idr, wq, grad_hidden, rows_in, wide_in, gain = refs[:12]
    tok, act, g1, go, in2, in3 = refs[12:18]
    grad_tok, out1, out2, outo, outq, outr, outw = refs[18:25]
    (km, vm, qm, dm, kt, idc, bias, acck, accv, accq, accw, delta, blk, actb) = refs[25:39]
    (dap, dgot, dfin, ownq, gotq, gotqb, sumq, outq_buf, gq, gotp, f1buf, f1got) = refs[39:51]
    (rowg, rowt, rowz, wideg, widet, widez, outp, outg) = refs[51:59]
    plane1, plane4, planeo = refs[59:64], refs[64:69], refs[69:74]
    own2, own3, half2, half3, zgot, zgive, zgave = refs[74:81]
    lateg, latet, latez, latesum = refs[81:85]
    send, recv, local, dsend, drecv = refs[85:]
    place = Place()
    z, y, x, c, s, dp = place.z, place.y, place.x, place.c, place.seq, place.dp
    group = NX * NC
    wire = Wire(place, send, recv)
    core, other, across = place.at(c=1 - c), place.at(x=1 - x), place.at(x=1 - x, c=1 - c)
    length, part = q.shape
    span, width = tok.shape
    head = part // heads
    blocks = length // span
    shift = pl.multiple_of(s * part, part)

    greet(place)
    load2 = pltpu.make_async_copy(in2, own2, local.at[0])
    load3 = pltpu.make_async_copy(in3, own3, local.at[1])
    load2.start()
    load3.start()
    per = in2.shape[1]
    load2.wait()
    load3.wait()
    plan = Plan(
        {
            "1": reduce_first(wire, place, 0, g1, f1buf, f1got, plane1, out1),
            "4": reduce_first(wire, place, 1, g1, f1buf, f1got, plane4, out1, swap=True),
            "o": reduce_outer(wire, place, go, outp, outg, local.at[12], planeo, outo),
            "2": reduce_line(wire, place, own2, half2, out2.at[pl.ds(0, per)]),
            "3": reduce_line(wire, place, own3, half3, out2.at[pl.ds(per, per)]),
            "q": reduce_quarter(wire, place, gq, ownq, gotq, gotqb, sumq, outq_buf, outq, local.at[pl.ds(6, NZ + 1)]),
            "r": reduce_quarter_zy(wire, place, gq, zgot, zgive, zgave, sumq, outq_buf, outq, local.at[13]),
            "v": reduce_vectors(wire, place, ((rowg, rowt, rowz, outr), (wideg, widet, widez, outw))),
            "w": reduce_vectors(wire, place, ((lateg, latet, latez, latesum),)),
        },
        BACKWARD,
    )
    plan.hook()

    mask_heads(qm, q, heads, head)
    accq[...] = jnp.zeros(accq.shape, F32)
    accw[...] = jnp.zeros(accw.shape, F32)
    delta[...] = jnp.zeros(delta.shape, F32)
    plan.hook()
    mask_heads(dm, do, heads, head)
    for b in range(blocks):
        at = slice(b * span, (b + 1) * span)
        weighted = do[at, :].T.astype(F32) * att[:, at]
        for h in range(heads):
            delta[h : h + 1, at] = jnp.sum(weighted[h * head : (h + 1) * head, :], 0, keepdims=True)

    hops = []
    for t in range(blocks):
        tx, tc = t // NC, t % NC
        inner = pltpu.make_async_remote_copy(
            src_ref=dap.at[t],
            dst_ref=dgot.at[tx],
            send_sem=dsend.at[2 * t],
            recv_sem=drecv.at[2 * t],
            device_id=core,
            device_id_type=MESH,
        )
        outerc = pltpu.make_async_remote_copy(
            src_ref=dap.at[t],
            dst_ref=dfin,
            send_sem=dsend.at[2 * t + 1],
            recv_sem=drecv.at[2 * t + 1],
            device_id=other,
            device_id_type=MESH,
        )
        hops.append((tx, tc, inner, outerc))

    def meet(t):
        tx, tc, inner, outerc = hops[t]

        @pl.when(c == tc)
        def _():
            inner.wait_recv()
            add_into(dap.at[t], dgot.at[tx])

            @pl.when(x != tx)
            def _():
                outerc.start()

    fetch = [
        pltpu.make_async_copy(act.at[pl.ds(b * span, span)], actb.at[b % 2], local.at[2 + b]) for b in range(blocks)
    ]
    fetch[0].start()

    for kb in range(blocks):
        ks = slice(kb * span, (kb + 1) * span)
        if kb + 1 < blocks:
            fetch[kb + 1].start()
        mask_heads(km, k.at[ks], heads, head)
        mask_heads(vm, v.at[ks], heads, head)
        kt[...] = k[ks, :].T
        idc[...] = jnp.broadcast_to(idr[:, ks], (8, span)).T
        acck[...] = jnp.zeros(acck.shape, F32)
        accv[...] = jnp.zeros(accv.shape, F32)

        def queries(qb, _, kb=kb, ks=ks):
            qs = pl.ds(pl.multiple_of(qb * span, span), span)
            bias[...] = pair_bias(idr, idc[:, 0:1], qb, kb, span)
            for h in range(heads):
                scores = nt(km[h], q[qs, :]) + bias[...]
                probs = jnp.exp(scores - lse[h : h + 1, qs])
                grad = nt(vm[h], do[qs, :])
                ds = (probs * (grad - delta[h : h + 1, qs])).astype(BF)
                accv[...] += nn(probs.astype(BF), dm[h, qs, :])
                acck[...] += nn(ds, qm[h, qs, :])
                hs = slice(h * head, (h + 1) * head)
                accq[hs, qs] += nn(kt[hs, :], ds)
            for n in range(kb, blocks):

                @pl.when(qb == n)
                def _():
                    if n == blocks - 1 and kb > 0:
                        meet(kb - 1)
                    plan.hook()

            return 0

        lax.fori_loop(kb, blocks, queries, 0)
        blk[:, :part] = (accq[:, ks].T * (head**-0.5)).astype(BF)
        blk[:, part : 2 * part] = acck[...].astype(BF)
        blk[:, 2 * part :] = accv[...].astype(BF)
        sums = jnp.sum(blk[...].astype(F32), 0, keepdims=True)
        if kb == 0:
            gotp[...] = jnp.zeros(gotp.shape, F32)
        gotp[0:1, :] += sums
        fetch[kb].wait()
        step = 256
        for n in range(0, width, step):
            accw[n : n + step, :] += lax.dot_general(
                actb[kb % 2, :, n : n + step], blk[...], (((0,), (0,)), ((), ())), preferred_element_type=F32
            )
        if kb == blocks - 1:
            gq[...] = accw[...].astype(BF).reshape(gq.shape)
            plan.hook()
        weights = wq[...].reshape(width, 3 * part)
        for n in range(0, width, step):
            dap[kb, :, n : n + step] = nt(blk[...], weights[n : n + step, :]).astype(BF)
        tx, tc, inner, outerc = hops[kb]

        @pl.when(c != tc)
        def _():
            inner.start()

    fetch_tok = pltpu.make_async_copy(tok, actb.at[0], local.at[11])
    fetch_tok.start()
    rowg[...] = rows_in[...]
    wideg[...] = wide_in[...]
    lane_sum = jnp.sum(delta[...], 1, keepdims=True)
    for j in range(group):
        rowg[16 + j * heads : 16 + (j + 1) * heads, :] = jnp.where(
            s == j, jnp.broadcast_to(lane_sum[:heads], (heads, width)), 0.0
        )
    rowg[2:3, pl.ds(shift, part)] = gotp[0:1, :part]
    rowg[3:4, pl.ds(shift, part)] = gotp[0:1, 2 * part :]
    plan.hook()
    meet(blocks - 1)
    plan.hook()

    step = 64
    for t in range(blocks):
        tx, tc, inner, outerc = hops[t]

        @pl.when((x == tx) & (c == tc))
        def _():
            outerc.wait_recv()

    fetch_tok.wait()

    def finish(n, carry):
        at = pl.ds(pl.multiple_of(n * step, step), step)
        da = dap[s, at, :].astype(F32) + dfin[at, :].astype(F32)
        normed, inv = normalize(actb[0, at, :].astype(F32))
        grad = norm_back(da * gain[0:1, :].astype(F32), normed, inv) + grad_hidden[at, :]
        grad_tok[at, :] = grad.astype(BF)
        return (
            carry[0] + jnp.sum(da * normed, 0, keepdims=True),
            carry[1] + jnp.sum(da, 0, keepdims=True),
        )

    zero = jnp.zeros((1, width), F32)
    gain_one, shift_one = lax.fori_loop(0, span // step, finish, (zero, zero))
    lateg[...] = jnp.zeros(lateg.shape, F32)
    lateg[0:1, :] = gain_one
    lateg[1:2, :] = shift_one

    plan.finish()
    outr[0:2, :] = latesum[0:2, :]
    for t in range(blocks):
        tx, tc, inner, outerc = hops[t]

        @pl.when(c != tc)
        def _():
            inner.wait_send()

        @pl.when((c == tc) & (x != tx))
        def _():
            outerc.wait_send()

    wire.drain()


def backward(do, q, k, v, att, lse, ids, wq, tok, grad_hidden, rows_in, wide_in, gain, act, g1, go, in2, in3, heads):
    length, part = q.shape
    span, width = tok.shape
    group = length // span
    b1, bo = g1.shape[3:], go.shape[4:]
    rows, triple = wq.shape[2:]
    bq = (group, rows, triple)
    bh = (group, rows, triple // 2)
    dps = NZ * NY
    out = (
        (VM, (span, width), BF),
        (VM, (b1[0] // NC, NC * b1[1]), F32),
        (VM, (2 * in2.shape[1], width), F32),
        (VM, bo, F32),
        (VM, (rows, group * triple), F32),
        (VM, (rows_in.shape[0], width // dps), F32),
        (VM, (wide_in.shape[0], wide_in.shape[1] // dps), F32),
    )
    scratch = [
        pltpu.VMEM((heads, span, part), BF),
        pltpu.VMEM((heads, span, part), BF),
        pltpu.VMEM((heads, length, part), BF),
        pltpu.VMEM((heads, length, part), BF),
        pltpu.VMEM((part, span), BF),
        pltpu.VMEM((span, 8), jnp.int32),
        pltpu.VMEM((span, span), F32),
        pltpu.VMEM((span, part), F32),
        pltpu.VMEM((span, part), F32),
        pltpu.VMEM((part, length), F32),
        pltpu.VMEM((width, triple), F32),
        pltpu.VMEM((8, length), F32),
        pltpu.VMEM((span, triple), BF),
        pltpu.VMEM((2, span, width), BF),
        pltpu.VMEM((group, span, width), BF),
        pltpu.VMEM((NX, span, width), BF),
        pltpu.VMEM((span, width), BF),
        pltpu.VMEM((NZ,) + bh, BF),
        pltpu.VMEM((NZ,) + bh, BF),
        pltpu.VMEM((NZ - 1,) + bh, BF),
        pltpu.VMEM(bq, BF),
        pltpu.VMEM(bq, BF),
        pltpu.VMEM((NZ, NY) + bq, BF),
        pltpu.VMEM((8, triple), F32),
        pltpu.VMEM(b1, F32),
        pltpu.VMEM((b1[0] // NC, b1[1]), F32),
        pltpu.VMEM(rows_in.shape, F32),
        pltpu.VMEM((3,) + rows_in.shape, F32),
        pltpu.VMEM((NZ, rows_in.shape[0], width // dps), F32),
        pltpu.VMEM(wide_in.shape, F32),
        pltpu.VMEM((3,) + wide_in.shape, F32),
        pltpu.VMEM((NZ, wide_in.shape[0], wide_in.shape[1] // dps), F32),
        pltpu.VMEM((NZ, NY, NX) + bo, BF),
        pltpu.VMEM((NZ, NY, NX) + bo, BF),
    ]
    scratch += plane_scratch((b1[0], b1[1] // 2)) * 2 + plane_scratch(bo)
    scratch += [pltpu.VMEM(in2.shape, BF)] * 2 + plane_scratch(in2.shape[1:])[3:4] * 2
    scratch += [pltpu.VMEM((NZ - 1, NY) + bh, BF), pltpu.VMEM(bh, BF), pltpu.VMEM(bh, BF)]
    scratch += [
        pltpu.VMEM((8, width), F32),
        pltpu.VMEM((3, 8, width), F32),
        pltpu.VMEM((NZ, 8, width // dps), F32),
        pltpu.VMEM((8, width // dps), F32),
    ]
    scratch += [
        pltpu.SemaphoreType.DMA((COPIES,)),
        pltpu.SemaphoreType.DMA((COPIES,)),
        pltpu.SemaphoreType.DMA((14,)),
        pltpu.SemaphoreType.DMA((2 * group,)),
        pltpu.SemaphoreType.DMA((2 * group,)),
    ]
    return pl.pallas_call(
        functools.partial(backward_kernel, heads),
        out_shape=tuple(jax.ShapeDtypeStruct(shape, dtype) for _, shape, dtype in out),
        in_specs=[VM] * 12 + [HBM] * 6,
        out_specs=[spec for spec, _, _ in out],
        scratch_shapes=scratch,
        compiler_params=pltpu.CompilerParams(
            collective_id=2, has_side_effects=True, vmem_limit_bytes=63 * 1024 * 1024
        ),
        name="backward_row",
    )(
        q, k, v, att, lse, do, ids.reshape(1, length), wq, grad_hidden, rows_in, wide_in, gain,
        tok, act, g1, go, in2, in3,
    )


MIDDLE = (
    "ce",
    "",
    "",
    "",
    "",
    "23ce",
    "",
    "23",
    "23",
    "",
    "23",
    "2233",
    "2233",
    "2233",
    "",
    "",
)


def middle_tasks(wire, place, f2, f2v, g2, got2, got2b, got3, got3b):
    half = g2.shape[3] // 2
    one, two = pl.ds(0, half), pl.ds(half, half)
    return {
        "c": spread_last(wire, place, f2.at[:, :, :, one], f2v.at[:, :, :, one]),
        "e": spread_last(wire, place, f2.at[:, :, :, two], f2v.at[:, :, :, two], swap=True),
        "2": reduce_head(wire, place, g2.at[:, :, :, one], got2, got2b, swap=True),
        "3": reduce_head(wire, place, g2.at[:, :, :, two], got3, got3b),
    }


def tn(a, b):
    return lax.dot_general(a, b, (((0,), (0,)), ((), ())), preferred_element_type=F32)


def fold(value, rows=16):
    total = value[:rows]
    for n in range(1, value.shape[0] // rows):
        total = total + value[n * rows : (n + 1) * rows]
    return total


def lanes_of(value):
    total = value[:, :128]
    for n in range(1, value.shape[1] // 128):
        total = total + value[:, n * 128 : (n + 1) * 128]
    return total


def row_steps(count, step, fn):
    def body(n, _):
        fn(pl.ds(pl.multiple_of(n * step, step), step))
        return 0

    lax.fori_loop(0, count // step, body, 0)


def ffn_kernel(*refs):
    own, rows_all, wide_all, lanes = refs[:4]
    tok, cot, f2, wo, f1 = refs[4:9]
    out, do, gh, g1, go, half2, half3, rows_g, wide_g = refs[9:18]
    wov, f1v, f2v, dt, act, buf, slope, mix, dm, br, hid, g2, dbuf, prb, prc, stg, wv = refs[18:35]
    stat, stat_got, back, back_got, sums, colsums = refs[35:41]
    gots = refs[41:45]
    send, recv, local = refs[45:48]
    lane_mean, lane_square = dm.at[:, pl.ds(0, 128)], dm.at[:, pl.ds(128, 128)]
    place = Place()
    z, y, x, c, s = place.z, place.y, place.x, place.c, place.seq
    wire = Wire(place, send, recv)
    core = place.at(c=1 - c)
    span, width = own.shape
    units = f1v.shape[4]
    group = NX * NC
    tile = 512
    tiles = units // tile
    total_units = units * NC

    half = f2.shape[3] // 2
    one, two = pl.ds(0, half), pl.ds(half, half)
    loads = [
        pltpu.make_async_copy(wo, wov, local.at[0]),
        pltpu.make_async_copy(f2.at[:, y, :, one], f2v.at[:, y, :, one], local.at[1]),
        pltpu.make_async_copy(cot, dt.at[c], local.at[2]),
        pltpu.make_async_copy(f1, f1v, local.at[3]),
        pltpu.make_async_copy(f2.at[:, :, x, two], f2v.at[:, :, x, two], local.at[4]),
        pltpu.make_async_copy(tok, prc, local.at[5]),
    ]
    for desc in loads:
        desc.start()
    chunk = span // 4
    chunks = [pl.ds(n * chunk, chunk) for n in range(4)]
    dt_copy = wire.copy(cot, dt.at[c], core)
    act_copies = [wire.copy(act.at[c, at], act.at[c, at], core) for at in chunks]
    stat_copies = [wire.copy(stat.at[h], stat_got.at[h], core) for h in range(NC)]
    back_copies = [wire.copy(back.at[h], back_got.at[h], core) for h in range(NC)]
    out_copy = wire.copy(dbuf, prb, core)
    da_copy = wire.copy(prb, prc, core)
    mine_at = pl.ds(pl.multiple_of(s * span, span), span)
    part_size = width // group

    def give(j):
        return prb.at[:, pl.ds(pl.multiple_of(j * part_size, part_size), part_size)]

    outgoing = [
        wire.copy(give(s ^ m), do.at[mine_at], dev)
        for dev, m in ((core, 1), (place.at(x=1 - x), 2), (place.at(x=1 - x, c=1 - c), 3))
    ]
    greet(place)
    dt_copy.go()
    plan = Plan(middle_tasks(wire, place, f2, f2v, g2, *gots), MIDDLE)
    plan.hook()

    def row(ref, n):
        return ref[n : n + 1, :].astype(F32)

    lane = wide_all.shape[1] // (NZ * NY * NX * NC)
    for n in range(NZ * NY * NX):
        at = pl.ds(pl.multiple_of((n * NC + c) * lane, lane), lane)
        wv[0:3, n * lane : (n + 1) * lane] = wide_all[0:3, at].astype(F32)
    colsums[...] = jnp.zeros(colsums.shape, F32)
    sums[...] = jnp.zeros(sums.shape, F32)
    loads[0].wait()
    loads[5].wait()

    for at, copy in zip(chunks, act_copies):
        branch = nn(own[at, :], wov[...].reshape(width, width)) + row(rows_all, 4)
        br[at, :] = branch

        def fn(inner, at=at):
            rows = pl.ds(at.start + inner.start, inner.size)
            hidden = prc[rows, :].astype(F32) + normalize(br[rows, :])[0] * row(rows_all, 5) + row(rows_all, 6)
            hid[rows, :] = hidden
            act[c, rows, :] = (normalize(hidden)[0] * row(rows_all, 7) + row(rows_all, 8)).astype(BF)

        row_steps(chunk, 64, fn)
        copy.go()
    plan.hook()
    loads[3].wait()

    for h in range(NC):

        @pl.when(c != h)
        def _():
            for copy in act_copies:
                copy.wait_recv()

        for n in range(tiles):
            cols = slice(n * tile, (n + 1) * tile)
            weights = f1v[:, :, :, :, cols].reshape(width, tile)
            buf[h, :, cols] = nn(act[h], weights) + wv[0:1, cols]

        def fn(at, h=h):
            count = units // 128
            pivot = None
            for n in range(tiles):
                cols = slice(n * tile, (n + 1) * tile)
                u = buf[h, at, cols]
                cdf = 0.5 + 0.5 * lax.erf(u * math.sqrt(0.5))
                value = u * cdf
                buf[h, at, cols] = value
                pdf = jnp.exp(-0.5 * u * u) * (1.0 / math.sqrt(2.0 * math.pi))
                slope[h, at, cols] = (cdf + u * pdf).astype(BF)
                if pivot is None:
                    pivot = value[:, :128]
                    total, square = jnp.zeros_like(pivot), jnp.zeros_like(pivot)
                for j in range(tile // 128):
                    gap = value[:, j * 128 : (j + 1) * 128] - pivot
                    total = total + gap
                    square = square + gap * gap
            shift = total * (1.0 / count)
            lane_mean[at, :] = pivot + shift
            lane_square[at, :] = square - total * shift

        row_steps(span, 32, fn)

        def fn(at, h=h):
            count = units // 128
            means = lane_mean[at, :]
            mean = jnp.mean(means, 1, keepdims=True)
            gap = means - mean
            square = jnp.sum(lane_square[at, :] + count * (gap * gap), 1, keepdims=True)
            column = lax.broadcasted_iota(jnp.int32, (at.size, 128), 1)
            stat[h, at, :] = jnp.where(column == 0, mean, square)

        row_steps(span, 128, fn)
        stat_copies[h].go()
        plan.hook()

    for h in range(NC):
        stat_copies[h].wait_recv()
        stat_copies[h].wait_send()

        def fn(at, h=h):
            mean_a, mean_b = stat[h, at, 0:1], stat_got[h, at, 0:1]
            gap = mean_a - mean_b
            square = stat[h, at, 1:2] + stat_got[h, at, 1:2] + gap * gap * (0.5 * units)
            mean = 0.5 * (mean_a + mean_b)
            inv = lax.rsqrt(square * (1.0 / total_units) + EPSILON)
            stat[h, at, :] = jnp.broadcast_to(inv, (at.size, 128))
            for n in range(tiles):
                cols = slice(n * tile, (n + 1) * tile)
                normed = (buf[h, at, cols] - mean) * inv
                buf[h, at, cols] = normed
                mix[h, at, cols] = (normed * wv[1:2, cols] + wv[2:3, cols]).astype(BF)

        row_steps(span, 64, fn)
    plan.hook()

    loads[2].wait()
    loads[1].wait()
    loads[4].wait()
    dt_copy.wait_recv()
    per = g2.shape[3]
    for n in range(units // (2 * per)):
        cols = slice(n * 2 * per, (n + 1) * 2 * per)
        part = tn(mix[0, :, cols], dt[0]) + tn(mix[1, :, cols], dt[1])
        g2[n // NY, n % NY] = part.astype(BF).reshape(NX, per, width)
    plan.hook()

    weights2 = f2v[...].reshape(units, width)
    for n in range(0, width, tile):
        dbuf[:, n : n + tile] = nn(mix[1 - c], weights2[:, n : n + tile]).astype(BF)
    out_copy.go()
    for n in range(0, width, tile):
        cols = slice(n, n + tile)
        gh[:, cols] = nn(mix[c], weights2[:, cols]) + hid[:, cols] + rows_all[9:10, cols].astype(F32)
    plan.hook()

    for h in range(NC):
        for n in range(tiles):
            cols = slice(n * tile, (n + 1) * tile)
            dm[:, cols] = nt(dt[h], weights2[cols, :])

        def fn(at, h=h):
            first = jnp.zeros((at.size, 128), F32)
            second = jnp.zeros((at.size, 128), F32)
            for n in range(tiles):
                cols = slice(n * tile, (n + 1) * tile)
                grad = dm[at, cols]
                product = grad * buf[h, at, cols]
                colsums[1, :, cols] += fold(product)
                colsums[2, :, cols] += fold(grad)
                first = first + lanes_of(grad * wv[1:2, cols])
                second = second + lanes_of(product * wv[1:2, cols])
            column = lax.broadcasted_iota(jnp.int32, (at.size, 128), 1)
            first = jnp.sum(first, 1, keepdims=True)
            second = jnp.sum(second, 1, keepdims=True)
            back[h, at, :] = jnp.where(column == 0, first, second)

        row_steps(span, 64, fn)
        back_copies[h].go()
        plan.hook()
        back_copies[h].wait_recv()

        def fn(at, h=h):
            scale = 1.0 / total_units
            first = (back[h, at, 0:1] + back_got[h, at, 0:1]) * scale
            second = (back[h, at, 1:2] + back_got[h, at, 1:2]) * scale
            inv = stat[h, at, 0:1]
            for n in range(tiles):
                cols = slice(n * tile, (n + 1) * tile)
                grad = inv * (dm[at, cols] * wv[1:2, cols] - first - buf[h, at, cols] * second)
                inner = (grad * slope[h, at, cols].astype(F32)).astype(BF)
                mix[h, at, cols] = inner
                colsums[0, :, cols] += fold(inner.astype(F32))

        row_steps(span, 64, fn)
        plan.hook()

    weights1 = f1v[...].reshape(width, units)
    out_copy.wait_recv()
    out[...] = (gh[...] + prb[...].astype(F32)).astype(BF)
    for n in range(0, width, tile):
        prb[:, n : n + tile] = nt(mix[1 - c], weights1[n : n + tile, :]).astype(BF)
    da_copy.go()
    for n in range(0, width, tile):
        gh[:, n : n + tile] = nt(mix[c], weights1[n : n + tile, :])
    plan.hook()
    size = stg.shape[1]
    writes = []

    def write(part, dst, wide):
        n = len(writes)
        if n >= 2:
            writes[n - 2].wait()
        stg[n % 2, :, 0:wide] = part.astype(BF)
        desc = pltpu.make_async_copy(stg.at[n % 2, :, pl.ds(0, wide)], dst, local.at[6 + n % 2])
        desc.start()
        writes.append(desc)

    for n in range(0, width, size):
        part = tn(act[0, :, n : n + size], mix[0]) + tn(act[1, :, n : n + size], mix[1])
        write(part, g1.at[pl.ds(n, size)], units)
    plan.hook()
    da_copy.wait_recv()
    out_copy.wait_send()

    def fn(at):
        da = gh[at, :] + prc[at, :].astype(F32)
        top = dt[c, at, :].astype(F32)
        normed, inv = normalize(hid[at, :])
        grad = top + norm_back(da * row(rows_all, 7), normed, inv)
        gh[at, :] = grad
        normed_b, inv_b = normalize(br[at, :])
        down = norm_back(grad * row(rows_all, 5), normed_b, inv_b).astype(BF)
        dbuf[at, :] = down
        for n, value in enumerate((down.astype(F32), grad * normed_b, grad, da * normed, da, top)):
            sums[n] += fold(value)

    row_steps(span, 64, fn)
    plan.hook()
    weights_o = wov[...].reshape(width, width)
    da_copy.wait_send()
    for j in range(group):
        at = slice(j * part_size, (j + 1) * part_size)
        prb[:, at] = (nt(dbuf[...], weights_o[at, :]) * lanes[:, at]).astype(BF)
    for copy in outgoing:
        copy.go()
    keep = pltpu.make_async_copy(give(s), do.at[mine_at], local.at[8])
    keep.start()
    plan.hook()
    for n in range(0, width, size):
        write(tn(own[:, n : n + size], dbuf[...]), go.at[pl.ds(n, size)], width)
    rows_g[...] = jnp.zeros(rows_g.shape, F32)
    for n in range(6):
        rows_g[4 + n : 5 + n, :] = jnp.sum(sums[n], 0, keepdims=True)
    wide_g[...] = jnp.zeros(wide_g.shape, F32)
    for n in range(NZ * NY * NX):
        at = pl.ds(pl.multiple_of((n * NC + c) * lane, lane), lane)
        for j in range(3):
            wide_g[j : j + 1, at] = jnp.sum(colsums[j, :, n * lane : (n + 1) * lane], 0, keepdims=True)
    plan.finish()
    for k in range(NZ):
        zk = place.zup((1, 2, 3, 0)[k])
        for src, dst, n in ((g2.at[zk, y, x, one], half2, 9), (g2.at[zk, y, x, two], half3, 10)):
            desc = pltpu.make_async_copy(src, dst.at[k], local.at[n + 2 * k])
            desc.start()
            writes.append(desc)
    for desc in writes[-2 * NZ :]:
        desc.wait()
    writes = writes[: -2 * NZ]
    keep.wait()
    for copy in outgoing:
        copy.wait_recv()
    for desc in writes[-2:]:
        desc.wait()
    wire.drain()


def feed_forward(own, rows_all, wide_all, lanes, tok, cot, f2, wo, f1):
    span, width = own.shape
    units = f1.shape[4]
    group = NX * NC
    per = f2.shape[3]
    out = (
        (VM, (span, width), BF),
        (HBM, (group * span, width // group), BF),
        (VM, (span, width), F32),
        (HBM, (width, units), BF),
        (HBM, (width, width), BF),
        (HBM, (NZ, per // 2, width), BF),
        (HBM, (NZ, per // 2, width), BF),
        (VM, (32, width), F32),
        (VM, (8, wide_all.shape[1]), F32),
    )
    scratch = [
        pltpu.VMEM(wo.shape, BF),
        pltpu.VMEM(f1.shape, BF),
        pltpu.VMEM((NZ, NY, NX) + (per, width), BF),
        pltpu.VMEM((NC, span, width), BF),
        pltpu.VMEM((NC, span, width), BF),
        pltpu.VMEM((NC, span, units), F32),
        pltpu.VMEM((NC, span, units), BF),
        pltpu.VMEM((NC, span, units), BF),
        pltpu.VMEM((span, units), F32),
        pltpu.VMEM((span, width), F32),
        pltpu.VMEM((span, width), F32),
        pltpu.VMEM((NZ, NY, NX) + (per, width), BF),
        pltpu.VMEM((span, width), BF),
        pltpu.VMEM((span, width), BF),
        pltpu.VMEM((span, width), BF),
        pltpu.VMEM((2, 128, units), BF),
        pltpu.VMEM((8, units), F32),
    ]
    scratch += [pltpu.VMEM((NC, span, 128), F32)] * 4
    scratch += [pltpu.VMEM((6, 16, width), F32), pltpu.VMEM((3, 16, units), F32)]
    scratch += plane_scratch((per // 2, width))[1:3] * 2
    scratch += [
        pltpu.SemaphoreType.DMA((COPIES,)),
        pltpu.SemaphoreType.DMA((COPIES,)),
        pltpu.SemaphoreType.DMA((17,)),
    ]
    return pl.pallas_call(
        ffn_kernel,
        out_shape=tuple(jax.ShapeDtypeStruct(shape, dtype) for _, shape, dtype in out),
        in_specs=[VM] * 4 + [HBM] * 5,
        out_specs=[spec for spec, _, _ in out],
        scratch_shapes=scratch,
        compiler_params=pltpu.CompilerParams(
            collective_id=3, has_side_effects=True, vmem_limit_bytes=63 * 1024 * 1024
        ),
        name="feed_forward",
    )(own, rows_all, wide_all, lanes, tok, cot, f2, wo, f1)


def fast(tokens, doc_ids, cotangent, w_qkv, w_out, attn_vecs, head_scale, w_fc1, w_fc2, ffn_vecs, ffn_wide):
    _, span, width = tokens.shape
    group = NX * NC
    length = span * group
    head_count = head_scale.shape[0]
    head = width // head_count
    heads = head_count // group
    part = heads * head
    seq = lax.axis_index("seq")
    chips = NZ * NY * NX
    block = w_fc2.shape[0]
    units = chips * block

    rows = w_qkv.shape[0]
    narrow = jnp.concatenate([attn_vecs, ffn_vecs], 0)
    count, each = narrow.shape
    lane = each * group
    column = lax.broadcasted_iota(jnp.int32, (16, lane), 1) // each
    narrow = jnp.pad(jnp.tile(narrow, (1, group)), ((0, 16 - count), (0, 0)))
    narrow = jnp.where(column == seq, narrow, 0.0)
    vec = jnp.stack([narrow, jnp.pad(ffn_wide, ((0, 16 - ffn_wide.shape[0]), (0, 0)))]).astype(BF)
    tok = tokens.reshape(span, width)
    lanes = jnp.repeat(head_scale, head).reshape(1, width)
    ids = doc_ids.reshape(length)
    act_one, q, k, v, att, lse, scaled_own, wq, rows_all, wide_all, wo, fc1, fc2 = forward(
        tok, w_qkv, vec, w_out, w_fc1, w_fc2, ids, lanes, heads
    )
    outputs, do, grad_hidden, grad_fc1, grad_out, half2, half3, rows_in, wide_grads = feed_forward(
        scaled_own,
        rows_all,
        wide_all,
        lanes,
        tok,
        cotangent.reshape(span, width),
        fc2,
        wo,
        fc1,
    )
    grad_tokens, grad_w1, grad_w2, grad_wo, grad_wqkv, rows_out, wide_out = backward(
        do,
        q,
        k,
        v,
        att,
        lse,
        ids,
        wq,
        tok,
        grad_hidden,
        rows_in,
        wide_grads,
        rows_all,
        act_one,
        grad_fc1.reshape(NZ, NY, NX, NC * rows, units),
        grad_out.reshape(NZ, NY, NX, NC, rows, width),
        half2,
        half3,
        heads,
    )
    mine = lax.dynamic_slice_in_dim(rows_out, seq * each, each, 1)
    wide_mine = lax.dynamic_slice_in_dim(wide_out, seq * block, block, 1)
    return (
        outputs.reshape(1, span, width),
        grad_tokens.reshape(1, span, width),
        grad_wqkv,
        grad_wo,
        mine[: attn_vecs.shape[0]],
        rows_out[16 : 16 + head_count, 0] / head_scale,
        grad_w1,
        grad_w2,
        mine[attn_vecs.shape[0] : count],
        wide_mine[: ffn_wide.shape[0]],
    )


def solution(mesh):
    placed = (
        P("dp", "seq", None),
        P("dp", None),
        P("dp", "seq", None),
        P(("dp", "seq"), None),
        P(("dp", "seq"), None),
        P(None, ("dp", "seq")),
        P(),
        P(("dp", "seq"), None),
        P(("dp", "seq"), None),
        P(None, ("dp", "seq")),
        P(None, ("dp", "seq")),
    )
    results = (
        P("dp", "seq", None),
        P("dp", "seq", None),
        P(("dp", "seq"), None),
        P(("dp", "seq"), None),
        P(None, ("dp", "seq")),
        P(),
        P(("dp", "seq"), None),
        P(("dp", "seq"), None),
        P(None, ("dp", "seq")),
        P(None, ("dp", "seq")),
    )
    suits = mesh.shape["dp"] == NZ * NY and mesh.shape["seq"] == NX * NC
    return jax.shard_map(
        fast if suits else local, mesh=mesh, in_specs=placed, out_specs=results, check_vma=False
    )
```
